32 devices in a mesh: fsdp: 8 (over y, x, core), dp: 4 (over z).
Axes of the slice: x: 2, y: 2, z: 4, core: 2. Of those that a mesh axis runs over, the one named last changes fastest.
Arguments:
- tokens: bfloat16 [8192, 2048], P(('fsdp', 'dp')), may hold values from -6 to 6
- cotangent: bfloat16 [8192, 2048], P(('fsdp', 'dp')), may hold values from -6 to 6
- order: int32 [32, 256], P(('fsdp', 'dp')), may hold values from 0 to 255, each once within a row
- lengths: int32 [64, 3], P(('fsdp', 'dp')), may hold values from 1 to 96, 128 in all within a row
- w_qkv: float32 [2048, 3072], P(('fsdp', 'dp')), may hold values from -0.125 to 0.125
- w_out: float32 [2048, 2048], P(('fsdp', 'dp')), may hold values from -0.375 to 0.375
- w_gate_up: float32 [2048, 16384], P(('fsdp', 'dp')), may hold values from -0.125 to 0.125
- w_down: float32 [8192, 2048], P(('fsdp', 'dp')), may hold values from -0.0625 to 0.0625
- gains: float32 [4224], replicated, may hold values from 0.5 to 7
- first_qkv: float32 [2048, 3072], P(('fsdp', 'dp')), may hold values from -9.1552734e-05 to 9.1552734e-05
- first_out: float32 [2048, 2048], P(('fsdp', 'dp')), may hold values from -9.1552734e-05 to 9.1552734e-05
- first_gate_up: float32 [2048, 16384], P(('fsdp', 'dp')), may hold values from -9.1552734e-05 to 9.1552734e-05
- first_down: float32 [8192, 2048], P(('fsdp', 'dp')), may hold values from -9.1552734e-05 to 9.1552734e-05
- first_gains: float32 [4224], replicated, may hold values from -0.00036621094 to 0.00036621094
- second_qkv: float32 [2048, 3072], P(('fsdp', 'dp')), may hold values from 8.714005e-10 to 3.452719e-09
- second_out: float32 [2048, 2048], P(('fsdp', 'dp')), may hold values from 8.714005e-10 to 3.452719e-09
- second_gate_up: float32 [2048, 16384], P(('fsdp', 'dp')), may hold values from 8.714005e-10 to 3.452719e-09
- second_down: float32 [8192, 2048], P(('fsdp', 'dp')), may hold values from 8.714005e-10 to 3.452719e-09
- second_gains: float32 [4224], replicated, may hold values from 1.3810876e-08 to 5.5901165e-08
Outputs:
- mixed: bfloat16 [8192, 2048], P(('fsdp', 'dp'))
- input_grad: float32 [8192, 2048], P(('fsdp', 'dp'))
- grad_norm: float32 [], replicated
- new_qkv: float32 [2048, 3072], P(('fsdp', 'dp'))
- new_out: float32 [2048, 2048], P(('fsdp', 'dp'))
- new_gate_up: float32 [2048, 16384], P(('fsdp', 'dp'))
- new_down: float32 [8192, 2048], P(('fsdp', 'dp'))
- new_gains: float32 [4224], replicated
- next_first_qkv: float32 [2048, 3072], P(('fsdp', 'dp'))
- next_first_out: float32 [2048, 2048], P(('fsdp', 'dp'))
- next_first_gate_up: float32 [2048, 16384], P(('fsdp', 'dp'))
- next_first_down: float32 [8192, 2048], P(('fsdp', 'dp'))
- next_first_gains: float32 [4224], replicated
- next_second_qkv: float32 [2048, 3072], P(('fsdp', 'dp'))
- next_second_out: float32 [2048, 2048], P(('fsdp', 'dp'))
- next_second_gate_up: float32 [2048, 16384], P(('fsdp', 'dp'))
- next_second_down: float32 [8192, 2048], P(('fsdp', 'dp'))
- next_second_gains: float32 [4224], replicated
The draws below stay inside these ranges and needn't reach their ends.
Inputs may be any that keep to these rules, and one draw needn't show every extreme that they name: `order`: each row is a permutation. Each row holds 3 lengths summing to 128; the last length of a row is padding.
All inputs are finite; a program needn't handle non-finite values.
Results may differ from the reference program's by a relative error of at most 0.025.
Values may be sent and summed in bfloat16 or wider, within the bound.
A program may use at most 512 MiB of HBM per device.

```python
import math
import jax
import jax.numpy as jnp
import numpy as np
from jax import lax

D = 2048
HEADS = 32
HD = 64
KVH = 8
FF = 8192
TOK_DEV = 256
MB = 2
SEQS = 3
STEP = 10
MB_TOK = 128
SEQ_MOST = 96
QKV = 3072
GN = 4224
NBLK = 32
TOKENS = 8192
NPARAM = 60821632


def draw_gains(key, part):
    key = jax.random.fold_in(key, 7)
    wide_key, small_key = jax.random.split(key)
    top_gain = 3.0
    rough = jnp.exp(jax.random.uniform(wide_key, (2, D), jnp.float32, -0.2, 0.2))
    ramp = 1.0 + (top_gain - 1.0) * jnp.arange(D, dtype=jnp.float32) / (D - 1)
    wide_part = (ramp[None, :] * rough).reshape(2 * D)
    small_part = jax.random.uniform(small_key, (2 * HD,), jnp.float32, 0.6, 1.6)
    return jnp.concatenate([wide_part, small_part])


def steps_of(stream_key, extent, cuts, smallest, largest):
    def one(axis_at, blocks):
        heights = jax.random.uniform(jax.random.fold_in(jax.random.fold_in(stream_key, 6), axis_at), (blocks,), jnp.float32, smallest / len(cuts), largest / len(cuts))
        return jnp.repeat(jnp.exp(heights), extent[axis_at] // blocks).reshape((-1,) + (1,) * (len(extent) - axis_at - 1))

    loudness = one(*cuts[0])
    for cut in cuts[1:]:
        loudness = loudness * one(*cut)
    return loudness


def profile(count, total, limit, skew):
    loads = [(1 << 20) // math.isqrt(standing ** skew) + 1 for standing in range(2, count + 1)]
    rest, counts = total - limit - (count - 1), [1] * (count - 1)
    while rest > 0:
        free = [i for i in range(count - 1) if counts[i] < limit]
        whole, remaining = sum([loads[i] for i in free]), rest
        for i in free:
            extra = min(limit - counts[i], max(1, remaining * loads[i] // whole), rest)
            counts[i] = counts[i] + extra
            rest = rest - extra
    return np.array([limit] + counts)


def uneven(stream_key, amount, total, limit, skew):
    if amount == 2:
        one = jax.random.randint(stream_key, (), max(1, total - limit), min(limit, total - 1) + 1)
        return jnp.stack([one, total - one])
    sizes = jnp.asarray(profile(amount, total, limit, skew), jnp.int32)
    twos = (amount - 1) // 2
    donor, sink = sizes[1:1 + 2 * twos:2], sizes[2:2 + 2 * twos:2]
    room = jnp.minimum(donor - 1, limit - sink)
    moved = jax.random.randint(jax.random.fold_in(stream_key, 1), (twos,), 0, 1 << 20) % (room + 1)
    sizes = sizes.at[1:1 + 2 * twos:2].set(donor - moved).at[2:2 + 2 * twos:2].set(sink + moved)
    return sizes[jax.random.permutation(jax.random.fold_in(stream_key, 2), amount)]


def normal_values(own_key, dims, width, reach, cuts=(), kind=jnp.bfloat16):
    entries = jax.random.normal(own_key, dims, jnp.float32) * width
    if len(cuts) > 0:
        entries = steps_of(own_key, dims, cuts, -0.22, 0.18) * entries
    return jnp.clip(entries, min=-reach, max=reach).astype(kind)


def setup_inputs(seed: int = 0) -> dict:
    keys = jax.random.split(jax.random.key(seed), 20)
    tokens = normal_values(keys[0], (TOKENS, D), 1.0, 6.0, ((0, 32),))
    cotangent = normal_values(keys[1], (TOKENS, D), 1.0, 6.0, ((0, 32),))
    order = jax.vmap(lambda own: jax.random.permutation(own, TOK_DEV))(jax.random.split(keys[2], NBLK)).reshape((NBLK, TOK_DEV)).astype(jnp.int32)
    lengths = jax.vmap(lambda own: uneven(own, SEQS, MB_TOK, SEQ_MOST, 2))(jax.random.split(keys[3], (NBLK * MB))).reshape((NBLK * MB, SEQS)).astype(jnp.int32)
    w_qkv = normal_values(keys[4], (D, QKV), D ** -0.5, 0.125, ((0, 32),), jnp.float32)
    w_out = normal_values(keys[5], (D, D), (D // 8) ** -0.5, 0.375, ((0, 32),), jnp.float32)
    w_gate_up = normal_values(keys[6], (D, 2 * FF), D ** -0.5, 0.125, ((0, 32),), jnp.float32)
    w_down = normal_values(keys[7], (FF, D), FF ** -0.5, 0.0625, ((0, 32),), jnp.float32)
    gains = draw_gains(jax.random.fold_in(keys[19], 71), 0)
    first_qkv = normal_values(keys[9], (D, QKV), (0.11 * NPARAM ** (0 - 0.5)), 9.1552734375e-05, ((0, 32),), jnp.float32)
    first_out = normal_values(keys[10], (D, D), (0.11 * NPARAM ** (0 - 0.5)), 9.1552734375e-05, ((0, 32),), jnp.float32)
    first_gate_up = normal_values(keys[11], (D, 2 * FF), (0.11 * NPARAM ** (0 - 0.5)), 9.1552734375e-05, ((0, 32),), jnp.float32)
    first_down = normal_values(keys[12], (FF, D), (0.11 * NPARAM ** (0 - 0.5)), 9.1552734375e-05, ((0, 32),), jnp.float32)
    first_gains = normal_values(keys[13], (GN,), (0.44 * NPARAM ** (0 - 0.5)), 0.00036621094, (), jnp.float32)
    second_qkv = jnp.clip(jnp.exp(math.log(3.452718999596982e-09) - 1.37681562 * jax.random.uniform(keys[14], (D, QKV), jnp.float32) ** steps_of(keys[14], (D, QKV), ((0, 32),), -0.2, 0.2)), 8.714005073073849e-10, 3.452718999596982e-09)
    second_out = jnp.clip(jnp.exp(math.log(3.452718999596982e-09) - 1.37681562 * jax.random.uniform(keys[15], (D, D), jnp.float32) ** steps_of(keys[15], (D, D), ((0, 32),), -0.2, 0.2)), 8.714005073073849e-10, 3.452718999596982e-09)
    second_gate_up = jnp.clip(jnp.exp(math.log(3.452718999596982e-09) - 1.37681562 * jax.random.uniform(keys[16], (D, 2 * FF), jnp.float32) ** steps_of(keys[16], (D, 2 * FF), ((0, 32),), -0.2, 0.2)), 8.714005073073849e-10, 3.452718999596982e-09)
    second_down = jnp.clip(jnp.exp(math.log(3.452718999596982e-09) - 1.37681562 * jax.random.uniform(keys[17], (FF, D), jnp.float32) ** steps_of(keys[17], (FF, D), ((0, 32),), -0.2, 0.2)), 8.714005073073849e-10, 3.452718999596982e-09)
    second_gains = jnp.clip(jnp.exp(jax.random.uniform(keys[18], (GN,), jnp.float32, math.log(1.3810875998387928e-08), math.log(5.590116458620287e-08))), 1.3810875998387928e-08, 5.590116458620287e-08)
    return {"tokens": tokens, "cotangent": cotangent, "order": order, "lengths": lengths, "w_qkv": w_qkv, "w_out": w_out, "w_gate_up": w_gate_up, "w_down": w_down, "gains": gains, "first_qkv": first_qkv, "first_out": first_out, "first_gate_up": first_gate_up, "first_down": first_down, "first_gains": first_gains, "second_qkv": second_qkv, "second_out": second_out, "second_gate_up": second_gate_up, "second_down": second_down, "second_gains": second_gains}


EPSILON = 1e-05
ROPE_BASE = 1000000.0
FIRST_DECAY = 0.9
SECOND_DECAY = 0.95
LEARN_RATE = 0.05
GAIN_RATE = 2.0
WEIGHT_DECAY = 0.1
ADAM_EPSILON = 1e-08
CLIP_NORM = 1.0
MASKED = -1e+30
HIGHEST = lax.Precision.HIGHEST

@jax.custom_vjp
def low(v):
    return lax.optimization_barrier(v.astype(jnp.bfloat16)).astype(jnp.float32)

@jax.custom_vjp
def low_back(v):
    return v

def low_keep(v):
    return (low(v), None)

def low_pass(kept, grad):
    return (grad,)

def back_keep(v):
    return (v, None)

def back_low(kept, grad):
    return (low(grad),)
low.defvjp(low_keep, low_pass)
low_back.defvjp(back_keep, back_low)

def matmul(left_side, right_side):
    return jnp.dot(left_side, right_side, precision=HIGHEST, preferred_element_type=jnp.float32)

def rms_norm(values, gain_vec):
    return values * lax.rsqrt(lax.optimization_barrier(jnp.mean(values * values, axis=-1, keepdims=True)) + EPSILON) * gain_vec

def rope_tables(position):
    half_width = HD // 2
    frequency = ROPE_BASE ** (jnp.arange(half_width, dtype=jnp.float32) * (-2.0 / HD))
    angles = position[:, None] * frequency[None, :]
    return (jnp.cos(angles)[:, None, :], jnp.sin(angles)[:, None, :])

def rotate(values, cosine_table, sine_table):
    half_width = HD // 2
    first_part = values[..., :half_width]
    second_part = values[..., half_width:]
    return jnp.concatenate([first_part * cosine_table - second_part * sine_table, second_part * cosine_table + first_part * sine_table], axis=-1)

def layout(lengths_row):
    seq_ends = jnp.cumsum(lengths_row).astype(jnp.int32)
    places = jnp.arange(MB_TOK, dtype=jnp.int32)
    passed = (places[:, None] >= seq_ends[None, :]).astype(jnp.int32)
    segment = lax.optimization_barrier(jnp.sum(passed, axis=1)).astype(jnp.int32)
    starts = lax.optimization_barrier(jnp.sum(passed * lengths_row[None, :], axis=1)).astype(jnp.int32)
    position = (places - starts).astype(jnp.float32)
    valid_rows = (segment < SEQS - 1).astype(jnp.float32)
    allowed = (segment[:, None] == segment[None, :]) & (places[None, :] <= places[:, None])
    return (position, valid_rows, allowed)

def micro_block(rows_in, lengths_row, w_qkv, w_out, w_gate_up, w_down, gains):
    position, valid_rows, allowed = layout(lengths_row)
    attn_gain = gains[:D]
    ffn_gain = gains[D:2 * D]
    query_gain = gains[2 * D:2 * D + HD]
    key_gain = gains[2 * D + HD:]
    kv_width = KVH * HD
    normed_one = low(rms_norm(rows_in, attn_gain))
    projected = low_back(matmul(normed_one, low(w_qkv)))
    query_raw = projected[:, :D].reshape(MB_TOK, HEADS, HD)
    key_raw = projected[:, D:D + kv_width].reshape(MB_TOK, KVH, HD)
    values_low = low(projected[:, D + kv_width:].reshape(MB_TOK, KVH, HD))
    cosine_table, sine_table = rope_tables(position)
    queries = low(rotate(rms_norm(query_raw, query_gain), cosine_table, sine_table))
    queries = queries.reshape(MB_TOK, KVH, HEADS // KVH, HD)
    keys_rot = low(rotate(rms_norm(key_raw, key_gain), cosine_table, sine_table))
    scores = jnp.einsum('tkgd,ukd->kgtu', queries, keys_rot, precision=HIGHEST) * HD ** (-0.5)
    scores = low_back(scores)
    scores = jnp.where(allowed, scores, MASKED)
    row_peak = lax.optimization_barrier(jnp.max(scores, axis=-1, keepdims=True))
    powers = jnp.exp(scores - row_peak)
    weights = low(powers / lax.optimization_barrier(jnp.sum(powers, axis=-1, keepdims=True)))
    attended = jnp.einsum('kgtu,ukd->tkgd', weights, values_low, precision=HIGHEST).reshape(MB_TOK, D)
    attended = low(low_back(attended))
    hidden = rows_in + valid_rows[:, None] * low_back(matmul(attended, low(w_out)))
    normed_two = low(rms_norm(hidden, ffn_gain))
    gate_up = low_back(matmul(normed_two, low(w_gate_up)))
    activation = low(jax.nn.silu(gate_up[:, :FF]) * gate_up[:, FF:])
    return hidden + valid_rows[:, None] * low_back(matmul(activation, low(w_down)))

def device_rows(rows_all, order_row, lengths_rows, w_qkv, w_out, w_gate_up, w_down, gains):
    packed = rows_all[order_row].reshape(MB, MB_TOK, D)
    outputs = jax.vmap(micro_block, in_axes=(0, 0, None, None, None, None, None))(packed, lengths_rows, w_qkv, w_out, w_gate_up, w_down, gains)
    places = jnp.arange(TOK_DEV, dtype=jnp.int32)
    inverse = jnp.zeros((TOK_DEV,), jnp.int32).at[order_row].set(places)
    return outputs.reshape(TOK_DEV, D)[inverse]

def forward(tokens_all, w_qkv, w_out, w_gate_up, w_down, gains, order, lengths):
    blocks = tokens_all.reshape(NBLK, TOK_DEV, D)
    lengths_all = lengths.reshape(NBLK, MB, SEQS)
    saved_rows = jax.checkpoint(device_rows)

    def advance(scan_carry, scan_items):
        return (scan_carry, saved_rows(scan_items[0], scan_items[1], scan_items[2], w_qkv, w_out, w_gate_up, w_down, gains))
    scan_carry, results = lax.scan(advance, jnp.zeros((), jnp.float32), (blocks, order, lengths_all))
    return results.reshape(TOKENS, D)

def adam_step(weight, first_state, second, gradient, factor, step_rate, decay_rate):
    clipped = gradient * factor
    first_new = FIRST_DECAY * first_state + (1.0 - FIRST_DECAY) * clipped
    second_new = SECOND_DECAY * second + (1.0 - SECOND_DECAY) * clipped * clipped
    first_hat = first_new / (1.0 - FIRST_DECAY ** STEP)
    second_hat = second_new / (1.0 - SECOND_DECAY ** STEP)
    weight_new = weight - step_rate * (first_hat / (jnp.sqrt(second_hat) + ADAM_EPSILON) + decay_rate * weight)
    return (weight_new, first_new, second_new)

def reference(tokens, cotangent, order, lengths, w_qkv, w_out, w_gate_up, w_down, gains, first_qkv, first_out, first_gate_up, first_down, first_gains, second_qkv, second_out, second_gate_up, second_down, second_gains):

    def run_layer(tokens_all, qkv_weight, out_weight, gate_up_weight, down_weight, gain_all):
        return forward(tokens_all, qkv_weight, out_weight, gate_up_weight, down_weight, gain_all, order, lengths)
    result, pullback = jax.vjp(run_layer, tokens.astype(jnp.float32), w_qkv, w_out, w_gate_up, w_down, gains)
    gradients = pullback(cotangent.astype(jnp.float32))
    square_sum = jnp.zeros((), jnp.float32)
    for gradient in gradients[1:]:
        square_sum = square_sum + jnp.sum(gradient * gradient)
    global_norm = jnp.sqrt(square_sum)
    factor = CLIP_NORM / jnp.maximum(global_norm, CLIP_NORM)
    new_qkv, next_first_qkv, next_second_qkv = adam_step(w_qkv, first_qkv, second_qkv, gradients[1], factor, LEARN_RATE, WEIGHT_DECAY)
    new_out, next_first_out, next_second_out = adam_step(w_out, first_out, second_out, gradients[2], factor, LEARN_RATE, WEIGHT_DECAY)
    new_gate_up, next_first_gate_up, next_second_gate_up = adam_step(w_gate_up, first_gate_up, second_gate_up, gradients[3], factor, LEARN_RATE, WEIGHT_DECAY)
    new_down, next_first_down, next_second_down = adam_step(w_down, first_down, second_down, gradients[4], factor, LEARN_RATE, WEIGHT_DECAY)
    new_gains, next_first_gains, next_second_gains = adam_step(gains, first_gains, second_gains, gradients[5], factor, GAIN_RATE, 0.0)
    return (result.astype(jnp.bfloat16), gradients[0], global_norm, new_qkv, new_out, new_gate_up, new_down, new_gains, next_first_qkv, next_first_out, next_first_gate_up, next_first_down, next_first_gains, next_second_qkv, next_second_out, next_second_gate_up, next_second_down, next_second_gains)
```

```python
import functools

import jax
import jax.numpy as jnp
from jax import lax
from jax.experimental import pallas as pl
from jax.experimental.pallas import tpu as pltpu
from jax.sharding import PartitionSpec as P

D = 2048
HEADS = 32
HD = 64
KVH = 8
FF = 8192
TOK_DEV = 256
MB = 2
SEQS = 3
STEP = 10
MB_TOK = 128


EPSILON = 1e-05
ROPE_BASE = 1000000.0
FIRST_DECAY = 0.9
SECOND_DECAY = 0.95
LEARN_RATE = 0.05
GAIN_RATE = 2.0
WEIGHT_DECAY = 0.1
ADAM_EPSILON = 1e-08
CLIP_NORM = 1.0
GAIN_LINES = (2 * D + 2 * HD) // 128
MASKED = -1e30


def rms_norm(values, gain_vec):
    return (
        values * lax.rsqrt(jnp.mean(values * values, axis=-1, keepdims=True) + EPSILON) * gain_vec
    )


def rope_tables(position):
    half_width = HD // 2
    frequency = ROPE_BASE ** (jnp.arange(half_width, dtype=jnp.float32) * (-2.0 / HD))
    angles = position[:, None] * frequency[None, :]
    return (jnp.cos(angles)[:, None, :], jnp.sin(angles)[:, None, :])


def rotate(values, cosine_table, sine_table):
    half_width = HD // 2
    first_part = values[..., :half_width]
    second_part = values[..., half_width:]
    return jnp.concatenate(
        [
            first_part * cosine_table - second_part * sine_table,
            second_part * cosine_table + first_part * sine_table,
        ],
        axis=-1,
    )


def layout(lengths_rows):
    seq_ends = jnp.cumsum(lengths_rows, axis=-1)
    places = jnp.arange(MB_TOK, dtype=jnp.int32)
    passed = (places[None, :, None] >= seq_ends[:, None, :]).astype(jnp.int32)
    segment = jnp.sum(passed, axis=-1)
    starts = jnp.sum(passed * lengths_rows[:, None, :], axis=-1)
    position = (places[None, :] - starts).astype(jnp.float32)
    valid_rows = (segment < SEQS - 1).astype(jnp.float32)
    allowed = (segment[:, :, None] == segment[:, None, :]) & (
        places[None, None, :] <= places[None, :, None]
    )
    return (position, valid_rows, allowed)


def swiglu(gate, up):
    return jax.nn.silu(gate) * up


def column_product(left_side, right_side):
    return lax.dot_general(
        left_side, right_side, (((0,), (0,)), ((), ())), preferred_element_type=jnp.float32
    )


def contract_last(left_side, right_side):
    return lax.dot_general(
        left_side, right_side, (((1,), (1,)), ((), ())), preferred_element_type=jnp.float32
    )


def product(left_side, right_side):
    return jnp.dot(left_side, right_side, preferred_element_type=jnp.float32)


def adam_step(weight, first_state, second, gradient, factor, step_rate, decay_rate):
    clipped = gradient * factor
    first_new = FIRST_DECAY * first_state + (1.0 - FIRST_DECAY) * clipped
    second_new = SECOND_DECAY * second + (1.0 - SECOND_DECAY) * clipped * clipped
    first_hat = first_new / (1.0 - FIRST_DECAY**STEP)
    second_hat = second_new / (1.0 - SECOND_DECAY**STEP)
    weight_new = weight - step_rate * (
        first_hat / (jnp.sqrt(second_hat) + ADAM_EPSILON) + decay_rate * weight
    )
    return (weight_new, first_new, second_new)


MESH = pl.DeviceIdType.MESH
ANY = pl.BlockSpec(memory_space=pl.ANY)
VMEM = pl.BlockSpec(memory_space=pltpu.VMEM)
PLANE = 8
TILE = 512
GLU_TILE = 256
SHORT = pl.CostEstimate(flops=0, bytes_accessed=1024, transcendentals=0)


def flip(index, bit):
    step = 2**bit
    return index + step * (1 - 2 * lax.rem(lax.div(index, step), 2))


def plane_others(me):
    others = []
    for number in range(1, PLANE):
        other = me
        for bit in range(3):
            if (number >> bit) & 1:
                other = flip(other, bit)
        others.append(other)
    return others


def greet(devices):
    barrier = pltpu.get_barrier_semaphore()
    for device in devices:
        pl.semaphore_signal(barrier, inc=1, device_id={"fsdp": device}, device_id_type=MESH)
    pl.semaphore_wait(barrier, len(devices))


def half_pieces(half_ref, wide_ref, me, other, count):
    half_width = half_ref.shape[1] // 2
    for side in range(2):
        first = pl.multiple_of(side * half_width * PLANE + me * half_width, 128)
        source = half_ref.at[pl.ds(pl.multiple_of(other * count, count), count)]
        yield (
            source.at[:, pl.ds(side * half_width, half_width)],
            wide_ref.at[:, pl.ds(first, half_width)],
        )


def put_half(half_ref, wide_ref, others, number, sems):
    me, other = lax.axis_index("fsdp"), others[number - 1]
    pairs = half_pieces(half_ref, wide_ref, me, other, wide_ref.shape[0])
    return [
        pltpu.make_async_remote_copy(
            src_ref=source,
            dst_ref=target,
            send_sem=sems.at[0, 2 * number + side],
            recv_sem=sems.at[1, 2 * number + side],
            device_id={"fsdp": other},
            device_id_type=MESH,
        )
        for side, (source, target) in enumerate(pairs)
    ]


def keep_half(half_ref, wide_ref, sems):
    me = lax.axis_index("fsdp")
    return [
        pltpu.make_async_copy(source, target, sems.at[side])
        for side, (source, target) in enumerate(
            half_pieces(half_ref, wide_ref, me, me, wide_ref.shape[0])
        )
    ]


def columns_kernel(half_ref, wide_ref, squares_ref, own_sem, sems):
    others = plane_others(lax.axis_index("fsdp"))
    greet(others)
    order = (6, 7, 2, 4, 3, 5, 1)
    for number in order:
        for copy in put_half(half_ref, wide_ref, others, number, sems):
            copy.start()
    keep = keep_half(half_ref, wide_ref, own_sem)
    for copy in keep:
        copy.start()
    squares_ref[...] = jnp.zeros_like(squares_ref)

    @pl.loop(0, half_ref.shape[0] // 128)
    def _(step):
        spot = pl.ds(pl.multiple_of(step * 128, 128), 128)
        values = half_ref[spot, :].astype(jnp.float32)
        squares_ref[...] += jnp.sum(values * values, axis=0, keepdims=True)

    for number in order:
        for copy in put_half(half_ref, wide_ref, others, number, sems):
            copy.wait()
    for copy in keep:
        copy.wait()


def half_scratch():
    return [pltpu.SemaphoreType.DMA((2,)), pltpu.SemaphoreType.DMA((2, 2 * PLANE))]


def exchange_half(half, count, number):
    return pl.pallas_call(
        columns_kernel,
        out_shape=[
            jax.ShapeDtypeStruct((count, half.shape[1] * PLANE), half.dtype),
            jax.ShapeDtypeStruct((1, half.shape[1]), jnp.float32),
        ],
        in_specs=[VMEM],
        out_specs=[ANY, VMEM],
        scratch_shapes=half_scratch(),
        compiler_params=pltpu.CompilerParams(collective_id=number, has_side_effects=True),
        cost_estimate=SHORT,
        name=f"exchange_half_{number}",
    )(half)


def sum_kernel(
    nd,
    x_ref,
    blocks_ref,
    out_ref,
    norm_ref,
    qkv_ref,
    gout_ref,
    swapped_ref,
    plane_in,
    line_in,
    total,
    mine,
    own_sem,
    plane_sems,
    line_sems,
    block_sems,
):
    me, line = lax.axis_index("fsdp"), lax.axis_index("dp")
    wide = swapped_ref.shape[2]
    q_width = wide - 2 * HD
    blocks = blocks_ref[...].astype(jnp.float32)
    squares = jnp.sum(blocks * blocks, axis=(0, 1, 2), keepdims=True).reshape(1, 1)
    lines = lax.broadcasted_iota(jnp.int32, x_ref.shape, 0)
    lane = lax.broadcasted_iota(jnp.int32, x_ref.shape, 1)
    spot = jnp.logical_and(lines == GAIN_LINES, lane == 0)
    mine[...] = x_ref[...] + jnp.where(spot, squares, 0.0)
    others = plane_others(me)
    steps = [lax.rem(line + step, nd) for step in range(1, nd)]
    barrier = pltpu.get_barrier_semaphore()
    for other in others:
        pl.semaphore_signal(barrier, inc=1, device_id={"fsdp": other}, device_id_type=MESH)
    for other in steps:
        pl.semaphore_signal(barrier, inc=1, device_id={"dp": other}, device_id_type=MESH)
    pl.semaphore_wait(barrier, len(others) + len(steps))

    def to_plane(number):
        return pltpu.make_async_remote_copy(
            src_ref=mine,
            dst_ref=plane_in.at[me],
            send_sem=plane_sems.at[0, number],
            recv_sem=plane_sems.at[1, number],
            device_id={"fsdp": others[number]},
            device_id_type=MESH,
        )

    def to_line(number):
        return pltpu.make_async_remote_copy(
            src_ref=total,
            dst_ref=line_in.at[line],
            send_sem=line_sems.at[0, number],
            recv_sem=line_sems.at[1, number],
            device_id={"dp": steps[number]},
            device_id_type=MESH,
        )

    def put_block(number):
        return pltpu.make_async_remote_copy(
            src_ref=blocks_ref.at[others[number], :, pl.ds(0, wide)],
            dst_ref=swapped_ref.at[me],
            send_sem=block_sems.at[0, number],
            recv_sem=block_sems.at[1, number],
            device_id={"fsdp": others[number]},
            device_id_type=MESH,
        )

    keep = [
        pltpu.make_async_copy(
            blocks_ref.at[me, :, pl.ds(0, wide)], swapped_ref.at[me], own_sem.at[PLANE]
        )
    ]
    for place in range(PLANE):
        keep.append(
            pltpu.make_async_copy(
                blocks_ref.at[place, :, pl.ds(wide, q_width)],
                gout_ref.at[:, pl.ds(place * q_width, q_width)],
                own_sem.at[place],
            )
        )
    for number in range(PLANE - 1):
        to_plane(number).start()
    for number in range(PLANE - 1):
        put_block(number).start()
    for copy in keep:
        copy.start()
    plane_in[me] = mine[...]
    for number in range(PLANE - 1):
        to_plane(number).wait()
    part = plane_in[0]
    for place in range(1, PLANE):
        part = part + plane_in[place]
    total[...] = part
    line_in[line] = part
    for number in range(nd - 1):
        to_line(number).start()
    for number in range(PLANE - 1):
        put_block(number).wait()
    for copy in keep:
        copy.wait()
    first_head = lax.broadcasted_iota(jnp.int32, (1, 2 * HD), 1) < HD
    for place in range(0, PLANE, 2):
        pair = []
        for block in (place, place + 1):
            values = swapped_ref[block].astype(jnp.float32)
            qkv_ref[:, block * q_width : (block + 1) * q_width] = swapped_ref[block, :, :q_width]
            pair.append(values[:, q_width:])
        columns = pl.ds(PLANE * q_width + place * HD, 2 * HD)
        both = jnp.where(first_head, pair[0], pltpu.roll(pair[1], HD, 1))
        qkv_ref[:, columns] = both.astype(qkv_ref.dtype)
        columns = pl.ds(PLANE * (q_width + HD) + place * HD, 2 * HD)
        both = jnp.where(first_head, pltpu.roll(pair[0], HD, 1), pair[1])
        qkv_ref[:, columns] = both.astype(qkv_ref.dtype)
    for number in range(nd - 1):
        to_line(number).wait()
    part = line_in[0]
    for place in range(1, nd):
        part = part + line_in[place]
    out_ref[...] = part
    gains = part[:GAIN_LINES]
    lane = lax.broadcasted_iota(jnp.int32, (1, 128), 1)
    squares = jnp.where(lane == 0, part[GAIN_LINES : GAIN_LINES + 1], 0.0)
    squares = squares + jnp.sum(gains * gains, axis=0, keepdims=True)
    norm = jnp.sqrt(jnp.sum(squares, axis=1, keepdims=True))
    factor = CLIP_NORM / jnp.maximum(norm, CLIP_NORM)
    line_number = lax.broadcasted_iota(jnp.int32, norm_ref.shape, 0)
    norm_ref[...] = jnp.where(line_number == 0, norm, factor)


def sum_everywhere(gain_sum, squares, blocks, wide, number):
    values = jnp.concatenate([gain_sum, squares.reshape(1)])
    nd = lax.axis_size("dp")
    count = values.shape[0]
    lines = -(-count // 1024) * 8
    padded = jnp.pad(values, (0, lines * 128 - count)).reshape(lines, 128)
    q_width = wide - 2 * HD
    summed, norm, grad_qkv, grad_out = pl.pallas_call(
        functools.partial(sum_kernel, nd),
        out_shape=[
            jax.ShapeDtypeStruct(padded.shape, jnp.float32),
            jax.ShapeDtypeStruct((8, 128), jnp.float32),
            jax.ShapeDtypeStruct((blocks.shape[1], PLANE * wide), blocks.dtype),
            jax.ShapeDtypeStruct((blocks.shape[1], PLANE * q_width), blocks.dtype),
        ],
        in_specs=[VMEM, VMEM],
        out_specs=[VMEM] * 4,
        scratch_shapes=[
            pltpu.VMEM((PLANE, blocks.shape[1], wide), blocks.dtype),
            pltpu.VMEM((PLANE,) + padded.shape, jnp.float32),
            pltpu.VMEM((nd,) + padded.shape, jnp.float32),
            pltpu.VMEM(padded.shape, jnp.float32),
            pltpu.VMEM(padded.shape, jnp.float32),
            pltpu.SemaphoreType.DMA((PLANE + 1,)),
            pltpu.SemaphoreType.DMA((2, PLANE - 1)),
            pltpu.SemaphoreType.DMA((2, nd - 1)),
            pltpu.SemaphoreType.DMA((2, PLANE - 1)),
        ],
        compiler_params=pltpu.CompilerParams(collective_id=number, has_side_effects=True),
        cost_estimate=SHORT,
        name=f"sum_everywhere_{number}",
    )(padded, blocks)
    return summed.reshape(-1)[: count - 1], norm, grad_qkv, grad_out


def greet_line(nd, others):
    line = lax.axis_index("dp")
    barrier = pltpu.get_barrier_semaphore()
    for other in others:
        pl.semaphore_signal(barrier, inc=1, device_id={"fsdp": other}, device_id_type=MESH)

    @pl.when(line < nd - 1)
    def _():
        pl.semaphore_signal(barrier, inc=1, device_id={"dp": line + 1}, device_id_type=MESH)

    @pl.when(line > 0)
    def _():
        pl.semaphore_signal(barrier, inc=1, device_id={"dp": line - 1}, device_id_type=MESH)

    neighbours = lax.div(line + nd - 1, nd) + lax.div(2 * nd - 2 - line, nd)
    pl.semaphore_wait(barrier, len(others) + neighbours)


class Gather:
    def __init__(self, own_ref, all_ref, send_sem, recv_sem):
        self.own_ref, self.all_ref = own_ref, all_ref
        self.send_sem, self.recv_sem = send_sem, recv_sem
        self.me = lax.axis_index("fsdp")
        self.sibling, self.x_next, self.y_next = flip(self.me, 0), flip(self.me, 1), flip(self.me, 2)
        self.diagonal = flip(self.x_next, 2)
        self.rows = own_ref.shape[0]
        self.sent = []

    def put(self, slot, owner, part, target, own=False):
        half = self.rows // 2
        if part is None:
            spot = self.all_ref.at[pl.ds(pl.multiple_of(owner * self.rows, half), self.rows)]
            source = self.own_ref
        else:
            first = pl.multiple_of(owner * self.rows + part * half, half)
            spot = self.all_ref.at[pl.ds(first, half)]
            source = self.own_ref.at[pl.ds(part * half, half)]
        return pltpu.make_async_remote_copy(
            src_ref=source if own else spot,
            dst_ref=spot,
            send_sem=self.send_sem.at[slot],
            recv_sem=self.recv_sem.at[slot],
            device_id={"fsdp": target},
            device_id_type=MESH,
        )

    def begin(self):
        for slot, part, target in (
            (0, 0, self.x_next),
            (2, 1, self.y_next),
            (4, None, self.sibling),
            (1, 1, self.x_next),
            (3, 0, self.y_next),
        ):
            copy = self.put(slot, self.me, part, target, own=True)
            copy.start()
            self.sent.append(copy)

    def take(self, slot):
        sibling = self.sibling
        owner, part, onward = {
            0: (self.x_next, 0, ((5, self.y_next), (7, sibling))),
            1: (self.x_next, 1, ((8, sibling),)),
            2: (self.y_next, 1, ((6, self.x_next), (9, sibling))),
            3: (self.y_next, 0, ((10, sibling),)),
            4: (sibling, None, ()),
            5: (self.diagonal, 0, ((11, sibling),)),
            6: (self.diagonal, 1, ((12, sibling),)),
            7: (flip(self.x_next, 0), 0, ()),
            8: (flip(self.x_next, 0), 1, ()),
            9: (flip(self.y_next, 0), 1, ()),
            10: (flip(self.y_next, 0), 0, ()),
            11: (flip(self.diagonal, 0), 0, ()),
            12: (flip(self.diagonal, 0), 1, ()),
        }[slot]
        self.put(slot, owner, part, sibling).wait_recv()
        for next_slot, target in onward:
            copy = self.put(next_slot, owner, part, target)
            copy.start()
            self.sent.append(copy)

    def finish(self):
        for copy in self.sent:
            copy.wait_send()


def gather_scratch():
    return [pltpu.SemaphoreType.DMA((13,)), pltpu.SemaphoreType.DMA((13,))]


class Scatter:
    def __init__(self, out_ref, block, refs):
        self.out_ref, self.block = out_ref, block
        (self.sib_out, self.sib_in, self.far_out, self.far_in, self.near_out, self.near_in) = refs[:6]
        self.late = refs[6]
        self.sib_sems, self.far_sems, self.near_sems = refs[7:9], refs[9:11], refs[11:13]
        self.me = lax.axis_index("fsdp")
        self.sibling, self.x_next, self.y_next = flip(self.me, 0), flip(self.me, 1), flip(self.me, 2)
        self.targets = (flip(self.x_next, 2), self.x_next, self.y_next, self.me)
        self.half = out_ref.shape[0] // 2

    def send(self, source, target, sems, slot, device):
        return pltpu.make_async_remote_copy(
            src_ref=source.at[slot],
            dst_ref=target.at[slot],
            send_sem=sems[0].at[slot],
            recv_sem=sems[1].at[slot],
            device_id={"fsdp": device},
            device_id_type=MESH,
        )

    def to_sibling(self, place):
        return self.send(self.sib_out, self.sib_in, self.sib_sems, place, self.sibling)

    def to_far(self, part):
        device = (self.x_next, self.y_next)[part]
        return self.send(self.far_out, self.far_in, self.far_sems, part, device)

    def to_near(self, place, part):
        device = (self.x_next, self.y_next)[place]
        return self.send(self.near_out, self.near_in, self.near_sems, 2 * place + part, device)

    def for_sibling(self, place):
        def write(columns, part):
            self.sib_out[place, :, columns] = part.astype(jnp.bfloat16)

        self.block(flip(self.targets[place], 0), write)
        self.to_sibling(place).start()

    def for_far(self):
        self.to_sibling(0).wait_recv()

        def write(columns, part):
            whole = (part + self.sib_in[0, :, columns].astype(jnp.float32)).astype(jnp.bfloat16)
            self.far_out[0, :, columns] = whole[: self.half]
            self.far_out[1, :, columns] = whole[self.half :]

        self.block(self.targets[0], write)
        self.to_far(0).start()
        self.to_far(1).start()

    def for_near(self, place):
        self.to_sibling(1 + place).wait_recv()
        other = 1 - place

        def write(columns, part):
            whole = part + self.sib_in[1 + place, :, columns].astype(jnp.float32)
            halves = (whole[: self.half], whole[self.half :])
            self.near_out[2 * place + place, :, columns] = halves[place].astype(jnp.bfloat16)
            self.late[place, :, columns] = halves[other]

        self.block(self.targets[1 + place], write)
        self.to_near(place, place).start()

    def finish_near(self, place):
        other = 1 - place
        self.to_far(other).wait_recv()
        whole = self.late[place] + self.far_in[other].astype(jnp.float32)
        self.near_out[2 * place + other] = whole.astype(jnp.bfloat16)
        self.to_near(place, other).start()

    def own(self):
        def write(columns, part):
            self.out_ref[:, columns] = part

        self.block(self.me, write)

    def finish(self):
        self.to_sibling(3).wait_recv()
        self.out_ref[...] = self.out_ref[...] + self.sib_in[3].astype(jnp.float32)
        for part, place in ((0, 0), (1, 1), (1, 0), (0, 1)):
            self.to_near(place, part).wait_recv()
            spot = pl.ds(part * self.half, self.half)
            part_in = self.near_in[2 * place + part].astype(jnp.float32)
            self.out_ref[spot, :] = self.out_ref[spot, :] + part_in
        for place in range(4):
            self.to_sibling(place).wait_send()
            self.to_near(place // 2, place % 2).wait_send()
        for part in range(2):
            self.to_far(part).wait_send()


def staged(kernel, n_in, places):
    def body(*refs):
        stage, sems = refs[-len(places) - 1 : -1], refs[-1]
        inputs, rest = list(refs[:n_in]), refs[n_in : -len(places) - 1]
        copies = [
            pltpu.make_async_copy(inputs[place], buffer, sems.at[index])
            for index, (place, buffer) in enumerate(zip(places, stage))
        ]
        for copy in copies:
            copy.start()
        for place, buffer in zip(places, stage):
            inputs[place] = buffer

        def ready():
            for copy in copies:
                copy.wait()

        kernel(ready, *inputs, *rest)

    return body


def staged_specs(arrays, places):
    specs = [ANY if place in places else VMEM for place in range(len(arrays))]
    scratch = [pltpu.VMEM(arrays[place].shape, arrays[place].dtype) for place in places]
    return specs, scratch + [pltpu.SemaphoreType.DMA((len(places),))]


def scatter_scratch(rows, width):
    low, half = jnp.bfloat16, rows // 2
    return [
        pltpu.VMEM((4, rows, width), low),
        pltpu.VMEM((4, rows, width), low),
        pltpu.VMEM((2, half, width), low),
        pltpu.VMEM((2, half, width), low),
        pltpu.VMEM((4, half, width), low),
        pltpu.VMEM((4, half, width), low),
        pltpu.VMEM((2, half, width), jnp.float32),
        pltpu.SemaphoreType.DMA((4,)),
        pltpu.SemaphoreType.DMA((4,)),
        pltpu.SemaphoreType.DMA((2,)),
        pltpu.SemaphoreType.DMA((2,)),
        pltpu.SemaphoreType.DMA((4,)),
        pltpu.SemaphoreType.DMA((4,)),
    ]


def block_product(left_refs, right_refs, rows, width, turned):
    def block(owner, write):
        @pl.loop(0, width // TILE)
        def _(step):
            columns = pl.ds(pl.multiple_of(step * TILE, TILE), TILE)
            spot = pl.ds(pl.multiple_of(owner * rows, rows), rows)
            total = None
            for left_ref, right_ref in zip(left_refs, right_refs):
                if turned:
                    part = contract_last(left_ref[spot, :], right_ref[columns, :])
                else:
                    part = product(left_ref[spot, :], right_ref[:, columns])
                total = part if total is None else total + part
            write(columns, total)

    return block


def scatter_kernel(turned, count, *refs):
    left_hbm, right_hbm, out_ref = refs[:count], refs[count : 2 * count], refs[2 * count]
    refs = refs[2 * count + 1 :]
    left_refs, right_refs = refs[:count], refs[count : 2 * count]
    left_sems, right_sems, refs = refs[2 * count], refs[2 * count + 1], refs[2 * count + 2 :]
    rows, width = out_ref.shape
    whole = block_product(left_refs, right_refs, rows, width, turned)

    def fetch(place, owner):
        spot = pl.ds(pl.multiple_of(owner * rows, rows), rows)
        return pltpu.make_async_copy(
            left_hbm[place].at[spot], left_refs[place].at[spot], left_sems.at[place, owner]
        )

    def block(owner, write):
        for place in range(count):
            fetch(place, owner).wait()
        whole(owner, write)

    scatter = Scatter(out_ref, block, refs)
    rights = [
        pltpu.make_async_copy(right_hbm[place], right_refs[place], right_sems.at[place])
        for place in range(count)
    ]
    for copy in rights:
        copy.start()
    far, x_next, y_next, me = scatter.targets
    for owner in (
        flip(far, 0),
        flip(x_next, 0),
        far,
        flip(y_next, 0),
        x_next,
        flip(me, 0),
        y_next,
        me,
    ):
        for place in range(count):
            fetch(place, owner).start()
    greet((scatter.sibling, scatter.x_next, scatter.y_next))
    for copy in rights:
        copy.wait()
    scatter.for_sibling(0)
    scatter.for_sibling(1)
    scatter.for_far()
    scatter.for_sibling(2)
    scatter.for_near(0)
    scatter.for_sibling(3)
    scatter.for_near(1)
    scatter.finish_near(0)
    scatter.finish_near(1)
    scatter.own()
    scatter.finish()


def pass_through(ready, gather, scatter, work, between):
    me, sibling, x_next, y_next = gather.me, gather.sibling, gather.x_next, gather.y_next
    diagonal = gather.diagonal
    greet((sibling, x_next, y_next))
    gather.begin()
    gather.all_ref[pl.ds(pl.multiple_of(me * gather.rows, gather.rows), gather.rows), :] = (
        gather.own_ref[...]
    )
    ready()
    work((me,))
    gather.take(0)
    gather.take(2)
    gather.take(4)
    work((sibling,))
    scatter.for_sibling(3)
    gather.take(1)
    gather.take(3)
    work((x_next, y_next))
    gather.take(5)
    gather.take(6)
    for slot in (7, 8, 9, 10):
        gather.take(slot)
    work((flip(x_next, 0), flip(y_next, 0)))
    scatter.for_sibling(1)
    scatter.for_sibling(2)
    scatter.for_near(0)
    scatter.for_near(1)
    gather.take(11)
    gather.take(12)
    work((flip(diagonal, 0),))
    scatter.for_sibling(0)
    work((diagonal,))
    scatter.for_far()
    scatter.own()
    between[0]()
    scatter.finish_near(0)
    scatter.finish_near(1)
    between[1]()
    scatter.finish()
    gather.finish()


def each_owner(owners, rows, one):
    if len(owners) == 1:
        one(owners[0])
        return

    @pl.loop(0, len(owners))
    def _(step):
        one(owners[0] + step * (owners[1] - owners[0]))


def lanes():
    lane = lax.broadcasted_iota(jnp.int32, (1, 2 * HD), 1)
    row_head = lax.broadcasted_iota(jnp.int32, (2 * HD, 2 * HD), 0) // HD
    column_head = lax.broadcasted_iota(jnp.int32, (2 * HD, 2 * HD), 1) // HD
    spread = jnp.where(row_head == column_head, 1.0 / HD, 0.0).astype(jnp.float32)

    def head_mean(values):
        return jnp.dot(
            values, spread, precision=lax.Precision.HIGHEST, preferred_element_type=jnp.float32
        )

    first_half = lax.rem(lane, HD) < HD // 2

    def turn_quarter(values):
        return jnp.where(
            first_half,
            -pltpu.roll(values, 2 * HD - HD // 2, 1),
            pltpu.roll(values, HD // 2, 1),
        )

    def sides(values):
        return [
            jnp.where(chosen, values, 0.0).astype(jnp.bfloat16)
            for chosen in (lane < HD, lane >= HD)
        ]

    return lane, sides, head_mean, turn_quarter


def twice(values):
    return jnp.concatenate([values, values], axis=0)


def stacked(ref, spot):
    width = 2 * HD
    return jnp.concatenate([ref[spot, :width], ref[spot, width : 2 * width]], axis=0)


def attend_kernel(
    ready,
    x_ref,
    wqkv_ref,
    wo_ref,
    cos_ref,
    sin_ref,
    mask_ref,
    gain_ref,
    out_ref,
    all_out_ref,
    proj_ref,
    q_ref,
    kk_ref,
    vv_ref,
    o_ref,
    lse_ref,
    all_ref,
    out_sem,
    gather_send,
    gather_recv,
    *refs,
):
    rows, width = out_ref.shape
    low = jnp.bfloat16
    pair_width = 2 * HD
    lane, sides, head_mean, turn_quarter = lanes()
    first_head = lane < HD
    scale = HD ** (-0.5)

    def normed(values, gain):
        return values * lax.rsqrt(head_mean(values * values) + EPSILON) * gain

    def one(owner):
        base = pl.multiple_of(owner * rows, rows)
        spot = pl.ds(base, rows)
        proj_ref[spot, :] = product(all_ref[spot, :], wqkv_ref[...])

        for part in range(MB):
            micro(pl.multiple_of(base + part * MB_TOK, MB_TOK), owner * MB + part)

    def micro(first, number):
        spot = pl.ds(first, MB_TOK)
        cosine, sine = cos_ref[spot, :], sin_ref[spot, :]
        allowed = twice(mask_ref[number]) > 0.5
        kv = proj_ref[spot, 2 * pair_width : 3 * pair_width]
        swapped = pltpu.roll(kv, HD, 1)
        values = jnp.where(first_head, swapped, kv)
        keys = normed(jnp.where(first_head, kv, swapped), gain_ref[1:2, :])
        keys = (keys * cosine + turn_quarter(keys) * sine).astype(low)
        kk_ref[spot, :] = keys
        vv_ref[spot, :] = values.astype(low)
        query = normed(stacked(proj_ref, spot), gain_ref[0:1, :])
        query = (query * twice(cosine) + turn_quarter(query) * twice(sine)).astype(low)
        q_ref[spot, :pair_width] = query[:MB_TOK]
        q_ref[spot, pair_width : 2 * pair_width] = query[MB_TOK:]
        probs, logs = [], []
        for one_query in sides(query.astype(jnp.float32) * scale):
            scores = jnp.where(allowed, contract_last(one_query, keys), MASKED)
            peak = jnp.max(scores, axis=-1, keepdims=True)
            powers = jnp.exp(scores - peak)
            total = jnp.sum(powers, axis=-1, keepdims=True)
            probs.append((powers * (1.0 / total)).astype(low))
            logs.append(peak + jnp.log(total))
        wide_values = jnp.concatenate(sides(values), axis=0)
        attended = product(jnp.concatenate(probs, axis=1), wide_values).astype(low)
        o_ref[spot, :pair_width] = attended[:MB_TOK]
        o_ref[spot, pair_width : 2 * pair_width] = attended[MB_TOK:]
        log_totals = jnp.where(lane == 0, logs[0][:MB_TOK], logs[1][:MB_TOK])
        log_totals = jnp.where(lane == 2, logs[0][MB_TOK:], log_totals)
        lse_ref[spot, :] = jnp.where(lane == 3, logs[1][MB_TOK:], log_totals)

    gather = Gather(x_ref, all_ref, gather_send, gather_recv)
    scatter = Scatter(out_ref, block_product((o_ref,), (wo_ref,), rows, width, False), refs)
    keep = pltpu.make_async_copy(all_ref, all_out_ref, out_sem)
    pass_through(
        ready,
        gather,
        scatter,
        lambda owners: each_owner(owners, rows, one),
        (keep.start, lambda: None),
    )
    keep.wait()


def attend_back_kernel(
    ready,
    x_ref,
    wqkv_ref,
    wo_ref,
    cos_ref,
    sin_ref,
    mask_ref,
    gain_ref,
    proj_ref,
    q_ref,
    kk_ref,
    vv_ref,
    o_ref,
    lse_ref,
    normed_hbm,
    out_ref,
    grad_ref,
    ggain_ref,
    all_ref,
    normed_ref,
    do_ref,
    dproj_ref,
    in_sem,
    gather_send,
    gather_recv,
    *refs,
):
    rows, width = out_ref.shape
    low = jnp.bfloat16
    pair_width = 2 * HD
    lane, sides, head_mean, turn_quarter = lanes()
    first_head = lane < HD
    scale = HD ** (-0.5)
    fetch = pltpu.make_async_copy(normed_hbm, normed_ref, in_sem)
    fetch.start()
    ggain_ref[...] = jnp.zeros_like(ggain_ref)

    def through_norm(grad, cosine, sine, raw, gain, row):
        grad = grad * cosine - turn_quarter(grad) * sine
        root = lax.rsqrt(head_mean(raw * raw) + EPSILON)
        normed = raw * root
        ggain_ref[row : row + 1, :] += jnp.sum(grad * normed, axis=0, keepdims=True)
        scaled = grad * gain
        return root * (scaled - normed * head_mean(scaled * normed))

    def one(owner):
        base = pl.multiple_of(owner * rows, rows)
        do_ref[...] = contract_last(all_ref[pl.ds(base, rows), :], wo_ref[...]).astype(low)

        for part in range(MB):
            here = pl.ds(part * MB_TOK, MB_TOK)
            micro(pl.multiple_of(base + part * MB_TOK, MB_TOK), here, owner * MB + part)

    def micro(first, here, number):
        spot = pl.ds(first, MB_TOK)
        cosine, sine = cos_ref[spot, :], sin_ref[spot, :]
        allowed = twice(mask_ref[number]) > 0.5
        keys, values = kk_ref[spot, :], vv_ref[spot, :]
        logs = lse_ref[spot, :]
        queries = sides(stacked(q_ref, spot).astype(jnp.float32) * scale)
        branches = sides(stacked(do_ref, here).astype(jnp.float32))
        probs_low, scores_back = [], []
        for side in range(2):
            log_total = jnp.concatenate(
                [logs[:, side : side + 1], logs[:, 2 + side : 3 + side]], axis=0
            )
            scores = jnp.where(allowed, contract_last(queries[side], keys), MASKED)
            probs = jnp.exp(scores - log_total)
            probs_grad = contract_last(branches[side], values)
            spread = jnp.sum(probs * probs_grad, axis=-1, keepdims=True)
            scores_back.append((probs * (probs_grad - spread)).astype(low))
            probs_low.append(probs.astype(low))
        wide_keys = jnp.concatenate(sides(keys.astype(jnp.float32)), axis=0)
        query_grad = product(jnp.concatenate(scores_back, axis=1), wide_keys) * scale
        key_grad = column_product(
            jnp.concatenate(scores_back, axis=0), jnp.concatenate(queries, axis=0)
        )
        value_grad = column_product(
            jnp.concatenate(probs_low, axis=0), jnp.concatenate(branches, axis=0)
        )
        raw = stacked(proj_ref, spot)
        grad = through_norm(query_grad, twice(cosine), twice(sine), raw, gain_ref[0:1, :], 0)
        dproj_ref[spot, :pair_width] = grad[:MB_TOK].astype(low)
        dproj_ref[spot, pair_width : 2 * pair_width] = grad[MB_TOK:].astype(low)
        kv = proj_ref[spot, 2 * pair_width : 3 * pair_width]
        raw = jnp.where(first_head, kv, pltpu.roll(kv, HD, 1))
        key_grad = key_grad + pltpu.roll(key_grad, HD, 1)
        value_grad = value_grad + pltpu.roll(value_grad, HD, 1)
        grad = through_norm(key_grad, cosine, sine, raw, gain_ref[1:2, :], 1)
        both = jnp.where(first_head, grad, value_grad).astype(low)
        dproj_ref[spot, 2 * pair_width : 3 * pair_width] = both

    wide, q_width = dproj_ref.shape[1], o_ref.shape[1]

    def out_grad():
        @pl.loop(0, width // TILE)
        def _(step):
            columns = pl.ds(pl.multiple_of(step * TILE, TILE), TILE)
            part = column_product(o_ref[...], all_ref[:, columns]).astype(low)
            for first in range(0, TILE, q_width):
                spot = pl.ds(pl.multiple_of(step * TILE + first, q_width), q_width)
                grad_ref[spot, wide:] = part[:, first : first + q_width]

    def qkv_grad():
        fetch.wait()

        @pl.loop(0, width // TILE)
        def _(step):
            columns = pl.ds(pl.multiple_of(step * TILE, TILE), TILE)
            part = column_product(dproj_ref[...], normed_ref[:, columns])
            grad_ref[columns, :wide] = jnp.transpose(part).astype(low)

    gather = Gather(x_ref, all_ref, gather_send, gather_recv)
    scatter = Scatter(out_ref, block_product((dproj_ref,), (wqkv_ref,), rows, width, True), refs)
    pass_through(
        ready, gather, scatter, lambda owners: each_owner(owners, rows, one), (out_grad, qkv_grad)
    )


def attend(own_rows, own_qkv, own_out, tables, number):
    rows, width = own_rows.shape
    count, wide, q_width = PLANE * rows, own_qkv.shape[1], own_out.shape[0]
    low = jnp.bfloat16
    arrays = (own_rows, own_qkv, own_out, *tables)
    places = tuple(range(1, len(arrays)))
    specs, stage = staged_specs(arrays, places)
    return pl.pallas_call(
        staged(attend_kernel, len(arrays), places),
        out_shape=[
            jax.ShapeDtypeStruct((rows, width), jnp.float32),
            jax.ShapeDtypeStruct((count, width), low),
            jax.ShapeDtypeStruct((count, wide), jnp.float32),
            jax.ShapeDtypeStruct((count, q_width), low),
            jax.ShapeDtypeStruct((count, 2 * HD), low),
            jax.ShapeDtypeStruct((count, 2 * HD), low),
            jax.ShapeDtypeStruct((count, q_width), low),
            jax.ShapeDtypeStruct((count, 2 * HD), jnp.float32),
        ],
        in_specs=specs,
        out_specs=[VMEM, ANY] + [VMEM] * 6,
        scratch_shapes=[pltpu.VMEM((count, width), low), pltpu.SemaphoreType.DMA]
        + gather_scratch()
        + scatter_scratch(rows, width)
        + stage,
        compiler_params=pltpu.CompilerParams(
            collective_id=number, has_side_effects=True, vmem_limit_bytes=56 * 2**20
        ),
        cost_estimate=SHORT,
        name=f"attend_{number}",
    )(*arrays)


def attend_back(own_rows, own_qkv, own_out, tables, kept, number):
    rows, width = own_rows.shape
    count, wide, q_width = PLANE * rows, own_qkv.shape[1], own_out.shape[0]
    low = jnp.bfloat16
    normed_all, proj, query, keys, values, attended, log_totals = kept
    arrays = (
        own_rows,
        own_qkv,
        own_out,
        *tables,
        proj,
        query,
        keys,
        values,
        attended,
        log_totals,
        normed_all,
    )
    places = tuple(range(1, len(arrays) - 1))
    specs, stage = staged_specs(arrays[:-1], places)
    return pl.pallas_call(
        staged(attend_back_kernel, len(arrays), places),
        out_shape=[
            jax.ShapeDtypeStruct((rows, width), jnp.float32),
            jax.ShapeDtypeStruct((width, wide + q_width), low),
            jax.ShapeDtypeStruct((8, 2 * HD), jnp.float32),
        ],
        in_specs=specs + [ANY],
        out_specs=[VMEM] * 3,
        scratch_shapes=[
            pltpu.VMEM((count, width), low),
            pltpu.VMEM((count, width), low),
            pltpu.VMEM((rows, q_width), low),
            pltpu.VMEM((count, wide), low),
            pltpu.SemaphoreType.DMA,
        ]
        + gather_scratch()
        + scatter_scratch(rows, width)
        + stage,
        compiler_params=pltpu.CompilerParams(
            collective_id=number, has_side_effects=True, vmem_limit_bytes=58 * 2**20
        ),
        cost_estimate=SHORT,
        name=f"attend_back_{number}",
    )(*arrays)


def product_scatter(left_sides, right_sides, number, turned=False):
    width = right_sides[0].shape[0] if turned else right_sides[0].shape[1]
    rows = left_sides[0].shape[0] // PLANE
    return pl.pallas_call(
        functools.partial(scatter_kernel, turned, len(left_sides)),
        out_shape=jax.ShapeDtypeStruct((rows, width), jnp.float32),
        in_specs=[ANY] * (2 * len(left_sides)),
        out_specs=VMEM,
        scratch_shapes=[pltpu.VMEM(side.shape, side.dtype) for side in left_sides + right_sides]
        + [
            pltpu.SemaphoreType.DMA((len(left_sides), PLANE)),
            pltpu.SemaphoreType.DMA((len(left_sides),)),
        ]
        + scatter_scratch(rows, width),
        compiler_params=pltpu.CompilerParams(
            collective_id=number, has_side_effects=True, vmem_limit_bytes=56 * 2**20
        ),
        cost_estimate=SHORT,
        name=f"product_scatter_{number}",
    )(*left_sides, *right_sides)


def start_kernel(
    nd,
    qkv_ref,
    out_rows_ref,
    wide_ref,
    df_ref,
    note_ref,
    own_qkv_ref,
    own_out_ref,
    half_a_ref,
    half_b_ref,
    df_all_ref,
    notes_ref,
    own_sem,
    gather_send,
    gather_recv,
    block_send,
    block_recv,
    note_send,
    note_recv,
    piece_send,
    piece_recv,
    line_send,
    line_recv,
):
    me, line = lax.axis_index("fsdp"), lax.axis_index("dp")
    others = plane_others(me)
    count = qkv_ref.shape[1]
    half_width = half_a_ref.shape[2] // 2
    hidden = 2 * half_width
    whole = hidden * PLANE
    gather = Gather(df_ref, df_all_ref, gather_send, gather_recv)
    greet_line(nd, others)

    def line_spot(array, owner):
        rows = pl.ds(pl.multiple_of(owner * count, count), count)
        return own_qkv_ref.at[:, rows] if array == 0 else own_out_ref.at[rows]

    def along(array, owner, side, source=None):
        spot = line_spot(array, owner)
        return pltpu.make_async_remote_copy(
            src_ref=spot if source is None else source,
            dst_ref=spot,
            send_sem=line_send.at[array, side, owner],
            recv_sem=line_recv.at[array, owner],
            device_id={"dp": line + 1 if side == 0 else line - 1},
            device_id_type=MESH,
        )

    def send_own(array, source=None):
        @pl.when(line < nd - 1)
        def _():
            along(array, line, 0, source).start()

        @pl.when(line > 0)
        def _():
            along(array, line, 1, source).start()

    def line_step(array, step):
        @pl.when(line >= step)
        def _():
            along(array, line - step, 0).wait_recv()

            @pl.when(line < nd - 1)
            def _():
                along(array, line - step, 0).start()

        @pl.when(line + step < nd)
        def _():
            along(array, line + step, 1).wait_recv()

            @pl.when(line > 0)
            def _():
                along(array, line + step, 1).start()

    def put_block(number):
        other = others[number - 1]
        return pltpu.make_async_remote_copy(
            src_ref=qkv_ref.at[other],
            dst_ref=own_qkv_ref.at[me, pl.ds(pl.multiple_of(line * count, count), count)],
            send_sem=block_send.at[number],
            recv_sem=block_recv.at[number],
            device_id={"fsdp": other},
            device_id_type=MESH,
        )

    def put_note(number):
        return pltpu.make_async_remote_copy(
            src_ref=note_ref,
            dst_ref=notes_ref.at[me],
            send_sem=note_send.at[number],
            recv_sem=note_recv.at[number],
            device_id={"fsdp": others[number - 1]},
            device_id_type=MESH,
        )

    def pieces(other):
        for half, half_ref in enumerate((half_a_ref, half_b_ref)):
            for side in range(2):
                first = side * whole + other * hidden + half * half_width
                source = wide_ref.at[:, pl.ds(pl.multiple_of(first, 128), half_width)]
                yield source, half_ref.at[me, :, pl.ds(side * half_width, half_width)]

    def put_pieces(number):
        return [
            pltpu.make_async_remote_copy(
                src_ref=source,
                dst_ref=target,
                send_sem=piece_send.at[4 * number + index],
                recv_sem=piece_recv.at[4 * number + index],
                device_id={"fsdp": others[number - 1]},
                device_id_type=MESH,
            )
            for index, (source, target) in enumerate(pieces(others[number - 1]))
        ]

    own_block = own_qkv_ref.at[me, pl.ds(pl.multiple_of(line * count, count), count)]
    rows = df_ref.shape[0]
    kept = [
        (qkv_ref.at[me], own_block),
        (out_rows_ref, line_spot(1, line)),
        (note_ref, notes_ref.at[me]),
        (df_ref, df_all_ref.at[pl.ds(pl.multiple_of(me * rows, rows), rows)]),
    ] + list(pieces(me))
    keep = [
        pltpu.make_async_copy(source, target, own_sem.at[index])
        for index, (source, target) in enumerate(kept)
    ]
    order = (6, 7, 2, 4, 3, 5, 1)
    for number in order:
        put_block(number).start()
        put_note(number).start()
    keep[0].start()
    send_own(1, out_rows_ref)
    gather.begin()
    for copy in keep[1:]:
        copy.start()
    for number in order:
        put_block(number).wait_recv()
    keep[0].wait()
    send_own(0)
    for steps, slots in (
        ((), (0, 2)),
        (((1, 1),), (4, 1, 3)),
        (((0, 1),), (5, 6)),
        (((1, 2),), ()),
        (((0, 2),), (7, 9, 8, 10)),
        (((1, 3), (0, 3)), (11, 12)),
    ):
        for array, step in steps:
            if step < nd:
                line_step(array, step)
        for slot in slots:
            gather.take(slot)
        if slots == (5, 6):
            for number in order:
                for copy in put_pieces(number):
                    copy.start()
    for step in range(4, nd):
        line_step(1, step)
        line_step(0, step)
    for number in order:
        put_block(number).wait_send()
        put_note(number).wait()
        for copy in put_pieces(number):
            copy.wait()
    gather.finish()
    for copy in keep[1:]:
        copy.wait()
    for array in (1, 0):
        source = out_rows_ref if array == 1 else None

        @pl.when(line < nd - 1)
        def _():
            along(array, line, 0, source).wait_send()

        @pl.when(line > 0)
        def _():
            along(array, line, 1, source).wait_send()

        for step in range(1, nd):

            @pl.when(jnp.logical_and(line >= step, line < nd - 1))
            def _():
                along(array, line - step, 0).wait_send()

            @pl.when(jnp.logical_and(line + step < nd, line > 0))
            def _():
                along(array, line + step, 1).wait_send()


def start(qkv_blocks, out_rows, wide_rows, df_own, note, number):
    nd = lax.axis_size("dp")
    count, whole = wide_rows.shape
    half = whole // 4 // PLANE
    low = wide_rows.dtype
    return pl.pallas_call(
        functools.partial(start_kernel, nd),
        out_shape=[
            jax.ShapeDtypeStruct((PLANE, nd * count, qkv_blocks.shape[2]), low),
            jax.ShapeDtypeStruct((nd * count, out_rows.shape[1]), low),
            jax.ShapeDtypeStruct((PLANE, count, 2 * half), low),
            jax.ShapeDtypeStruct((PLANE, count, 2 * half), low),
            jax.ShapeDtypeStruct((PLANE * df_own.shape[0], df_own.shape[1]), low),
            jax.ShapeDtypeStruct((PLANE,) + note.shape, note.dtype),
        ],
        in_specs=[ANY] * 5,
        out_specs=[ANY] * 6,
        scratch_shapes=[pltpu.SemaphoreType.DMA((8,))]
        + gather_scratch()
        + [pltpu.SemaphoreType.DMA((PLANE,))] * 4
        + [pltpu.SemaphoreType.DMA((4 * PLANE,))] * 2
        + [pltpu.SemaphoreType.DMA((2, 2, nd)), pltpu.SemaphoreType.DMA((2, nd))],
        compiler_params=pltpu.CompilerParams(collective_id=number, has_side_effects=True),
        cost_estimate=SHORT,
        name=f"start_{number}",
    )(qkv_blocks, out_rows, wide_rows, df_own, note)


def glu_block(
    rows_ref, df_ref, wgu, wd, act_ref, dgu_ref, down_sum, wide_sum, results=None
):
    half = wd.shape[0]
    count, width = rows_ref.shape

    @pl.loop(0, count // 256)
    def _(step):
        spot = pl.ds(pl.multiple_of(step * 256, 256), 256)
        for first in range(0, half, GLU_TILE):
            units = slice(first, first + GLU_TILE)
            up_units = slice(half + first, half + first + GLU_TILE)
            gate = product(rows_ref[spot, :], wgu[:, units])
            up = product(rows_ref[spot, :], wgu[:, up_units])
            back = contract_last(df_ref[spot, :], wd[units, :])
            sigmoid = jax.nn.sigmoid(gate)
            silu = gate * sigmoid
            act_ref[spot, units] = (silu * up).astype(jnp.bfloat16)
            gate_back = back * up * sigmoid * (1.0 + gate * (1.0 - sigmoid))
            dgu_ref[spot, units] = gate_back.astype(jnp.bfloat16)
            dgu_ref[spot, up_units] = (back * silu).astype(jnp.bfloat16)

    @pl.loop(0, width // TILE)
    def _(step):
        columns = pl.ds(pl.multiple_of(step * TILE, TILE), TILE)
        down = column_product(act_ref[...], df_ref[:, columns])
        wide = column_product(rows_ref[:, columns], dgu_ref[...])
        if results is None:
            down_sum[:, columns] += down
            wide_sum[columns, :] += wide
        else:
            down_ref, wide_ref = results
            down_ref[:, columns] = (down_sum[:, columns] + down).astype(down_ref.dtype)
            wide_ref[columns, :] = (wide_sum[columns, :] + wide).astype(wide_ref.dtype)


def gather_glu_kernel(
    x_ref,
    wgu_hbm,
    wd_hbm,
    df_hbm,
    all_out_ref,
    act_ref,
    dgu_ref,
    down_ref,
    wide_ref,
    all_ref,
    wgu_ref,
    wd_ref,
    df_ref,
    down_sum,
    wide_sum,
    in_sem,
    out_sem,
    gather_send,
    gather_recv,
):
    rows = x_ref.shape[0]
    half = wd_ref.shape[0]
    fetch = [
        pltpu.make_async_copy(wgu_hbm, wgu_ref, in_sem.at[0]),
        pltpu.make_async_copy(wd_hbm.at[pl.ds(0, half)], wd_ref, in_sem.at[1]),
        pltpu.make_async_copy(df_hbm, df_ref, in_sem.at[2]),
    ]
    for copy in fetch:
        copy.start()
    gather = Gather(x_ref, all_ref, gather_send, gather_recv)
    me, x_next, y_next = gather.me, gather.x_next, gather.y_next
    greet((gather.sibling, x_next, y_next))
    gather.begin()
    all_ref[pl.ds(pl.multiple_of(me * rows, rows), rows), :] = x_ref[...]
    down_sum[...] = jnp.zeros_like(down_sum)
    wide_sum[...] = jnp.zeros_like(wide_sum)
    for copy in fetch:
        copy.wait()

    def work(owner, results=None):
        first = owner - lax.rem(owner, 2)
        spot = pl.ds(pl.multiple_of(first * rows, 2 * rows), 2 * rows)
        glu_block(
            all_ref.at[spot],
            df_ref.at[spot],
            wgu_ref,
            wd_ref,
            act_ref.at[spot],
            dgu_ref.at[spot],
            down_sum,
            wide_sum,
            results,
        )

    gather.take(4)
    work(me)
    for slot in (0, 2, 1, 3, 7, 8):
        gather.take(slot)
    work(x_next)
    for slot in (5, 6, 9, 10):
        gather.take(slot)
    work(y_next)
    gather.take(11)
    gather.take(12)
    keep = pltpu.make_async_copy(all_ref, all_out_ref, out_sem)
    keep.start()
    work(gather.diagonal, (down_ref, wide_ref))
    gather.finish()
    keep.wait()


def gather_glu(own_rows, wgu, own_down, df_all, number):
    rows, width = own_rows.shape
    count, half = PLANE * rows, wgu.shape[1] // 2
    low = jnp.bfloat16
    return pl.pallas_call(
        gather_glu_kernel,
        out_shape=[
            jax.ShapeDtypeStruct((count, width), low),
            jax.ShapeDtypeStruct((count, half), low),
            jax.ShapeDtypeStruct((count, 2 * half), low),
            jax.ShapeDtypeStruct((half, width), low),
            jax.ShapeDtypeStruct((width, 2 * half), low),
        ],
        in_specs=[VMEM, ANY, ANY, ANY],
        out_specs=[ANY] + [VMEM] * 4,
        scratch_shapes=[
            pltpu.VMEM((count, width), low),
            pltpu.VMEM(wgu.shape, low),
            pltpu.VMEM((half, width), low),
            pltpu.VMEM((count, width), low),
            pltpu.VMEM((half, width), jnp.float32),
            pltpu.VMEM((width, 2 * half), jnp.float32),
            pltpu.SemaphoreType.DMA((3,)),
            pltpu.SemaphoreType.DMA,
        ]
        + gather_scratch(),
        compiler_params=pltpu.CompilerParams(
            collective_id=number, has_side_effects=True, vmem_limit_bytes=58 * 2**20
        ),
        cost_estimate=SHORT,
        name=f"gather_glu_{number}",
    )(own_rows, wgu, own_down, df_all)


def glu_kernel(
    x_ref, df_ref, wgu_ref, wd_ref, first_ref, act_ref, dgu_ref, grad_ref, down_sum, wide_sum
):
    step = pl.program_id(0)
    half = wd_ref.shape[0]

    @pl.when(step == 0)
    def _():
        down_sum[...] = jnp.zeros_like(down_sum)
        wide_sum[...] = jnp.zeros_like(wide_sum)

    glu_block(
        x_ref, df_ref, wgu_ref, wd_ref, act_ref, dgu_ref, down_sum, wide_sum
    )

    @pl.when(step == pl.num_programs(0) - 1)
    def _():
        nd, _, both = grad_ref.shape
        count, units = wide_sum.shape[0] // PLANE // nd, 2 * half // nd
        low = grad_ref.dtype
        for owner in range(nd):
            for place in range(PLANE):
                first = (place * nd + owner) * count
                part = wide_sum[first : first + count, :].astype(low)
                grad_ref[owner, place * count : (place + 1) * count, :] = part
            source, first = first_ref, owner * units
            if first >= half:
                source, first = down_sum, first - half
            for side in range(2):
                part = source[first : first + units, side * both : (side + 1) * both].astype(low)
                start = PLANE * count + side * units
                grad_ref[owner, start : start + units, :] = part


def glu(rows_all, df_all, wgu, own_down, down_first, number):
    nd = lax.axis_size("dp")
    count, width = rows_all.shape
    half = wgu.shape[1] // 2
    low = jnp.bfloat16
    step = 512
    once = pl.Buffered(1)
    return pl.pallas_call(
        glu_kernel,
        grid=(count // step,),
        out_shape=[
            jax.ShapeDtypeStruct((count, half), low),
            jax.ShapeDtypeStruct((count, 2 * half), low),
            jax.ShapeDtypeStruct((nd, 2 * width // nd, 2 * half), low),
        ],
        in_specs=[
            pl.BlockSpec((step, width), lambda i: (i, 0)),
            pl.BlockSpec((step, width), lambda i: (i, 0)),
            pl.BlockSpec((width, 2 * half), lambda i: (0, 0), pipeline_mode=once),
            pl.BlockSpec((half, width), lambda i: (1, 0), pipeline_mode=once),
            pl.BlockSpec((half, width), lambda i: (0, 0), pipeline_mode=once),
        ],
        out_specs=[
            pl.BlockSpec((step, half), lambda i: (i, 0)),
            pl.BlockSpec((step, 2 * half), lambda i: (i, 0)),
            pl.BlockSpec(
                (nd, 2 * width // nd, 2 * half), lambda i: (0, 0, 0), pipeline_mode=once
            ),
        ],
        scratch_shapes=[
            pltpu.VMEM((half, width), jnp.float32),
            pltpu.VMEM((width, 2 * half), jnp.float32),
        ],
        compiler_params=pltpu.CompilerParams(vmem_limit_bytes=56 * 2**20),
        cost_estimate=SHORT,
        name=f"glu_{number}",
    )(rows_all, df_all, wgu, own_down, down_first)


def attention(normed_low, own_qkv, own_out, lengths_all, query_gain, key_gain):
    position, _, allowed = layout(lengths_all)
    half_width = HD // 2
    frequency = ROPE_BASE ** (jnp.arange(half_width, dtype=jnp.float32) * (-2.0 / HD))
    angles = position.reshape(-1, 1) * frequency[None, :]
    tables = (
        jnp.tile(jnp.cos(angles), (1, 4)),
        jnp.tile(jnp.sin(angles), (1, 4)),
        allowed.astype(jnp.float32),
        jnp.pad(
            jnp.stack([jnp.tile(query_gain, 2), jnp.tile(key_gain, 2)]), ((0, 6), (0, 0))
        ),
    )
    sums, *kept = attend(normed_low, own_qkv, own_out, tables, 3)

    def back(branch_own):
        normed_one_grad, part_attn, gain_grads = attend_back(
            branch_own, own_qkv, own_out, tables, kept, 9
        )
        query_gain_grad = gain_grads[0, :HD] + gain_grads[0, HD:]
        return normed_one_grad, part_attn, query_gain_grad, gain_grads[1, :HD]

    return sums, back


def last_kernel(
    ready,
    hidden_ref,
    valid_ref,
    act_a_ref,
    act_b_ref,
    wd_ref,
    half_ref,
    out_ref,
    wide_ref,
    sum_ref,
    own_sem,
    sems,
    *refs,
):
    others = plane_others(lax.axis_index("fsdp"))
    rows, width = out_ref.shape
    half_rows = wd_ref.shape[0] // 2
    block = block_product(
        (act_a_ref, act_b_ref),
        (wd_ref.at[pl.ds(0, half_rows)], wd_ref.at[pl.ds(half_rows, half_rows)]),
        rows,
        width,
        False,
    )
    scatter = Scatter(sum_ref, block, refs)
    greet(others)
    order = (6, 7, 2, 4, 3, 5, 1)
    for number in order:
        for copy in put_half(half_ref, wide_ref, others, number, sems):
            copy.start()
    keep = keep_half(half_ref, wide_ref, own_sem)
    for copy in keep:
        copy.start()
    ready()
    scatter.for_sibling(0)
    scatter.for_sibling(1)
    scatter.for_far()
    scatter.for_sibling(2)
    scatter.for_near(0)
    scatter.for_sibling(3)
    scatter.for_near(1)
    scatter.finish_near(0)
    scatter.finish_near(1)
    scatter.own()
    scatter.finish()
    out_ref[...] = (hidden_ref[...] + valid_ref[...] * sum_ref[...]).astype(out_ref.dtype)
    for number in order:
        for copy in put_half(half_ref, wide_ref, others, number, sems):
            copy.wait()
    for copy in keep:
        copy.wait()


def last(hidden, valid_col, act_a, act_b, own_down, half, count, number):
    rows, width = hidden.shape
    arrays = (hidden, valid_col, act_a, act_b, own_down)
    places = (0, 2, 3, 4)
    specs, stage = staged_specs(arrays, places)
    return pl.pallas_call(
        staged(last_kernel, len(arrays) + 1, places),
        out_shape=[
            jax.ShapeDtypeStruct((rows, width), jnp.bfloat16),
            jax.ShapeDtypeStruct((count, half.shape[1] * PLANE), half.dtype),
        ],
        in_specs=specs + [ANY],
        out_specs=[VMEM, ANY],
        scratch_shapes=[pltpu.VMEM((rows, width), jnp.float32)]
        + half_scratch()
        + scatter_scratch(rows, width)
        + stage,
        compiler_params=pltpu.CompilerParams(
            collective_id=number, has_side_effects=True, vmem_limit_bytes=56 * 2**20
        ),
        cost_estimate=SHORT,
        name=f"last_{number}",
    )(*arrays, half)


def adam_kernel(chunks, n_grads, per, norm_ref, *refs):
    grads, refs = refs[:n_grads], refs[n_grads:]
    groups = [refs[place * per : (place + 1) * per] for place in range(6)]
    in_buf, grad_buf, out_buf, in_sems, out_sems = refs[6 * per :]
    depth = in_buf.shape[0]
    factor = norm_ref[1:2, 0:1]
    first_scale = 1.0 / (1.0 - FIRST_DECAY**STEP)
    second_scale = 1.0 / (1.0 - SECOND_DECAY**STEP)

    def fetch(number):
        which, rows, columns, pieces = chunks[number]
        slot, width = number % depth, columns.size
        copies = [
            pltpu.make_async_copy(
                groups[place][which].at[rows, columns],
                in_buf.at[slot, place, :, pl.ds(0, width)],
                in_sems.at[slot, place],
            )
            for place in range(3)
        ]
        for place, (array, source, first) in enumerate(pieces):
            target = grad_buf.at[slot, :, pl.ds(first, source[1].size)]
            copies.append(
                pltpu.make_async_copy(
                    grads[array].at[source], target, in_sems.at[slot, 3 + place]
                )
            )
        return copies

    def put(number):
        which, rows, columns, _ = chunks[number]
        slot, width = number % depth, columns.size
        return [
            pltpu.make_async_copy(
                out_buf.at[slot, place, :, pl.ds(0, width)],
                groups[3 + place][which].at[rows, columns],
                out_sems.at[slot, place],
            )
            for place in range(3)
        ]

    def update(slot, width):
        columns = slice(0, width)

        @pl.loop(0, in_buf.shape[2] // 16)
        def _(step):
            rows = pl.ds(pl.multiple_of(step * 16, 16), 16)
            clipped = grad_buf[slot, rows, columns].astype(jnp.float32) * factor
            weight = in_buf[slot, 0, rows, columns]
            first = FIRST_DECAY * in_buf[slot, 1, rows, columns] + (1.0 - FIRST_DECAY) * clipped
            second = SECOND_DECAY * in_buf[slot, 2, rows, columns]
            second = second + (1.0 - SECOND_DECAY) * clipped * clipped
            root = jnp.sqrt(second * second_scale) + ADAM_EPSILON
            change = first * first_scale / root + WEIGHT_DECAY * weight
            out_buf[slot, 0, rows, columns] = weight - LEARN_RATE * change
            out_buf[slot, 1, rows, columns] = first
            out_buf[slot, 2, rows, columns] = second

    for number in range(min(depth, len(chunks))):
        for copy in fetch(number):
            copy.start()
    for number in range(len(chunks)):
        for copy in fetch(number):
            copy.wait()
        if number >= depth:
            for copy in put(number - depth):
                copy.wait()
        update(number % depth, chunks[number][2].size)
        for copy in put(number):
            copy.start()
        if number + depth < len(chunks):
            for copy in fetch(number + depth):
                copy.start()
    for number in range(max(0, len(chunks) - depth), len(chunks)):
        for copy in put(number):
            copy.wait()


def adam_matrices(norm, grad_qkv, grad_out, grad_a, grad_b, sums_b, weights, firsts, seconds):
    rows, width, depth = 64, 2048, 6
    half = grad_a.shape[1] // 2 // PLANE
    count = weights[3].shape[0]
    behind = sums_b.shape[0] - 2 * count

    def pieces(which, row, column, size):
        here = pl.ds(row, rows)
        if which < 2:
            return [(which, (here, pl.ds(column, size)), 0)]
        if which == 3:
            return [
                (4, (pl.ds(behind + side * count + row, rows), pl.ds(0, width // 2)), side * width // 2)
                for side in range(2)
            ]
        first = column // 2
        return [
            (2 + part, (here, pl.ds(first + unit * half, half)), (2 * unit + part) * half)
            for unit in range(width // 2 // half)
            for part in range(2)
        ]

    chunks = []
    for which, weight in enumerate(weights):
        for row in range(0, weight.shape[0], rows):
            for column in range(0, weight.shape[1], width):
                size = min(width, weight.shape[1] - column)
                parts = pieces(which, row, column, size)
                chunks.append((which, pl.ds(row, rows), pl.ds(column, size), parts))
    grads = (grad_qkv, grad_out, grad_a, grad_b, sums_b)
    per = len(weights)
    outs = pl.pallas_call(
        functools.partial(adam_kernel, chunks, len(grads), per),
        out_shape=[jax.ShapeDtypeStruct(weight.shape, jnp.float32) for weight in weights] * 3,
        in_specs=[VMEM] + [ANY] * (len(grads) + 3 * per),
        out_specs=[ANY] * (3 * per),
        scratch_shapes=[
            pltpu.VMEM((depth, 3, rows, width), jnp.float32),
            pltpu.VMEM((depth, rows, width), jnp.bfloat16),
            pltpu.VMEM((depth, 3, rows, width), jnp.float32),
            pltpu.SemaphoreType.DMA((depth, 7)),
            pltpu.SemaphoreType.DMA((depth, 3)),
        ],
        compiler_params=pltpu.CompilerParams(vmem_limit_bytes=60 * 2**20),
        name="adam_matrices",
    )(norm, *grads, *weights, *firsts, *seconds)
    return outs[:per], outs[per : 2 * per], outs[2 * per :]


def scatter_rows(values, axis):
    return lax.psum_scatter(values, "dp", scatter_dimension=axis, tiled=True)


def per_device_plane(
    nf,
    nd,
    tokens,
    cotangent,
    order,
    lengths,
    w_qkv,
    w_out,
    w_gate_up,
    w_down,
    gains,
    first_qkv,
    first_out,
    first_gate_up,
    first_down,
    first_gains,
    second_qkv,
    second_out,
    second_gate_up,
    second_down,
    second_gains,
):
    low = jnp.bfloat16
    q_width = HEADS // nf * HD
    kv_all = KVH * HD
    hidden_own = FF // nf
    rows_own = w_qkv.shape[0]

    order_row = order[0]
    places = jnp.arange(TOK_DEV, dtype=jnp.int32)
    inverse = jnp.zeros((TOK_DEV,), jnp.int32).at[order_row].set(places)
    rows_in = tokens[order_row].astype(jnp.float32)
    back_rows = cotangent[order_row].astype(jnp.float32)
    attn_gain = gains[:D]
    ffn_gain = gains[D : 2 * D]
    query_gain = gains[2 * D : 2 * D + HD]
    key_gain = gains[2 * D + HD :]

    _, valid_rows, _ = layout(lengths)
    valid_col = valid_rows.reshape(TOK_DEV, 1)

    qkv_low = w_qkv.astype(low)

    def head_blocks(rows, width):
        return jnp.swapaxes(rows.reshape(rows_own, -1, width), 0, 1)

    qkv_blocks = jnp.concatenate(
        [
            head_blocks(qkv_low[:, :D], q_width),
            head_blocks(qkv_low[:, D : D + kv_all], HD),
            head_blocks(qkv_low[:, D + kv_all :], HD),
        ],
        axis=2,
    )
    wide = q_width + 2 * HD
    own_down = lax.all_gather(w_down.astype(low), "dp", axis=0, tiled=True)
    own_qkv, own_out, half_a, half_b, down_back, notes = start(
        qkv_blocks,
        w_out.astype(low),
        w_gate_up.astype(low),
        (valid_col * back_rows).astype(low),
        jnp.pad(lengths, ((0, 8 - MB), (0, 128 - SEQS))),
        1,
    )
    own_qkv = own_qkv.reshape(D, wide)
    lengths_all = notes[:, :MB, :SEQS].reshape(nf * MB, SEQS)
    half_a, own_down = lax.optimization_barrier((half_a, own_down))
    own_a = lax.all_gather(half_a, "dp", axis=1, tiled=True).reshape(D, hidden_own)
    own_b = lax.all_gather(half_b, "dp", axis=1, tiled=True).reshape(D, hidden_own)

    normed_one, norm_one_pull = jax.vjp(rms_norm, rows_in, attn_gain)
    attention_sums, attention_back = attention(
        normed_one.astype(low), own_qkv, own_out, lengths_all, query_gain, key_gain
    )
    hidden = rows_in + valid_col * attention_sums

    normed_two, norm_two_pull = jax.vjp(rms_norm, hidden, ffn_gain)
    norm_two_all, act_a, back_a, down_a, part_a = gather_glu(
        normed_two.astype(low), own_a, own_down, down_back, 5
    )
    sums_a = scatter_rows(part_a.reshape(nf, nd * rows_own, hidden_own), 1)
    act_b, back_b, part_b = glu(norm_two_all, down_back, own_b, own_down, down_a, 6)
    sums_b = scatter_rows(part_b, 0)[0]
    normed_two_grad = product_scatter((back_a, back_b), (own_a, own_b), 8, turned=True)
    hidden_norm_grad, ffn_gain_grad = norm_two_pull(normed_two_grad)
    hidden_grad = back_rows + hidden_norm_grad

    branch_own = (valid_col * hidden_grad).astype(low)
    branch_own, sums_a = lax.optimization_barrier((branch_own, sums_a))
    normed_one_grad, part_attn, query_gain_grad, key_gain_grad = attention_back(branch_own)
    sums_attn = scatter_rows(part_attn.reshape(nf, nd * rows_own, wide + q_width), 1)
    normed_one_grad, act_a = lax.optimization_barrier((normed_one_grad, act_a))
    output, grad_a = last(
        hidden,
        valid_col,
        act_a,
        act_b,
        own_down,
        sums_a.reshape(nf * rows_own, hidden_own),
        rows_own,
        7,
    )
    output, sums_b = lax.optimization_barrier((output, sums_b))
    grad_b, squares_b = exchange_half(sums_b, rows_own, 11)
    rows_grad, attn_gain_grad = norm_one_pull(normed_one_grad)
    input_grad = (hidden_grad + rows_grad)[inverse]
    output_all = output[inverse]

    early = jnp.sum(jnp.square(sums_a.astype(jnp.float32)))
    input_grad, output_all, early, sums_attn, squares_b = lax.optimization_barrier(
        (input_grad, output_all, early, sums_attn, squares_b)
    )
    early_squares = early + jnp.sum(squares_b)
    gain_sum = jnp.concatenate([attn_gain_grad, ffn_gain_grad, query_gain_grad, key_gain_grad])
    gain_total, norm, grad_qkv, grad_out = sum_everywhere(
        gain_sum, early_squares, sums_attn, wide, 13
    )
    global_norm, factor = norm[0, 0], norm[1, 0]
    new_matrices, next_firsts, next_seconds = adam_matrices(
        norm,
        grad_qkv,
        grad_out,
        grad_a,
        grad_b,
        sums_b,
        (w_qkv, w_out, w_gate_up, w_down),
        (first_qkv, first_out, first_gate_up, first_down),
        (second_qkv, second_out, second_gate_up, second_down),
    )
    new_gains, next_first_gains, next_second_gains = adam_step(
        gains, first_gains, second_gains, gain_total, factor, GAIN_RATE, 0.0
    )
    return (
        output_all,
        input_grad,
        global_norm,
        *new_matrices,
        new_gains,
        *next_firsts,
        next_first_gains,
        *next_seconds,
        next_second_gains,
    )


def gather_tokens(rows):
    return lax.all_gather(rows, "fsdp", axis=0, tiled=True)


def scatter_tokens(rows):
    return lax.psum_scatter(
        rows.astype(jnp.bfloat16), "fsdp", scatter_dimension=0, tiled=True
    ).astype(jnp.float32)


def swap(blocks):
    return lax.all_to_all(blocks, "fsdp", split_axis=0, concat_axis=0, tiled=True)


def per_device_plain(
    nf,
    nd,
    tokens,
    cotangent,
    order,
    lengths,
    w_qkv,
    w_out,
    w_gate_up,
    w_down,
    gains,
    first_qkv,
    first_out,
    first_gate_up,
    first_down,
    first_gains,
    second_qkv,
    second_out,
    second_gate_up,
    second_down,
    second_gains,
):
    low = jnp.bfloat16
    kvl = max(KVH // nf, 1)
    rep = max(nf // KVH, 1)
    heads_own = HEADS // nf
    group = heads_own // kvl
    q_width, kv_width = heads_own * HD, kvl * HD
    kv_all = KVH * HD
    hidden_own = FF // nf
    rows_own = w_qkv.shape[0]
    n_mb = nf * MB

    def head_blocks(rows, width):
        return jnp.swapaxes(rows.reshape(rows_own, -1, width), 0, 1)

    qkv_low = w_qkv.astype(low)
    qkv_blocks = jnp.concatenate(
        [
            head_blocks(qkv_low[:, :D], q_width),
            jnp.repeat(head_blocks(qkv_low[:, D : D + kv_all], kv_width), rep, axis=0),
            jnp.repeat(head_blocks(qkv_low[:, D + kv_all :], kv_width), rep, axis=0),
        ],
        axis=2,
    )
    wide = q_width + 2 * kv_width
    own_qkv = lax.all_gather(swap(qkv_blocks), "dp", axis=1, tiled=True).reshape(D, wide)
    own_out = lax.all_gather(w_out.astype(low), "dp", axis=0, tiled=True)
    gate_up_blocks = jnp.transpose(
        w_gate_up.astype(low).reshape(rows_own, 2, nf, hidden_own), (2, 0, 1, 3)
    ).reshape(nf, rows_own, 2 * hidden_own)
    own_gate_up = lax.all_gather(swap(gate_up_blocks), "dp", axis=1, tiled=True).reshape(
        D, 2 * hidden_own
    )
    own_down = lax.all_gather(w_down.astype(low), "dp", axis=0, tiled=True)

    order_row = order[0]
    places = jnp.arange(TOK_DEV, dtype=jnp.int32)
    inverse = jnp.zeros((TOK_DEV,), jnp.int32).at[order_row].set(places)
    rows_in = tokens[order_row].astype(jnp.float32)
    back_rows = cotangent[order_row].astype(jnp.float32)
    attn_gain = gains[:D]
    ffn_gain = gains[D : 2 * D]
    query_gain = gains[2 * D : 2 * D + HD]
    key_gain = gains[2 * D + HD :]
    score_scale = HD ** (-0.5)

    lengths_all = gather_tokens(lengths)
    position, _, allowed = layout(lengths_all)
    _, valid_rows, _ = layout(lengths)
    valid_col = valid_rows.reshape(TOK_DEV, 1)
    allowed = allowed[:, None, None]
    cosine_table, sine_table = rope_tables(position.reshape(-1))

    normed_one, norm_one_pull = jax.vjp(rms_norm, rows_in, attn_gain)
    norm_one_all = gather_tokens(normed_one.astype(low))
    projected = product(norm_one_all, own_qkv)
    n_rows = norm_one_all.shape[0]
    query_raw = projected[:, :q_width].reshape(n_rows, heads_own, HD)
    key_raw = projected[:, q_width : q_width + kv_width].reshape(n_rows, kvl, HD)
    values_low = projected[:, q_width + kv_width :].reshape(n_mb, MB_TOK, kvl, HD).astype(low)

    def turn_heads(query_in, key_in, query_scale, key_scale):
        return (
            rotate(rms_norm(query_in, query_scale), cosine_table, sine_table),
            rotate(rms_norm(key_in, key_scale), cosine_table, sine_table),
        )

    turned, turn_pull = jax.vjp(turn_heads, query_raw, key_raw, query_gain, key_gain)
    queries_low = turned[0].astype(low).reshape(n_mb, MB_TOK, kvl, group, HD)
    keys_low = turned[1].astype(low).reshape(n_mb, MB_TOK, kvl, HD)
    scores = (
        jnp.einsum("mtkgd,mukd->mkgtu", queries_low, keys_low, preferred_element_type=jnp.float32)
        * score_scale
    )
    scores = jnp.where(allowed, scores, MASKED)
    row_peak = jnp.max(scores, axis=-1, keepdims=True)
    powers = jnp.exp(scores - row_peak)
    totals = jnp.sum(powers, axis=-1, keepdims=True)
    probs = powers / totals
    probs_low = probs.astype(low)
    attended = jnp.einsum(
        "mkgtu,mukd->mtkgd", probs_low, values_low, preferred_element_type=jnp.float32
    )
    attended_low = attended.reshape(n_rows, q_width).astype(low)
    hidden = rows_in + valid_col * scatter_tokens(product(attended_low, own_out))

    normed_two, norm_two_pull = jax.vjp(rms_norm, hidden, ffn_gain)
    norm_two_all = gather_tokens(normed_two.astype(low))
    down_back = gather_tokens((valid_col * back_rows).astype(low))
    gate_up = product(norm_two_all, own_gate_up)
    activation, glu_pull = jax.vjp(swiglu, gate_up[:, :hidden_own], gate_up[:, hidden_own:])
    activation_low = activation.astype(low)
    output = hidden + valid_col * scatter_tokens(product(activation_low, own_down))
    gate_back, up_back = glu_pull(contract_last(down_back, own_down))
    gate_up_back = jnp.concatenate([gate_back.astype(low), up_back.astype(low)], axis=1)
    normed_two_grad = scatter_tokens(contract_last(gate_up_back, own_gate_up))
    grad_down = lax.psum_scatter(
        column_product(activation_low, down_back).astype(low),
        "dp",
        scatter_dimension=0,
        tiled=True,
    ).astype(jnp.float32)
    grad_gate_up = lax.psum_scatter(
        column_product(norm_two_all, gate_up_back)
        .astype(low)
        .reshape(nf, nd * rows_own, 2 * hidden_own),
        "dp",
        scatter_dimension=1,
        tiled=True,
    )
    grad_gate_up = jnp.transpose(
        swap(grad_gate_up).reshape(nf, rows_own, 2, hidden_own), (1, 2, 0, 3)
    ).reshape(rows_own, 2 * FF)
    grad_gate_up = grad_gate_up.astype(jnp.float32)
    hidden_norm_grad, ffn_gain_grad = norm_two_pull(normed_two_grad)
    hidden_grad = back_rows + hidden_norm_grad

    branch_back = gather_tokens((valid_col * hidden_grad).astype(low))
    attended_back = contract_last(branch_back, own_out).astype(low)
    grad_out = lax.psum_scatter(
        column_product(attended_low, branch_back).astype(low),
        "dp",
        scatter_dimension=0,
        tiled=True,
    ).astype(jnp.float32)
    attended_five = attended_back.reshape(n_mb, MB_TOK, kvl, group, HD)
    probs_grad = jnp.einsum(
        "mtkgd,mukd->mkgtu", attended_five, values_low, preferred_element_type=jnp.float32
    )
    spread = jnp.sum(probs * probs_grad, axis=-1, keepdims=True)
    score_back = (probs * (probs_grad - spread)).astype(low)
    query_grad = (
        jnp.einsum("mkgtu,mukd->mtkgd", score_back, keys_low, preferred_element_type=jnp.float32)
        * score_scale
    )
    key_grad = (
        jnp.einsum("mkgtu,mtkgd->mukd", score_back, queries_low, preferred_element_type=jnp.float32)
        * score_scale
    )
    value_grad = jnp.einsum(
        "mkgtu,mtkgd->mukd", probs_low, attended_five, preferred_element_type=jnp.float32
    )
    query_in_grad, key_in_grad, query_gain_grad, key_gain_grad = turn_pull(
        (query_grad.reshape(n_rows, heads_own, HD), key_grad.reshape(n_rows, kvl, HD))
    )
    projected_back = jnp.concatenate(
        [
            query_in_grad.reshape(n_rows, q_width),
            key_in_grad.reshape(n_rows, kv_width),
            value_grad.reshape(n_rows, kv_width),
        ],
        axis=1,
    ).astype(low)
    normed_one_grad = scatter_tokens(contract_last(projected_back, own_qkv))
    grad_qkv = lax.psum_scatter(
        column_product(norm_one_all, projected_back)
        .astype(low)
        .reshape(nf, nd * rows_own, wide),
        "dp",
        scatter_dimension=1,
        tiled=True,
    )
    grad_blocks = swap(grad_qkv).astype(jnp.float32)

    def head_rows(blocks, times):
        merged = jnp.sum(blocks.reshape(nf // times, times, rows_own, -1), axis=1)
        return jnp.swapaxes(merged, 0, 1).reshape(rows_own, -1)

    grad_qkv = jnp.concatenate(
        [
            head_rows(grad_blocks[:, :, :q_width], 1),
            head_rows(grad_blocks[:, :, q_width : q_width + kv_width], rep),
            head_rows(grad_blocks[:, :, q_width + kv_width :], rep),
        ],
        axis=1,
    )
    rows_grad, attn_gain_grad = norm_one_pull(normed_one_grad)
    input_grad = (hidden_grad + rows_grad)[inverse]
    output_all = output.astype(low)[inverse]

    owned = (grad_qkv, grad_out, grad_gate_up, grad_down)
    local_squares = (
        jnp.sum(owned[0] * owned[0])
        + jnp.sum(owned[1] * owned[1])
        + jnp.sum(owned[2] * owned[2])
        + jnp.sum(owned[3] * owned[3])
    )
    gain_sum = jnp.concatenate([attn_gain_grad, ffn_gain_grad, query_gain_grad, key_gain_grad])
    gain_total, square_total = lax.psum((gain_sum, local_squares), ("fsdp", "dp"))
    global_norm = jnp.sqrt(square_total + jnp.sum(gain_total * gain_total))
    factor = CLIP_NORM / jnp.maximum(global_norm, CLIP_NORM)
    new_qkv, next_first_qkv, next_second_qkv = adam_step(
        w_qkv, first_qkv, second_qkv, owned[0], factor, LEARN_RATE, WEIGHT_DECAY
    )
    new_out, next_first_out, next_second_out = adam_step(
        w_out, first_out, second_out, owned[1], factor, LEARN_RATE, WEIGHT_DECAY
    )
    new_gate_up, next_first_gate_up, next_second_gate_up = adam_step(
        w_gate_up, first_gate_up, second_gate_up, owned[2], factor, LEARN_RATE, WEIGHT_DECAY
    )
    new_down, next_first_down, next_second_down = adam_step(
        w_down, first_down, second_down, owned[3], factor, LEARN_RATE, WEIGHT_DECAY
    )
    new_gains, next_first_gains, next_second_gains = adam_step(
        gains, first_gains, second_gains, gain_total, factor, GAIN_RATE, 0.0
    )
    return (
        output_all,
        input_grad,
        global_norm,
        new_qkv,
        new_out,
        new_gate_up,
        new_down,
        new_gains,
        next_first_qkv,
        next_first_out,
        next_first_gate_up,
        next_first_down,
        next_first_gains,
        next_second_qkv,
        next_second_out,
        next_second_gate_up,
        next_second_down,
        next_second_gains,
    )


def solution(mesh):
    nf, nd = mesh.shape["fsdp"], mesh.shape["dp"]
    fits = nf == PLANE and KVH == PLANE and nd % 2 == 0
    per_device = per_device_plane if fits else per_device_plain
    in_specs = (
        P(("fsdp", "dp"), None),
        P(("fsdp", "dp"), None),
        P(("fsdp", "dp"), None),
        P(("fsdp", "dp"), None),
        P(("fsdp", "dp"), None),
        P(("fsdp", "dp"), None),
        P(("fsdp", "dp"), None),
        P(("fsdp", "dp"), None),
        P(),
        P(("fsdp", "dp"), None),
        P(("fsdp", "dp"), None),
        P(("fsdp", "dp"), None),
        P(("fsdp", "dp"), None),
        P(),
        P(("fsdp", "dp"), None),
        P(("fsdp", "dp"), None),
        P(("fsdp", "dp"), None),
        P(("fsdp", "dp"), None),
        P(),
    )
    out_specs = (
        P(("fsdp", "dp"), None),
        P(("fsdp", "dp"), None),
        P(),
        P(("fsdp", "dp"), None),
        P(("fsdp", "dp"), None),
        P(("fsdp", "dp"), None),
        P(("fsdp", "dp"), None),
        P(),
        P(("fsdp", "dp"), None),
        P(("fsdp", "dp"), None),
        P(("fsdp", "dp"), None),
        P(("fsdp", "dp"), None),
        P(),
        P(("fsdp", "dp"), None),
        P(("fsdp", "dp"), None),
        P(("fsdp", "dp"), None),
        P(("fsdp", "dp"), None),
        P(),
    )
    return jax.shard_map(
        functools.partial(per_device, nf, nd), mesh=mesh, in_specs=in_specs, out_specs=out_specs, check_vma=False
    )
```

```python
import functools

import jax
import jax.numpy as jnp
from jax import lax
from jax.experimental import pallas as pl
from jax.experimental.pallas import tpu as pltpu
from jax.sharding import PartitionSpec as P

D = 2048
HEADS = 32
HD = 64
KVH = 8
FF = 8192
TOK_DEV = 256
MB = 2
SEQS = 3
STEP = 10
MB_TOK = 128


EPSILON = 1e-05
ROPE_BASE = 1000000.0
FIRST_DECAY = 0.9
SECOND_DECAY = 0.95
LEARN_RATE = 0.05
GAIN_RATE = 2.0
WEIGHT_DECAY = 0.1
ADAM_EPSILON = 1e-08
CLIP_NORM = 1.0
GAIN_LINES = (2 * D + 2 * HD) // 128
MASKED = -1e30


def rms_norm(values, gain_vec):
    return (
        values * lax.rsqrt(jnp.mean(values * values, axis=-1, keepdims=True) + EPSILON) * gain_vec
    )


def rope_tables(position):
    half_width = HD // 2
    frequency = ROPE_BASE ** (jnp.arange(half_width, dtype=jnp.float32) * (-2.0 / HD))
    angles = position[:, None] * frequency[None, :]
    return (jnp.cos(angles)[:, None, :], jnp.sin(angles)[:, None, :])


def rotate(values, cosine_table, sine_table):
    half_width = HD // 2
    first_part = values[..., :half_width]
    second_part = values[..., half_width:]
    return jnp.concatenate(
        [
            first_part * cosine_table - second_part * sine_table,
            second_part * cosine_table + first_part * sine_table,
        ],
        axis=-1,
    )


def layout(lengths_rows):
    seq_ends = jnp.cumsum(lengths_rows, axis=-1)
    places = jnp.arange(MB_TOK, dtype=jnp.int32)
    passed = (places[None, :, None] >= seq_ends[:, None, :]).astype(jnp.int32)
    segment = jnp.sum(passed, axis=-1)
    starts = jnp.sum(passed * lengths_rows[:, None, :], axis=-1)
    position = (places[None, :] - starts).astype(jnp.float32)
    valid_rows = (segment < SEQS - 1).astype(jnp.float32)
    allowed = (segment[:, :, None] == segment[:, None, :]) & (
        places[None, None, :] <= places[None, :, None]
    )
    return (position, valid_rows, allowed)


def swiglu(gate, up):
    return jax.nn.silu(gate) * up


def column_product(left_side, right_side):
    return lax.dot_general(
        left_side, right_side, (((0,), (0,)), ((), ())), preferred_element_type=jnp.float32
    )


def contract_last(left_side, right_side):
    return lax.dot_general(
        left_side, right_side, (((1,), (1,)), ((), ())), preferred_element_type=jnp.float32
    )


def product(left_side, right_side):
    return jnp.dot(left_side, right_side, preferred_element_type=jnp.float32)


def adam_step(weight, first_state, second, gradient, factor, step_rate, decay_rate):
    clipped = gradient * factor
    first_new = FIRST_DECAY * first_state + (1.0 - FIRST_DECAY) * clipped
    second_new = SECOND_DECAY * second + (1.0 - SECOND_DECAY) * clipped * clipped
    first_hat = first_new / (1.0 - FIRST_DECAY**STEP)
    second_hat = second_new / (1.0 - SECOND_DECAY**STEP)
    weight_new = weight - step_rate * (
        first_hat / (jnp.sqrt(second_hat) + ADAM_EPSILON) + decay_rate * weight
    )
    return (weight_new, first_new, second_new)


MESH = pl.DeviceIdType.MESH
ANY = pl.BlockSpec(memory_space=pl.ANY)
VMEM = pl.BlockSpec(memory_space=pltpu.VMEM)
PLANE = 8
TILE = 512
GLU_TILE = 256
SHORT = pl.CostEstimate(flops=0, bytes_accessed=1024, transcendentals=0)


def flip(index, bit):
    step = 2**bit
    return index + step * (1 - 2 * lax.rem(lax.div(index, step), 2))


def plane_others(me):
    others = []
    for number in range(1, PLANE):
        other = me
        for bit in range(3):
            if (number >> bit) & 1:
                other = flip(other, bit)
        others.append(other)
    return others


def greet(devices):
    barrier = pltpu.get_barrier_semaphore()
    for device in devices:
        pl.semaphore_signal(barrier, inc=1, device_id={"fsdp": device}, device_id_type=MESH)
    pl.semaphore_wait(barrier, len(devices))


def half_pieces(half_ref, wide_ref, me, other, count):
    half_width = half_ref.shape[1] // 2
    for side in range(2):
        first = pl.multiple_of(side * half_width * PLANE + me * half_width, 128)
        source = half_ref.at[pl.ds(pl.multiple_of(other * count, count), count)]
        yield (
            source.at[:, pl.ds(side * half_width, half_width)],
            wide_ref.at[:, pl.ds(first, half_width)],
        )


def put_half(half_ref, wide_ref, others, number, sems):
    me, other = lax.axis_index("fsdp"), others[number - 1]
    pairs = half_pieces(half_ref, wide_ref, me, other, wide_ref.shape[0])
    return [
        pltpu.make_async_remote_copy(
            src_ref=source,
            dst_ref=target,
            send_sem=sems.at[0, 2 * number + side],
            recv_sem=sems.at[1, 2 * number + side],
            device_id={"fsdp": other},
            device_id_type=MESH,
        )
        for side, (source, target) in enumerate(pairs)
    ]


def keep_half(half_ref, wide_ref, sems):
    me = lax.axis_index("fsdp")
    return [
        pltpu.make_async_copy(source, target, sems.at[side])
        for side, (source, target) in enumerate(
            half_pieces(half_ref, wide_ref, me, me, wide_ref.shape[0])
        )
    ]


def columns_kernel(half_ref, wide_ref, squares_ref, own_sem, sems):
    others = plane_others(lax.axis_index("fsdp"))
    greet(others)
    order = (6, 7, 2, 4, 3, 5, 1)
    for number in order:
        for copy in put_half(half_ref, wide_ref, others, number, sems):
            copy.start()
    keep = keep_half(half_ref, wide_ref, own_sem)
    for copy in keep:
        copy.start()
    squares_ref[...] = jnp.zeros_like(squares_ref)

    @pl.loop(0, half_ref.shape[0] // 128)
    def _(step):
        spot = pl.ds(pl.multiple_of(step * 128, 128), 128)
        values = half_ref[spot, :].astype(jnp.float32)
        squares_ref[...] += jnp.sum(values * values, axis=0, keepdims=True)

    for number in order:
        for copy in put_half(half_ref, wide_ref, others, number, sems):
            copy.wait()
    for copy in keep:
        copy.wait()


def half_scratch():
    return [pltpu.SemaphoreType.DMA((2,)), pltpu.SemaphoreType.DMA((2, 2 * PLANE))]


def exchange_half(half, count, number):
    return pl.pallas_call(
        columns_kernel,
        out_shape=[
            jax.ShapeDtypeStruct((count, half.shape[1] * PLANE), half.dtype),
            jax.ShapeDtypeStruct((1, half.shape[1]), jnp.float32),
        ],
        in_specs=[VMEM],
        out_specs=[ANY, VMEM],
        scratch_shapes=half_scratch(),
        compiler_params=pltpu.CompilerParams(collective_id=number, has_side_effects=True),
        cost_estimate=SHORT,
        name=f"exchange_half_{number}",
    )(half)


def sum_kernel(
    nd,
    x_ref,
    blocks_ref,
    out_ref,
    norm_ref,
    qkv_ref,
    gout_ref,
    swapped_ref,
    plane_in,
    line_in,
    total,
    mine,
    own_sem,
    plane_sems,
    line_sems,
    block_sems,
):
    me, line = lax.axis_index("fsdp"), lax.axis_index("dp")
    wide = swapped_ref.shape[2]
    q_width = wide - 2 * HD
    blocks = blocks_ref[...].astype(jnp.float32)
    squares = jnp.sum(blocks * blocks, axis=(0, 1, 2), keepdims=True).reshape(1, 1)
    lines = lax.broadcasted_iota(jnp.int32, x_ref.shape, 0)
    lane = lax.broadcasted_iota(jnp.int32, x_ref.shape, 1)
    spot = jnp.logical_and(lines == GAIN_LINES, lane == 0)
    mine[...] = x_ref[...] + jnp.where(spot, squares, 0.0)
    others = plane_others(me)
    steps = [lax.rem(line + step, nd) for step in range(1, nd)]
    barrier = pltpu.get_barrier_semaphore()
    for other in others:
        pl.semaphore_signal(barrier, inc=1, device_id={"fsdp": other}, device_id_type=MESH)
    for other in steps:
        pl.semaphore_signal(barrier, inc=1, device_id={"dp": other}, device_id_type=MESH)
    pl.semaphore_wait(barrier, len(others) + len(steps))

    def to_plane(number):
        return pltpu.make_async_remote_copy(
            src_ref=mine,
            dst_ref=plane_in.at[me],
            send_sem=plane_sems.at[0, number],
            recv_sem=plane_sems.at[1, number],
            device_id={"fsdp": others[number]},
            device_id_type=MESH,
        )

    def to_line(number):
        return pltpu.make_async_remote_copy(
            src_ref=total,
            dst_ref=line_in.at[line],
            send_sem=line_sems.at[0, number],
            recv_sem=line_sems.at[1, number],
            device_id={"dp": steps[number]},
            device_id_type=MESH,
        )

    def put_block(number):
        return pltpu.make_async_remote_copy(
            src_ref=blocks_ref.at[others[number], :, pl.ds(0, wide)],
            dst_ref=swapped_ref.at[me],
            send_sem=block_sems.at[0, number],
            recv_sem=block_sems.at[1, number],
            device_id={"fsdp": others[number]},
            device_id_type=MESH,
        )

    keep = [
        pltpu.make_async_copy(
            blocks_ref.at[me, :, pl.ds(0, wide)], swapped_ref.at[me], own_sem.at[PLANE]
        )
    ]
    for place in range(PLANE):
        keep.append(
            pltpu.make_async_copy(
                blocks_ref.at[place, :, pl.ds(wide, q_width)],
                gout_ref.at[:, pl.ds(place * q_width, q_width)],
                own_sem.at[place],
            )
        )
    for number in range(PLANE - 1):
        to_plane(number).start()
    for number in range(PLANE - 1):
        put_block(number).start()
    for copy in keep:
        copy.start()
    plane_in[me] = mine[...]
    for number in range(PLANE - 1):
        to_plane(number).wait()
    part = plane_in[0]
    for place in range(1, PLANE):
        part = part + plane_in[place]
    total[...] = part
    line_in[line] = part
    for number in range(nd - 1):
        to_line(number).start()
    for number in range(PLANE - 1):
        put_block(number).wait()
    for copy in keep:
        copy.wait()
    first_head = lax.broadcasted_iota(jnp.int32, (1, 2 * HD), 1) < HD
    for place in range(0, PLANE, 2):
        pair = []
        for block in (place, place + 1):
            values = swapped_ref[block].astype(jnp.float32)
            qkv_ref[:, block * q_width : (block + 1) * q_width] = swapped_ref[block, :, :q_width]
            pair.append(values[:, q_width:])
        columns = pl.ds(PLANE * q_width + place * HD, 2 * HD)
        both = jnp.where(first_head, pair[0], pltpu.roll(pair[1], HD, 1))
        qkv_ref[:, columns] = both.astype(qkv_ref.dtype)
        columns = pl.ds(PLANE * (q_width + HD) + place * HD, 2 * HD)
        both = jnp.where(first_head, pltpu.roll(pair[0], HD, 1), pair[1])
        qkv_ref[:, columns] = both.astype(qkv_ref.dtype)
    for number in range(nd - 1):
        to_line(number).wait()
    part = line_in[0]
    for place in range(1, nd):
        part = part + line_in[place]
    out_ref[...] = part
    gains = part[:GAIN_LINES]
    lane = lax.broadcasted_iota(jnp.int32, (1, 128), 1)
    squares = jnp.where(lane == 0, part[GAIN_LINES : GAIN_LINES + 1], 0.0)
    squares = squares + jnp.sum(gains * gains, axis=0, keepdims=True)
    norm = jnp.sqrt(jnp.sum(squares, axis=1, keepdims=True))
    factor = CLIP_NORM / jnp.maximum(norm, CLIP_NORM)
    line_number = lax.broadcasted_iota(jnp.int32, norm_ref.shape, 0)
    norm_ref[...] = jnp.where(line_number == 0, norm, factor)


def sum_everywhere(gain_sum, squares, blocks, wide, number):
    values = jnp.concatenate([gain_sum, squares.reshape(1)])
    nd = lax.axis_size("dp")
    count = values.shape[0]
    lines = -(-count // 1024) * 8
    padded = jnp.pad(values, (0, lines * 128 - count)).reshape(lines, 128)
    q_width = wide - 2 * HD
    summed, norm, grad_qkv, grad_out = pl.pallas_call(
        functools.partial(sum_kernel, nd),
        out_shape=[
            jax.ShapeDtypeStruct(padded.shape, jnp.float32),
            jax.ShapeDtypeStruct((8, 128), jnp.float32),
            jax.ShapeDtypeStruct((blocks.shape[1], PLANE * wide), blocks.dtype),
            jax.ShapeDtypeStruct((blocks.shape[1], PLANE * q_width), blocks.dtype),
        ],
        in_specs=[VMEM, VMEM],
        out_specs=[VMEM] * 4,
        scratch_shapes=[
            pltpu.VMEM((PLANE, blocks.shape[1], wide), blocks.dtype),
            pltpu.VMEM((PLANE,) + padded.shape, jnp.float32),
            pltpu.VMEM((nd,) + padded.shape, jnp.float32),
            pltpu.VMEM(padded.shape, jnp.float32),
            pltpu.VMEM(padded.shape, jnp.float32),
            pltpu.SemaphoreType.DMA((PLANE + 1,)),
            pltpu.SemaphoreType.DMA((2, PLANE - 1)),
            pltpu.SemaphoreType.DMA((2, nd - 1)),
            pltpu.SemaphoreType.DMA((2, PLANE - 1)),
        ],
        compiler_params=pltpu.CompilerParams(collective_id=number, has_side_effects=True),
        cost_estimate=SHORT,
        name=f"sum_everywhere_{number}",
    )(padded, blocks)
    return summed.reshape(-1)[: count - 1], norm, grad_qkv, grad_out


def greet_line(nd, others):
    line = lax.axis_index("dp")
    barrier = pltpu.get_barrier_semaphore()
    for other in others:
        pl.semaphore_signal(barrier, inc=1, device_id={"fsdp": other}, device_id_type=MESH)

    @pl.when(line < nd - 1)
    def _():
        pl.semaphore_signal(barrier, inc=1, device_id={"dp": line + 1}, device_id_type=MESH)

    @pl.when(line > 0)
    def _():
        pl.semaphore_signal(barrier, inc=1, device_id={"dp": line - 1}, device_id_type=MESH)

    neighbours = lax.div(line + nd - 1, nd) + lax.div(2 * nd - 2 - line, nd)
    pl.semaphore_wait(barrier, len(others) + neighbours)


class Gather:
    def __init__(self, own_ref, all_ref, send_sem, recv_sem):
        self.own_ref, self.all_ref = own_ref, all_ref
        self.send_sem, self.recv_sem = send_sem, recv_sem
        self.me = lax.axis_index("fsdp")
        self.sibling, self.x_next, self.y_next = flip(self.me, 0), flip(self.me, 1), flip(self.me, 2)
        self.diagonal = flip(self.x_next, 2)
        self.rows = own_ref.shape[0]
        self.sent = []

    def put(self, slot, owner, part, target, own=False):
        half = self.rows // 2
        if part is None:
            spot = self.all_ref.at[pl.ds(pl.multiple_of(owner * self.rows, half), self.rows)]
            source = self.own_ref
        else:
            first = pl.multiple_of(owner * self.rows + part * half, half)
            spot = self.all_ref.at[pl.ds(first, half)]
            source = self.own_ref.at[pl.ds(part * half, half)]
        return pltpu.make_async_remote_copy(
            src_ref=source if own else spot,
            dst_ref=spot,
            send_sem=self.send_sem.at[slot],
            recv_sem=self.recv_sem.at[slot],
            device_id={"fsdp": target},
            device_id_type=MESH,
        )

    def begin(self):
        for slot, part, target in (
            (0, 0, self.x_next),
            (2, 1, self.y_next),
            (4, None, self.sibling),
            (1, 1, self.x_next),
            (3, 0, self.y_next),
        ):
            copy = self.put(slot, self.me, part, target, own=True)
            copy.start()
            self.sent.append(copy)

    def take(self, slot):
        sibling = self.sibling
        owner, part, onward = {
            0: (self.x_next, 0, ((5, self.y_next), (7, sibling))),
            1: (self.x_next, 1, ((8, sibling),)),
            2: (self.y_next, 1, ((6, self.x_next), (9, sibling))),
            3: (self.y_next, 0, ((10, sibling),)),
            4: (sibling, None, ()),
            5: (self.diagonal, 0, ((11, sibling),)),
            6: (self.diagonal, 1, ((12, sibling),)),
            7: (flip(self.x_next, 0), 0, ()),
            8: (flip(self.x_next, 0), 1, ()),
            9: (flip(self.y_next, 0), 1, ()),
            10: (flip(self.y_next, 0), 0, ()),
            11: (flip(self.diagonal, 0), 0, ()),
            12: (flip(self.diagonal, 0), 1, ()),
        }[slot]
        self.put(slot, owner, part, sibling).wait_recv()
        for next_slot, target in onward:
            copy = self.put(next_slot, owner, part, target)
            copy.start()
            self.sent.append(copy)

    def finish(self):
        for copy in self.sent:
            copy.wait_send()


def gather_scratch():
    return [pltpu.SemaphoreType.DMA((13,)), pltpu.SemaphoreType.DMA((13,))]


class Scatter:
    def __init__(self, out_ref, block, refs):
        self.out_ref, self.block = out_ref, block
        (self.sib_out, self.sib_in, self.far_out, self.far_in, self.near_out, self.near_in) = refs[:6]
        self.late = refs[6]
        self.sib_sems, self.far_sems, self.near_sems = refs[7:9], refs[9:11], refs[11:13]
        self.me = lax.axis_index("fsdp")
        self.sibling, self.x_next, self.y_next = flip(self.me, 0), flip(self.me, 1), flip(self.me, 2)
        self.targets = (flip(self.x_next, 2), self.x_next, self.y_next, self.me)
        self.half = out_ref.shape[0] // 2

    def send(self, source, target, sems, slot, device):
        return pltpu.make_async_remote_copy(
            src_ref=source.at[slot],
            dst_ref=target.at[slot],
            send_sem=sems[0].at[slot],
            recv_sem=sems[1].at[slot],
            device_id={"fsdp": device},
            device_id_type=MESH,
        )

    def to_sibling(self, place):
        return self.send(self.sib_out, self.sib_in, self.sib_sems, place, self.sibling)

    def to_far(self, part):
        device = (self.x_next, self.y_next)[part]
        return self.send(self.far_out, self.far_in, self.far_sems, part, device)

    def to_near(self, place, part):
        device = (self.x_next, self.y_next)[place]
        return self.send(self.near_out, self.near_in, self.near_sems, 2 * place + part, device)

    def for_sibling(self, place):
        def write(columns, part):
            self.sib_out[place, :, columns] = part.astype(jnp.bfloat16)

        self.block(flip(self.targets[place], 0), write)
        self.to_sibling(place).start()

    def for_far(self):
        self.to_sibling(0).wait_recv()

        def write(columns, part):
            whole = (part + self.sib_in[0, :, columns].astype(jnp.float32)).astype(jnp.bfloat16)
            self.far_out[0, :, columns] = whole[: self.half]
            self.far_out[1, :, columns] = whole[self.half :]

        self.block(self.targets[0], write)
        self.to_far(0).start()
        self.to_far(1).start()

    def for_near(self, place):
        self.to_sibling(1 + place).wait_recv()
        other = 1 - place

        def write(columns, part):
            whole = part + self.sib_in[1 + place, :, columns].astype(jnp.float32)
            halves = (whole[: self.half], whole[self.half :])
            self.near_out[2 * place + place, :, columns] = halves[place].astype(jnp.bfloat16)
            self.late[place, :, columns] = halves[other]

        self.block(self.targets[1 + place], write)
        self.to_near(place, place).start()

    def finish_near(self, place):
        other = 1 - place
        self.to_far(other).wait_recv()
        whole = self.late[place] + self.far_in[other].astype(jnp.float32)
        self.near_out[2 * place + other] = whole.astype(jnp.bfloat16)
        self.to_near(place, other).start()

    def own(self):
        def write(columns, part):
            self.out_ref[:, columns] = part

        self.block(self.me, write)

    def finish(self):
        self.to_sibling(3).wait_recv()
        self.out_ref[...] = self.out_ref[...] + self.sib_in[3].astype(jnp.float32)
        for part, place in ((0, 0), (1, 1), (1, 0), (0, 1)):
            self.to_near(place, part).wait_recv()
            spot = pl.ds(part * self.half, self.half)
            part_in = self.near_in[2 * place + part].astype(jnp.float32)
            self.out_ref[spot, :] = self.out_ref[spot, :] + part_in
        for place in range(4):
            self.to_sibling(place).wait_send()
            self.to_near(place // 2, place % 2).wait_send()
        for part in range(2):
            self.to_far(part).wait_send()


def staged(kernel, n_in, places):
    def body(*refs):
        stage, sems = refs[-len(places) - 1 : -1], refs[-1]
        inputs, rest = list(refs[:n_in]), refs[n_in : -len(places) - 1]
        copies = [
            pltpu.make_async_copy(inputs[place], buffer, sems.at[index])
            for index, (place, buffer) in enumerate(zip(places, stage))
        ]
        for copy in copies:
            copy.start()
        for place, buffer in zip(places, stage):
            inputs[place] = buffer

        def ready():
            for copy in copies:
                copy.wait()

        kernel(ready, *inputs, *rest)

    return body


def staged_specs(arrays, places):
    specs = [ANY if place in places else VMEM for place in range(len(arrays))]
    scratch = [pltpu.VMEM(arrays[place].shape, arrays[place].dtype) for place in places]
    return specs, scratch + [pltpu.SemaphoreType.DMA((len(places),))]


def scatter_scratch(rows, width):
    low, half = jnp.bfloat16, rows // 2
    return [
        pltpu.VMEM((4, rows, width), low),
        pltpu.VMEM((4, rows, width), low),
        pltpu.VMEM((2, half, width), low),
        pltpu.VMEM((2, half, width), low),
        pltpu.VMEM((4, half, width), low),
        pltpu.VMEM((4, half, width), low),
        pltpu.VMEM((2, half, width), jnp.float32),
        pltpu.SemaphoreType.DMA((4,)),
        pltpu.SemaphoreType.DMA((4,)),
        pltpu.SemaphoreType.DMA((2,)),
        pltpu.SemaphoreType.DMA((2,)),
        pltpu.SemaphoreType.DMA((4,)),
        pltpu.SemaphoreType.DMA((4,)),
    ]


def block_product(left_refs, right_refs, rows, width, turned):
    def block(owner, write):
        @pl.loop(0, width // TILE)
        def _(step):
            columns = pl.ds(pl.multiple_of(step * TILE, TILE), TILE)
            spot = pl.ds(pl.multiple_of(owner * rows, rows), rows)
            total = None
            for left_ref, right_ref in zip(left_refs, right_refs):
                if turned:
                    part = contract_last(left_ref[spot, :], right_ref[columns, :])
                else:
                    part = product(left_ref[spot, :], right_ref[:, columns])
                total = part if total is None else total + part
            write(columns, total)

    return block


def scatter_kernel(turned, count, *refs):
    left_hbm, right_hbm, out_ref = refs[:count], refs[count : 2 * count], refs[2 * count]
    refs = refs[2 * count + 1 :]
    left_refs, right_refs = refs[:count], refs[count : 2 * count]
    left_sems, right_sems, refs = refs[2 * count], refs[2 * count + 1], refs[2 * count + 2 :]
    rows, width = out_ref.shape
    whole = block_product(left_refs, right_refs, rows, width, turned)

    def fetch(place, owner):
        spot = pl.ds(pl.multiple_of(owner * rows, rows), rows)
        return pltpu.make_async_copy(
            left_hbm[place].at[spot], left_refs[place].at[spot], left_sems.at[place, owner]
        )

    def block(owner, write):
        for place in range(count):
            fetch(place, owner).wait()
        whole(owner, write)

    scatter = Scatter(out_ref, block, refs)
    rights = [
        pltpu.make_async_copy(right_hbm[place], right_refs[place], right_sems.at[place])
        for place in range(count)
    ]
    for copy in rights:
        copy.start()
    far, x_next, y_next, me = scatter.targets
    for owner in (
        flip(far, 0),
        flip(x_next, 0),
        far,
        flip(y_next, 0),
        x_next,
        flip(me, 0),
        y_next,
        me,
    ):
        for place in range(count):
            fetch(place, owner).start()
    greet((scatter.sibling, scatter.x_next, scatter.y_next))
    for copy in rights:
        copy.wait()
    scatter.for_sibling(0)
    scatter.for_sibling(1)
    scatter.for_far()
    scatter.for_sibling(2)
    scatter.for_near(0)
    scatter.for_sibling(3)
    scatter.for_near(1)
    scatter.finish_near(0)
    scatter.finish_near(1)
    scatter.own()
    scatter.finish()


def pass_through(ready, gather, scatter, work, between):
    me, sibling, x_next, y_next = gather.me, gather.sibling, gather.x_next, gather.y_next
    diagonal = gather.diagonal
    greet((sibling, x_next, y_next))
    gather.begin()
    gather.all_ref[pl.ds(pl.multiple_of(me * gather.rows, gather.rows), gather.rows), :] = (
        gather.own_ref[...]
    )
    ready()
    work((me,))
    gather.take(0)
    gather.take(2)
    gather.take(4)
    work((sibling,))
    scatter.for_sibling(3)
    gather.take(1)
    gather.take(3)
    work((x_next, y_next))
    gather.take(5)
    gather.take(6)
    for slot in (7, 8, 9, 10):
        gather.take(slot)
    work((flip(x_next, 0), flip(y_next, 0)))
    scatter.for_sibling(1)
    scatter.for_sibling(2)
    scatter.for_near(0)
    scatter.for_near(1)
    gather.take(11)
    gather.take(12)
    work((flip(diagonal, 0),))
    scatter.for_sibling(0)
    work((diagonal,))
    scatter.for_far()
    scatter.own()
    between[0]()
    scatter.finish_near(0)
    scatter.finish_near(1)
    between[1]()
    scatter.finish()
    gather.finish()


def each_owner(owners, rows, one):
    if len(owners) == 1:
        one(owners[0])
        return

    @pl.loop(0, len(owners))
    def _(step):
        one(owners[0] + step * (owners[1] - owners[0]))


def lanes():
    lane = lax.broadcasted_iota(jnp.int32, (1, 2 * HD), 1)
    row_head = lax.broadcasted_iota(jnp.int32, (2 * HD, 2 * HD), 0) // HD
    column_head = lax.broadcasted_iota(jnp.int32, (2 * HD, 2 * HD), 1) // HD
    spread = jnp.where(row_head == column_head, 1.0 / HD, 0.0).astype(jnp.float32)

    def head_mean(values):
        return jnp.dot(
            values, spread, precision=lax.Precision.HIGHEST, preferred_element_type=jnp.float32
        )

    first_half = lax.rem(lane, HD) < HD // 2

    def turn_quarter(values):
        return jnp.where(
            first_half,
            -pltpu.roll(values, 2 * HD - HD // 2, 1),
            pltpu.roll(values, HD // 2, 1),
        )

    def sides(values):
        return [
            jnp.where(chosen, values, 0.0).astype(jnp.bfloat16)
            for chosen in (lane < HD, lane >= HD)
        ]

    return lane, sides, head_mean, turn_quarter


def twice(values):
    return jnp.concatenate([values, values], axis=0)


def stacked(ref, spot):
    width = 2 * HD
    return jnp.concatenate([ref[spot, :width], ref[spot, width : 2 * width]], axis=0)


def attend_kernel(
    ready,
    x_ref,
    wqkv_ref,
    wo_ref,
    cos_ref,
    sin_ref,
    mask_ref,
    gain_ref,
    out_ref,
    all_out_ref,
    proj_ref,
    q_ref,
    kk_ref,
    vv_ref,
    o_ref,
    lse_ref,
    all_ref,
    out_sem,
    gather_send,
    gather_recv,
    *refs,
):
    rows, width = out_ref.shape
    low = jnp.bfloat16
    pair_width = 2 * HD
    lane, sides, head_mean, turn_quarter = lanes()
    first_head = lane < HD
    scale = HD ** (-0.5)

    def normed(values, gain):
        return values * lax.rsqrt(head_mean(values * values) + EPSILON) * gain

    def one(owner):
        base = pl.multiple_of(owner * rows, rows)
        spot = pl.ds(base, rows)
        proj_ref[spot, :] = product(all_ref[spot, :], wqkv_ref[...])

        for part in range(MB):
            micro(pl.multiple_of(base + part * MB_TOK, MB_TOK), owner * MB + part)

    def micro(first, number):
        spot = pl.ds(first, MB_TOK)
        cosine, sine = cos_ref[spot, :], sin_ref[spot, :]
        allowed = twice(mask_ref[number]) > 0.5
        kv = proj_ref[spot, 2 * pair_width : 3 * pair_width]
        swapped = pltpu.roll(kv, HD, 1)
        values = jnp.where(first_head, swapped, kv)
        keys = normed(jnp.where(first_head, kv, swapped), gain_ref[1:2, :])
        keys = (keys * cosine + turn_quarter(keys) * sine).astype(low)
        kk_ref[spot, :] = keys
        vv_ref[spot, :] = values.astype(low)
        query = normed(stacked(proj_ref, spot), gain_ref[0:1, :])
        query = (query * twice(cosine) + turn_quarter(query) * twice(sine)).astype(low)
        q_ref[spot, :pair_width] = query[:MB_TOK]
        q_ref[spot, pair_width : 2 * pair_width] = query[MB_TOK:]
        probs, logs = [], []
        for one_query in sides(query.astype(jnp.float32) * scale):
            scores = jnp.where(allowed, contract_last(one_query, keys), MASKED)
            peak = jnp.max(scores, axis=-1, keepdims=True)
            powers = jnp.exp(scores - peak)
            total = jnp.sum(powers, axis=-1, keepdims=True)
            probs.append((powers * (1.0 / total)).astype(low))
            logs.append(peak + jnp.log(total))
        wide_values = jnp.concatenate(sides(values), axis=0)
        attended = product(jnp.concatenate(probs, axis=1), wide_values).astype(low)
        o_ref[spot, :pair_width] = attended[:MB_TOK]
        o_ref[spot, pair_width : 2 * pair_width] = attended[MB_TOK:]
        log_totals = jnp.where(lane == 0, logs[0][:MB_TOK], logs[1][:MB_TOK])
        log_totals = jnp.where(lane == 2, logs[0][MB_TOK:], log_totals)
        lse_ref[spot, :] = jnp.where(lane == 3, logs[1][MB_TOK:], log_totals)

    gather = Gather(x_ref, all_ref, gather_send, gather_recv)
    scatter = Scatter(out_ref, block_product((o_ref,), (wo_ref,), rows, width, False), refs)
    keep = pltpu.make_async_copy(all_ref, all_out_ref, out_sem)
    pass_through(
        ready,
        gather,
        scatter,
        lambda owners: each_owner(owners, rows, one),
        (keep.start, lambda: None),
    )
    keep.wait()


def attend_back_kernel(
    ready,
    x_ref,
    wqkv_ref,
    wo_ref,
    cos_ref,
    sin_ref,
    mask_ref,
    gain_ref,
    proj_ref,
    q_ref,
    kk_ref,
    vv_ref,
    o_ref,
    lse_ref,
    normed_hbm,
    out_ref,
    grad_ref,
    ggain_ref,
    all_ref,
    normed_ref,
    do_ref,
    dproj_ref,
    in_sem,
    gather_send,
    gather_recv,
    *refs,
):
    rows, width = out_ref.shape
    low = jnp.bfloat16
    pair_width = 2 * HD
    lane, sides, head_mean, turn_quarter = lanes()
    first_head = lane < HD
    scale = HD ** (-0.5)
    fetch = pltpu.make_async_copy(normed_hbm, normed_ref, in_sem)
    fetch.start()
    ggain_ref[...] = jnp.zeros_like(ggain_ref)

    def through_norm(grad, cosine, sine, raw, gain, row):
        grad = grad * cosine - turn_quarter(grad) * sine
        root = lax.rsqrt(head_mean(raw * raw) + EPSILON)
        normed = raw * root
        ggain_ref[row : row + 1, :] += jnp.sum(grad * normed, axis=0, keepdims=True)
        scaled = grad * gain
        return root * (scaled - normed * head_mean(scaled * normed))

    def one(owner):
        base = pl.multiple_of(owner * rows, rows)
        do_ref[...] = contract_last(all_ref[pl.ds(base, rows), :], wo_ref[...]).astype(low)

        for part in range(MB):
            here = pl.ds(part * MB_TOK, MB_TOK)
            micro(pl.multiple_of(base + part * MB_TOK, MB_TOK), here, owner * MB + part)

    def micro(first, here, number):
        spot = pl.ds(first, MB_TOK)
        cosine, sine = cos_ref[spot, :], sin_ref[spot, :]
        allowed = twice(mask_ref[number]) > 0.5
        keys, values = kk_ref[spot, :], vv_ref[spot, :]
        logs = lse_ref[spot, :]
        queries = sides(stacked(q_ref, spot).astype(jnp.float32) * scale)
        branches = sides(stacked(do_ref, here).astype(jnp.float32))
        probs_low, scores_back = [], []
        for side in range(2):
            log_total = jnp.concatenate(
                [logs[:, side : side + 1], logs[:, 2 + side : 3 + side]], axis=0
            )
            scores = jnp.where(allowed, contract_last(queries[side], keys), MASKED)
            probs = jnp.exp(scores - log_total)
            probs_grad = contract_last(branches[side], values)
            spread = jnp.sum(probs * probs_grad, axis=-1, keepdims=True)
            scores_back.append((probs * (probs_grad - spread)).astype(low))
            probs_low.append(probs.astype(low))
        wide_keys = jnp.concatenate(sides(keys.astype(jnp.float32)), axis=0)
        query_grad = product(jnp.concatenate(scores_back, axis=1), wide_keys) * scale
        key_grad = column_product(
            jnp.concatenate(scores_back, axis=0), jnp.concatenate(queries, axis=0)
        )
        value_grad = column_product(
            jnp.concatenate(probs_low, axis=0), jnp.concatenate(branches, axis=0)
        )
        raw = stacked(proj_ref, spot)
        grad = through_norm(query_grad, twice(cosine), twice(sine), raw, gain_ref[0:1, :], 0)
        dproj_ref[spot, :pair_width] = grad[:MB_TOK].astype(low)
        dproj_ref[spot, pair_width : 2 * pair_width] = grad[MB_TOK:].astype(low)
        kv = proj_ref[spot, 2 * pair_width : 3 * pair_width]
        raw = jnp.where(first_head, kv, pltpu.roll(kv, HD, 1))
        key_grad = key_grad + pltpu.roll(key_grad, HD, 1)
        value_grad = value_grad + pltpu.roll(value_grad, HD, 1)
        grad = through_norm(key_grad, cosine, sine, raw, gain_ref[1:2, :], 1)
        both = jnp.where(first_head, grad, value_grad).astype(low)
        dproj_ref[spot, 2 * pair_width : 3 * pair_width] = both

    wide, q_width = dproj_ref.shape[1], o_ref.shape[1]

    def out_grad():
        @pl.loop(0, width // TILE)
        def _(step):
            columns = pl.ds(pl.multiple_of(step * TILE, TILE), TILE)
            part = column_product(o_ref[...], all_ref[:, columns]).astype(low)
            for first in range(0, TILE, q_width):
                spot = pl.ds(pl.multiple_of(step * TILE + first, q_width), q_width)
                grad_ref[spot, wide:] = part[:, first : first + q_width]

    def qkv_grad():
        fetch.wait()

        @pl.loop(0, width // TILE)
        def _(step):
            columns = pl.ds(pl.multiple_of(step * TILE, TILE), TILE)
            part = column_product(dproj_ref[...], normed_ref[:, columns])
            grad_ref[columns, :wide] = jnp.transpose(part).astype(low)

    gather = Gather(x_ref, all_ref, gather_send, gather_recv)
    scatter = Scatter(out_ref, block_product((dproj_ref,), (wqkv_ref,), rows, width, True), refs)
    pass_through(
        ready, gather, scatter, lambda owners: each_owner(owners, rows, one), (out_grad, qkv_grad)
    )


def attend(own_rows, own_qkv, own_out, tables, number):
    rows, width = own_rows.shape
    count, wide, q_width = PLANE * rows, own_qkv.shape[1], own_out.shape[0]
    low = jnp.bfloat16
    arrays = (own_rows, own_qkv, own_out, *tables)
    places = tuple(range(1, len(arrays)))
    specs, stage = staged_specs(arrays, places)
    return pl.pallas_call(
        staged(attend_kernel, len(arrays), places),
        out_shape=[
            jax.ShapeDtypeStruct((rows, width), jnp.float32),
            jax.ShapeDtypeStruct((count, width), low),
            jax.ShapeDtypeStruct((count, wide), jnp.float32),
            jax.ShapeDtypeStruct((count, q_width), low),
            jax.ShapeDtypeStruct((count, 2 * HD), low),
            jax.ShapeDtypeStruct((count, 2 * HD), low),
            jax.ShapeDtypeStruct((count, q_width), low),
            jax.ShapeDtypeStruct((count, 2 * HD), jnp.float32),
        ],
        in_specs=specs,
        out_specs=[VMEM, ANY] + [VMEM] * 6,
        scratch_shapes=[pltpu.VMEM((count, width), low), pltpu.SemaphoreType.DMA]
        + gather_scratch()
        + scatter_scratch(rows, width)
        + stage,
        compiler_params=pltpu.CompilerParams(
            collective_id=number, has_side_effects=True, vmem_limit_bytes=56 * 2**20
        ),
        cost_estimate=SHORT,
        name=f"attend_{number}",
    )(*arrays)


def attend_back(own_rows, own_qkv, own_out, tables, kept, number):
    rows, width = own_rows.shape
    count, wide, q_width = PLANE * rows, own_qkv.shape[1], own_out.shape[0]
    low = jnp.bfloat16
    normed_all, proj, query, keys, values, attended, log_totals = kept
    arrays = (
        own_rows,
        own_qkv,
        own_out,
        *tables,
        proj,
        query,
        keys,
        values,
        attended,
        log_totals,
        normed_all,
    )
    places = tuple(range(1, len(arrays) - 1))
    specs, stage = staged_specs(arrays[:-1], places)
    return pl.pallas_call(
        staged(attend_back_kernel, len(arrays), places),
        out_shape=[
            jax.ShapeDtypeStruct((rows, width), jnp.float32),
            jax.ShapeDtypeStruct((width, wide + q_width), low),
            jax.ShapeDtypeStruct((8, 2 * HD), jnp.float32),
        ],
        in_specs=specs + [ANY],
        out_specs=[VMEM] * 3,
        scratch_shapes=[
            pltpu.VMEM((count, width), low),
            pltpu.VMEM((count, width), low),
            pltpu.VMEM((rows, q_width), low),
            pltpu.VMEM((count, wide), low),
            pltpu.SemaphoreType.DMA,
        ]
        + gather_scratch()
        + scatter_scratch(rows, width)
        + stage,
        compiler_params=pltpu.CompilerParams(
            collective_id=number, has_side_effects=True, vmem_limit_bytes=58 * 2**20
        ),
        cost_estimate=SHORT,
        name=f"attend_back_{number}",
    )(*arrays)


def product_scatter(left_sides, right_sides, number, turned=False):
    width = right_sides[0].shape[0] if turned else right_sides[0].shape[1]
    rows = left_sides[0].shape[0] // PLANE
    return pl.pallas_call(
        functools.partial(scatter_kernel, turned, len(left_sides)),
        out_shape=jax.ShapeDtypeStruct((rows, width), jnp.float32),
        in_specs=[ANY] * (2 * len(left_sides)),
        out_specs=VMEM,
        scratch_shapes=[pltpu.VMEM(side.shape, side.dtype) for side in left_sides + right_sides]
        + [
            pltpu.SemaphoreType.DMA((len(left_sides), PLANE)),
            pltpu.SemaphoreType.DMA((len(left_sides),)),
        ]
        + scatter_scratch(rows, width),
        compiler_params=pltpu.CompilerParams(
            collective_id=number, has_side_effects=True, vmem_limit_bytes=56 * 2**20
        ),
        cost_estimate=SHORT,
        name=f"product_scatter_{number}",
    )(*left_sides, *right_sides)


def start_kernel(
    nd,
    qkv_ref,
    out_rows_ref,
    wide_ref,
    df_ref,
    note_ref,
    own_qkv_ref,
    own_out_ref,
    half_a_ref,
    half_b_ref,
    df_all_ref,
    notes_ref,
    own_sem,
    gather_send,
    gather_recv,
    block_send,
    block_recv,
    note_send,
    note_recv,
    piece_send,
    piece_recv,
    line_send,
    line_recv,
):
    me, line = lax.axis_index("fsdp"), lax.axis_index("dp")
    others = plane_others(me)
    count = qkv_ref.shape[1]
    half_width = half_a_ref.shape[2] // 2
    hidden = 2 * half_width
    whole = hidden * PLANE
    gather = Gather(df_ref, df_all_ref, gather_send, gather_recv)
    greet_line(nd, others)

    def line_spot(array, owner):
        rows = pl.ds(pl.multiple_of(owner * count, count), count)
        return own_qkv_ref.at[:, rows] if array == 0 else own_out_ref.at[rows]

    def along(array, owner, side, source=None):
        spot = line_spot(array, owner)
        return pltpu.make_async_remote_copy(
            src_ref=spot if source is None else source,
            dst_ref=spot,
            send_sem=line_send.at[array, side, owner],
            recv_sem=line_recv.at[array, owner],
            device_id={"dp": line + 1 if side == 0 else line - 1},
            device_id_type=MESH,
        )

    def send_own(array, source=None):
        @pl.when(line < nd - 1)
        def _():
            along(array, line, 0, source).start()

        @pl.when(line > 0)
        def _():
            along(array, line, 1, source).start()

    def line_step(array, step):
        @pl.when(line >= step)
        def _():
            along(array, line - step, 0).wait_recv()

            @pl.when(line < nd - 1)
            def _():
                along(array, line - step, 0).start()

        @pl.when(line + step < nd)
        def _():
            along(array, line + step, 1).wait_recv()

            @pl.when(line > 0)
            def _():
                along(array, line + step, 1).start()

    def put_block(number):
        other = others[number - 1]
        return pltpu.make_async_remote_copy(
            src_ref=qkv_ref.at[other],
            dst_ref=own_qkv_ref.at[me, pl.ds(pl.multiple_of(line * count, count), count)],
            send_sem=block_send.at[number],
            recv_sem=block_recv.at[number],
            device_id={"fsdp": other},
            device_id_type=MESH,
        )

    def put_note(number):
        return pltpu.make_async_remote_copy(
            src_ref=note_ref,
            dst_ref=notes_ref.at[me],
            send_sem=note_send.at[number],
            recv_sem=note_recv.at[number],
            device_id={"fsdp": others[number - 1]},
            device_id_type=MESH,
        )

    def pieces(other):
        for half, half_ref in enumerate((half_a_ref, half_b_ref)):
            for side in range(2):
                first = side * whole + other * hidden + half * half_width
                source = wide_ref.at[:, pl.ds(pl.multiple_of(first, 128), half_width)]
                yield source, half_ref.at[me, :, pl.ds(side * half_width, half_width)]

    def put_pieces(number):
        return [
            pltpu.make_async_remote_copy(
                src_ref=source,
                dst_ref=target,
                send_sem=piece_send.at[4 * number + index],
                recv_sem=piece_recv.at[4 * number + index],
                device_id={"fsdp": others[number - 1]},
                device_id_type=MESH,
            )
            for index, (source, target) in enumerate(pieces(others[number - 1]))
        ]

    own_block = own_qkv_ref.at[me, pl.ds(pl.multiple_of(line * count, count), count)]
    rows = df_ref.shape[0]
    kept = [
        (qkv_ref.at[me], own_block),
        (out_rows_ref, line_spot(1, line)),
        (note_ref, notes_ref.at[me]),
        (df_ref, df_all_ref.at[pl.ds(pl.multiple_of(me * rows, rows), rows)]),
    ] + list(pieces(me))
    keep = [
        pltpu.make_async_copy(source, target, own_sem.at[index])
        for index, (source, target) in enumerate(kept)
    ]
    order = (6, 7, 2, 4, 3, 5, 1)
    for number in order:
        put_block(number).start()
        put_note(number).start()
    keep[0].start()
    send_own(1, out_rows_ref)
    gather.begin()
    for copy in keep[1:]:
        copy.start()
    for number in order:
        put_block(number).wait_recv()
    keep[0].wait()
    send_own(0)
    for steps, slots in (
        ((), (0, 2)),
        (((1, 1),), (4, 1, 3)),
        (((0, 1),), (5, 6)),
        (((1, 2),), ()),
        (((0, 2),), (7, 9, 8, 10)),
        (((1, 3), (0, 3)), (11, 12)),
    ):
        for array, step in steps:
            if step < nd:
                line_step(array, step)
        for slot in slots:
            gather.take(slot)
        if slots == (5, 6):
            for number in order:
                for copy in put_pieces(number):
                    copy.start()
    for step in range(4, nd):
        line_step(1, step)
        line_step(0, step)
    for number in order:
        put_block(number).wait_send()
        put_note(number).wait()
        for copy in put_pieces(number):
            copy.wait()
    gather.finish()
    for copy in keep[1:]:
        copy.wait()
    for array in (1, 0):
        source = out_rows_ref if array == 1 else None

        @pl.when(line < nd - 1)
        def _():
            along(array, line, 0, source).wait_send()

        @pl.when(line > 0)
        def _():
            along(array, line, 1, source).wait_send()

        for step in range(1, nd):

            @pl.when(jnp.logical_and(line >= step, line < nd - 1))
            def _():
                along(array, line - step, 0).wait_send()

            @pl.when(jnp.logical_and(line + step < nd, line > 0))
            def _():
                along(array, line + step, 1).wait_send()


def start(qkv_blocks, out_rows, wide_rows, df_own, note, number):
    nd = lax.axis_size("dp")
    count, whole = wide_rows.shape
    half = whole // 4 // PLANE
    low = wide_rows.dtype
    return pl.pallas_call(
        functools.partial(start_kernel, nd),
        out_shape=[
            jax.ShapeDtypeStruct((PLANE, nd * count, qkv_blocks.shape[2]), low),
            jax.ShapeDtypeStruct((nd * count, out_rows.shape[1]), low),
            jax.ShapeDtypeStruct((PLANE, count, 2 * half), low),
            jax.ShapeDtypeStruct((PLANE, count, 2 * half), low),
            jax.ShapeDtypeStruct((PLANE * df_own.shape[0], df_own.shape[1]), low),
            jax.ShapeDtypeStruct((PLANE,) + note.shape, note.dtype),
        ],
        in_specs=[ANY] * 5,
        out_specs=[ANY] * 6,
        scratch_shapes=[pltpu.SemaphoreType.DMA((8,))]
        + gather_scratch()
        + [pltpu.SemaphoreType.DMA((PLANE,))] * 4
        + [pltpu.SemaphoreType.DMA((4 * PLANE,))] * 2
        + [pltpu.SemaphoreType.DMA((2, 2, nd)), pltpu.SemaphoreType.DMA((2, nd))],
        compiler_params=pltpu.CompilerParams(collective_id=number, has_side_effects=True),
        cost_estimate=SHORT,
        name=f"start_{number}",
    )(qkv_blocks, out_rows, wide_rows, df_own, note)


def glu_block(
    rows_ref, df_ref, wgu, wd, act_ref, dgu_ref, down_sum, wide_sum, results=None
):
    half = wd.shape[0]
    count, width = rows_ref.shape

    @pl.loop(0, count // 256)
    def _(step):
        spot = pl.ds(pl.multiple_of(step * 256, 256), 256)
        for first in range(0, half, GLU_TILE):
            units = slice(first, first + GLU_TILE)
            up_units = slice(half + first, half + first + GLU_TILE)
            gate = product(rows_ref[spot, :], wgu[:, units])
            up = product(rows_ref[spot, :], wgu[:, up_units])
            back = contract_last(df_ref[spot, :], wd[units, :])
            sigmoid = jax.nn.sigmoid(gate)
            silu = gate * sigmoid
            act_ref[spot, units] = (silu * up).astype(jnp.bfloat16)
            gate_back = back * up * sigmoid * (1.0 + gate * (1.0 - sigmoid))
            dgu_ref[spot, units] = gate_back.astype(jnp.bfloat16)
            dgu_ref[spot, up_units] = (back * silu).astype(jnp.bfloat16)

    @pl.loop(0, width // TILE)
    def _(step):
        columns = pl.ds(pl.multiple_of(step * TILE, TILE), TILE)
        down = column_product(act_ref[...], df_ref[:, columns])
        wide = column_product(rows_ref[:, columns], dgu_ref[...])
        if results is None:
            down_sum[:, columns] += down
            wide_sum[columns, :] += wide
        else:
            down_ref, wide_ref = results
            down_ref[:, columns] = (down_sum[:, columns] + down).astype(down_ref.dtype)
            wide_ref[columns, :] = (wide_sum[columns, :] + wide).astype(wide_ref.dtype)


def gather_glu_kernel(
    x_ref,
    wgu_hbm,
    wd_hbm,
    df_hbm,
    all_out_ref,
    act_ref,
    dgu_ref,
    down_ref,
    wide_ref,
    all_ref,
    wgu_ref,
    wd_ref,
    df_ref,
    down_sum,
    wide_sum,
    in_sem,
    out_sem,
    gather_send,
    gather_recv,
):
    rows = x_ref.shape[0]
    half = wd_ref.shape[0]
    fetch = [
        pltpu.make_async_copy(wgu_hbm, wgu_ref, in_sem.at[0]),
        pltpu.make_async_copy(wd_hbm.at[pl.ds(0, half)], wd_ref, in_sem.at[1]),
        pltpu.make_async_copy(df_hbm, df_ref, in_sem.at[2]),
    ]
    for copy in fetch:
        copy.start()
    gather = Gather(x_ref, all_ref, gather_send, gather_recv)
    me, x_next, y_next = gather.me, gather.x_next, gather.y_next
    greet((gather.sibling, x_next, y_next))
    gather.begin()
    all_ref[pl.ds(pl.multiple_of(me * rows, rows), rows), :] = x_ref[...]
    down_sum[...] = jnp.zeros_like(down_sum)
    wide_sum[...] = jnp.zeros_like(wide_sum)
    for copy in fetch:
        copy.wait()

    def work(owner, results=None):
        first = owner - lax.rem(owner, 2)
        spot = pl.ds(pl.multiple_of(first * rows, 2 * rows), 2 * rows)
        glu_block(
            all_ref.at[spot],
            df_ref.at[spot],
            wgu_ref,
            wd_ref,
            act_ref.at[spot],
            dgu_ref.at[spot],
            down_sum,
            wide_sum,
            results,
        )

    gather.take(4)
    work(me)
    for slot in (0, 2, 1, 3, 7, 8):
        gather.take(slot)
    work(x_next)
    for slot in (5, 6, 9, 10):
        gather.take(slot)
    work(y_next)
    gather.take(11)
    gather.take(12)
    keep = pltpu.make_async_copy(all_ref, all_out_ref, out_sem)
    keep.start()
    work(gather.diagonal, (down_ref, wide_ref))
    gather.finish()
    keep.wait()


def gather_glu(own_rows, wgu, own_down, df_all, number):
    rows, width = own_rows.shape
    count, half = PLANE * rows, wgu.shape[1] // 2
    low = jnp.bfloat16
    return pl.pallas_call(
        gather_glu_kernel,
        out_shape=[
            jax.ShapeDtypeStruct((count, width), low),
            jax.ShapeDtypeStruct((count, half), low),
            jax.ShapeDtypeStruct((count, 2 * half), low),
            jax.ShapeDtypeStruct((half, width), low),
            jax.ShapeDtypeStruct((width, 2 * half), low),
        ],
        in_specs=[VMEM, ANY, ANY, ANY],
        out_specs=[ANY] + [VMEM] * 4,
        scratch_shapes=[
            pltpu.VMEM((count, width), low),
            pltpu.VMEM(wgu.shape, low),
            pltpu.VMEM((half, width), low),
            pltpu.VMEM((count, width), low),
            pltpu.VMEM((half, width), jnp.float32),
            pltpu.VMEM((width, 2 * half), jnp.float32),
            pltpu.SemaphoreType.DMA((3,)),
            pltpu.SemaphoreType.DMA,
        ]
        + gather_scratch(),
        compiler_params=pltpu.CompilerParams(
            collective_id=number, has_side_effects=True, vmem_limit_bytes=58 * 2**20
        ),
        cost_estimate=SHORT,
        name=f"gather_glu_{number}",
    )(own_rows, wgu, own_down, df_all)


def glu_kernel(
    x_ref, df_ref, wgu_ref, wd_ref, first_ref, act_ref, dgu_ref, grad_ref, down_sum, wide_sum
):
    step = pl.program_id(0)
    half = wd_ref.shape[0]

    @pl.when(step == 0)
    def _():
        down_sum[...] = jnp.zeros_like(down_sum)
        wide_sum[...] = jnp.zeros_like(wide_sum)

    glu_block(
        x_ref, df_ref, wgu_ref, wd_ref, act_ref, dgu_ref, down_sum, wide_sum
    )

    @pl.when(step == pl.num_programs(0) - 1)
    def _():
        nd, _, both = grad_ref.shape
        count, units = wide_sum.shape[0] // PLANE // nd, 2 * half // nd
        low = grad_ref.dtype
        for owner in range(nd):
            for place in range(PLANE):
                first = (place * nd + owner) * count
                part = wide_sum[first : first + count, :].astype(low)
                grad_ref[owner, place * count : (place + 1) * count, :] = part
            source, first = first_ref, owner * units
            if first >= half:
                source, first = down_sum, first - half
            for side in range(2):
                part = source[first : first + units, side * both : (side + 1) * both].astype(low)
                start = PLANE * count + side * units
                grad_ref[owner, start : start + units, :] = part


def glu(rows_all, df_all, wgu, own_down, down_first, number):
    nd = lax.axis_size("dp")
    count, width = rows_all.shape
    half = wgu.shape[1] // 2
    low = jnp.bfloat16
    step = 512
    once = pl.Buffered(1)
    return pl.pallas_call(
        glu_kernel,
        grid=(count // step,),
        out_shape=[
            jax.ShapeDtypeStruct((count, half), low),
            jax.ShapeDtypeStruct((count, 2 * half), low),
            jax.ShapeDtypeStruct((nd, 2 * width // nd, 2 * half), low),
        ],
        in_specs=[
            pl.BlockSpec((step, width), lambda i: (i, 0)),
            pl.BlockSpec((step, width), lambda i: (i, 0)),
            pl.BlockSpec((width, 2 * half), lambda i: (0, 0), pipeline_mode=once),
            pl.BlockSpec((half, width), lambda i: (1, 0), pipeline_mode=once),
            pl.BlockSpec((half, width), lambda i: (0, 0), pipeline_mode=once),
        ],
        out_specs=[
            pl.BlockSpec((step, half), lambda i: (i, 0)),
            pl.BlockSpec((step, 2 * half), lambda i: (i, 0)),
            pl.BlockSpec(
                (nd, 2 * width // nd, 2 * half), lambda i: (0, 0, 0), pipeline_mode=once
            ),
        ],
        scratch_shapes=[
            pltpu.VMEM((half, width), jnp.float32),
            pltpu.VMEM((width, 2 * half), jnp.float32),
        ],
        compiler_params=pltpu.CompilerParams(vmem_limit_bytes=56 * 2**20),
        cost_estimate=SHORT,
        name=f"glu_{number}",
    )(rows_all, df_all, wgu, own_down, down_first)


def attention(normed_low, own_qkv, own_out, lengths_all, query_gain, key_gain):
    position, _, allowed = layout(lengths_all)
    half_width = HD // 2
    frequency = ROPE_BASE ** (jnp.arange(half_width, dtype=jnp.float32) * (-2.0 / HD))
    angles = position.reshape(-1, 1) * frequency[None, :]
    tables = (
        jnp.tile(jnp.cos(angles), (1, 4)),
        jnp.tile(jnp.sin(angles), (1, 4)),
        allowed.astype(jnp.float32),
        jnp.pad(
            jnp.stack([jnp.tile(query_gain, 2), jnp.tile(key_gain, 2)]), ((0, 6), (0, 0))
        ),
    )
    sums, *kept = attend(normed_low, own_qkv, own_out, tables, 3)

    def back(branch_own):
        normed_one_grad, part_attn, gain_grads = attend_back(
            branch_own, own_qkv, own_out, tables, kept, 9
        )
        query_gain_grad = gain_grads[0, :HD] + gain_grads[0, HD:]
        return normed_one_grad, part_attn, query_gain_grad, gain_grads[1, :HD]

    return sums, back


def last_kernel(
    ready,
    hidden_ref,
    valid_ref,
    act_a_ref,
    act_b_ref,
    wd_ref,
    half_ref,
    out_ref,
    wide_ref,
    sum_ref,
    own_sem,
    sems,
    *refs,
):
    others = plane_others(lax.axis_index("fsdp"))
    rows, width = out_ref.shape
    half_rows = wd_ref.shape[0] // 2
    block = block_product(
        (act_a_ref, act_b_ref),
        (wd_ref.at[pl.ds(0, half_rows)], wd_ref.at[pl.ds(half_rows, half_rows)]),
        rows,
        width,
        False,
    )
    scatter = Scatter(sum_ref, block, refs)
    greet(others)
    order = (6, 7, 2, 4, 3, 5, 1)
    for number in order:
        for copy in put_half(half_ref, wide_ref, others, number, sems):
            copy.start()
    keep = keep_half(half_ref, wide_ref, own_sem)
    for copy in keep:
        copy.start()
    ready()
    scatter.for_sibling(0)
    scatter.for_sibling(1)
    scatter.for_far()
    scatter.for_sibling(2)
    scatter.for_near(0)
    scatter.for_sibling(3)
    scatter.for_near(1)
    scatter.finish_near(0)
    scatter.finish_near(1)
    scatter.own()
    scatter.finish()
    out_ref[...] = (hidden_ref[...] + valid_ref[...] * sum_ref[...]).astype(out_ref.dtype)
    for number in order:
        for copy in put_half(half_ref, wide_ref, others, number, sems):
            copy.wait()
    for copy in keep:
        copy.wait()


def last(hidden, valid_col, act_a, act_b, own_down, half, count, number):
    rows, width = hidden.shape
    arrays = (hidden, valid_col, act_a, act_b, own_down)
    places = (0, 2, 3, 4)
    specs, stage = staged_specs(arrays, places)
    return pl.pallas_call(
        staged(last_kernel, len(arrays) + 1, places),
        out_shape=[
            jax.ShapeDtypeStruct((rows, width), jnp.bfloat16),
            jax.ShapeDtypeStruct((count, half.shape[1] * PLANE), half.dtype),
        ],
        in_specs=specs + [ANY],
        out_specs=[VMEM, ANY],
        scratch_shapes=[pltpu.VMEM((rows, width), jnp.float32)]
        + half_scratch()
        + scatter_scratch(rows, width)
        + stage,
        compiler_params=pltpu.CompilerParams(
            collective_id=number, has_side_effects=True, vmem_limit_bytes=56 * 2**20
        ),
        cost_estimate=SHORT,
        name=f"last_{number}",
    )(*arrays, half)


def adam_kernel(chunks, n_grads, per, norm_ref, *refs):
    grads, refs = refs[:n_grads], refs[n_grads:]
    states = [refs[place * per : (place + 1) * per] for place in range(3)]
    outs = [refs[(3 + place) * per : (4 + place) * per] for place in range(3)]
    refs = refs[6 * per :]
    grad_bufs, refs = refs[:n_grads], refs[n_grads:]
    bufs = [refs[place * per : (place + 1) * per] for place in range(3)]
    grad_sems, in_sems, out_sems = refs[3 * per :]
    factor = norm_ref[1:2, 0:1]
    first_scale = 1.0 / (1.0 - FIRST_DECAY**STEP)
    second_scale = 1.0 / (1.0 - SECOND_DECAY**STEP)

    def fetch(number):
        which, rows, sources, _ = chunks[number]
        copies = [
            pltpu.make_async_copy(
                grads[array].at[spot], grad_bufs[array].at[spot], grad_sems.at[number, place]
            )
            for place, (array, spot) in enumerate(sources)
        ]
        for place in range(3):
            copies.append(
                pltpu.make_async_copy(
                    states[place][which].at[rows],
                    bufs[place][which].at[rows],
                    in_sems.at[number, place],
                )
            )
        return copies

    def put(number):
        which, rows, _, _ = chunks[number]
        return [
            pltpu.make_async_copy(
                bufs[place][which].at[rows], outs[place][which].at[rows], out_sems.at[number, place]
            )
            for place in range(3)
        ]

    def update(which, rows, columns, grad):
        weights, firsts, seconds = (bufs[place][which] for place in range(3))
        clipped = grad.astype(jnp.float32) * factor
        weight = weights[rows, columns]
        first = FIRST_DECAY * firsts[rows, columns] + (1.0 - FIRST_DECAY) * clipped
        second = SECOND_DECAY * seconds[rows, columns] + (1.0 - SECOND_DECAY) * clipped * clipped
        root = jnp.sqrt(second * second_scale) + ADAM_EPSILON
        change = first * first_scale / root + WEIGHT_DECAY * weight
        weights[rows, columns] = weight - LEARN_RATE * change
        firsts[rows, columns] = first
        seconds[rows, columns] = second

    for number in range(len(chunks)):
        for copy in fetch(number):
            copy.start()
    for number in range(len(chunks)):
        which, rows, _, loops = chunks[number]
        for copy in fetch(number):
            copy.wait()
        for array, grad_rows, steps, columns_of, grad_columns_of, width in loops:

            @pl.loop(0, steps)
            def _(step):
                columns = pl.ds(pl.multiple_of(columns_of(step), 128), width)
                grad_columns = pl.ds(pl.multiple_of(grad_columns_of(step), 128), width)
                update(which, rows, columns, grad_bufs[array][grad_rows, grad_columns])

        for copy in put(number):
            copy.start()
    for number in range(len(chunks)):
        for copy in put(number):
            copy.wait()


def adam_matrices(norm, grad_qkv, grad_out, grad_a, grad_b, sums_b, weights, firsts, seconds):
    half = grad_a.shape[1] // 2 // PLANE
    whole = weights[2].shape[1] // 2
    count = weights[3].shape[0]
    behind = sums_b.shape[0] - 2 * count
    side_width = sums_b.shape[1]
    width = 512
    chunks = []

    def straight(step):
        return step * width

    for row in range(0, weights[2].shape[0], 16):
        rows = pl.ds(row, 16)
        loops = []
        for part in range(2):

            def columns_of(step, part=part):
                side, unit = lax.div(step, PLANE), lax.rem(step, PLANE)
                return side * whole + unit * 2 * half + part * half

            loops.append((2 + part, rows, 2 * PLANE, columns_of, lambda step: step * half, half))
        chunks.append((2, rows, [(2, rows), (3, rows)], loops))
    for row in range(0, count, 64):
        sources, loops = [], []
        for side in range(2):
            spot = pl.ds(behind + side * count + row, 64)
            sources.append((4, spot))

            def columns_of(step, side=side):
                return side * side_width + step * width

            loops.append((4, spot, side_width // width, columns_of, straight, width))
        chunks.append((3, pl.ds(row, 64), sources, loops))
    for which in range(2):
        for row in range(0, weights[which].shape[0], 32):
            rows = pl.ds(row, 32)
            steps = weights[which].shape[1] // width
            loops = [(which, rows, steps, straight, straight, width)]
            chunks.append((which, rows, [(which, rows)], loops))
    grads = (grad_qkv, grad_out, grad_a, grad_b, sums_b)
    per = len(weights)
    number = len(chunks)
    outs = pl.pallas_call(
        functools.partial(adam_kernel, chunks, len(grads), per),
        out_shape=[jax.ShapeDtypeStruct(weight.shape, jnp.float32) for weight in weights] * 3,
        in_specs=[VMEM] + [ANY] * (len(grads) + 3 * per),
        out_specs=[ANY] * (3 * per),
        scratch_shapes=[pltpu.VMEM(grad.shape, grad.dtype) for grad in grads]
        + [pltpu.VMEM(weight.shape, jnp.float32) for weight in weights] * 3
        + [
            pltpu.SemaphoreType.DMA((number, 2)),
            pltpu.SemaphoreType.DMA((number, 3)),
            pltpu.SemaphoreType.DMA((number, 3)),
        ],
        compiler_params=pltpu.CompilerParams(vmem_limit_bytes=60 * 2**20),
        name="adam_matrices",
    )(norm, *grads, *weights, *firsts, *seconds)
    return outs[:per], outs[per : 2 * per], outs[2 * per :]


def scatter_rows(values, axis):
    return lax.psum_scatter(values, "dp", scatter_dimension=axis, tiled=True)


def per_device_plane(
    nf,
    nd,
    tokens,
    cotangent,
    order,
    lengths,
    w_qkv,
    w_out,
    w_gate_up,
    w_down,
    gains,
    first_qkv,
    first_out,
    first_gate_up,
    first_down,
    first_gains,
    second_qkv,
    second_out,
    second_gate_up,
    second_down,
    second_gains,
):
    low = jnp.bfloat16
    q_width = HEADS // nf * HD
    kv_all = KVH * HD
    hidden_own = FF // nf
    rows_own = w_qkv.shape[0]

    order_row = order[0]
    places = jnp.arange(TOK_DEV, dtype=jnp.int32)
    inverse = jnp.zeros((TOK_DEV,), jnp.int32).at[order_row].set(places)
    rows_in = tokens[order_row].astype(jnp.float32)
    back_rows = cotangent[order_row].astype(jnp.float32)
    attn_gain = gains[:D]
    ffn_gain = gains[D : 2 * D]
    query_gain = gains[2 * D : 2 * D + HD]
    key_gain = gains[2 * D + HD :]

    _, valid_rows, _ = layout(lengths)
    valid_col = valid_rows.reshape(TOK_DEV, 1)

    qkv_low = w_qkv.astype(low)

    def head_blocks(rows, width):
        return jnp.swapaxes(rows.reshape(rows_own, -1, width), 0, 1)

    qkv_blocks = jnp.concatenate(
        [
            head_blocks(qkv_low[:, :D], q_width),
            head_blocks(qkv_low[:, D : D + kv_all], HD),
            head_blocks(qkv_low[:, D + kv_all :], HD),
        ],
        axis=2,
    )
    wide = q_width + 2 * HD
    own_down = lax.all_gather(w_down.astype(low), "dp", axis=0, tiled=True)
    own_qkv, own_out, half_a, half_b, down_back, notes = start(
        qkv_blocks,
        w_out.astype(low),
        w_gate_up.astype(low),
        (valid_col * back_rows).astype(low),
        jnp.pad(lengths, ((0, 8 - MB), (0, 128 - SEQS))),
        1,
    )
    own_qkv = own_qkv.reshape(D, wide)
    lengths_all = notes[:, :MB, :SEQS].reshape(nf * MB, SEQS)
    half_a, own_down = lax.optimization_barrier((half_a, own_down))
    own_a = lax.all_gather(half_a, "dp", axis=1, tiled=True).reshape(D, hidden_own)
    own_b = lax.all_gather(half_b, "dp", axis=1, tiled=True).reshape(D, hidden_own)

    normed_one, norm_one_pull = jax.vjp(rms_norm, rows_in, attn_gain)
    attention_sums, attention_back = attention(
        normed_one.astype(low), own_qkv, own_out, lengths_all, query_gain, key_gain
    )
    hidden = rows_in + valid_col * attention_sums

    normed_two, norm_two_pull = jax.vjp(rms_norm, hidden, ffn_gain)
    norm_two_all, act_a, back_a, down_a, part_a = gather_glu(
        normed_two.astype(low), own_a, own_down, down_back, 5
    )
    sums_a = scatter_rows(part_a.reshape(nf, nd * rows_own, hidden_own), 1)
    act_b, back_b, part_b = glu(norm_two_all, down_back, own_b, own_down, down_a, 6)
    sums_b = scatter_rows(part_b, 0)[0]
    normed_two_grad = product_scatter((back_a, back_b), (own_a, own_b), 8, turned=True)
    hidden_norm_grad, ffn_gain_grad = norm_two_pull(normed_two_grad)
    hidden_grad = back_rows + hidden_norm_grad

    branch_own = (valid_col * hidden_grad).astype(low)
    branch_own, sums_a = lax.optimization_barrier((branch_own, sums_a))
    normed_one_grad, part_attn, query_gain_grad, key_gain_grad = attention_back(branch_own)
    sums_attn = scatter_rows(part_attn.reshape(nf, nd * rows_own, wide + q_width), 1)
    normed_one_grad, act_a = lax.optimization_barrier((normed_one_grad, act_a))
    output, grad_a = last(
        hidden,
        valid_col,
        act_a,
        act_b,
        own_down,
        sums_a.reshape(nf * rows_own, hidden_own),
        rows_own,
        7,
    )
    output, sums_b = lax.optimization_barrier((output, sums_b))
    grad_b, squares_b = exchange_half(sums_b, rows_own, 11)
    rows_grad, attn_gain_grad = norm_one_pull(normed_one_grad)
    input_grad = (hidden_grad + rows_grad)[inverse]
    output_all = output[inverse]

    early_squares = jnp.sum(jnp.square(sums_a.astype(jnp.float32))) + jnp.sum(squares_b)
    input_grad, output_all, early_squares, sums_attn = lax.optimization_barrier(
        (input_grad, output_all, early_squares, sums_attn)
    )
    gain_sum = jnp.concatenate([attn_gain_grad, ffn_gain_grad, query_gain_grad, key_gain_grad])
    gain_total, norm, grad_qkv, grad_out = sum_everywhere(
        gain_sum, early_squares, sums_attn, wide, 13
    )
    global_norm, factor = norm[0, 0], norm[1, 0]
    new_matrices, next_firsts, next_seconds = adam_matrices(
        norm,
        grad_qkv,
        grad_out,
        grad_a,
        grad_b,
        sums_b,
        (w_qkv, w_out, w_gate_up, w_down),
        (first_qkv, first_out, first_gate_up, first_down),
        (second_qkv, second_out, second_gate_up, second_down),
    )
    new_gains, next_first_gains, next_second_gains = adam_step(
        gains, first_gains, second_gains, gain_total, factor, GAIN_RATE, 0.0
    )
    return (
        output_all,
        input_grad,
        global_norm,
        *new_matrices,
        new_gains,
        *next_firsts,
        next_first_gains,
        *next_seconds,
        next_second_gains,
    )


def gather_tokens(rows):
    return lax.all_gather(rows, "fsdp", axis=0, tiled=True)


def scatter_tokens(rows):
    return lax.psum_scatter(
        rows.astype(jnp.bfloat16), "fsdp", scatter_dimension=0, tiled=True
    ).astype(jnp.float32)


def swap(blocks):
    return lax.all_to_all(blocks, "fsdp", split_axis=0, concat_axis=0, tiled=True)


def per_device_plain(
    nf,
    nd,
    tokens,
    cotangent,
    order,
    lengths,
    w_qkv,
    w_out,
    w_gate_up,
    w_down,
    gains,
    first_qkv,
    first_out,
    first_gate_up,
    first_down,
    first_gains,
    second_qkv,
    second_out,
    second_gate_up,
    second_down,
    second_gains,
):
    low = jnp.bfloat16
    kvl = max(KVH // nf, 1)
    rep = max(nf // KVH, 1)
    heads_own = HEADS // nf
    group = heads_own // kvl
    q_width, kv_width = heads_own * HD, kvl * HD
    kv_all = KVH * HD
    hidden_own = FF // nf
    rows_own = w_qkv.shape[0]
    n_mb = nf * MB

    def head_blocks(rows, width):
        return jnp.swapaxes(rows.reshape(rows_own, -1, width), 0, 1)

    qkv_low = w_qkv.astype(low)
    qkv_blocks = jnp.concatenate(
        [
            head_blocks(qkv_low[:, :D], q_width),
            jnp.repeat(head_blocks(qkv_low[:, D : D + kv_all], kv_width), rep, axis=0),
            jnp.repeat(head_blocks(qkv_low[:, D + kv_all :], kv_width), rep, axis=0),
        ],
        axis=2,
    )
    wide = q_width + 2 * kv_width
    own_qkv = lax.all_gather(swap(qkv_blocks), "dp", axis=1, tiled=True).reshape(D, wide)
    own_out = lax.all_gather(w_out.astype(low), "dp", axis=0, tiled=True)
    gate_up_blocks = jnp.transpose(
        w_gate_up.astype(low).reshape(rows_own, 2, nf, hidden_own), (2, 0, 1, 3)
    ).reshape(nf, rows_own, 2 * hidden_own)
    own_gate_up = lax.all_gather(swap(gate_up_blocks), "dp", axis=1, tiled=True).reshape(
        D, 2 * hidden_own
    )
    own_down = lax.all_gather(w_down.astype(low), "dp", axis=0, tiled=True)

    order_row = order[0]
    places = jnp.arange(TOK_DEV, dtype=jnp.int32)
    inverse = jnp.zeros((TOK_DEV,), jnp.int32).at[order_row].set(places)
    rows_in = tokens[order_row].astype(jnp.float32)
    back_rows = cotangent[order_row].astype(jnp.float32)
    attn_gain = gains[:D]
    ffn_gain = gains[D : 2 * D]
    query_gain = gains[2 * D : 2 * D + HD]
    key_gain = gains[2 * D + HD :]
    score_scale = HD ** (-0.5)

    lengths_all = gather_tokens(lengths)
    position, _, allowed = layout(lengths_all)
    _, valid_rows, _ = layout(lengths)
    valid_col = valid_rows.reshape(TOK_DEV, 1)
    allowed = allowed[:, None, None]
    cosine_table, sine_table = rope_tables(position.reshape(-1))

    normed_one, norm_one_pull = jax.vjp(rms_norm, rows_in, attn_gain)
    norm_one_all = gather_tokens(normed_one.astype(low))
    projected = product(norm_one_all, own_qkv)
    n_rows = norm_one_all.shape[0]
    query_raw = projected[:, :q_width].reshape(n_rows, heads_own, HD)
    key_raw = projected[:, q_width : q_width + kv_width].reshape(n_rows, kvl, HD)
    values_low = projected[:, q_width + kv_width :].reshape(n_mb, MB_TOK, kvl, HD).astype(low)

    def turn_heads(query_in, key_in, query_scale, key_scale):
        return (
            rotate(rms_norm(query_in, query_scale), cosine_table, sine_table),
            rotate(rms_norm(key_in, key_scale), cosine_table, sine_table),
        )

    turned, turn_pull = jax.vjp(turn_heads, query_raw, key_raw, query_gain, key_gain)
    queries_low = turned[0].astype(low).reshape(n_mb, MB_TOK, kvl, group, HD)
    keys_low = turned[1].astype(low).reshape(n_mb, MB_TOK, kvl, HD)
    scores = (
        jnp.einsum("mtkgd,mukd->mkgtu", queries_low, keys_low, preferred_element_type=jnp.float32)
        * score_scale
    )
    scores = jnp.where(allowed, scores, MASKED)
    row_peak = jnp.max(scores, axis=-1, keepdims=True)
    powers = jnp.exp(scores - row_peak)
    totals = jnp.sum(powers, axis=-1, keepdims=True)
    probs = powers / totals
    probs_low = probs.astype(low)
    attended = jnp.einsum(
        "mkgtu,mukd->mtkgd", probs_low, values_low, preferred_element_type=jnp.float32
    )
    attended_low = attended.reshape(n_rows, q_width).astype(low)
    hidden = rows_in + valid_col * scatter_tokens(product(attended_low, own_out))

    normed_two, norm_two_pull = jax.vjp(rms_norm, hidden, ffn_gain)
    norm_two_all = gather_tokens(normed_two.astype(low))
    down_back = gather_tokens((valid_col * back_rows).astype(low))
    gate_up = product(norm_two_all, own_gate_up)
    activation, glu_pull = jax.vjp(swiglu, gate_up[:, :hidden_own], gate_up[:, hidden_own:])
    activation_low = activation.astype(low)
    output = hidden + valid_col * scatter_tokens(product(activation_low, own_down))
    gate_back, up_back = glu_pull(contract_last(down_back, own_down))
    gate_up_back = jnp.concatenate([gate_back.astype(low), up_back.astype(low)], axis=1)
    normed_two_grad = scatter_tokens(contract_last(gate_up_back, own_gate_up))
    grad_down = lax.psum_scatter(
        column_product(activation_low, down_back).astype(low),
        "dp",
        scatter_dimension=0,
        tiled=True,
    ).astype(jnp.float32)
    grad_gate_up = lax.psum_scatter(
        column_product(norm_two_all, gate_up_back)
        .astype(low)
        .reshape(nf, nd * rows_own, 2 * hidden_own),
        "dp",
        scatter_dimension=1,
        tiled=True,
    )
    grad_gate_up = jnp.transpose(
        swap(grad_gate_up).reshape(nf, rows_own, 2, hidden_own), (1, 2, 0, 3)
    ).reshape(rows_own, 2 * FF)
    grad_gate_up = grad_gate_up.astype(jnp.float32)
    hidden_norm_grad, ffn_gain_grad = norm_two_pull(normed_two_grad)
    hidden_grad = back_rows + hidden_norm_grad

    branch_back = gather_tokens((valid_col * hidden_grad).astype(low))
    attended_back = contract_last(branch_back, own_out).astype(low)
    grad_out = lax.psum_scatter(
        column_product(attended_low, branch_back).astype(low),
        "dp",
        scatter_dimension=0,
        tiled=True,
    ).astype(jnp.float32)
    attended_five = attended_back.reshape(n_mb, MB_TOK, kvl, group, HD)
    probs_grad = jnp.einsum(
        "mtkgd,mukd->mkgtu", attended_five, values_low, preferred_element_type=jnp.float32
    )
    spread = jnp.sum(probs * probs_grad, axis=-1, keepdims=True)
    score_back = (probs * (probs_grad - spread)).astype(low)
    query_grad = (
        jnp.einsum("mkgtu,mukd->mtkgd", score_back, keys_low, preferred_element_type=jnp.float32)
        * score_scale
    )
    key_grad = (
        jnp.einsum("mkgtu,mtkgd->mukd", score_back, queries_low, preferred_element_type=jnp.float32)
        * score_scale
    )
    value_grad = jnp.einsum(
        "mkgtu,mtkgd->mukd", probs_low, attended_five, preferred_element_type=jnp.float32
    )
    query_in_grad, key_in_grad, query_gain_grad, key_gain_grad = turn_pull(
        (query_grad.reshape(n_rows, heads_own, HD), key_grad.reshape(n_rows, kvl, HD))
    )
    projected_back = jnp.concatenate(
        [
            query_in_grad.reshape(n_rows, q_width),
            key_in_grad.reshape(n_rows, kv_width),
            value_grad.reshape(n_rows, kv_width),
        ],
        axis=1,
    ).astype(low)
    normed_one_grad = scatter_tokens(contract_last(projected_back, own_qkv))
    grad_qkv = lax.psum_scatter(
        column_product(norm_one_all, projected_back)
        .astype(low)
        .reshape(nf, nd * rows_own, wide),
        "dp",
        scatter_dimension=1,
        tiled=True,
    )
    grad_blocks = swap(grad_qkv).astype(jnp.float32)

    def head_rows(blocks, times):
        merged = jnp.sum(blocks.reshape(nf // times, times, rows_own, -1), axis=1)
        return jnp.swapaxes(merged, 0, 1).reshape(rows_own, -1)

    grad_qkv = jnp.concatenate(
        [
            head_rows(grad_blocks[:, :, :q_width], 1),
            head_rows(grad_blocks[:, :, q_width : q_width + kv_width], rep),
            head_rows(grad_blocks[:, :, q_width + kv_width :], rep),
        ],
        axis=1,
    )
    rows_grad, attn_gain_grad = norm_one_pull(normed_one_grad)
    input_grad = (hidden_grad + rows_grad)[inverse]
    output_all = output.astype(low)[inverse]

    owned = (grad_qkv, grad_out, grad_gate_up, grad_down)
    local_squares = (
        jnp.sum(owned[0] * owned[0])
        + jnp.sum(owned[1] * owned[1])
        + jnp.sum(owned[2] * owned[2])
        + jnp.sum(owned[3] * owned[3])
    )
    gain_sum = jnp.concatenate([attn_gain_grad, ffn_gain_grad, query_gain_grad, key_gain_grad])
    gain_total, square_total = lax.psum((gain_sum, local_squares), ("fsdp", "dp"))
    global_norm = jnp.sqrt(square_total + jnp.sum(gain_total * gain_total))
    factor = CLIP_NORM / jnp.maximum(global_norm, CLIP_NORM)
    new_qkv, next_first_qkv, next_second_qkv = adam_step(
        w_qkv, first_qkv, second_qkv, owned[0], factor, LEARN_RATE, WEIGHT_DECAY
    )
    new_out, next_first_out, next_second_out = adam_step(
        w_out, first_out, second_out, owned[1], factor, LEARN_RATE, WEIGHT_DECAY
    )
    new_gate_up, next_first_gate_up, next_second_gate_up = adam_step(
        w_gate_up, first_gate_up, second_gate_up, owned[2], factor, LEARN_RATE, WEIGHT_DECAY
    )
    new_down, next_first_down, next_second_down = adam_step(
        w_down, first_down, second_down, owned[3], factor, LEARN_RATE, WEIGHT_DECAY
    )
    new_gains, next_first_gains, next_second_gains = adam_step(
        gains, first_gains, second_gains, gain_total, factor, GAIN_RATE, 0.0
    )
    return (
        output_all,
        input_grad,
        global_norm,
        new_qkv,
        new_out,
        new_gate_up,
        new_down,
        new_gains,
        next_first_qkv,
        next_first_out,
        next_first_gate_up,
        next_first_down,
        next_first_gains,
        next_second_qkv,
        next_second_out,
        next_second_gate_up,
        next_second_down,
        next_second_gains,
    )


def solution(mesh):
    nf, nd = mesh.shape["fsdp"], mesh.shape["dp"]
    fits = nf == PLANE and KVH == PLANE and nd % 2 == 0
    per_device = per_device_plane if fits else per_device_plain
    in_specs = (
        P(("fsdp", "dp"), None),
        P(("fsdp", "dp"), None),
        P(("fsdp", "dp"), None),
        P(("fsdp", "dp"), None),
        P(("fsdp", "dp"), None),
        P(("fsdp", "dp"), None),
        P(("fsdp", "dp"), None),
        P(("fsdp", "dp"), None),
        P(),
        P(("fsdp", "dp"), None),
        P(("fsdp", "dp"), None),
        P(("fsdp", "dp"), None),
        P(("fsdp", "dp"), None),
        P(),
        P(("fsdp", "dp"), None),
        P(("fsdp", "dp"), None),
        P(("fsdp", "dp"), None),
        P(("fsdp", "dp"), None),
        P(),
    )
    out_specs = (
        P(("fsdp", "dp"), None),
        P(("fsdp", "dp"), None),
        P(),
        P(("fsdp", "dp"), None),
        P(("fsdp", "dp"), None),
        P(("fsdp", "dp"), None),
        P(("fsdp", "dp"), None),
        P(),
        P(("fsdp", "dp"), None),
        P(("fsdp", "dp"), None),
        P(("fsdp", "dp"), None),
        P(("fsdp", "dp"), None),
        P(),
        P(("fsdp", "dp"), None),
        P(("fsdp", "dp"), None),
        P(("fsdp", "dp"), None),
        P(("fsdp", "dp"), None),
        P(),
    )
    return jax.shard_map(
        functools.partial(per_device, nf, nd), mesh=mesh, in_specs=in_specs, out_specs=out_specs, check_vma=False
    )
```

```python
import functools

import jax
import jax.numpy as jnp
from jax import lax
from jax.experimental import pallas as pl
from jax.experimental.pallas import tpu as pltpu
from jax.sharding import PartitionSpec as P

D = 2048
HEADS = 32
HD = 64
KVH = 8
FF = 8192
TOK_DEV = 256
MB = 2
SEQS = 3
STEP = 10
MB_TOK = 128


EPSILON = 1e-05
ROPE_BASE = 1000000.0
FIRST_DECAY = 0.9
SECOND_DECAY = 0.95
LEARN_RATE = 0.05
GAIN_RATE = 2.0
WEIGHT_DECAY = 0.1
ADAM_EPSILON = 1e-08
CLIP_NORM = 1.0
GAIN_LINES = (2 * D + 2 * HD) // 128
MASKED = -1e30


def rms_norm(values, gain_vec):
    return (
        values * lax.rsqrt(jnp.mean(values * values, axis=-1, keepdims=True) + EPSILON) * gain_vec
    )


def rope_tables(position):
    half_width = HD // 2
    frequency = ROPE_BASE ** (jnp.arange(half_width, dtype=jnp.float32) * (-2.0 / HD))
    angles = position[:, None] * frequency[None, :]
    return (jnp.cos(angles)[:, None, :], jnp.sin(angles)[:, None, :])


def rotate(values, cosine_table, sine_table):
    half_width = HD // 2
    first_part = values[..., :half_width]
    second_part = values[..., half_width:]
    return jnp.concatenate(
        [
            first_part * cosine_table - second_part * sine_table,
            second_part * cosine_table + first_part * sine_table,
        ],
        axis=-1,
    )


def layout(lengths_rows):
    seq_ends = jnp.cumsum(lengths_rows, axis=-1)
    places = jnp.arange(MB_TOK, dtype=jnp.int32)
    passed = (places[None, :, None] >= seq_ends[:, None, :]).astype(jnp.int32)
    segment = jnp.sum(passed, axis=-1)
    starts = jnp.sum(passed * lengths_rows[:, None, :], axis=-1)
    position = (places[None, :] - starts).astype(jnp.float32)
    valid_rows = (segment < SEQS - 1).astype(jnp.float32)
    allowed = (segment[:, :, None] == segment[:, None, :]) & (
        places[None, None, :] <= places[None, :, None]
    )
    return (position, valid_rows, allowed)


def swiglu(gate, up):
    return jax.nn.silu(gate) * up


def column_product(left_side, right_side):
    return lax.dot_general(
        left_side, right_side, (((0,), (0,)), ((), ())), preferred_element_type=jnp.float32
    )


def contract_last(left_side, right_side):
    return lax.dot_general(
        left_side, right_side, (((1,), (1,)), ((), ())), preferred_element_type=jnp.float32
    )


def product(left_side, right_side):
    return jnp.dot(left_side, right_side, preferred_element_type=jnp.float32)


def adam_step(weight, first_state, second, gradient, factor, step_rate, decay_rate):
    clipped = gradient * factor
    first_new = FIRST_DECAY * first_state + (1.0 - FIRST_DECAY) * clipped
    second_new = SECOND_DECAY * second + (1.0 - SECOND_DECAY) * clipped * clipped
    first_hat = first_new / (1.0 - FIRST_DECAY**STEP)
    second_hat = second_new / (1.0 - SECOND_DECAY**STEP)
    weight_new = weight - step_rate * (
        first_hat / (jnp.sqrt(second_hat) + ADAM_EPSILON) + decay_rate * weight
    )
    return (weight_new, first_new, second_new)


MESH = pl.DeviceIdType.MESH
ANY = pl.BlockSpec(memory_space=pl.ANY)
VMEM = pl.BlockSpec(memory_space=pltpu.VMEM)
PLANE = 8
TILE = 512
GLU_TILE = 256
SHORT = pl.CostEstimate(flops=0, bytes_accessed=1024, transcendentals=0)


def flip(index, bit):
    step = 2**bit
    return index + step * (1 - 2 * lax.rem(lax.div(index, step), 2))


def plane_others(me):
    others = []
    for number in range(1, PLANE):
        other = me
        for bit in range(3):
            if (number >> bit) & 1:
                other = flip(other, bit)
        others.append(other)
    return others


def greet(devices):
    barrier = pltpu.get_barrier_semaphore()
    for device in devices:
        pl.semaphore_signal(barrier, inc=1, device_id={"fsdp": device}, device_id_type=MESH)
    pl.semaphore_wait(barrier, len(devices))


def half_pieces(half_ref, wide_ref, me, other, count):
    half_width = half_ref.shape[1] // 2
    for side in range(2):
        first = pl.multiple_of(side * half_width * PLANE + me * half_width, 128)
        source = half_ref.at[pl.ds(pl.multiple_of(other * count, count), count)]
        yield (
            source.at[:, pl.ds(side * half_width, half_width)],
            wide_ref.at[:, pl.ds(first, half_width)],
        )


def put_half(half_ref, wide_ref, others, number, sems):
    me, other = lax.axis_index("fsdp"), others[number - 1]
    pairs = half_pieces(half_ref, wide_ref, me, other, wide_ref.shape[0])
    return [
        pltpu.make_async_remote_copy(
            src_ref=source,
            dst_ref=target,
            send_sem=sems.at[0, 2 * number + side],
            recv_sem=sems.at[1, 2 * number + side],
            device_id={"fsdp": other},
            device_id_type=MESH,
        )
        for side, (source, target) in enumerate(pairs)
    ]


def keep_half(half_ref, wide_ref, sems):
    me = lax.axis_index("fsdp")
    return [
        pltpu.make_async_copy(source, target, sems.at[side])
        for side, (source, target) in enumerate(
            half_pieces(half_ref, wide_ref, me, me, wide_ref.shape[0])
        )
    ]


def columns_kernel(half_ref, wide_ref, squares_ref, own_sem, sems):
    others = plane_others(lax.axis_index("fsdp"))
    greet(others)
    order = (6, 7, 2, 4, 3, 5, 1)
    for number in order:
        for copy in put_half(half_ref, wide_ref, others, number, sems):
            copy.start()
    keep = keep_half(half_ref, wide_ref, own_sem)
    for copy in keep:
        copy.start()
    squares_ref[...] = jnp.zeros_like(squares_ref)

    @pl.loop(0, half_ref.shape[0] // 128)
    def _(step):
        spot = pl.ds(pl.multiple_of(step * 128, 128), 128)
        values = half_ref[spot, :].astype(jnp.float32)
        squares_ref[...] += jnp.sum(values * values, axis=0, keepdims=True)

    for number in order:
        for copy in put_half(half_ref, wide_ref, others, number, sems):
            copy.wait()
    for copy in keep:
        copy.wait()


def half_scratch():
    return [pltpu.SemaphoreType.DMA((2,)), pltpu.SemaphoreType.DMA((2, 2 * PLANE))]


def exchange_half(half, count, number):
    return pl.pallas_call(
        columns_kernel,
        out_shape=[
            jax.ShapeDtypeStruct((count, half.shape[1] * PLANE), half.dtype),
            jax.ShapeDtypeStruct((1, half.shape[1]), jnp.float32),
        ],
        in_specs=[VMEM],
        out_specs=[ANY, VMEM],
        scratch_shapes=half_scratch(),
        compiler_params=pltpu.CompilerParams(collective_id=number, has_side_effects=True),
        cost_estimate=SHORT,
        name=f"exchange_half_{number}",
    )(half)


def sum_kernel(
    nd,
    x_ref,
    blocks_ref,
    out_ref,
    norm_ref,
    qkv_ref,
    gout_ref,
    swapped_ref,
    plane_in,
    line_in,
    total,
    mine,
    own_sem,
    plane_sems,
    line_sems,
    block_sems,
):
    me, line = lax.axis_index("fsdp"), lax.axis_index("dp")
    wide = swapped_ref.shape[2]
    q_width = wide - 2 * HD
    blocks = blocks_ref[...].astype(jnp.float32)
    squares = jnp.sum(blocks * blocks, axis=(0, 1, 2), keepdims=True).reshape(1, 1)
    lines = lax.broadcasted_iota(jnp.int32, x_ref.shape, 0)
    lane = lax.broadcasted_iota(jnp.int32, x_ref.shape, 1)
    spot = jnp.logical_and(lines == GAIN_LINES, lane == 0)
    mine[...] = x_ref[...] + jnp.where(spot, squares, 0.0)
    others = plane_others(me)
    steps = [lax.rem(line + step, nd) for step in range(1, nd)]
    barrier = pltpu.get_barrier_semaphore()
    for other in others:
        pl.semaphore_signal(barrier, inc=1, device_id={"fsdp": other}, device_id_type=MESH)
    for other in steps:
        pl.semaphore_signal(barrier, inc=1, device_id={"dp": other}, device_id_type=MESH)
    pl.semaphore_wait(barrier, len(others) + len(steps))

    def to_plane(number):
        return pltpu.make_async_remote_copy(
            src_ref=mine,
            dst_ref=plane_in.at[me],
            send_sem=plane_sems.at[0, number],
            recv_sem=plane_sems.at[1, number],
            device_id={"fsdp": others[number]},
            device_id_type=MESH,
        )

    def to_line(number):
        return pltpu.make_async_remote_copy(
            src_ref=total,
            dst_ref=line_in.at[line],
            send_sem=line_sems.at[0, number],
            recv_sem=line_sems.at[1, number],
            device_id={"dp": steps[number]},
            device_id_type=MESH,
        )

    def put_block(number):
        return pltpu.make_async_remote_copy(
            src_ref=blocks_ref.at[others[number], :, pl.ds(0, wide)],
            dst_ref=swapped_ref.at[me],
            send_sem=block_sems.at[0, number],
            recv_sem=block_sems.at[1, number],
            device_id={"fsdp": others[number]},
            device_id_type=MESH,
        )

    keep = [
        pltpu.make_async_copy(
            blocks_ref.at[me, :, pl.ds(0, wide)], swapped_ref.at[me], own_sem.at[PLANE]
        )
    ]
    for place in range(PLANE):
        keep.append(
            pltpu.make_async_copy(
                blocks_ref.at[place, :, pl.ds(wide, q_width)],
                gout_ref.at[:, pl.ds(place * q_width, q_width)],
                own_sem.at[place],
            )
        )
    for number in range(PLANE - 1):
        to_plane(number).start()
    for number in range(PLANE - 1):
        put_block(number).start()
    for copy in keep:
        copy.start()
    plane_in[me] = mine[...]
    for number in range(PLANE - 1):
        to_plane(number).wait()
    part = plane_in[0]
    for place in range(1, PLANE):
        part = part + plane_in[place]
    total[...] = part
    line_in[line] = part
    for number in range(nd - 1):
        to_line(number).start()
    for number in range(PLANE - 1):
        put_block(number).wait()
    for copy in keep:
        copy.wait()
    first_head = lax.broadcasted_iota(jnp.int32, (1, 2 * HD), 1) < HD
    for place in range(0, PLANE, 2):
        pair = []
        for block in (place, place + 1):
            values = swapped_ref[block].astype(jnp.float32)
            qkv_ref[:, block * q_width : (block + 1) * q_width] = swapped_ref[block, :, :q_width]
            pair.append(values[:, q_width:])
        columns = pl.ds(PLANE * q_width + place * HD, 2 * HD)
        both = jnp.where(first_head, pair[0], pltpu.roll(pair[1], HD, 1))
        qkv_ref[:, columns] = both.astype(qkv_ref.dtype)
        columns = pl.ds(PLANE * (q_width + HD) + place * HD, 2 * HD)
        both = jnp.where(first_head, pltpu.roll(pair[0], HD, 1), pair[1])
        qkv_ref[:, columns] = both.astype(qkv_ref.dtype)
    for number in range(nd - 1):
        to_line(number).wait()
    part = line_in[0]
    for place in range(1, nd):
        part = part + line_in[place]
    out_ref[...] = part
    gains = part[:GAIN_LINES]
    lane = lax.broadcasted_iota(jnp.int32, (1, 128), 1)
    squares = jnp.where(lane == 0, part[GAIN_LINES : GAIN_LINES + 1], 0.0)
    squares = squares + jnp.sum(gains * gains, axis=0, keepdims=True)
    norm = jnp.sqrt(jnp.sum(squares, axis=1, keepdims=True))
    factor = CLIP_NORM / jnp.maximum(norm, CLIP_NORM)
    line_number = lax.broadcasted_iota(jnp.int32, norm_ref.shape, 0)
    norm_ref[...] = jnp.where(line_number == 0, norm, factor)


def sum_everywhere(gain_sum, squares, blocks, wide, number):
    values = jnp.concatenate([gain_sum, squares.reshape(1)])
    nd = lax.axis_size("dp")
    count = values.shape[0]
    lines = -(-count // 1024) * 8
    padded = jnp.pad(values, (0, lines * 128 - count)).reshape(lines, 128)
    q_width = wide - 2 * HD
    summed, norm, grad_qkv, grad_out = pl.pallas_call(
        functools.partial(sum_kernel, nd),
        out_shape=[
            jax.ShapeDtypeStruct(padded.shape, jnp.float32),
            jax.ShapeDtypeStruct((8, 128), jnp.float32),
            jax.ShapeDtypeStruct((blocks.shape[1], PLANE * wide), blocks.dtype),
            jax.ShapeDtypeStruct((blocks.shape[1], PLANE * q_width), blocks.dtype),
        ],
        in_specs=[VMEM, VMEM],
        out_specs=[VMEM] * 4,
        scratch_shapes=[
            pltpu.VMEM((PLANE, blocks.shape[1], wide), blocks.dtype),
            pltpu.VMEM((PLANE,) + padded.shape, jnp.float32),
            pltpu.VMEM((nd,) + padded.shape, jnp.float32),
            pltpu.VMEM(padded.shape, jnp.float32),
            pltpu.VMEM(padded.shape, jnp.float32),
            pltpu.SemaphoreType.DMA((PLANE + 1,)),
            pltpu.SemaphoreType.DMA((2, PLANE - 1)),
            pltpu.SemaphoreType.DMA((2, nd - 1)),
            pltpu.SemaphoreType.DMA((2, PLANE - 1)),
        ],
        compiler_params=pltpu.CompilerParams(collective_id=number, has_side_effects=True),
        cost_estimate=SHORT,
        name=f"sum_everywhere_{number}",
    )(padded, blocks)
    return summed.reshape(-1)[: count - 1], norm, grad_qkv, grad_out


def greet_line(nd, others):
    line = lax.axis_index("dp")
    barrier = pltpu.get_barrier_semaphore()
    for other in others:
        pl.semaphore_signal(barrier, inc=1, device_id={"fsdp": other}, device_id_type=MESH)

    @pl.when(line < nd - 1)
    def _():
        pl.semaphore_signal(barrier, inc=1, device_id={"dp": line + 1}, device_id_type=MESH)

    @pl.when(line > 0)
    def _():
        pl.semaphore_signal(barrier, inc=1, device_id={"dp": line - 1}, device_id_type=MESH)

    neighbours = lax.div(line + nd - 1, nd) + lax.div(2 * nd - 2 - line, nd)
    pl.semaphore_wait(barrier, len(others) + neighbours)


class Gather:
    def __init__(self, own_ref, all_ref, send_sem, recv_sem):
        self.own_ref, self.all_ref = own_ref, all_ref
        self.send_sem, self.recv_sem = send_sem, recv_sem
        self.me = lax.axis_index("fsdp")
        self.sibling, self.x_next, self.y_next = flip(self.me, 0), flip(self.me, 1), flip(self.me, 2)
        self.diagonal = flip(self.x_next, 2)
        self.rows = own_ref.shape[0]
        self.sent = []

    def put(self, slot, owner, part, target, own=False):
        half = self.rows // 2
        if part is None:
            spot = self.all_ref.at[pl.ds(pl.multiple_of(owner * self.rows, half), self.rows)]
            source = self.own_ref
        else:
            first = pl.multiple_of(owner * self.rows + part * half, half)
            spot = self.all_ref.at[pl.ds(first, half)]
            source = self.own_ref.at[pl.ds(part * half, half)]
        return pltpu.make_async_remote_copy(
            src_ref=source if own else spot,
            dst_ref=spot,
            send_sem=self.send_sem.at[slot],
            recv_sem=self.recv_sem.at[slot],
            device_id={"fsdp": target},
            device_id_type=MESH,
        )

    def begin(self):
        for slot, part, target in (
            (0, 0, self.x_next),
            (2, 1, self.y_next),
            (4, None, self.sibling),
            (1, 1, self.x_next),
            (3, 0, self.y_next),
        ):
            copy = self.put(slot, self.me, part, target, own=True)
            copy.start()
            self.sent.append(copy)

    def take(self, slot):
        sibling = self.sibling
        owner, part, onward = {
            0: (self.x_next, 0, ((5, self.y_next), (7, sibling))),
            1: (self.x_next, 1, ((8, sibling),)),
            2: (self.y_next, 1, ((6, self.x_next), (9, sibling))),
            3: (self.y_next, 0, ((10, sibling),)),
            4: (sibling, None, ()),
            5: (self.diagonal, 0, ((11, sibling),)),
            6: (self.diagonal, 1, ((12, sibling),)),
            7: (flip(self.x_next, 0), 0, ()),
            8: (flip(self.x_next, 0), 1, ()),
            9: (flip(self.y_next, 0), 1, ()),
            10: (flip(self.y_next, 0), 0, ()),
            11: (flip(self.diagonal, 0), 0, ()),
            12: (flip(self.diagonal, 0), 1, ()),
        }[slot]
        self.put(slot, owner, part, sibling).wait_recv()
        for next_slot, target in onward:
            copy = self.put(next_slot, owner, part, target)
            copy.start()
            self.sent.append(copy)

    def finish(self):
        for copy in self.sent:
            copy.wait_send()


def gather_scratch():
    return [pltpu.SemaphoreType.DMA((13,)), pltpu.SemaphoreType.DMA((13,))]


class Scatter:
    def __init__(self, out_ref, block, refs):
        self.out_ref, self.block = out_ref, block
        (self.sib_out, self.sib_in, self.far_out, self.far_in, self.near_out, self.near_in) = refs[:6]
        self.late = refs[6]
        self.sib_sems, self.far_sems, self.near_sems = refs[7:9], refs[9:11], refs[11:13]
        self.me = lax.axis_index("fsdp")
        self.sibling, self.x_next, self.y_next = flip(self.me, 0), flip(self.me, 1), flip(self.me, 2)
        self.targets = (flip(self.x_next, 2), self.x_next, self.y_next, self.me)
        self.half = out_ref.shape[0] // 2

    def send(self, source, target, sems, slot, device):
        return pltpu.make_async_remote_copy(
            src_ref=source.at[slot],
            dst_ref=target.at[slot],
            send_sem=sems[0].at[slot],
            recv_sem=sems[1].at[slot],
            device_id={"fsdp": device},
            device_id_type=MESH,
        )

    def to_sibling(self, place):
        return self.send(self.sib_out, self.sib_in, self.sib_sems, place, self.sibling)

    def to_far(self, part):
        device = (self.x_next, self.y_next)[part]
        return self.send(self.far_out, self.far_in, self.far_sems, part, device)

    def to_near(self, place, part):
        device = (self.x_next, self.y_next)[place]
        return self.send(self.near_out, self.near_in, self.near_sems, 2 * place + part, device)

    def for_sibling(self, place):
        def write(columns, part):
            self.sib_out[place, :, columns] = part.astype(jnp.bfloat16)

        self.block(flip(self.targets[place], 0), write)
        self.to_sibling(place).start()

    def for_far(self):
        self.to_sibling(0).wait_recv()

        def write(columns, part):
            whole = (part + self.sib_in[0, :, columns].astype(jnp.float32)).astype(jnp.bfloat16)
            self.far_out[0, :, columns] = whole[: self.half]
            self.far_out[1, :, columns] = whole[self.half :]

        self.block(self.targets[0], write)
        self.to_far(0).start()
        self.to_far(1).start()

    def for_near(self, place):
        self.to_sibling(1 + place).wait_recv()
        other = 1 - place

        def write(columns, part):
            whole = part + self.sib_in[1 + place, :, columns].astype(jnp.float32)
            halves = (whole[: self.half], whole[self.half :])
            self.near_out[2 * place + place, :, columns] = halves[place].astype(jnp.bfloat16)
            self.late[place, :, columns] = halves[other]

        self.block(self.targets[1 + place], write)
        self.to_near(place, place).start()

    def finish_near(self, place):
        other = 1 - place
        self.to_far(other).wait_recv()
        whole = self.late[place] + self.far_in[other].astype(jnp.float32)
        self.near_out[2 * place + other] = whole.astype(jnp.bfloat16)
        self.to_near(place, other).start()

    def own(self):
        def write(columns, part):
            self.out_ref[:, columns] = part

        self.block(self.me, write)

    def finish(self):
        self.to_sibling(3).wait_recv()
        self.out_ref[...] = self.out_ref[...] + self.sib_in[3].astype(jnp.float32)
        for part, place in ((0, 0), (1, 1), (1, 0), (0, 1)):
            self.to_near(place, part).wait_recv()
            spot = pl.ds(part * self.half, self.half)
            part_in = self.near_in[2 * place + part].astype(jnp.float32)
            self.out_ref[spot, :] = self.out_ref[spot, :] + part_in
        for place in range(4):
            self.to_sibling(place).wait_send()
            self.to_near(place // 2, place % 2).wait_send()
        for part in range(2):
            self.to_far(part).wait_send()


def staged(kernel, n_in, places):
    def body(*refs):
        stage, sems = refs[-len(places) - 1 : -1], refs[-1]
        inputs, rest = list(refs[:n_in]), refs[n_in : -len(places) - 1]
        copies = [
            pltpu.make_async_copy(inputs[place], buffer, sems.at[index])
            for index, (place, buffer) in enumerate(zip(places, stage))
        ]
        for copy in copies:
            copy.start()
        for place, buffer in zip(places, stage):
            inputs[place] = buffer

        def ready():
            for copy in copies:
                copy.wait()

        kernel(ready, *inputs, *rest)

    return body


def staged_specs(arrays, places):
    specs = [ANY if place in places else VMEM for place in range(len(arrays))]
    scratch = [pltpu.VMEM(arrays[place].shape, arrays[place].dtype) for place in places]
    return specs, scratch + [pltpu.SemaphoreType.DMA((len(places),))]


def scatter_scratch(rows, width):
    low, half = jnp.bfloat16, rows // 2
    return [
        pltpu.VMEM((4, rows, width), low),
        pltpu.VMEM((4, rows, width), low),
        pltpu.VMEM((2, half, width), low),
        pltpu.VMEM((2, half, width), low),
        pltpu.VMEM((4, half, width), low),
        pltpu.VMEM((4, half, width), low),
        pltpu.VMEM((2, half, width), jnp.float32),
        pltpu.SemaphoreType.DMA((4,)),
        pltpu.SemaphoreType.DMA((4,)),
        pltpu.SemaphoreType.DMA((2,)),
        pltpu.SemaphoreType.DMA((2,)),
        pltpu.SemaphoreType.DMA((4,)),
        pltpu.SemaphoreType.DMA((4,)),
    ]


def block_product(left_refs, right_refs, rows, width, turned):
    def block(owner, write):
        @pl.loop(0, width // TILE)
        def _(step):
            columns = pl.ds(pl.multiple_of(step * TILE, TILE), TILE)
            spot = pl.ds(pl.multiple_of(owner * rows, rows), rows)
            total = None
            for left_ref, right_ref in zip(left_refs, right_refs):
                if turned:
                    part = contract_last(left_ref[spot, :], right_ref[columns, :])
                else:
                    part = product(left_ref[spot, :], right_ref[:, columns])
                total = part if total is None else total + part
            write(columns, total)

    return block


def scatter_kernel(turned, count, *refs):
    left_hbm, right_hbm, out_ref = refs[:count], refs[count : 2 * count], refs[2 * count]
    refs = refs[2 * count + 1 :]
    left_refs, right_refs = refs[:count], refs[count : 2 * count]
    left_sems, right_sems, refs = refs[2 * count], refs[2 * count + 1], refs[2 * count + 2 :]
    rows, width = out_ref.shape
    whole = block_product(left_refs, right_refs, rows, width, turned)

    def fetch(place, owner):
        spot = pl.ds(pl.multiple_of(owner * rows, rows), rows)
        return pltpu.make_async_copy(
            left_hbm[place].at[spot], left_refs[place].at[spot], left_sems.at[place, owner]
        )

    def block(owner, write):
        for place in range(count):
            fetch(place, owner).wait()
        whole(owner, write)

    scatter = Scatter(out_ref, block, refs)
    rights = [
        pltpu.make_async_copy(right_hbm[place], right_refs[place], right_sems.at[place])
        for place in range(count)
    ]
    for copy in rights:
        copy.start()
    far, x_next, y_next, me = scatter.targets
    for owner in (
        flip(far, 0),
        flip(x_next, 0),
        far,
        flip(y_next, 0),
        x_next,
        flip(me, 0),
        y_next,
        me,
    ):
        for place in range(count):
            fetch(place, owner).start()
    greet((scatter.sibling, scatter.x_next, scatter.y_next))
    for copy in rights:
        copy.wait()
    scatter.for_sibling(0)
    scatter.for_sibling(1)
    scatter.for_far()
    scatter.for_sibling(2)
    scatter.for_near(0)
    scatter.for_sibling(3)
    scatter.for_near(1)
    scatter.finish_near(0)
    scatter.finish_near(1)
    scatter.own()
    scatter.finish()


def pass_through(ready, gather, scatter, work, between):
    me, sibling, x_next, y_next = gather.me, gather.sibling, gather.x_next, gather.y_next
    diagonal = gather.diagonal
    greet((sibling, x_next, y_next))
    gather.begin()
    gather.all_ref[pl.ds(pl.multiple_of(me * gather.rows, gather.rows), gather.rows), :] = (
        gather.own_ref[...]
    )
    ready()
    work((me,))
    gather.take(0)
    gather.take(2)
    gather.take(4)
    work((sibling,))
    scatter.for_sibling(3)
    gather.take(1)
    gather.take(3)
    work((x_next, y_next))
    gather.take(5)
    gather.take(6)
    for slot in (7, 8, 9, 10):
        gather.take(slot)
    work((flip(x_next, 0), flip(y_next, 0)))
    scatter.for_sibling(1)
    scatter.for_sibling(2)
    scatter.for_near(0)
    scatter.for_near(1)
    gather.take(11)
    gather.take(12)
    work((flip(diagonal, 0),))
    scatter.for_sibling(0)
    work((diagonal,))
    scatter.for_far()
    scatter.own()
    between[0]()
    scatter.finish_near(0)
    scatter.finish_near(1)
    between[1]()
    scatter.finish()
    gather.finish()


def each_owner(owners, rows, one):
    if len(owners) == 1:
        one(owners[0])
        return

    @pl.loop(0, len(owners))
    def _(step):
        one(owners[0] + step * (owners[1] - owners[0]))


def lanes():
    lane = lax.broadcasted_iota(jnp.int32, (1, 2 * HD), 1)
    row_head = lax.broadcasted_iota(jnp.int32, (2 * HD, 2 * HD), 0) // HD
    column_head = lax.broadcasted_iota(jnp.int32, (2 * HD, 2 * HD), 1) // HD
    spread = jnp.where(row_head == column_head, 1.0 / HD, 0.0).astype(jnp.float32)

    def head_mean(values):
        return jnp.dot(
            values, spread, precision=lax.Precision.HIGHEST, preferred_element_type=jnp.float32
        )

    first_half = lax.rem(lane, HD) < HD // 2

    def turn_quarter(values):
        return jnp.where(
            first_half,
            -pltpu.roll(values, 2 * HD - HD // 2, 1),
            pltpu.roll(values, HD // 2, 1),
        )

    def sides(values):
        return [
            jnp.where(chosen, values, 0.0).astype(jnp.bfloat16)
            for chosen in (lane < HD, lane >= HD)
        ]

    return lane, sides, head_mean, turn_quarter


def twice(values):
    return jnp.concatenate([values, values], axis=0)


def stacked(ref, spot):
    width = 2 * HD
    return jnp.concatenate([ref[spot, :width], ref[spot, width : 2 * width]], axis=0)


def attend_kernel(
    ready,
    x_ref,
    wqkv_ref,
    wo_ref,
    cos_ref,
    sin_ref,
    mask_ref,
    gain_ref,
    out_ref,
    all_out_ref,
    proj_ref,
    q_ref,
    kk_ref,
    vv_ref,
    o_ref,
    lse_ref,
    all_ref,
    out_sem,
    gather_send,
    gather_recv,
    *refs,
):
    rows, width = out_ref.shape
    low = jnp.bfloat16
    pair_width = 2 * HD
    lane, sides, head_mean, turn_quarter = lanes()
    first_head = lane < HD
    scale = HD ** (-0.5)

    def normed(values, gain):
        return values * lax.rsqrt(head_mean(values * values) + EPSILON) * gain

    def one(owner):
        base = pl.multiple_of(owner * rows, rows)
        spot = pl.ds(base, rows)
        proj_ref[spot, :] = product(all_ref[spot, :], wqkv_ref[...])

        for part in range(MB):
            micro(pl.multiple_of(base + part * MB_TOK, MB_TOK), owner * MB + part)

    def micro(first, number):
        spot = pl.ds(first, MB_TOK)
        cosine, sine = cos_ref[spot, :], sin_ref[spot, :]
        allowed = twice(mask_ref[number]) > 0.5
        kv = proj_ref[spot, 2 * pair_width : 3 * pair_width]
        swapped = pltpu.roll(kv, HD, 1)
        values = jnp.where(first_head, swapped, kv)
        keys = normed(jnp.where(first_head, kv, swapped), gain_ref[1:2, :])
        keys = (keys * cosine + turn_quarter(keys) * sine).astype(low)
        kk_ref[spot, :] = keys
        vv_ref[spot, :] = values.astype(low)
        query = normed(stacked(proj_ref, spot), gain_ref[0:1, :])
        query = (query * twice(cosine) + turn_quarter(query) * twice(sine)).astype(low)
        q_ref[spot, :pair_width] = query[:MB_TOK]
        q_ref[spot, pair_width : 2 * pair_width] = query[MB_TOK:]
        probs, logs = [], []
        for one_query in sides(query.astype(jnp.float32) * scale):
            scores = jnp.where(allowed, contract_last(one_query, keys), MASKED)
            peak = jnp.max(scores, axis=-1, keepdims=True)
            powers = jnp.exp(scores - peak)
            total = jnp.sum(powers, axis=-1, keepdims=True)
            probs.append((powers * (1.0 / total)).astype(low))
            logs.append(peak + jnp.log(total))
        wide_values = jnp.concatenate(sides(values), axis=0)
        attended = product(jnp.concatenate(probs, axis=1), wide_values).astype(low)
        o_ref[spot, :pair_width] = attended[:MB_TOK]
        o_ref[spot, pair_width : 2 * pair_width] = attended[MB_TOK:]
        log_totals = jnp.where(lane == 0, logs[0][:MB_TOK], logs[1][:MB_TOK])
        log_totals = jnp.where(lane == 2, logs[0][MB_TOK:], log_totals)
        lse_ref[spot, :] = jnp.where(lane == 3, logs[1][MB_TOK:], log_totals)

    gather = Gather(x_ref, all_ref, gather_send, gather_recv)
    scatter = Scatter(out_ref, block_product((o_ref,), (wo_ref,), rows, width, False), refs)
    keep = pltpu.make_async_copy(all_ref, all_out_ref, out_sem)
    pass_through(
        ready,
        gather,
        scatter,
        lambda owners: each_owner(owners, rows, one),
        (keep.start, lambda: None),
    )
    keep.wait()


def attend_back_kernel(
    ready,
    x_ref,
    wqkv_ref,
    wo_ref,
    cos_ref,
    sin_ref,
    mask_ref,
    gain_ref,
    proj_ref,
    q_ref,
    kk_ref,
    vv_ref,
    o_ref,
    lse_ref,
    normed_hbm,
    out_ref,
    grad_ref,
    ggain_ref,
    all_ref,
    normed_ref,
    do_ref,
    dproj_ref,
    in_sem,
    gather_send,
    gather_recv,
    *refs,
):
    rows, width = out_ref.shape
    low = jnp.bfloat16
    pair_width = 2 * HD
    lane, sides, head_mean, turn_quarter = lanes()
    first_head = lane < HD
    scale = HD ** (-0.5)
    fetch = pltpu.make_async_copy(normed_hbm, normed_ref, in_sem)
    fetch.start()
    ggain_ref[...] = jnp.zeros_like(ggain_ref)

    def through_norm(grad, cosine, sine, raw, gain, row):
        grad = grad * cosine - turn_quarter(grad) * sine
        root = lax.rsqrt(head_mean(raw * raw) + EPSILON)
        normed = raw * root
        ggain_ref[row : row + 1, :] += jnp.sum(grad * normed, axis=0, keepdims=True)
        scaled = grad * gain
        return root * (scaled - normed * head_mean(scaled * normed))

    def one(owner):
        base = pl.multiple_of(owner * rows, rows)
        do_ref[...] = contract_last(all_ref[pl.ds(base, rows), :], wo_ref[...]).astype(low)

        for part in range(MB):
            here = pl.ds(part * MB_TOK, MB_TOK)
            micro(pl.multiple_of(base + part * MB_TOK, MB_TOK), here, owner * MB + part)

    def micro(first, here, number):
        spot = pl.ds(first, MB_TOK)
        cosine, sine = cos_ref[spot, :], sin_ref[spot, :]
        allowed = twice(mask_ref[number]) > 0.5
        keys, values = kk_ref[spot, :], vv_ref[spot, :]
        logs = lse_ref[spot, :]
        queries = sides(stacked(q_ref, spot).astype(jnp.float32) * scale)
        branches = sides(stacked(do_ref, here).astype(jnp.float32))
        probs_low, scores_back = [], []
        for side in range(2):
            log_total = jnp.concatenate(
                [logs[:, side : side + 1], logs[:, 2 + side : 3 + side]], axis=0
            )
            scores = jnp.where(allowed, contract_last(queries[side], keys), MASKED)
            probs = jnp.exp(scores - log_total)
            probs_grad = contract_last(branches[side], values)
            spread = jnp.sum(probs * probs_grad, axis=-1, keepdims=True)
            scores_back.append((probs * (probs_grad - spread)).astype(low))
            probs_low.append(probs.astype(low))
        wide_keys = jnp.concatenate(sides(keys.astype(jnp.float32)), axis=0)
        query_grad = product(jnp.concatenate(scores_back, axis=1), wide_keys) * scale
        key_grad = column_product(
            jnp.concatenate(scores_back, axis=0), jnp.concatenate(queries, axis=0)
        )
        value_grad = column_product(
            jnp.concatenate(probs_low, axis=0), jnp.concatenate(branches, axis=0)
        )
        raw = stacked(proj_ref, spot)
        grad = through_norm(query_grad, twice(cosine), twice(sine), raw, gain_ref[0:1, :], 0)
        dproj_ref[spot, :pair_width] = grad[:MB_TOK].astype(low)
        dproj_ref[spot, pair_width : 2 * pair_width] = grad[MB_TOK:].astype(low)
        kv = proj_ref[spot, 2 * pair_width : 3 * pair_width]
        raw = jnp.where(first_head, kv, pltpu.roll(kv, HD, 1))
        key_grad = key_grad + pltpu.roll(key_grad, HD, 1)
        value_grad = value_grad + pltpu.roll(value_grad, HD, 1)
        grad = through_norm(key_grad, cosine, sine, raw, gain_ref[1:2, :], 1)
        both = jnp.where(first_head, grad, value_grad).astype(low)
        dproj_ref[spot, 2 * pair_width : 3 * pair_width] = both

    wide, q_width = dproj_ref.shape[1], o_ref.shape[1]

    def out_grad():
        @pl.loop(0, width // TILE)
        def _(step):
            columns = pl.ds(pl.multiple_of(step * TILE, TILE), TILE)
            part = column_product(o_ref[...], all_ref[:, columns]).astype(low)
            for first in range(0, TILE, q_width):
                spot = pl.ds(pl.multiple_of(step * TILE + first, q_width), q_width)
                grad_ref[spot, wide:] = part[:, first : first + q_width]

    def qkv_grad():
        fetch.wait()

        @pl.loop(0, width // TILE)
        def _(step):
            columns = pl.ds(pl.multiple_of(step * TILE, TILE), TILE)
            part = column_product(dproj_ref[...], normed_ref[:, columns])
            grad_ref[columns, :wide] = jnp.transpose(part).astype(low)

    gather = Gather(x_ref, all_ref, gather_send, gather_recv)
    scatter = Scatter(out_ref, block_product((dproj_ref,), (wqkv_ref,), rows, width, True), refs)
    pass_through(
        ready, gather, scatter, lambda owners: each_owner(owners, rows, one), (out_grad, qkv_grad)
    )


def attend(own_rows, own_qkv, own_out, tables, number):
    rows, width = own_rows.shape
    count, wide, q_width = PLANE * rows, own_qkv.shape[1], own_out.shape[0]
    low = jnp.bfloat16
    arrays = (own_rows, own_qkv, own_out, *tables)
    places = tuple(range(1, len(arrays)))
    specs, stage = staged_specs(arrays, places)
    return pl.pallas_call(
        staged(attend_kernel, len(arrays), places),
        out_shape=[
            jax.ShapeDtypeStruct((rows, width), jnp.float32),
            jax.ShapeDtypeStruct((count, width), low),
            jax.ShapeDtypeStruct((count, wide), jnp.float32),
            jax.ShapeDtypeStruct((count, q_width), low),
            jax.ShapeDtypeStruct((count, 2 * HD), low),
            jax.ShapeDtypeStruct((count, 2 * HD), low),
            jax.ShapeDtypeStruct((count, q_width), low),
            jax.ShapeDtypeStruct((count, 2 * HD), jnp.float32),
        ],
        in_specs=specs,
        out_specs=[VMEM, ANY] + [VMEM] * 6,
        scratch_shapes=[pltpu.VMEM((count, width), low), pltpu.SemaphoreType.DMA]
        + gather_scratch()
        + scatter_scratch(rows, width)
        + stage,
        compiler_params=pltpu.CompilerParams(
            collective_id=number, has_side_effects=True, vmem_limit_bytes=56 * 2**20
        ),
        cost_estimate=SHORT,
        name=f"attend_{number}",
    )(*arrays)


def attend_back(own_rows, own_qkv, own_out, tables, kept, number):
    rows, width = own_rows.shape
    count, wide, q_width = PLANE * rows, own_qkv.shape[1], own_out.shape[0]
    low = jnp.bfloat16
    normed_all, proj, query, keys, values, attended, log_totals = kept
    arrays = (
        own_rows,
        own_qkv,
        own_out,
        *tables,
        proj,
        query,
        keys,
        values,
        attended,
        log_totals,
        normed_all,
    )
    places = tuple(range(1, len(arrays) - 1))
    specs, stage = staged_specs(arrays[:-1], places)
    return pl.pallas_call(
        staged(attend_back_kernel, len(arrays), places),
        out_shape=[
            jax.ShapeDtypeStruct((rows, width), jnp.float32),
            jax.ShapeDtypeStruct((width, wide + q_width), low),
            jax.ShapeDtypeStruct((8, 2 * HD), jnp.float32),
        ],
        in_specs=specs + [ANY],
        out_specs=[VMEM] * 3,
        scratch_shapes=[
            pltpu.VMEM((count, width), low),
            pltpu.VMEM((count, width), low),
            pltpu.VMEM((rows, q_width), low),
            pltpu.VMEM((count, wide), low),
            pltpu.SemaphoreType.DMA,
        ]
        + gather_scratch()
        + scatter_scratch(rows, width)
        + stage,
        compiler_params=pltpu.CompilerParams(
            collective_id=number, has_side_effects=True, vmem_limit_bytes=58 * 2**20
        ),
        cost_estimate=SHORT,
        name=f"attend_back_{number}",
    )(*arrays)


def product_scatter(left_sides, right_sides, number, turned=False):
    width = right_sides[0].shape[0] if turned else right_sides[0].shape[1]
    rows = left_sides[0].shape[0] // PLANE
    return pl.pallas_call(
        functools.partial(scatter_kernel, turned, len(left_sides)),
        out_shape=jax.ShapeDtypeStruct((rows, width), jnp.float32),
        in_specs=[ANY] * (2 * len(left_sides)),
        out_specs=VMEM,
        scratch_shapes=[pltpu.VMEM(side.shape, side.dtype) for side in left_sides + right_sides]
        + [
            pltpu.SemaphoreType.DMA((len(left_sides), PLANE)),
            pltpu.SemaphoreType.DMA((len(left_sides),)),
        ]
        + scatter_scratch(rows, width),
        compiler_params=pltpu.CompilerParams(
            collective_id=number, has_side_effects=True, vmem_limit_bytes=56 * 2**20
        ),
        cost_estimate=SHORT,
        name=f"product_scatter_{number}",
    )(*left_sides, *right_sides)


def start_kernel(
    nd,
    qkv_ref,
    out_rows_ref,
    wide_hbm,
    df_ref,
    note_ref,
    own_qkv_ref,
    own_out_ref,
    half_a_ref,
    half_b_ref,
    df_all_ref,
    notes_ref,
    own_sem,
    gather_send,
    gather_recv,
    block_send,
    block_recv,
    note_send,
    note_recv,
    piece_send,
    piece_recv,
    line_send,
    line_recv,
    wide_full,
    wide_ref,
    wide_sem,
):
    me, line = lax.axis_index("fsdp"), lax.axis_index("dp")
    others = plane_others(me)
    count = qkv_ref.shape[1]
    half_width = half_a_ref.shape[2] // 2
    hidden = 2 * half_width
    whole = hidden * PLANE
    fetch = pltpu.make_async_copy(wide_hbm, wide_full, wide_sem)
    fetch.start()
    gather = Gather(df_ref, df_all_ref, gather_send, gather_recv)
    greet_line(nd, others)

    def line_spot(array, owner):
        rows = pl.ds(pl.multiple_of(owner * count, count), count)
        if array == 1:
            return own_out_ref.at[rows]
        return own_qkv_ref.at[pl.ds(array // 2 * (PLANE // 2), PLANE // 2), rows]

    def along(array, owner, side, source=None):
        spot = line_spot(array, owner)
        return pltpu.make_async_remote_copy(
            src_ref=spot if source is None else source,
            dst_ref=spot,
            send_sem=line_send.at[array, side, owner],
            recv_sem=line_recv.at[array, owner],
            device_id={"dp": line + 1 if side == 0 else line - 1},
            device_id_type=MESH,
        )

    def send_own(array, source=None):
        @pl.when(line < nd - 1)
        def _():
            along(array, line, 0, source).start()

        @pl.when(line > 0)
        def _():
            along(array, line, 1, source).start()

    def line_step(array, step):
        @pl.when(line >= step)
        def _():
            along(array, line - step, 0).wait_recv()

            @pl.when(line < nd - 1)
            def _():
                along(array, line - step, 0).start()

        @pl.when(line + step < nd)
        def _():
            along(array, line + step, 1).wait_recv()

            @pl.when(line > 0)
            def _():
                along(array, line + step, 1).start()

    def put_block(number):
        other = others[number - 1]
        return pltpu.make_async_remote_copy(
            src_ref=qkv_ref.at[other],
            dst_ref=own_qkv_ref.at[me, pl.ds(pl.multiple_of(line * count, count), count)],
            send_sem=block_send.at[number],
            recv_sem=block_recv.at[number],
            device_id={"fsdp": other},
            device_id_type=MESH,
        )

    def put_note(number):
        return pltpu.make_async_remote_copy(
            src_ref=note_ref,
            dst_ref=notes_ref.at[me],
            send_sem=note_send.at[number],
            recv_sem=note_recv.at[number],
            device_id={"fsdp": others[number - 1]},
            device_id_type=MESH,
        )

    def pieces(other):
        for half, half_ref in enumerate((half_a_ref, half_b_ref)):
            for side in range(2):
                first = side * whole + other * hidden + half * half_width
                source = wide_ref.at[:, pl.ds(pl.multiple_of(first, 128), half_width)]
                yield source, half_ref.at[me, :, pl.ds(side * half_width, half_width)]

    def put_pieces(number):
        return [
            pltpu.make_async_remote_copy(
                src_ref=source,
                dst_ref=target,
                send_sem=piece_send.at[4 * number + index],
                recv_sem=piece_recv.at[4 * number + index],
                device_id={"fsdp": others[number - 1]},
                device_id_type=MESH,
            )
            for index, (source, target) in enumerate(pieces(others[number - 1]))
        ]

    own_block = own_qkv_ref.at[me, pl.ds(pl.multiple_of(line * count, count), count)]
    rows = df_ref.shape[0]

    def local(index, source, target):
        return pltpu.make_async_copy(source, target, own_sem.at[index])

    keep = [
        local(0, qkv_ref.at[me], own_block),
        local(1, out_rows_ref, line_spot(1, line)),
        local(2, note_ref, notes_ref.at[me]),
        local(3, df_ref, df_all_ref.at[pl.ds(pl.multiple_of(me * rows, rows), rows)]),
    ]
    keep_pieces = [
        local(4 + index, source, target) for index, (source, target) in enumerate(pieces(me))
    ]
    order = (6, 7, 2, 4, 3, 5, 1)
    for number in order:
        put_block(number).start()
        put_note(number).start()
    keep[0].start()
    send_own(1, out_rows_ref)
    gather.begin()
    for copy in keep[1:]:
        copy.start()
    for number in order:
        put_block(number).wait_recv()
    keep[0].wait()
    send_own(0)
    send_own(2)
    fetch.wait()

    @pl.loop(0, wide_full.shape[1] // TILE)
    def _(step):
        columns = pl.ds(pl.multiple_of(step * TILE, TILE), TILE)
        wide_ref[:, columns] = wide_full[:, columns].astype(wide_ref.dtype)

    for steps, slots in (
        ((), (0, 2)),
        (((1, 1),), (4, 1, 3)),
        (((0, 1), (2, 1)), (5, 6)),
        (((1, 2),), ()),
        (((0, 2), (2, 2)), (7, 9, 8, 10)),
        (((1, 3), (0, 3), (2, 3)), (11, 12)),
    ):
        for array, step in steps:
            if step < nd:
                line_step(array, step)
        for slot in slots:
            gather.take(slot)
        if slots == (5, 6):
            for number in order:
                for copy in put_pieces(number):
                    copy.start()
            for copy in keep_pieces:
                copy.start()
    for step in range(4, nd):
        for array in (1, 0, 2):
            line_step(array, step)
    for number in order:
        put_block(number).wait_send()
        put_note(number).wait()
        for copy in put_pieces(number):
            copy.wait()
    gather.finish()
    for copy in keep[1:] + keep_pieces:
        copy.wait()
    for array in (1, 0, 2):
        source = out_rows_ref if array == 1 else None

        @pl.when(line < nd - 1)
        def _():
            along(array, line, 0, source).wait_send()

        @pl.when(line > 0)
        def _():
            along(array, line, 1, source).wait_send()

        for step in range(1, nd):

            @pl.when(jnp.logical_and(line >= step, line < nd - 1))
            def _():
                along(array, line - step, 0).wait_send()

            @pl.when(jnp.logical_and(line + step < nd, line > 0))
            def _():
                along(array, line + step, 1).wait_send()


def start(qkv_blocks, out_rows, wide_rows, df_own, note, number):
    nd = lax.axis_size("dp")
    count, whole = wide_rows.shape
    half = whole // 4 // PLANE
    low = jnp.bfloat16
    return pl.pallas_call(
        functools.partial(start_kernel, nd),
        out_shape=[
            jax.ShapeDtypeStruct((PLANE, nd * count, qkv_blocks.shape[2]), low),
            jax.ShapeDtypeStruct((nd * count, out_rows.shape[1]), low),
            jax.ShapeDtypeStruct((PLANE, count, 2 * half), low),
            jax.ShapeDtypeStruct((PLANE, count, 2 * half), low),
            jax.ShapeDtypeStruct((PLANE * df_own.shape[0], df_own.shape[1]), low),
            jax.ShapeDtypeStruct((PLANE,) + note.shape, note.dtype),
        ],
        in_specs=[ANY] * 5,
        out_specs=[ANY] * 6,
        scratch_shapes=[pltpu.SemaphoreType.DMA((8,))]
        + gather_scratch()
        + [pltpu.SemaphoreType.DMA((PLANE,))] * 4
        + [pltpu.SemaphoreType.DMA((4 * PLANE,))] * 2
        + [pltpu.SemaphoreType.DMA((3, 2, nd)), pltpu.SemaphoreType.DMA((3, nd))]
        + [
            pltpu.VMEM(wide_rows.shape, wide_rows.dtype),
            pltpu.VMEM(wide_rows.shape, low),
            pltpu.SemaphoreType.DMA,
        ],
        compiler_params=pltpu.CompilerParams(
            collective_id=number, has_side_effects=True, vmem_limit_bytes=56 * 2**20
        ),
        cost_estimate=SHORT,
        name=f"start_{number}",
    )(qkv_blocks, out_rows, wide_rows, df_own, note)


def glu_block(
    rows_ref, df_ref, wgu, wd, act_ref, dgu_ref, down_sum, wide_sum, results=None
):
    half = wd.shape[0]
    count, width = rows_ref.shape

    @pl.loop(0, count // 256)
    def _(step):
        spot = pl.ds(pl.multiple_of(step * 256, 256), 256)
        for first in range(0, half, GLU_TILE):
            units = slice(first, first + GLU_TILE)
            up_units = slice(half + first, half + first + GLU_TILE)
            gate = product(rows_ref[spot, :], wgu[:, units])
            up = product(rows_ref[spot, :], wgu[:, up_units])
            back = contract_last(df_ref[spot, :], wd[units, :])
            sigmoid = jax.nn.sigmoid(gate)
            silu = gate * sigmoid
            act_ref[spot, units] = (silu * up).astype(jnp.bfloat16)
            gate_back = back * up * sigmoid * (1.0 + gate * (1.0 - sigmoid))
            dgu_ref[spot, units] = gate_back.astype(jnp.bfloat16)
            dgu_ref[spot, up_units] = (back * silu).astype(jnp.bfloat16)

    @pl.loop(0, width // TILE)
    def _(step):
        columns = pl.ds(pl.multiple_of(step * TILE, TILE), TILE)
        down = column_product(act_ref[...], df_ref[:, columns])
        wide = column_product(rows_ref[:, columns], dgu_ref[...])
        if results is None:
            down_sum[:, columns] += down
            wide_sum[columns, :] += wide
        else:
            down_ref, wide_ref = results
            down_ref[:, columns] = (down_sum[:, columns] + down).astype(down_ref.dtype)
            wide_ref[columns, :] = (wide_sum[columns, :] + wide).astype(wide_ref.dtype)


def gather_glu_kernel(
    x_ref,
    wgu_hbm,
    wd_hbm,
    df_hbm,
    all_out_ref,
    act_ref,
    dgu_ref,
    down_ref,
    wide_ref,
    all_ref,
    wgu_ref,
    wd_ref,
    df_ref,
    down_sum,
    wide_sum,
    in_sem,
    out_sem,
    gather_send,
    gather_recv,
):
    rows = x_ref.shape[0]
    half = wd_ref.shape[0]
    fetch = [
        pltpu.make_async_copy(wgu_hbm, wgu_ref, in_sem.at[0]),
        pltpu.make_async_copy(wd_hbm.at[pl.ds(0, half)], wd_ref, in_sem.at[1]),
        pltpu.make_async_copy(df_hbm, df_ref, in_sem.at[2]),
    ]
    for copy in fetch:
        copy.start()
    gather = Gather(x_ref, all_ref, gather_send, gather_recv)
    me, x_next, y_next = gather.me, gather.x_next, gather.y_next
    greet((gather.sibling, x_next, y_next))
    gather.begin()
    all_ref[pl.ds(pl.multiple_of(me * rows, rows), rows), :] = x_ref[...]
    down_sum[...] = jnp.zeros_like(down_sum)
    wide_sum[...] = jnp.zeros_like(wide_sum)
    for copy in fetch:
        copy.wait()

    def work(owner, results=None):
        first = owner - lax.rem(owner, 2)
        spot = pl.ds(pl.multiple_of(first * rows, 2 * rows), 2 * rows)
        glu_block(
            all_ref.at[spot],
            df_ref.at[spot],
            wgu_ref,
            wd_ref,
            act_ref.at[spot],
            dgu_ref.at[spot],
            down_sum,
            wide_sum,
            results,
        )

    gather.take(4)
    work(me)
    for slot in (0, 2, 1, 3, 7, 8):
        gather.take(slot)
    work(x_next)
    for slot in (5, 6, 9, 10):
        gather.take(slot)
    work(y_next)
    gather.take(11)
    gather.take(12)
    keep = pltpu.make_async_copy(all_ref, all_out_ref, out_sem)
    keep.start()
    work(gather.diagonal, (down_ref, wide_ref))
    gather.finish()
    keep.wait()


def gather_glu(own_rows, wgu, own_down, df_all, number):
    rows, width = own_rows.shape
    count, half = PLANE * rows, wgu.shape[1] // 2
    low = jnp.bfloat16
    return pl.pallas_call(
        gather_glu_kernel,
        out_shape=[
            jax.ShapeDtypeStruct((count, width), low),
            jax.ShapeDtypeStruct((count, half), low),
            jax.ShapeDtypeStruct((count, 2 * half), low),
            jax.ShapeDtypeStruct((half, width), low),
            jax.ShapeDtypeStruct((width, 2 * half), low),
        ],
        in_specs=[VMEM, ANY, ANY, ANY],
        out_specs=[ANY] + [VMEM] * 4,
        scratch_shapes=[
            pltpu.VMEM((count, width), low),
            pltpu.VMEM(wgu.shape, low),
            pltpu.VMEM((half, width), low),
            pltpu.VMEM((count, width), low),
            pltpu.VMEM((half, width), jnp.float32),
            pltpu.VMEM((width, 2 * half), jnp.float32),
            pltpu.SemaphoreType.DMA((3,)),
            pltpu.SemaphoreType.DMA,
        ]
        + gather_scratch(),
        compiler_params=pltpu.CompilerParams(
            collective_id=number, has_side_effects=True, vmem_limit_bytes=58 * 2**20
        ),
        cost_estimate=SHORT,
        name=f"gather_glu_{number}",
    )(own_rows, wgu, own_down, df_all)


def glu_kernel(
    x_ref, df_ref, wgu_ref, wd_ref, first_ref, act_ref, dgu_ref, grad_ref, down_sum, wide_sum
):
    step = pl.program_id(0)
    half = wd_ref.shape[0]

    @pl.when(step == 0)
    def _():
        down_sum[...] = jnp.zeros_like(down_sum)
        wide_sum[...] = jnp.zeros_like(wide_sum)

    glu_block(
        x_ref, df_ref, wgu_ref, wd_ref, act_ref, dgu_ref, down_sum, wide_sum
    )

    @pl.when(step == pl.num_programs(0) - 1)
    def _():
        nd, _, both = grad_ref.shape
        count, units = wide_sum.shape[0] // PLANE // nd, 2 * half // nd
        low = grad_ref.dtype
        for owner in range(nd):
            for place in range(PLANE):
                first = (place * nd + owner) * count
                part = wide_sum[first : first + count, :].astype(low)
                grad_ref[owner, place * count : (place + 1) * count, :] = part
            source, first = first_ref, owner * units
            if first >= half:
                source, first = down_sum, first - half
            for side in range(2):
                part = source[first : first + units, side * both : (side + 1) * both].astype(low)
                start = PLANE * count + side * units
                grad_ref[owner, start : start + units, :] = part


def glu(rows_all, df_all, wgu, own_down, down_first, number):
    nd = lax.axis_size("dp")
    count, width = rows_all.shape
    half = wgu.shape[1] // 2
    low = jnp.bfloat16
    step = 512
    once = pl.Buffered(1)
    return pl.pallas_call(
        glu_kernel,
        grid=(count // step,),
        out_shape=[
            jax.ShapeDtypeStruct((count, half), low),
            jax.ShapeDtypeStruct((count, 2 * half), low),
            jax.ShapeDtypeStruct((nd, 2 * width // nd, 2 * half), low),
        ],
        in_specs=[
            pl.BlockSpec((step, width), lambda i: (i, 0)),
            pl.BlockSpec((step, width), lambda i: (i, 0)),
            pl.BlockSpec((width, 2 * half), lambda i: (0, 0), pipeline_mode=once),
            pl.BlockSpec((half, width), lambda i: (1, 0), pipeline_mode=once),
            pl.BlockSpec((half, width), lambda i: (0, 0), pipeline_mode=once),
        ],
        out_specs=[
            pl.BlockSpec((step, half), lambda i: (i, 0)),
            pl.BlockSpec((step, 2 * half), lambda i: (i, 0)),
            pl.BlockSpec(
                (nd, 2 * width // nd, 2 * half), lambda i: (0, 0, 0), pipeline_mode=once
            ),
        ],
        scratch_shapes=[
            pltpu.VMEM((half, width), jnp.float32),
            pltpu.VMEM((width, 2 * half), jnp.float32),
        ],
        compiler_params=pltpu.CompilerParams(vmem_limit_bytes=56 * 2**20),
        cost_estimate=SHORT,
        name=f"glu_{number}",
    )(rows_all, df_all, wgu, own_down, down_first)


def attention(normed_low, own_qkv, own_out, lengths_all, query_gain, key_gain):
    position, _, allowed = layout(lengths_all)
    half_width = HD // 2
    frequency = ROPE_BASE ** (jnp.arange(half_width, dtype=jnp.float32) * (-2.0 / HD))
    angles = position.reshape(-1, 1) * frequency[None, :]
    tables = (
        jnp.tile(jnp.cos(angles), (1, 4)),
        jnp.tile(jnp.sin(angles), (1, 4)),
        allowed.astype(jnp.float32),
        jnp.pad(
            jnp.stack([jnp.tile(query_gain, 2), jnp.tile(key_gain, 2)]), ((0, 6), (0, 0))
        ),
    )
    sums, *kept = attend(normed_low, own_qkv, own_out, tables, 3)

    def back(branch_own):
        normed_one_grad, part_attn, gain_grads = attend_back(
            branch_own, own_qkv, own_out, tables, kept, 9
        )
        query_gain_grad = gain_grads[0, :HD] + gain_grads[0, HD:]
        return normed_one_grad, part_attn, query_gain_grad, gain_grads[1, :HD]

    return sums, back


def last_kernel(
    ready,
    hidden_ref,
    valid_ref,
    act_a_ref,
    act_b_ref,
    wd_ref,
    half_ref,
    out_ref,
    wide_ref,
    sum_ref,
    own_sem,
    sems,
    *refs,
):
    others = plane_others(lax.axis_index("fsdp"))
    rows, width = out_ref.shape
    half_rows = wd_ref.shape[0] // 2
    block = block_product(
        (act_a_ref, act_b_ref),
        (wd_ref.at[pl.ds(0, half_rows)], wd_ref.at[pl.ds(half_rows, half_rows)]),
        rows,
        width,
        False,
    )
    scatter = Scatter(sum_ref, block, refs)
    greet(others)
    order = (6, 7, 2, 4, 3, 5, 1)
    for number in order:
        for copy in put_half(half_ref, wide_ref, others, number, sems):
            copy.start()
    keep = keep_half(half_ref, wide_ref, own_sem)
    for copy in keep:
        copy.start()
    ready()
    scatter.for_sibling(0)
    scatter.for_sibling(1)
    scatter.for_far()
    scatter.for_sibling(2)
    scatter.for_near(0)
    scatter.for_sibling(3)
    scatter.for_near(1)
    scatter.finish_near(0)
    scatter.finish_near(1)
    scatter.own()
    scatter.finish()
    out_ref[...] = (hidden_ref[...] + valid_ref[...] * sum_ref[...]).astype(out_ref.dtype)
    for number in order:
        for copy in put_half(half_ref, wide_ref, others, number, sems):
            copy.wait()
    for copy in keep:
        copy.wait()


def last(hidden, valid_col, act_a, act_b, own_down, half, count, number):
    rows, width = hidden.shape
    arrays = (hidden, valid_col, act_a, act_b, own_down)
    places = (0, 2, 3, 4)
    specs, stage = staged_specs(arrays, places)
    return pl.pallas_call(
        staged(last_kernel, len(arrays) + 1, places),
        out_shape=[
            jax.ShapeDtypeStruct((rows, width), jnp.bfloat16),
            jax.ShapeDtypeStruct((count, half.shape[1] * PLANE), half.dtype),
        ],
        in_specs=specs + [ANY],
        out_specs=[VMEM, ANY],
        scratch_shapes=[pltpu.VMEM((rows, width), jnp.float32)]
        + half_scratch()
        + scatter_scratch(rows, width)
        + stage,
        compiler_params=pltpu.CompilerParams(
            collective_id=number, has_side_effects=True, vmem_limit_bytes=56 * 2**20
        ),
        cost_estimate=SHORT,
        name=f"last_{number}",
    )(*arrays, half)


def adam_kernel(chunks, n_grads, per, norm_ref, *refs):
    grads, refs = refs[:n_grads], refs[n_grads:]
    states = [refs[place * per : (place + 1) * per] for place in range(3)]
    outs = [refs[(3 + place) * per : (4 + place) * per] for place in range(3)]
    refs = refs[6 * per :]
    grad_bufs, refs = refs[:n_grads], refs[n_grads:]
    bufs = [refs[place * per : (place + 1) * per] for place in range(3)]
    grad_sems, in_sems, out_sems = refs[3 * per :]
    factor = norm_ref[1:2, 0:1]
    first_scale = 1.0 / (1.0 - FIRST_DECAY**STEP)
    second_scale = 1.0 / (1.0 - SECOND_DECAY**STEP)

    def fetch(number):
        which, rows, sources, _ = chunks[number]
        copies = [
            pltpu.make_async_copy(
                grads[array].at[spot], grad_bufs[array].at[spot], grad_sems.at[number, place]
            )
            for place, (array, spot) in enumerate(sources)
        ]
        for place in range(3):
            copies.append(
                pltpu.make_async_copy(
                    states[place][which].at[rows],
                    bufs[place][which].at[rows],
                    in_sems.at[number, place],
                )
            )
        return copies

    def put(number):
        which, rows, _, _ = chunks[number]
        return [
            pltpu.make_async_copy(
                bufs[place][which].at[rows], outs[place][which].at[rows], out_sems.at[number, place]
            )
            for place in range(3)
        ]

    def update(which, rows, columns, grad):
        weights, firsts, seconds = (bufs[place][which] for place in range(3))
        clipped = grad.astype(jnp.float32) * factor
        weight = weights[rows, columns]
        first = FIRST_DECAY * firsts[rows, columns] + (1.0 - FIRST_DECAY) * clipped
        second = SECOND_DECAY * seconds[rows, columns] + (1.0 - SECOND_DECAY) * clipped * clipped
        root = jnp.sqrt(second * second_scale) + ADAM_EPSILON
        change = first * first_scale / root + WEIGHT_DECAY * weight
        weights[rows, columns] = weight - LEARN_RATE * change
        firsts[rows, columns] = first
        seconds[rows, columns] = second

    for number in range(len(chunks)):
        for copy in fetch(number):
            copy.start()
    for number in range(len(chunks)):
        which, rows, _, loops = chunks[number]
        for copy in fetch(number):
            copy.wait()
        for array, grad_rows, steps, columns_of, grad_columns_of, width in loops:

            @pl.loop(0, steps)
            def _(step):
                columns = pl.ds(pl.multiple_of(columns_of(step), 128), width)
                grad_columns = pl.ds(pl.multiple_of(grad_columns_of(step), 128), width)
                update(which, rows, columns, grad_bufs[array][grad_rows, grad_columns])

        for copy in put(number):
            copy.start()
    for number in range(len(chunks)):
        for copy in put(number):
            copy.wait()


def adam_matrices(norm, grad_qkv, grad_out, grad_a, grad_b, sums_b, weights, firsts, seconds):
    half = grad_a.shape[1] // 2 // PLANE
    whole = weights[2].shape[1] // 2
    count = weights[3].shape[0]
    behind = sums_b.shape[0] - 2 * count
    side_width = sums_b.shape[1]
    width = 512
    chunks = []

    def straight(step):
        return step * width

    for row in range(0, weights[2].shape[0], 16):
        rows = pl.ds(row, 16)
        loops = []
        for part in range(2):

            def columns_of(step, part=part):
                side, unit = lax.div(step, PLANE), lax.rem(step, PLANE)
                return side * whole + unit * 2 * half + part * half

            loops.append((2 + part, rows, 2 * PLANE, columns_of, lambda step: step * half, half))
        chunks.append((2, rows, [(2, rows), (3, rows)], loops))
    for row in range(0, count, 64):
        sources, loops = [], []
        for side in range(2):
            spot = pl.ds(behind + side * count + row, 64)
            sources.append((4, spot))

            def columns_of(step, side=side):
                return side * side_width + step * width

            loops.append((4, spot, side_width // width, columns_of, straight, width))
        chunks.append((3, pl.ds(row, 64), sources, loops))
    for which in range(2):
        for row in range(0, weights[which].shape[0], 32):
            rows = pl.ds(row, 32)
            steps = weights[which].shape[1] // width
            loops = [(which, rows, steps, straight, straight, width)]
            chunks.append((which, rows, [(which, rows)], loops))
    grads = (grad_qkv, grad_out, grad_a, grad_b, sums_b)
    per = len(weights)
    number = len(chunks)
    outs = pl.pallas_call(
        functools.partial(adam_kernel, chunks, len(grads), per),
        out_shape=[jax.ShapeDtypeStruct(weight.shape, jnp.float32) for weight in weights] * 3,
        in_specs=[VMEM] + [ANY] * (len(grads) + 3 * per),
        out_specs=[ANY] * (3 * per),
        scratch_shapes=[pltpu.VMEM(grad.shape, grad.dtype) for grad in grads]
        + [pltpu.VMEM(weight.shape, jnp.float32) for weight in weights] * 3
        + [
            pltpu.SemaphoreType.DMA((number, 2)),
            pltpu.SemaphoreType.DMA((number, 3)),
            pltpu.SemaphoreType.DMA((number, 3)),
        ],
        compiler_params=pltpu.CompilerParams(vmem_limit_bytes=60 * 2**20),
        name="adam_matrices",
    )(norm, *grads, *weights, *firsts, *seconds)
    return outs[:per], outs[per : 2 * per], outs[2 * per :]


def scatter_rows(values, axis):
    return lax.psum_scatter(values, "dp", scatter_dimension=axis, tiled=True)


def per_device_plane(
    nf,
    nd,
    tokens,
    cotangent,
    order,
    lengths,
    w_qkv,
    w_out,
    w_gate_up,
    w_down,
    gains,
    first_qkv,
    first_out,
    first_gate_up,
    first_down,
    first_gains,
    second_qkv,
    second_out,
    second_gate_up,
    second_down,
    second_gains,
):
    low = jnp.bfloat16
    q_width = HEADS // nf * HD
    kv_all = KVH * HD
    hidden_own = FF // nf
    rows_own = w_qkv.shape[0]

    order_row = order[0]
    places = jnp.arange(TOK_DEV, dtype=jnp.int32)
    inverse = jnp.zeros((TOK_DEV,), jnp.int32).at[order_row].set(places)
    rows_in = tokens[order_row].astype(jnp.float32)
    back_rows = cotangent[order_row].astype(jnp.float32)
    attn_gain = gains[:D]
    ffn_gain = gains[D : 2 * D]
    query_gain = gains[2 * D : 2 * D + HD]
    key_gain = gains[2 * D + HD :]

    _, valid_rows, _ = layout(lengths)
    valid_col = valid_rows.reshape(TOK_DEV, 1)

    qkv_low = w_qkv.astype(low)

    def head_blocks(rows, width):
        return jnp.swapaxes(rows.reshape(rows_own, -1, width), 0, 1)

    qkv_blocks = jnp.concatenate(
        [
            head_blocks(qkv_low[:, :D], q_width),
            head_blocks(qkv_low[:, D : D + kv_all], HD),
            head_blocks(qkv_low[:, D + kv_all :], HD),
        ],
        axis=2,
    )
    wide = q_width + 2 * HD
    own_down = lax.all_gather(w_down.astype(low), "dp", axis=0, tiled=True)
    own_qkv, own_out, half_a, half_b, down_back, notes = start(
        qkv_blocks,
        w_out.astype(low),
        w_gate_up,
        (valid_col * back_rows).astype(low),
        jnp.pad(lengths, ((0, 8 - MB), (0, 128 - SEQS))),
        1,
    )
    own_qkv = own_qkv.reshape(D, wide)
    lengths_all = notes[:, :MB, :SEQS].reshape(nf * MB, SEQS)
    half_a, own_down = lax.optimization_barrier((half_a, own_down))
    own_a = lax.all_gather(half_a, "dp", axis=1, tiled=True).reshape(D, hidden_own)
    own_b = lax.all_gather(half_b, "dp", axis=1, tiled=True).reshape(D, hidden_own)

    normed_one, norm_one_pull = jax.vjp(rms_norm, rows_in, attn_gain)
    attention_sums, attention_back = attention(
        normed_one.astype(low), own_qkv, own_out, lengths_all, query_gain, key_gain
    )
    hidden = rows_in + valid_col * attention_sums

    normed_two, norm_two_pull = jax.vjp(rms_norm, hidden, ffn_gain)
    norm_two_all, act_a, back_a, down_a, part_a = gather_glu(
        normed_two.astype(low), own_a, own_down, down_back, 5
    )
    sums_a = scatter_rows(part_a.reshape(nf, nd * rows_own, hidden_own), 1)
    act_b, back_b, part_b = glu(norm_two_all, down_back, own_b, own_down, down_a, 6)
    sums_b = scatter_rows(part_b, 0)[0]
    normed_two_grad = product_scatter((back_a, back_b), (own_a, own_b), 8, turned=True)
    hidden_norm_grad, ffn_gain_grad = norm_two_pull(normed_two_grad)
    hidden_grad = back_rows + hidden_norm_grad

    branch_own = (valid_col * hidden_grad).astype(low)
    branch_own, sums_a = lax.optimization_barrier((branch_own, sums_a))
    normed_one_grad, part_attn, query_gain_grad, key_gain_grad = attention_back(branch_own)
    sums_attn = scatter_rows(part_attn.reshape(nf, nd * rows_own, wide + q_width), 1)
    normed_one_grad, act_a = lax.optimization_barrier((normed_one_grad, act_a))
    output, grad_a = last(
        hidden,
        valid_col,
        act_a,
        act_b,
        own_down,
        sums_a.reshape(nf * rows_own, hidden_own),
        rows_own,
        7,
    )
    output, sums_b = lax.optimization_barrier((output, sums_b))
    grad_b, squares_b = exchange_half(sums_b, rows_own, 11)
    rows_grad, attn_gain_grad = norm_one_pull(normed_one_grad)
    input_grad = (hidden_grad + rows_grad)[inverse]
    output_all = output[inverse]

    early_squares = jnp.sum(jnp.square(sums_a.astype(jnp.float32))) + jnp.sum(squares_b)
    input_grad, output_all, early_squares, sums_attn = lax.optimization_barrier(
        (input_grad, output_all, early_squares, sums_attn)
    )
    gain_sum = jnp.concatenate([attn_gain_grad, ffn_gain_grad, query_gain_grad, key_gain_grad])
    gain_total, norm, grad_qkv, grad_out = sum_everywhere(
        gain_sum, early_squares, sums_attn, wide, 13
    )
    global_norm, factor = norm[0, 0], norm[1, 0]
    new_matrices, next_firsts, next_seconds = adam_matrices(
        norm,
        grad_qkv,
        grad_out,
        grad_a,
        grad_b,
        sums_b,
        (w_qkv, w_out, w_gate_up, w_down),
        (first_qkv, first_out, first_gate_up, first_down),
        (second_qkv, second_out, second_gate_up, second_down),
    )
    new_gains, next_first_gains, next_second_gains = adam_step(
        gains, first_gains, second_gains, gain_total, factor, GAIN_RATE, 0.0
    )
    return (
        output_all,
        input_grad,
        global_norm,
        *new_matrices,
        new_gains,
        *next_firsts,
        next_first_gains,
        *next_seconds,
        next_second_gains,
    )


def gather_tokens(rows):
    return lax.all_gather(rows, "fsdp", axis=0, tiled=True)


def scatter_tokens(rows):
    return lax.psum_scatter(
        rows.astype(jnp.bfloat16), "fsdp", scatter_dimension=0, tiled=True
    ).astype(jnp.float32)


def swap(blocks):
    return lax.all_to_all(blocks, "fsdp", split_axis=0, concat_axis=0, tiled=True)


def per_device_plain(
    nf,
    nd,
    tokens,
    cotangent,
    order,
    lengths,
    w_qkv,
    w_out,
    w_gate_up,
    w_down,
    gains,
    first_qkv,
    first_out,
    first_gate_up,
    first_down,
    first_gains,
    second_qkv,
    second_out,
    second_gate_up,
    second_down,
    second_gains,
):
    low = jnp.bfloat16
    kvl = max(KVH // nf, 1)
    rep = max(nf // KVH, 1)
    heads_own = HEADS // nf
    group = heads_own // kvl
    q_width, kv_width = heads_own * HD, kvl * HD
    kv_all = KVH * HD
    hidden_own = FF // nf
    rows_own = w_qkv.shape[0]
    n_mb = nf * MB

    def head_blocks(rows, width):
        return jnp.swapaxes(rows.reshape(rows_own, -1, width), 0, 1)

    qkv_low = w_qkv.astype(low)
    qkv_blocks = jnp.concatenate(
        [
            head_blocks(qkv_low[:, :D], q_width),
            jnp.repeat(head_blocks(qkv_low[:, D : D + kv_all], kv_width), rep, axis=0),
            jnp.repeat(head_blocks(qkv_low[:, D + kv_all :], kv_width), rep, axis=0),
        ],
        axis=2,
    )
    wide = q_width + 2 * kv_width
    own_qkv = lax.all_gather(swap(qkv_blocks), "dp", axis=1, tiled=True).reshape(D, wide)
    own_out = lax.all_gather(w_out.astype(low), "dp", axis=0, tiled=True)
    gate_up_blocks = jnp.transpose(
        w_gate_up.astype(low).reshape(rows_own, 2, nf, hidden_own), (2, 0, 1, 3)
    ).reshape(nf, rows_own, 2 * hidden_own)
    own_gate_up = lax.all_gather(swap(gate_up_blocks), "dp", axis=1, tiled=True).reshape(
        D, 2 * hidden_own
    )
    own_down = lax.all_gather(w_down.astype(low), "dp", axis=0, tiled=True)

    order_row = order[0]
    places = jnp.arange(TOK_DEV, dtype=jnp.int32)
    inverse = jnp.zeros((TOK_DEV,), jnp.int32).at[order_row].set(places)
    rows_in = tokens[order_row].astype(jnp.float32)
    back_rows = cotangent[order_row].astype(jnp.float32)
    attn_gain = gains[:D]
    ffn_gain = gains[D : 2 * D]
    query_gain = gains[2 * D : 2 * D + HD]
    key_gain = gains[2 * D + HD :]
    score_scale = HD ** (-0.5)

    lengths_all = gather_tokens(lengths)
    position, _, allowed = layout(lengths_all)
    _, valid_rows, _ = layout(lengths)
    valid_col = valid_rows.reshape(TOK_DEV, 1)
    allowed = allowed[:, None, None]
    cosine_table, sine_table = rope_tables(position.reshape(-1))

    normed_one, norm_one_pull = jax.vjp(rms_norm, rows_in, attn_gain)
    norm_one_all = gather_tokens(normed_one.astype(low))
    projected = product(norm_one_all, own_qkv)
    n_rows = norm_one_all.shape[0]
    query_raw = projected[:, :q_width].reshape(n_rows, heads_own, HD)
    key_raw = projected[:, q_width : q_width + kv_width].reshape(n_rows, kvl, HD)
    values_low = projected[:, q_width + kv_width :].reshape(n_mb, MB_TOK, kvl, HD).astype(low)

    def turn_heads(query_in, key_in, query_scale, key_scale):
        return (
            rotate(rms_norm(query_in, query_scale), cosine_table, sine_table),
            rotate(rms_norm(key_in, key_scale), cosine_table, sine_table),
        )

    turned, turn_pull = jax.vjp(turn_heads, query_raw, key_raw, query_gain, key_gain)
    queries_low = turned[0].astype(low).reshape(n_mb, MB_TOK, kvl, group, HD)
    keys_low = turned[1].astype(low).reshape(n_mb, MB_TOK, kvl, HD)
    scores = (
        jnp.einsum("mtkgd,mukd->mkgtu", queries_low, keys_low, preferred_element_type=jnp.float32)
        * score_scale
    )
    scores = jnp.where(allowed, scores, MASKED)
    row_peak = jnp.max(scores, axis=-1, keepdims=True)
    powers = jnp.exp(scores - row_peak)
    totals = jnp.sum(powers, axis=-1, keepdims=True)
    probs = powers / totals
    probs_low = probs.astype(low)
    attended = jnp.einsum(
        "mkgtu,mukd->mtkgd", probs_low, values_low, preferred_element_type=jnp.float32
    )
    attended_low = attended.reshape(n_rows, q_width).astype(low)
    hidden = rows_in + valid_col * scatter_tokens(product(attended_low, own_out))

    normed_two, norm_two_pull = jax.vjp(rms_norm, hidden, ffn_gain)
    norm_two_all = gather_tokens(normed_two.astype(low))
    down_back = gather_tokens((valid_col * back_rows).astype(low))
    gate_up = product(norm_two_all, own_gate_up)
    activation, glu_pull = jax.vjp(swiglu, gate_up[:, :hidden_own], gate_up[:, hidden_own:])
    activation_low = activation.astype(low)
    output = hidden + valid_col * scatter_tokens(product(activation_low, own_down))
    gate_back, up_back = glu_pull(contract_last(down_back, own_down))
    gate_up_back = jnp.concatenate([gate_back.astype(low), up_back.astype(low)], axis=1)
    normed_two_grad = scatter_tokens(contract_last(gate_up_back, own_gate_up))
    grad_down = lax.psum_scatter(
        column_product(activation_low, down_back).astype(low),
        "dp",
        scatter_dimension=0,
        tiled=True,
    ).astype(jnp.float32)
    grad_gate_up = lax.psum_scatter(
        column_product(norm_two_all, gate_up_back)
        .astype(low)
        .reshape(nf, nd * rows_own, 2 * hidden_own),
        "dp",
        scatter_dimension=1,
        tiled=True,
    )
    grad_gate_up = jnp.transpose(
        swap(grad_gate_up).reshape(nf, rows_own, 2, hidden_own), (1, 2, 0, 3)
    ).reshape(rows_own, 2 * FF)
    grad_gate_up = grad_gate_up.astype(jnp.float32)
    hidden_norm_grad, ffn_gain_grad = norm_two_pull(normed_two_grad)
    hidden_grad = back_rows + hidden_norm_grad

    branch_back = gather_tokens((valid_col * hidden_grad).astype(low))
    attended_back = contract_last(branch_back, own_out).astype(low)
    grad_out = lax.psum_scatter(
        column_product(attended_low, branch_back).astype(low),
        "dp",
        scatter_dimension=0,
        tiled=True,
    ).astype(jnp.float32)
    attended_five = attended_back.reshape(n_mb, MB_TOK, kvl, group, HD)
    probs_grad = jnp.einsum(
        "mtkgd,mukd->mkgtu", attended_five, values_low, preferred_element_type=jnp.float32
    )
    spread = jnp.sum(probs * probs_grad, axis=-1, keepdims=True)
    score_back = (probs * (probs_grad - spread)).astype(low)
    query_grad = (
        jnp.einsum("mkgtu,mukd->mtkgd", score_back, keys_low, preferred_element_type=jnp.float32)
        * score_scale
    )
    key_grad = (
        jnp.einsum("mkgtu,mtkgd->mukd", score_back, queries_low, preferred_element_type=jnp.float32)
        * score_scale
    )
    value_grad = jnp.einsum(
        "mkgtu,mtkgd->mukd", probs_low, attended_five, preferred_element_type=jnp.float32
    )
    query_in_grad, key_in_grad, query_gain_grad, key_gain_grad = turn_pull(
        (query_grad.reshape(n_rows, heads_own, HD), key_grad.reshape(n_rows, kvl, HD))
    )
    projected_back = jnp.concatenate(
        [
            query_in_grad.reshape(n_rows, q_width),
            key_in_grad.reshape(n_rows, kv_width),
            value_grad.reshape(n_rows, kv_width),
        ],
        axis=1,
    ).astype(low)
    normed_one_grad = scatter_tokens(contract_last(projected_back, own_qkv))
    grad_qkv = lax.psum_scatter(
        column_product(norm_one_all, projected_back)
        .astype(low)
        .reshape(nf, nd * rows_own, wide),
        "dp",
        scatter_dimension=1,
        tiled=True,
    )
    grad_blocks = swap(grad_qkv).astype(jnp.float32)

    def head_rows(blocks, times):
        merged = jnp.sum(blocks.reshape(nf // times, times, rows_own, -1), axis=1)
        return jnp.swapaxes(merged, 0, 1).reshape(rows_own, -1)

    grad_qkv = jnp.concatenate(
        [
            head_rows(grad_blocks[:, :, :q_width], 1),
            head_rows(grad_blocks[:, :, q_width : q_width + kv_width], rep),
            head_rows(grad_blocks[:, :, q_width + kv_width :], rep),
        ],
        axis=1,
    )
    rows_grad, attn_gain_grad = norm_one_pull(normed_one_grad)
    input_grad = (hidden_grad + rows_grad)[inverse]
    output_all = output.astype(low)[inverse]

    owned = (grad_qkv, grad_out, grad_gate_up, grad_down)
    local_squares = (
        jnp.sum(owned[0] * owned[0])
        + jnp.sum(owned[1] * owned[1])
        + jnp.sum(owned[2] * owned[2])
        + jnp.sum(owned[3] * owned[3])
    )
    gain_sum = jnp.concatenate([attn_gain_grad, ffn_gain_grad, query_gain_grad, key_gain_grad])
    gain_total, square_total = lax.psum((gain_sum, local_squares), ("fsdp", "dp"))
    global_norm = jnp.sqrt(square_total + jnp.sum(gain_total * gain_total))
    factor = CLIP_NORM / jnp.maximum(global_norm, CLIP_NORM)
    new_qkv, next_first_qkv, next_second_qkv = adam_step(
        w_qkv, first_qkv, second_qkv, owned[0], factor, LEARN_RATE, WEIGHT_DECAY
    )
    new_out, next_first_out, next_second_out = adam_step(
        w_out, first_out, second_out, owned[1], factor, LEARN_RATE, WEIGHT_DECAY
    )
    new_gate_up, next_first_gate_up, next_second_gate_up = adam_step(
        w_gate_up, first_gate_up, second_gate_up, owned[2], factor, LEARN_RATE, WEIGHT_DECAY
    )
    new_down, next_first_down, next_second_down = adam_step(
        w_down, first_down, second_down, owned[3], factor, LEARN_RATE, WEIGHT_DECAY
    )
    new_gains, next_first_gains, next_second_gains = adam_step(
        gains, first_gains, second_gains, gain_total, factor, GAIN_RATE, 0.0
    )
    return (
        output_all,
        input_grad,
        global_norm,
        new_qkv,
        new_out,
        new_gate_up,
        new_down,
        new_gains,
        next_first_qkv,
        next_first_out,
        next_first_gate_up,
        next_first_down,
        next_first_gains,
        next_second_qkv,
        next_second_out,
        next_second_gate_up,
        next_second_down,
        next_second_gains,
    )


def solution(mesh):
    nf, nd = mesh.shape["fsdp"], mesh.shape["dp"]
    fits = nf == PLANE and KVH == PLANE and nd % 2 == 0
    per_device = per_device_plane if fits else per_device_plain
    in_specs = (
        P(("fsdp", "dp"), None),
        P(("fsdp", "dp"), None),
        P(("fsdp", "dp"), None),
        P(("fsdp", "dp"), None),
        P(("fsdp", "dp"), None),
        P(("fsdp", "dp"), None),
        P(("fsdp", "dp"), None),
        P(("fsdp", "dp"), None),
        P(),
        P(("fsdp", "dp"), None),
        P(("fsdp", "dp"), None),
        P(("fsdp", "dp"), None),
        P(("fsdp", "dp"), None),
        P(),
        P(("fsdp", "dp"), None),
        P(("fsdp", "dp"), None),
        P(("fsdp", "dp"), None),
        P(("fsdp", "dp"), None),
        P(),
    )
    out_specs = (
        P(("fsdp", "dp"), None),
        P(("fsdp", "dp"), None),
        P(),
        P(("fsdp", "dp"), None),
        P(("fsdp", "dp"), None),
        P(("fsdp", "dp"), None),
        P(("fsdp", "dp"), None),
        P(),
        P(("fsdp", "dp"), None),
        P(("fsdp", "dp"), None),
        P(("fsdp", "dp"), None),
        P(("fsdp", "dp"), None),
        P(),
        P(("fsdp", "dp"), None),
        P(("fsdp", "dp"), None),
        P(("fsdp", "dp"), None),
        P(("fsdp", "dp"), None),
        P(),
    )
    return jax.shard_map(
        functools.partial(per_device, nf, nd), mesh=mesh, in_specs=in_specs, out_specs=out_specs, check_vma=False
    )
```

```python
import functools

import jax
import jax.numpy as jnp
from jax import lax
from jax.experimental import pallas as pl
from jax.experimental.pallas import tpu as pltpu
from jax.sharding import PartitionSpec as P

D = 2048
HEADS = 32
HD = 64
KVH = 8
FF = 8192
TOK_DEV = 256
MB = 2
SEQS = 3
STEP = 10
MB_TOK = 128


EPSILON = 1e-05
ROPE_BASE = 1000000.0
FIRST_DECAY = 0.9
SECOND_DECAY = 0.95
LEARN_RATE = 0.05
GAIN_RATE = 2.0
WEIGHT_DECAY = 0.1
ADAM_EPSILON = 1e-08
CLIP_NORM = 1.0
GAIN_LINES = (2 * D + 2 * HD) // 128
MASKED = -1e30


def rms_norm(values, gain_vec):
    return (
        values * lax.rsqrt(jnp.mean(values * values, axis=-1, keepdims=True) + EPSILON) * gain_vec
    )


def rope_tables(position):
    half_width = HD // 2
    frequency = ROPE_BASE ** (jnp.arange(half_width, dtype=jnp.float32) * (-2.0 / HD))
    angles = position[:, None] * frequency[None, :]
    return (jnp.cos(angles)[:, None, :], jnp.sin(angles)[:, None, :])


def rotate(values, cosine_table, sine_table):
    half_width = HD // 2
    first_part = values[..., :half_width]
    second_part = values[..., half_width:]
    return jnp.concatenate(
        [
            first_part * cosine_table - second_part * sine_table,
            second_part * cosine_table + first_part * sine_table,
        ],
        axis=-1,
    )


def layout(lengths_rows):
    seq_ends = jnp.cumsum(lengths_rows, axis=-1)
    places = jnp.arange(MB_TOK, dtype=jnp.int32)
    passed = (places[None, :, None] >= seq_ends[:, None, :]).astype(jnp.int32)
    segment = jnp.sum(passed, axis=-1)
    starts = jnp.sum(passed * lengths_rows[:, None, :], axis=-1)
    position = (places[None, :] - starts).astype(jnp.float32)
    valid_rows = (segment < SEQS - 1).astype(jnp.float32)
    allowed = (segment[:, :, None] == segment[:, None, :]) & (
        places[None, None, :] <= places[None, :, None]
    )
    return (position, valid_rows, allowed)


def swiglu(gate, up):
    return jax.nn.silu(gate) * up


def column_product(left_side, right_side):
    return lax.dot_general(
        left_side, right_side, (((0,), (0,)), ((), ())), preferred_element_type=jnp.float32
    )


def contract_last(left_side, right_side):
    return lax.dot_general(
        left_side, right_side, (((1,), (1,)), ((), ())), preferred_element_type=jnp.float32
    )


def product(left_side, right_side):
    return jnp.dot(left_side, right_side, preferred_element_type=jnp.float32)


def adam_step(weight, first_state, second, gradient, factor, step_rate, decay_rate):
    clipped = gradient * factor
    first_new = FIRST_DECAY * first_state + (1.0 - FIRST_DECAY) * clipped
    second_new = SECOND_DECAY * second + (1.0 - SECOND_DECAY) * clipped * clipped
    first_hat = first_new / (1.0 - FIRST_DECAY**STEP)
    second_hat = second_new / (1.0 - SECOND_DECAY**STEP)
    weight_new = weight - step_rate * (
        first_hat / (jnp.sqrt(second_hat) + ADAM_EPSILON) + decay_rate * weight
    )
    return (weight_new, first_new, second_new)


MESH = pl.DeviceIdType.MESH
ANY = pl.BlockSpec(memory_space=pl.ANY)
VMEM = pl.BlockSpec(memory_space=pltpu.VMEM)
PLANE = 8
TILE = 512
GLU_TILE = 256
SHORT = pl.CostEstimate(flops=0, bytes_accessed=1024, transcendentals=0)


def flip(index, bit):
    step = 2**bit
    return index + step * (1 - 2 * lax.rem(lax.div(index, step), 2))


def plane_others(me):
    others = []
    for number in range(1, PLANE):
        other = me
        for bit in range(3):
            if (number >> bit) & 1:
                other = flip(other, bit)
        others.append(other)
    return others


def greet(devices):
    barrier = pltpu.get_barrier_semaphore()
    for device in devices:
        pl.semaphore_signal(barrier, inc=1, device_id={"fsdp": device}, device_id_type=MESH)
    pl.semaphore_wait(barrier, len(devices))


def half_pieces(half_ref, wide_ref, me, other, count):
    half_width = half_ref.shape[1] // 2
    for side in range(2):
        first = pl.multiple_of(side * half_width * PLANE + me * half_width, 128)
        source = half_ref.at[pl.ds(pl.multiple_of(other * count, count), count)]
        yield (
            source.at[:, pl.ds(side * half_width, half_width)],
            wide_ref.at[:, pl.ds(first, half_width)],
        )


def put_half(half_ref, wide_ref, others, number, sems):
    me, other = lax.axis_index("fsdp"), others[number - 1]
    pairs = half_pieces(half_ref, wide_ref, me, other, wide_ref.shape[0])
    return [
        pltpu.make_async_remote_copy(
            src_ref=source,
            dst_ref=target,
            send_sem=sems.at[0, 2 * number + side],
            recv_sem=sems.at[1, 2 * number + side],
            device_id={"fsdp": other},
            device_id_type=MESH,
        )
        for side, (source, target) in enumerate(pairs)
    ]


def keep_half(half_ref, wide_ref, sems):
    me = lax.axis_index("fsdp")
    return [
        pltpu.make_async_copy(source, target, sems.at[side])
        for side, (source, target) in enumerate(
            half_pieces(half_ref, wide_ref, me, me, wide_ref.shape[0])
        )
    ]


def columns_kernel(half_ref, wide_ref, squares_ref, own_sem, sems):
    others = plane_others(lax.axis_index("fsdp"))
    greet(others)
    order = (6, 7, 2, 4, 3, 5, 1)
    for number in order:
        for copy in put_half(half_ref, wide_ref, others, number, sems):
            copy.start()
    keep = keep_half(half_ref, wide_ref, own_sem)
    for copy in keep:
        copy.start()
    squares_ref[...] = jnp.zeros_like(squares_ref)

    @pl.loop(0, half_ref.shape[0] // 128)
    def _(step):
        spot = pl.ds(pl.multiple_of(step * 128, 128), 128)
        values = half_ref[spot, :].astype(jnp.float32)
        squares_ref[...] += jnp.sum(values * values, axis=0, keepdims=True)

    for number in order:
        for copy in put_half(half_ref, wide_ref, others, number, sems):
            copy.wait()
    for copy in keep:
        copy.wait()


def half_scratch():
    return [pltpu.SemaphoreType.DMA((2,)), pltpu.SemaphoreType.DMA((2, 2 * PLANE))]


def exchange_half(half, count, number):
    return pl.pallas_call(
        columns_kernel,
        out_shape=[
            jax.ShapeDtypeStruct((count, half.shape[1] * PLANE), half.dtype),
            jax.ShapeDtypeStruct((1, half.shape[1]), jnp.float32),
        ],
        in_specs=[VMEM],
        out_specs=[ANY, VMEM],
        scratch_shapes=half_scratch(),
        compiler_params=pltpu.CompilerParams(collective_id=number, has_side_effects=True),
        cost_estimate=SHORT,
        name=f"exchange_half_{number}",
    )(half)


def sum_kernel(
    nd,
    x_ref,
    blocks_ref,
    out_ref,
    norm_ref,
    qkv_ref,
    gout_ref,
    swapped_ref,
    plane_in,
    line_in,
    total,
    mine,
    own_sem,
    plane_sems,
    line_sems,
    block_sems,
):
    me, line = lax.axis_index("fsdp"), lax.axis_index("dp")
    wide = swapped_ref.shape[2]
    q_width = wide - 2 * HD
    blocks = blocks_ref[...].astype(jnp.float32)
    squares = jnp.sum(blocks * blocks, axis=(0, 1, 2), keepdims=True).reshape(1, 1)
    lines = lax.broadcasted_iota(jnp.int32, x_ref.shape, 0)
    lane = lax.broadcasted_iota(jnp.int32, x_ref.shape, 1)
    spot = jnp.logical_and(lines == GAIN_LINES, lane == 0)
    mine[...] = x_ref[...] + jnp.where(spot, squares, 0.0)
    others = plane_others(me)
    steps = [lax.rem(line + step, nd) for step in range(1, nd)]
    barrier = pltpu.get_barrier_semaphore()
    for other in others:
        pl.semaphore_signal(barrier, inc=1, device_id={"fsdp": other}, device_id_type=MESH)
    for other in steps:
        pl.semaphore_signal(barrier, inc=1, device_id={"dp": other}, device_id_type=MESH)
    pl.semaphore_wait(barrier, len(others) + len(steps))

    def to_plane(number):
        return pltpu.make_async_remote_copy(
            src_ref=mine,
            dst_ref=plane_in.at[me],
            send_sem=plane_sems.at[0, number],
            recv_sem=plane_sems.at[1, number],
            device_id={"fsdp": others[number]},
            device_id_type=MESH,
        )

    def to_line(number):
        return pltpu.make_async_remote_copy(
            src_ref=total,
            dst_ref=line_in.at[line],
            send_sem=line_sems.at[0, number],
            recv_sem=line_sems.at[1, number],
            device_id={"dp": steps[number]},
            device_id_type=MESH,
        )

    def put_block(number):
        return pltpu.make_async_remote_copy(
            src_ref=blocks_ref.at[others[number], :, pl.ds(0, wide)],
            dst_ref=swapped_ref.at[me],
            send_sem=block_sems.at[0, number],
            recv_sem=block_sems.at[1, number],
            device_id={"fsdp": others[number]},
            device_id_type=MESH,
        )

    keep = [
        pltpu.make_async_copy(
            blocks_ref.at[me, :, pl.ds(0, wide)], swapped_ref.at[me], own_sem.at[PLANE]
        )
    ]
    for place in range(PLANE):
        keep.append(
            pltpu.make_async_copy(
                blocks_ref.at[place, :, pl.ds(wide, q_width)],
                gout_ref.at[:, pl.ds(place * q_width, q_width)],
                own_sem.at[place],
            )
        )
    for number in range(PLANE - 1):
        to_plane(number).start()
    for number in range(PLANE - 1):
        put_block(number).start()
    for copy in keep:
        copy.start()
    plane_in[me] = mine[...]
    for number in range(PLANE - 1):
        to_plane(number).wait()
    part = plane_in[0]
    for place in range(1, PLANE):
        part = part + plane_in[place]
    total[...] = part
    line_in[line] = part
    for number in range(nd - 1):
        to_line(number).start()
    for number in range(PLANE - 1):
        put_block(number).wait()
    for copy in keep:
        copy.wait()
    first_head = lax.broadcasted_iota(jnp.int32, (1, 2 * HD), 1) < HD
    for place in range(0, PLANE, 2):
        pair = []
        for block in (place, place + 1):
            values = swapped_ref[block].astype(jnp.float32)
            qkv_ref[:, block * q_width : (block + 1) * q_width] = swapped_ref[block, :, :q_width]
            pair.append(values[:, q_width:])
        columns = pl.ds(PLANE * q_width + place * HD, 2 * HD)
        both = jnp.where(first_head, pair[0], pltpu.roll(pair[1], HD, 1))
        qkv_ref[:, columns] = both.astype(qkv_ref.dtype)
        columns = pl.ds(PLANE * (q_width + HD) + place * HD, 2 * HD)
        both = jnp.where(first_head, pltpu.roll(pair[0], HD, 1), pair[1])
        qkv_ref[:, columns] = both.astype(qkv_ref.dtype)
    for number in range(nd - 1):
        to_line(number).wait()
    part = line_in[0]
    for place in range(1, nd):
        part = part + line_in[place]
    out_ref[...] = part
    gains = part[:GAIN_LINES]
    lane = lax.broadcasted_iota(jnp.int32, (1, 128), 1)
    squares = jnp.where(lane == 0, part[GAIN_LINES : GAIN_LINES + 1], 0.0)
    squares = squares + jnp.sum(gains * gains, axis=0, keepdims=True)
    norm = jnp.sqrt(jnp.sum(squares, axis=1, keepdims=True))
    factor = CLIP_NORM / jnp.maximum(norm, CLIP_NORM)
    line_number = lax.broadcasted_iota(jnp.int32, norm_ref.shape, 0)
    norm_ref[...] = jnp.where(line_number == 0, norm, factor)


def sum_everywhere(gain_sum, squares, blocks, wide, number):
    values = jnp.concatenate([gain_sum, squares.reshape(1)])
    nd = lax.axis_size("dp")
    count = values.shape[0]
    lines = -(-count // 1024) * 8
    padded = jnp.pad(values, (0, lines * 128 - count)).reshape(lines, 128)
    q_width = wide - 2 * HD
    summed, norm, grad_qkv, grad_out = pl.pallas_call(
        functools.partial(sum_kernel, nd),
        out_shape=[
            jax.ShapeDtypeStruct(padded.shape, jnp.float32),
            jax.ShapeDtypeStruct((8, 128), jnp.float32),
            jax.ShapeDtypeStruct((blocks.shape[1], PLANE * wide), blocks.dtype),
            jax.ShapeDtypeStruct((blocks.shape[1], PLANE * q_width), blocks.dtype),
        ],
        in_specs=[VMEM, VMEM],
        out_specs=[VMEM] * 4,
        scratch_shapes=[
            pltpu.VMEM((PLANE, blocks.shape[1], wide), blocks.dtype),
            pltpu.VMEM((PLANE,) + padded.shape, jnp.float32),
            pltpu.VMEM((nd,) + padded.shape, jnp.float32),
            pltpu.VMEM(padded.shape, jnp.float32),
            pltpu.VMEM(padded.shape, jnp.float32),
            pltpu.SemaphoreType.DMA((PLANE + 1,)),
            pltpu.SemaphoreType.DMA((2, PLANE - 1)),
            pltpu.SemaphoreType.DMA((2, nd - 1)),
            pltpu.SemaphoreType.DMA((2, PLANE - 1)),
        ],
        compiler_params=pltpu.CompilerParams(collective_id=number, has_side_effects=True),
        cost_estimate=SHORT,
        name=f"sum_everywhere_{number}",
    )(padded, blocks)
    return summed.reshape(-1)[: count - 1], norm, grad_qkv, grad_out


def greet_line(nd, others):
    line = lax.axis_index("dp")
    barrier = pltpu.get_barrier_semaphore()
    for other in others:
        pl.semaphore_signal(barrier, inc=1, device_id={"fsdp": other}, device_id_type=MESH)

    @pl.when(line < nd - 1)
    def _():
        pl.semaphore_signal(barrier, inc=1, device_id={"dp": line + 1}, device_id_type=MESH)

    @pl.when(line > 0)
    def _():
        pl.semaphore_signal(barrier, inc=1, device_id={"dp": line - 1}, device_id_type=MESH)

    neighbours = lax.div(line + nd - 1, nd) + lax.div(2 * nd - 2 - line, nd)
    pl.semaphore_wait(barrier, len(others) + neighbours)


class Gather:
    def __init__(self, own_ref, all_ref, send_sem, recv_sem):
        self.own_ref, self.all_ref = own_ref, all_ref
        self.send_sem, self.recv_sem = send_sem, recv_sem
        self.me = lax.axis_index("fsdp")
        self.sibling, self.x_next, self.y_next = flip(self.me, 0), flip(self.me, 1), flip(self.me, 2)
        self.diagonal = flip(self.x_next, 2)
        self.rows = own_ref.shape[0]
        self.sent = []

    def put(self, slot, owner, part, target, own=False):
        half = self.rows // 2
        if part is None:
            spot = self.all_ref.at[pl.ds(pl.multiple_of(owner * self.rows, half), self.rows)]
            source = self.own_ref
        else:
            first = pl.multiple_of(owner * self.rows + part * half, half)
            spot = self.all_ref.at[pl.ds(first, half)]
            source = self.own_ref.at[pl.ds(part * half, half)]
        return pltpu.make_async_remote_copy(
            src_ref=source if own else spot,
            dst_ref=spot,
            send_sem=self.send_sem.at[slot],
            recv_sem=self.recv_sem.at[slot],
            device_id={"fsdp": target},
            device_id_type=MESH,
        )

    def begin(self):
        for slot, part, target in (
            (0, 0, self.x_next),
            (2, 1, self.y_next),
            (4, None, self.sibling),
            (1, 1, self.x_next),
            (3, 0, self.y_next),
        ):
            copy = self.put(slot, self.me, part, target, own=True)
            copy.start()
            self.sent.append(copy)

    def take(self, slot):
        sibling = self.sibling
        owner, part, onward = {
            0: (self.x_next, 0, ((5, self.y_next), (7, sibling))),
            1: (self.x_next, 1, ((8, sibling),)),
            2: (self.y_next, 1, ((6, self.x_next), (9, sibling))),
            3: (self.y_next, 0, ((10, sibling),)),
            4: (sibling, None, ()),
            5: (self.diagonal, 0, ((11, sibling),)),
            6: (self.diagonal, 1, ((12, sibling),)),
            7: (flip(self.x_next, 0), 0, ()),
            8: (flip(self.x_next, 0), 1, ()),
            9: (flip(self.y_next, 0), 1, ()),
            10: (flip(self.y_next, 0), 0, ()),
            11: (flip(self.diagonal, 0), 0, ()),
            12: (flip(self.diagonal, 0), 1, ()),
        }[slot]
        self.put(slot, owner, part, sibling).wait_recv()
        for next_slot, target in onward:
            copy = self.put(next_slot, owner, part, target)
            copy.start()
            self.sent.append(copy)

    def finish(self):
        for copy in self.sent:
            copy.wait_send()


def gather_scratch():
    return [pltpu.SemaphoreType.DMA((13,)), pltpu.SemaphoreType.DMA((13,))]


class Scatter:
    def __init__(self, out_ref, block, refs):
        self.out_ref, self.block = out_ref, block
        (self.sib_out, self.sib_in, self.far_out, self.far_in, self.near_out, self.near_in) = refs[:6]
        self.late = refs[6]
        self.sib_sems, self.far_sems, self.near_sems = refs[7:9], refs[9:11], refs[11:13]
        self.me = lax.axis_index("fsdp")
        self.sibling, self.x_next, self.y_next = flip(self.me, 0), flip(self.me, 1), flip(self.me, 2)
        self.targets = (flip(self.x_next, 2), self.x_next, self.y_next, self.me)
        self.half = out_ref.shape[0] // 2

    def send(self, source, target, sems, slot, device):
        return pltpu.make_async_remote_copy(
            src_ref=source.at[slot],
            dst_ref=target.at[slot],
            send_sem=sems[0].at[slot],
            recv_sem=sems[1].at[slot],
            device_id={"fsdp": device},
            device_id_type=MESH,
        )

    def to_sibling(self, place):
        return self.send(self.sib_out, self.sib_in, self.sib_sems, place, self.sibling)

    def to_far(self, part):
        device = (self.x_next, self.y_next)[part]
        return self.send(self.far_out, self.far_in, self.far_sems, part, device)

    def to_near(self, place, part):
        device = (self.x_next, self.y_next)[place]
        return self.send(self.near_out, self.near_in, self.near_sems, 2 * place + part, device)

    def for_sibling(self, place):
        def write(columns, part):
            self.sib_out[place, :, columns] = part.astype(jnp.bfloat16)

        self.block(flip(self.targets[place], 0), write)
        self.to_sibling(place).start()

    def for_far(self):
        self.to_sibling(0).wait_recv()

        def write(columns, part):
            whole = (part + self.sib_in[0, :, columns].astype(jnp.float32)).astype(jnp.bfloat16)
            self.far_out[0, :, columns] = whole[: self.half]
            self.far_out[1, :, columns] = whole[self.half :]

        self.block(self.targets[0], write)
        self.to_far(0).start()
        self.to_far(1).start()

    def for_near(self, place):
        self.to_sibling(1 + place).wait_recv()
        other = 1 - place

        def write(columns, part):
            whole = part + self.sib_in[1 + place, :, columns].astype(jnp.float32)
            halves = (whole[: self.half], whole[self.half :])
            self.near_out[2 * place + place, :, columns] = halves[place].astype(jnp.bfloat16)
            self.late[place, :, columns] = halves[other]

        self.block(self.targets[1 + place], write)
        self.to_near(place, place).start()

    def finish_near(self, place):
        other = 1 - place
        self.to_far(other).wait_recv()
        whole = self.late[place] + self.far_in[other].astype(jnp.float32)
        self.near_out[2 * place + other] = whole.astype(jnp.bfloat16)
        self.to_near(place, other).start()

    def own(self):
        def write(columns, part):
            self.out_ref[:, columns] = part

        self.block(self.me, write)

    def finish(self):
        self.to_sibling(3).wait_recv()
        self.out_ref[...] = self.out_ref[...] + self.sib_in[3].astype(jnp.float32)
        for part, place in ((0, 0), (1, 1), (1, 0), (0, 1)):
            self.to_near(place, part).wait_recv()
            spot = pl.ds(part * self.half, self.half)
            part_in = self.near_in[2 * place + part].astype(jnp.float32)
            self.out_ref[spot, :] = self.out_ref[spot, :] + part_in
        for place in range(4):
            self.to_sibling(place).wait_send()
            self.to_near(place // 2, place % 2).wait_send()
        for part in range(2):
            self.to_far(part).wait_send()


def staged(kernel, n_in, places):
    def body(*refs):
        stage, sems = refs[-len(places) - 1 : -1], refs[-1]
        inputs, rest = list(refs[:n_in]), refs[n_in : -len(places) - 1]
        copies = [
            pltpu.make_async_copy(inputs[place], buffer, sems.at[index])
            for index, (place, buffer) in enumerate(zip(places, stage))
        ]
        for copy in copies:
            copy.start()
        for place, buffer in zip(places, stage):
            inputs[place] = buffer

        def ready():
            for copy in copies:
                copy.wait()

        kernel(ready, *inputs, *rest)

    return body


def staged_specs(arrays, places):
    specs = [ANY if place in places else VMEM for place in range(len(arrays))]
    scratch = [pltpu.VMEM(arrays[place].shape, arrays[place].dtype) for place in places]
    return specs, scratch + [pltpu.SemaphoreType.DMA((len(places),))]


def scatter_scratch(rows, width):
    low, half = jnp.bfloat16, rows // 2
    return [
        pltpu.VMEM((4, rows, width), low),
        pltpu.VMEM((4, rows, width), low),
        pltpu.VMEM((2, half, width), low),
        pltpu.VMEM((2, half, width), low),
        pltpu.VMEM((4, half, width), low),
        pltpu.VMEM((4, half, width), low),
        pltpu.VMEM((2, half, width), jnp.float32),
        pltpu.SemaphoreType.DMA((4,)),
        pltpu.SemaphoreType.DMA((4,)),
        pltpu.SemaphoreType.DMA((2,)),
        pltpu.SemaphoreType.DMA((2,)),
        pltpu.SemaphoreType.DMA((4,)),
        pltpu.SemaphoreType.DMA((4,)),
    ]


def block_product(left_refs, right_refs, rows, width, turned):
    def block(owner, write):
        @pl.loop(0, width // TILE)
        def _(step):
            columns = pl.ds(pl.multiple_of(step * TILE, TILE), TILE)
            spot = pl.ds(pl.multiple_of(owner * rows, rows), rows)
            total = None
            for left_ref, right_ref in zip(left_refs, right_refs):
                if turned:
                    part = contract_last(left_ref[spot, :], right_ref[columns, :])
                else:
                    part = product(left_ref[spot, :], right_ref[:, columns])
                total = part if total is None else total + part
            write(columns, total)

    return block


def scatter_kernel(turned, count, *refs):
    left_hbm, right_hbm, out_ref = refs[:count], refs[count : 2 * count], refs[2 * count]
    refs = refs[2 * count + 1 :]
    left_refs, right_refs = refs[:count], refs[count : 2 * count]
    left_sems, right_sems, refs = refs[2 * count], refs[2 * count + 1], refs[2 * count + 2 :]
    rows, width = out_ref.shape
    whole = block_product(left_refs, right_refs, rows, width, turned)

    def fetch(place, owner):
        spot = pl.ds(pl.multiple_of(owner * rows, rows), rows)
        return pltpu.make_async_copy(
            left_hbm[place].at[spot], left_refs[place].at[spot], left_sems.at[place, owner]
        )

    def block(owner, write):
        for place in range(count):
            fetch(place, owner).wait()
        whole(owner, write)

    scatter = Scatter(out_ref, block, refs)
    rights = [
        pltpu.make_async_copy(right_hbm[place], right_refs[place], right_sems.at[place])
        for place in range(count)
    ]
    for copy in rights:
        copy.start()
    far, x_next, y_next, me = scatter.targets
    for owner in (
        flip(far, 0),
        flip(x_next, 0),
        far,
        flip(y_next, 0),
        x_next,
        flip(me, 0),
        y_next,
        me,
    ):
        for place in range(count):
            fetch(place, owner).start()
    greet((scatter.sibling, scatter.x_next, scatter.y_next))
    for copy in rights:
        copy.wait()
    scatter.for_sibling(0)
    scatter.for_sibling(1)
    scatter.for_far()
    scatter.for_sibling(2)
    scatter.for_near(0)
    scatter.for_sibling(3)
    scatter.for_near(1)
    scatter.finish_near(0)
    scatter.finish_near(1)
    scatter.own()
    scatter.finish()


def pass_through(ready, gather, scatter, work, between):
    me, sibling, x_next, y_next = gather.me, gather.sibling, gather.x_next, gather.y_next
    diagonal = gather.diagonal
    greet((sibling, x_next, y_next))
    gather.begin()
    gather.all_ref[pl.ds(pl.multiple_of(me * gather.rows, gather.rows), gather.rows), :] = (
        gather.own_ref[...]
    )
    ready()
    work((me,))
    gather.take(0)
    gather.take(2)
    gather.take(4)
    work((sibling,))
    scatter.for_sibling(3)
    gather.take(1)
    gather.take(3)
    work((x_next, y_next))
    gather.take(5)
    gather.take(6)
    for slot in (7, 8, 9, 10):
        gather.take(slot)
    work((flip(x_next, 0), flip(y_next, 0)))
    scatter.for_sibling(1)
    scatter.for_sibling(2)
    scatter.for_near(0)
    scatter.for_near(1)
    gather.take(11)
    gather.take(12)
    work((flip(diagonal, 0),))
    scatter.for_sibling(0)
    work((diagonal,))
    scatter.for_far()
    scatter.own()
    between[0]()
    scatter.finish_near(0)
    scatter.finish_near(1)
    between[1]()
    scatter.finish()
    gather.finish()


def each_owner(owners, rows, one):
    if len(owners) == 1:
        one(owners[0])
        return

    @pl.loop(0, len(owners))
    def _(step):
        one(owners[0] + step * (owners[1] - owners[0]))


def lanes():
    lane = lax.broadcasted_iota(jnp.int32, (1, 2 * HD), 1)
    row_head = lax.broadcasted_iota(jnp.int32, (2 * HD, 2 * HD), 0) // HD
    column_head = lax.broadcasted_iota(jnp.int32, (2 * HD, 2 * HD), 1) // HD
    spread = jnp.where(row_head == column_head, 1.0 / HD, 0.0).astype(jnp.float32)

    def head_mean(values):
        return jnp.dot(
            values, spread, precision=lax.Precision.HIGHEST, preferred_element_type=jnp.float32
        )

    first_half = lax.rem(lane, HD) < HD // 2

    def turn_quarter(values):
        return jnp.where(
            first_half,
            -pltpu.roll(values, 2 * HD - HD // 2, 1),
            pltpu.roll(values, HD // 2, 1),
        )

    def sides(values):
        return [
            jnp.where(chosen, values, 0.0).astype(jnp.bfloat16)
            for chosen in (lane < HD, lane >= HD)
        ]

    return lane, sides, head_mean, turn_quarter


def twice(values):
    return jnp.concatenate([values, values], axis=0)


def stacked(ref, spot):
    width = 2 * HD
    return jnp.concatenate([ref[spot, :width], ref[spot, width : 2 * width]], axis=0)


def attend_kernel(
    ready,
    x_ref,
    wqkv_ref,
    wo_ref,
    cos_ref,
    sin_ref,
    mask_ref,
    gain_ref,
    out_ref,
    all_out_ref,
    proj_ref,
    q_ref,
    kk_ref,
    vv_ref,
    o_ref,
    lse_ref,
    all_ref,
    out_sem,
    gather_send,
    gather_recv,
    *refs,
):
    rows, width = out_ref.shape
    low = jnp.bfloat16
    pair_width = 2 * HD
    lane, sides, head_mean, turn_quarter = lanes()
    first_head = lane < HD
    scale = HD ** (-0.5)

    def normed(values, gain):
        return values * lax.rsqrt(head_mean(values * values) + EPSILON) * gain

    def one(owner):
        base = pl.multiple_of(owner * rows, rows)
        spot = pl.ds(base, rows)
        proj_ref[spot, :] = product(all_ref[spot, :], wqkv_ref[...])

        for part in range(MB):
            micro(pl.multiple_of(base + part * MB_TOK, MB_TOK), owner * MB + part)

    def micro(first, number):
        spot = pl.ds(first, MB_TOK)
        cosine, sine = cos_ref[spot, :], sin_ref[spot, :]
        allowed = twice(mask_ref[number]) > 0.5
        kv = proj_ref[spot, 2 * pair_width : 3 * pair_width]
        swapped = pltpu.roll(kv, HD, 1)
        values = jnp.where(first_head, swapped, kv)
        keys = normed(jnp.where(first_head, kv, swapped), gain_ref[1:2, :])
        keys = (keys * cosine + turn_quarter(keys) * sine).astype(low)
        kk_ref[spot, :] = keys
        vv_ref[spot, :] = values.astype(low)
        query = normed(stacked(proj_ref, spot), gain_ref[0:1, :])
        query = (query * twice(cosine) + turn_quarter(query) * twice(sine)).astype(low)
        q_ref[spot, :pair_width] = query[:MB_TOK]
        q_ref[spot, pair_width : 2 * pair_width] = query[MB_TOK:]
        probs, logs = [], []
        for one_query in sides(query.astype(jnp.float32) * scale):
            scores = jnp.where(allowed, contract_last(one_query, keys), MASKED)
            peak = jnp.max(scores, axis=-1, keepdims=True)
            powers = jnp.exp(scores - peak)
            total = jnp.sum(powers, axis=-1, keepdims=True)
            probs.append((powers * (1.0 / total)).astype(low))
            logs.append(peak + jnp.log(total))
        wide_values = jnp.concatenate(sides(values), axis=0)
        attended = product(jnp.concatenate(probs, axis=1), wide_values).astype(low)
        o_ref[spot, :pair_width] = attended[:MB_TOK]
        o_ref[spot, pair_width : 2 * pair_width] = attended[MB_TOK:]
        log_totals = jnp.where(lane == 0, logs[0][:MB_TOK], logs[1][:MB_TOK])
        log_totals = jnp.where(lane == 2, logs[0][MB_TOK:], log_totals)
        lse_ref[spot, :] = jnp.where(lane == 3, logs[1][MB_TOK:], log_totals)

    gather = Gather(x_ref, all_ref, gather_send, gather_recv)
    scatter = Scatter(out_ref, block_product((o_ref,), (wo_ref,), rows, width, False), refs)
    keep = pltpu.make_async_copy(all_ref, all_out_ref, out_sem)
    pass_through(
        ready,
        gather,
        scatter,
        lambda owners: each_owner(owners, rows, one),
        (keep.start, lambda: None),
    )
    keep.wait()


def attend_back_kernel(
    ready,
    x_ref,
    wqkv_ref,
    wo_ref,
    cos_ref,
    sin_ref,
    mask_ref,
    gain_ref,
    proj_ref,
    q_ref,
    kk_ref,
    vv_ref,
    o_ref,
    lse_ref,
    normed_hbm,
    out_ref,
    grad_ref,
    ggain_ref,
    all_ref,
    normed_ref,
    do_ref,
    dproj_ref,
    in_sem,
    gather_send,
    gather_recv,
    *refs,
):
    rows, width = out_ref.shape
    low = jnp.bfloat16
    pair_width = 2 * HD
    lane, sides, head_mean, turn_quarter = lanes()
    first_head = lane < HD
    scale = HD ** (-0.5)
    fetch = pltpu.make_async_copy(normed_hbm, normed_ref, in_sem)
    fetch.start()
    ggain_ref[...] = jnp.zeros_like(ggain_ref)

    def through_norm(grad, cosine, sine, raw, gain, row):
        grad = grad * cosine - turn_quarter(grad) * sine
        root = lax.rsqrt(head_mean(raw * raw) + EPSILON)
        normed = raw * root
        ggain_ref[row : row + 1, :] += jnp.sum(grad * normed, axis=0, keepdims=True)
        scaled = grad * gain
        return root * (scaled - normed * head_mean(scaled * normed))

    def one(owner):
        base = pl.multiple_of(owner * rows, rows)
        do_ref[...] = contract_last(all_ref[pl.ds(base, rows), :], wo_ref[...]).astype(low)

        for part in range(MB):
            here = pl.ds(part * MB_TOK, MB_TOK)
            micro(pl.multiple_of(base + part * MB_TOK, MB_TOK), here, owner * MB + part)

    def micro(first, here, number):
        spot = pl.ds(first, MB_TOK)
        cosine, sine = cos_ref[spot, :], sin_ref[spot, :]
        allowed = twice(mask_ref[number]) > 0.5
        keys, values = kk_ref[spot, :], vv_ref[spot, :]
        logs = lse_ref[spot, :]
        queries = sides(stacked(q_ref, spot).astype(jnp.float32) * scale)
        branches = sides(stacked(do_ref, here).astype(jnp.float32))
        probs_low, scores_back = [], []
        for side in range(2):
            log_total = jnp.concatenate(
                [logs[:, side : side + 1], logs[:, 2 + side : 3 + side]], axis=0
            )
            scores = jnp.where(allowed, contract_last(queries[side], keys), MASKED)
            probs = jnp.exp(scores - log_total)
            probs_grad = contract_last(branches[side], values)
            spread = jnp.sum(probs * probs_grad, axis=-1, keepdims=True)
            scores_back.append((probs * (probs_grad - spread)).astype(low))
            probs_low.append(probs.astype(low))
        wide_keys = jnp.concatenate(sides(keys.astype(jnp.float32)), axis=0)
        query_grad = product(jnp.concatenate(scores_back, axis=1), wide_keys) * scale
        key_grad = column_product(
            jnp.concatenate(scores_back, axis=0), jnp.concatenate(queries, axis=0)
        )
        value_grad = column_product(
            jnp.concatenate(probs_low, axis=0), jnp.concatenate(branches, axis=0)
        )
        raw = stacked(proj_ref, spot)
        grad = through_norm(query_grad, twice(cosine), twice(sine), raw, gain_ref[0:1, :], 0)
        dproj_ref[spot, :pair_width] = grad[:MB_TOK].astype(low)
        dproj_ref[spot, pair_width : 2 * pair_width] = grad[MB_TOK:].astype(low)
        kv = proj_ref[spot, 2 * pair_width : 3 * pair_width]
        raw = jnp.where(first_head, kv, pltpu.roll(kv, HD, 1))
        key_grad = key_grad + pltpu.roll(key_grad, HD, 1)
        value_grad = value_grad + pltpu.roll(value_grad, HD, 1)
        grad = through_norm(key_grad, cosine, sine, raw, gain_ref[1:2, :], 1)
        both = jnp.where(first_head, grad, value_grad).astype(low)
        dproj_ref[spot, 2 * pair_width : 3 * pair_width] = both

    wide, q_width = dproj_ref.shape[1], o_ref.shape[1]

    def out_grad():
        @pl.loop(0, width // TILE)
        def _(step):
            columns = pl.ds(pl.multiple_of(step * TILE, TILE), TILE)
            part = column_product(o_ref[...], all_ref[:, columns]).astype(low)
            for first in range(0, TILE, q_width):
                spot = pl.ds(pl.multiple_of(step * TILE + first, q_width), q_width)
                grad_ref[spot, wide:] = part[:, first : first + q_width]

    def qkv_grad():
        fetch.wait()

        @pl.loop(0, width // TILE)
        def _(step):
            columns = pl.ds(pl.multiple_of(step * TILE, TILE), TILE)
            part = column_product(dproj_ref[...], normed_ref[:, columns])
            grad_ref[columns, :wide] = jnp.transpose(part).astype(low)

    gather = Gather(x_ref, all_ref, gather_send, gather_recv)
    scatter = Scatter(out_ref, block_product((dproj_ref,), (wqkv_ref,), rows, width, True), refs)
    pass_through(
        ready, gather, scatter, lambda owners: each_owner(owners, rows, one), (out_grad, qkv_grad)
    )


def attend(own_rows, own_qkv, own_out, tables, number):
    rows, width = own_rows.shape
    count, wide, q_width = PLANE * rows, own_qkv.shape[1], own_out.shape[0]
    low = jnp.bfloat16
    arrays = (own_rows, own_qkv, own_out, *tables)
    places = tuple(range(1, len(arrays)))
    specs, stage = staged_specs(arrays, places)
    return pl.pallas_call(
        staged(attend_kernel, len(arrays), places),
        out_shape=[
            jax.ShapeDtypeStruct((rows, width), jnp.float32),
            jax.ShapeDtypeStruct((count, width), low),
            jax.ShapeDtypeStruct((count, wide), jnp.float32),
            jax.ShapeDtypeStruct((count, q_width), low),
            jax.ShapeDtypeStruct((count, 2 * HD), low),
            jax.ShapeDtypeStruct((count, 2 * HD), low),
            jax.ShapeDtypeStruct((count, q_width), low),
            jax.ShapeDtypeStruct((count, 2 * HD), jnp.float32),
        ],
        in_specs=specs,
        out_specs=[VMEM, ANY] + [VMEM] * 6,
        scratch_shapes=[pltpu.VMEM((count, width), low), pltpu.SemaphoreType.DMA]
        + gather_scratch()
        + scatter_scratch(rows, width)
        + stage,
        compiler_params=pltpu.CompilerParams(
            collective_id=number, has_side_effects=True, vmem_limit_bytes=56 * 2**20
        ),
        cost_estimate=SHORT,
        name=f"attend_{number}",
    )(*arrays)


def attend_back(own_rows, own_qkv, own_out, tables, kept, number):
    rows, width = own_rows.shape
    count, wide, q_width = PLANE * rows, own_qkv.shape[1], own_out.shape[0]
    low = jnp.bfloat16
    normed_all, proj, query, keys, values, attended, log_totals = kept
    arrays = (
        own_rows,
        own_qkv,
        own_out,
        *tables,
        proj,
        query,
        keys,
        values,
        attended,
        log_totals,
        normed_all,
    )
    places = tuple(range(1, len(arrays) - 1))
    specs, stage = staged_specs(arrays[:-1], places)
    return pl.pallas_call(
        staged(attend_back_kernel, len(arrays), places),
        out_shape=[
            jax.ShapeDtypeStruct((rows, width), jnp.float32),
            jax.ShapeDtypeStruct((width, wide + q_width), low),
            jax.ShapeDtypeStruct((8, 2 * HD), jnp.float32),
        ],
        in_specs=specs + [ANY],
        out_specs=[VMEM] * 3,
        scratch_shapes=[
            pltpu.VMEM((count, width), low),
            pltpu.VMEM((count, width), low),
            pltpu.VMEM((rows, q_width), low),
            pltpu.VMEM((count, wide), low),
            pltpu.SemaphoreType.DMA,
        ]
        + gather_scratch()
        + scatter_scratch(rows, width)
        + stage,
        compiler_params=pltpu.CompilerParams(
            collective_id=number, has_side_effects=True, vmem_limit_bytes=58 * 2**20
        ),
        cost_estimate=SHORT,
        name=f"attend_back_{number}",
    )(*arrays)


def product_scatter(left_sides, right_sides, number, turned=False):
    width = right_sides[0].shape[0] if turned else right_sides[0].shape[1]
    rows = left_sides[0].shape[0] // PLANE
    return pl.pallas_call(
        functools.partial(scatter_kernel, turned, len(left_sides)),
        out_shape=jax.ShapeDtypeStruct((rows, width), jnp.float32),
        in_specs=[ANY] * (2 * len(left_sides)),
        out_specs=VMEM,
        scratch_shapes=[pltpu.VMEM(side.shape, side.dtype) for side in left_sides + right_sides]
        + [
            pltpu.SemaphoreType.DMA((len(left_sides), PLANE)),
            pltpu.SemaphoreType.DMA((len(left_sides),)),
        ]
        + scatter_scratch(rows, width),
        compiler_params=pltpu.CompilerParams(
            collective_id=number, has_side_effects=True, vmem_limit_bytes=56 * 2**20
        ),
        cost_estimate=SHORT,
        name=f"product_scatter_{number}",
    )(*left_sides, *right_sides)


def start_kernel(
    nd,
    qkv_ref,
    out_rows_ref,
    wide_hbm,
    df_ref,
    note_ref,
    own_qkv_ref,
    own_out_ref,
    half_a_ref,
    half_b_ref,
    df_all_ref,
    notes_ref,
    own_sem,
    gather_send,
    gather_recv,
    block_send,
    block_recv,
    note_send,
    note_recv,
    piece_send,
    piece_recv,
    line_send,
    line_recv,
    wide_full,
    wide_ref,
    wide_sem,
):
    me, line = lax.axis_index("fsdp"), lax.axis_index("dp")
    others = plane_others(me)
    count = qkv_ref.shape[1]
    half_width = half_a_ref.shape[2] // 2
    hidden = 2 * half_width
    whole = hidden * PLANE
    fetch = pltpu.make_async_copy(wide_hbm, wide_full, wide_sem)
    fetch.start()
    gather = Gather(df_ref, df_all_ref, gather_send, gather_recv)
    greet_line(nd, others)

    def line_spot(array, owner):
        rows = pl.ds(pl.multiple_of(owner * count, count), count)
        if array == 1:
            return own_out_ref.at[rows]
        return own_qkv_ref.at[pl.ds(array // 2 * (PLANE // 2), PLANE // 2), rows]

    def along(array, owner, side, source=None):
        spot = line_spot(array, owner)
        return pltpu.make_async_remote_copy(
            src_ref=spot if source is None else source,
            dst_ref=spot,
            send_sem=line_send.at[array, side, owner],
            recv_sem=line_recv.at[array, owner],
            device_id={"dp": line + 1 if side == 0 else line - 1},
            device_id_type=MESH,
        )

    def send_own(array, source=None):
        @pl.when(line < nd - 1)
        def _():
            along(array, line, 0, source).start()

        @pl.when(line > 0)
        def _():
            along(array, line, 1, source).start()

    def line_step(array, step):
        @pl.when(line >= step)
        def _():
            along(array, line - step, 0).wait_recv()

            @pl.when(line < nd - 1)
            def _():
                along(array, line - step, 0).start()

        @pl.when(line + step < nd)
        def _():
            along(array, line + step, 1).wait_recv()

            @pl.when(line > 0)
            def _():
                along(array, line + step, 1).start()

    def put_block(number):
        other = others[number - 1]
        return pltpu.make_async_remote_copy(
            src_ref=qkv_ref.at[other],
            dst_ref=own_qkv_ref.at[me, pl.ds(pl.multiple_of(line * count, count), count)],
            send_sem=block_send.at[number],
            recv_sem=block_recv.at[number],
            device_id={"fsdp": other},
            device_id_type=MESH,
        )

    def put_note(number):
        return pltpu.make_async_remote_copy(
            src_ref=note_ref,
            dst_ref=notes_ref.at[me],
            send_sem=note_send.at[number],
            recv_sem=note_recv.at[number],
            device_id={"fsdp": others[number - 1]},
            device_id_type=MESH,
        )

    def pieces(other):
        for half, half_ref in enumerate((half_a_ref, half_b_ref)):
            for side in range(2):
                first = side * whole + other * hidden + half * half_width
                source = wide_ref.at[:, pl.ds(pl.multiple_of(first, 128), half_width)]
                yield source, half_ref.at[me, :, pl.ds(side * half_width, half_width)]

    def put_pieces(number):
        return [
            pltpu.make_async_remote_copy(
                src_ref=source,
                dst_ref=target,
                send_sem=piece_send.at[4 * number + index],
                recv_sem=piece_recv.at[4 * number + index],
                device_id={"fsdp": others[number - 1]},
                device_id_type=MESH,
            )
            for index, (source, target) in enumerate(pieces(others[number - 1]))
        ]

    own_block = own_qkv_ref.at[me, pl.ds(pl.multiple_of(line * count, count), count)]
    rows = df_ref.shape[0]

    def local(index, source, target):
        return pltpu.make_async_copy(source, target, own_sem.at[index])

    keep = [
        local(0, qkv_ref.at[me], own_block),
        local(1, out_rows_ref, line_spot(1, line)),
        local(2, note_ref, notes_ref.at[me]),
        local(3, df_ref, df_all_ref.at[pl.ds(pl.multiple_of(me * rows, rows), rows)]),
    ]
    keep_pieces = [
        local(4 + index, source, target) for index, (source, target) in enumerate(pieces(me))
    ]
    order = (6, 7, 2, 4, 3, 5, 1)
    for number in order:
        put_block(number).start()
        put_note(number).start()
    keep[0].start()
    send_own(1, out_rows_ref)
    gather.begin()
    for copy in keep[1:]:
        copy.start()
    for number in order:
        put_block(number).wait_recv()
    keep[0].wait()
    send_own(0)
    send_own(2)
    fetch.wait()

    part_width = half_width // nd

    @pl.loop(0, 2 * PLANE)
    def _(step):
        for owner in range(nd):
            for half in range(2):
                first = step * hidden + (2 * owner + half) * part_width
                target = step * hidden + half * half_width + owner * part_width
                columns = pl.ds(pl.multiple_of(first, 128), part_width)
                target = pl.ds(pl.multiple_of(target, 128), part_width)
                wide_ref[:, target] = wide_full[:, columns].astype(wide_ref.dtype)

    for steps, slots in (
        ((), (0, 2)),
        (((1, 1),), (4, 1, 3)),
        (((0, 1), (2, 1)), (5, 6)),
        (((1, 2),), ()),
        (((0, 2), (2, 2)), (7, 9, 8, 10)),
        (((1, 3), (0, 3), (2, 3)), (11, 12)),
    ):
        for array, step in steps:
            if step < nd:
                line_step(array, step)
        for slot in slots:
            gather.take(slot)
        if slots == (5, 6):
            for number in order:
                for copy in put_pieces(number):
                    copy.start()
            for copy in keep_pieces:
                copy.start()
    for step in range(4, nd):
        for array in (1, 0, 2):
            line_step(array, step)
    for number in order:
        put_block(number).wait_send()
        put_note(number).wait()
        for copy in put_pieces(number):
            copy.wait()
    gather.finish()
    for copy in keep[1:] + keep_pieces:
        copy.wait()
    for array in (1, 0, 2):
        source = out_rows_ref if array == 1 else None

        @pl.when(line < nd - 1)
        def _():
            along(array, line, 0, source).wait_send()

        @pl.when(line > 0)
        def _():
            along(array, line, 1, source).wait_send()

        for step in range(1, nd):

            @pl.when(jnp.logical_and(line >= step, line < nd - 1))
            def _():
                along(array, line - step, 0).wait_send()

            @pl.when(jnp.logical_and(line + step < nd, line > 0))
            def _():
                along(array, line + step, 1).wait_send()


def start(qkv_blocks, out_rows, wide_rows, df_own, note, number):
    nd = lax.axis_size("dp")
    count, whole = wide_rows.shape
    half = whole // 4 // PLANE
    low = jnp.bfloat16
    return pl.pallas_call(
        functools.partial(start_kernel, nd),
        out_shape=[
            jax.ShapeDtypeStruct((PLANE, nd * count, qkv_blocks.shape[2]), low),
            jax.ShapeDtypeStruct((nd * count, out_rows.shape[1]), low),
            jax.ShapeDtypeStruct((PLANE, count, 2 * half), low),
            jax.ShapeDtypeStruct((PLANE, count, 2 * half), low),
            jax.ShapeDtypeStruct((PLANE * df_own.shape[0], df_own.shape[1]), low),
            jax.ShapeDtypeStruct((PLANE,) + note.shape, note.dtype),
        ],
        in_specs=[ANY] * 5,
        out_specs=[ANY] * 6,
        scratch_shapes=[pltpu.SemaphoreType.DMA((8,))]
        + gather_scratch()
        + [pltpu.SemaphoreType.DMA((PLANE,))] * 4
        + [pltpu.SemaphoreType.DMA((4 * PLANE,))] * 2
        + [pltpu.SemaphoreType.DMA((3, 2, nd)), pltpu.SemaphoreType.DMA((3, nd))]
        + [
            pltpu.VMEM(wide_rows.shape, wide_rows.dtype),
            pltpu.VMEM(wide_rows.shape, low),
            pltpu.SemaphoreType.DMA,
        ],
        compiler_params=pltpu.CompilerParams(
            collective_id=number, has_side_effects=True, vmem_limit_bytes=56 * 2**20
        ),
        cost_estimate=SHORT,
        name=f"start_{number}",
    )(qkv_blocks, out_rows, wide_rows, df_own, note)


def glu_block(
    rows_ref, df_ref, wgu, wd, act_ref, dgu_ref, down_sum, wide_sum, results=None
):
    half = wd.shape[0]
    count, width = rows_ref.shape

    @pl.loop(0, count // 256)
    def _(step):
        spot = pl.ds(pl.multiple_of(step * 256, 256), 256)
        for first in range(0, half, GLU_TILE):
            units = slice(first, first + GLU_TILE)
            up_units = slice(half + first, half + first + GLU_TILE)
            gate = product(rows_ref[spot, :], wgu[:, units])
            up = product(rows_ref[spot, :], wgu[:, up_units])
            back = contract_last(df_ref[spot, :], wd[units, :])
            sigmoid = jax.nn.sigmoid(gate)
            silu = gate * sigmoid
            act_ref[spot, units] = (silu * up).astype(jnp.bfloat16)
            gate_back = back * up * sigmoid * (1.0 + gate * (1.0 - sigmoid))
            dgu_ref[spot, units] = gate_back.astype(jnp.bfloat16)
            dgu_ref[spot, up_units] = (back * silu).astype(jnp.bfloat16)

    @pl.loop(0, width // TILE)
    def _(step):
        columns = pl.ds(pl.multiple_of(step * TILE, TILE), TILE)
        down = column_product(act_ref[...], df_ref[:, columns])
        wide = column_product(rows_ref[:, columns], dgu_ref[...])
        if results is None:
            down_sum[:, columns] += down
            wide_sum[columns, :] += wide
        else:
            down_ref, wide_ref = results
            down_ref[:, columns] = (down_sum[:, columns] + down).astype(down_ref.dtype)
            wide_ref[columns, :] = (wide_sum[columns, :] + wide).astype(wide_ref.dtype)


def gather_glu_kernel(
    x_ref,
    wgu_hbm,
    wd_hbm,
    df_hbm,
    all_out_ref,
    act_ref,
    dgu_ref,
    down_ref,
    wide_ref,
    all_ref,
    wgu_ref,
    wd_ref,
    df_ref,
    down_sum,
    wide_sum,
    in_sem,
    out_sem,
    gather_send,
    gather_recv,
):
    rows = x_ref.shape[0]
    half = wd_ref.shape[0]
    fetch = [
        pltpu.make_async_copy(wgu_hbm, wgu_ref, in_sem.at[0]),
        pltpu.make_async_copy(wd_hbm.at[pl.ds(0, half)], wd_ref, in_sem.at[1]),
        pltpu.make_async_copy(df_hbm, df_ref, in_sem.at[2]),
    ]
    for copy in fetch:
        copy.start()
    gather = Gather(x_ref, all_ref, gather_send, gather_recv)
    me, x_next, y_next = gather.me, gather.x_next, gather.y_next
    greet((gather.sibling, x_next, y_next))
    gather.begin()
    all_ref[pl.ds(pl.multiple_of(me * rows, rows), rows), :] = x_ref[...]
    down_sum[...] = jnp.zeros_like(down_sum)
    wide_sum[...] = jnp.zeros_like(wide_sum)
    for copy in fetch:
        copy.wait()

    def work(owner, results=None):
        first = owner - lax.rem(owner, 2)
        spot = pl.ds(pl.multiple_of(first * rows, 2 * rows), 2 * rows)
        glu_block(
            all_ref.at[spot],
            df_ref.at[spot],
            wgu_ref,
            wd_ref,
            act_ref.at[spot],
            dgu_ref.at[spot],
            down_sum,
            wide_sum,
            results,
        )

    gather.take(4)
    work(me)
    for slot in (0, 2, 1, 3, 7, 8):
        gather.take(slot)
    work(x_next)
    for slot in (5, 6, 9, 10):
        gather.take(slot)
    work(y_next)
    gather.take(11)
    gather.take(12)
    keep = pltpu.make_async_copy(all_ref, all_out_ref, out_sem)
    keep.start()
    work(gather.diagonal, (down_ref, wide_ref))
    gather.finish()
    keep.wait()


def gather_glu(own_rows, wgu, own_down, df_all, number):
    rows, width = own_rows.shape
    count, half = PLANE * rows, wgu.shape[1] // 2
    low = jnp.bfloat16
    return pl.pallas_call(
        gather_glu_kernel,
        out_shape=[
            jax.ShapeDtypeStruct((count, width), low),
            jax.ShapeDtypeStruct((count, half), low),
            jax.ShapeDtypeStruct((count, 2 * half), low),
            jax.ShapeDtypeStruct((half, width), low),
            jax.ShapeDtypeStruct((width, 2 * half), low),
        ],
        in_specs=[VMEM, ANY, ANY, ANY],
        out_specs=[ANY] + [VMEM] * 4,
        scratch_shapes=[
            pltpu.VMEM((count, width), low),
            pltpu.VMEM(wgu.shape, low),
            pltpu.VMEM((half, width), low),
            pltpu.VMEM((count, width), low),
            pltpu.VMEM((half, width), jnp.float32),
            pltpu.VMEM((width, 2 * half), jnp.float32),
            pltpu.SemaphoreType.DMA((3,)),
            pltpu.SemaphoreType.DMA,
        ]
        + gather_scratch(),
        compiler_params=pltpu.CompilerParams(
            collective_id=number, has_side_effects=True, vmem_limit_bytes=58 * 2**20
        ),
        cost_estimate=SHORT,
        name=f"gather_glu_{number}",
    )(own_rows, wgu, own_down, df_all)


def glu_kernel(
    x_ref,
    df_ref,
    first_ref,
    both_hbm,
    act_ref,
    dgu_ref,
    grad_ref,
    wgu_ref,
    wd_ref,
    down_sum,
    wide_sum,
    sems,
):
    step = pl.program_id(0)
    half = wd_ref.shape[0]
    nd, _, both = grad_ref.shape
    count, units = wide_sum.shape[0] // PLANE // nd, half // nd

    @pl.when(step == 0)
    def _():
        copies = []
        for owner in range(nd):
            for place in range(PLANE):
                source = both_hbm.at[owner, pl.ds(place * count, count)]
                target = wgu_ref.at[pl.ds((place * nd + owner) * count, count)]
                copies.append(pltpu.make_async_copy(source, target, sems.at[owner, place]))
            for side in range(2):
                source = both_hbm.at[owner, pl.ds(PLANE * count + side * units, units)]
                target = wd_ref.at[pl.ds(owner * units, units), pl.ds(side * both, both)]
                copies.append(
                    pltpu.make_async_copy(source, target, sems.at[owner, PLANE + side])
                )
        for copy in copies:
            copy.start()
        down_sum[...] = jnp.zeros_like(down_sum)
        wide_sum[...] = jnp.zeros_like(wide_sum)
        for copy in copies:
            copy.wait()

    glu_block(x_ref, df_ref, wgu_ref, wd_ref, act_ref, dgu_ref, down_sum, wide_sum)

    @pl.when(step == pl.num_programs(0) - 1)
    def _():
        low = grad_ref.dtype
        for owner in range(nd):
            for place in range(PLANE):
                first = (place * nd + owner) * count
                part = wide_sum[first : first + count, :].astype(low)
                grad_ref[owner, place * count : (place + 1) * count, :] = part
            spot = slice(owner * units, (owner + 1) * units)
            for side in range(2):
                columns = slice(side * both, (side + 1) * both)
                start = PLANE * count + side * 2 * units
                grad_ref[owner, start : start + units, :] = first_ref[spot, columns]
                part = down_sum[spot, columns].astype(low)
                grad_ref[owner, start + units : start + 2 * units, :] = part


def glu(rows_all, df_all, gathered, down_first, number):
    nd = lax.axis_size("dp")
    count, width = rows_all.shape
    half, both = down_first.shape[0], gathered.shape[2]
    low = jnp.bfloat16
    step = 512
    once = pl.Buffered(1)
    return pl.pallas_call(
        glu_kernel,
        grid=(count // step,),
        out_shape=[
            jax.ShapeDtypeStruct((count, half), low),
            jax.ShapeDtypeStruct((count, 2 * half), low),
            jax.ShapeDtypeStruct((nd, 2 * width // nd, 2 * half), low),
            jax.ShapeDtypeStruct((width, both), low),
            jax.ShapeDtypeStruct((half, width), low),
        ],
        in_specs=[
            pl.BlockSpec((step, width), lambda i: (i, 0)),
            pl.BlockSpec((step, width), lambda i: (i, 0)),
            pl.BlockSpec((half, width), lambda i: (0, 0), pipeline_mode=once),
            ANY,
        ],
        out_specs=[
            pl.BlockSpec((step, half), lambda i: (i, 0)),
            pl.BlockSpec((step, 2 * half), lambda i: (i, 0)),
            pl.BlockSpec(
                (nd, 2 * width // nd, 2 * half), lambda i: (0, 0, 0), pipeline_mode=once
            ),
            pl.BlockSpec((width, both), lambda i: (0, 0), pipeline_mode=once),
            pl.BlockSpec((half, width), lambda i: (0, 0), pipeline_mode=once),
        ],
        scratch_shapes=[
            pltpu.VMEM((half, width), jnp.float32),
            pltpu.VMEM((width, 2 * half), jnp.float32),
            pltpu.SemaphoreType.DMA((nd, PLANE + 2)),
        ],
        compiler_params=pltpu.CompilerParams(vmem_limit_bytes=56 * 2**20),
        cost_estimate=SHORT,
        name=f"glu_{number}",
    )(rows_all, df_all, down_first, gathered)


def attention(normed_low, own_qkv, own_out, lengths_all, query_gain, key_gain):
    position, _, allowed = layout(lengths_all)
    half_width = HD // 2
    frequency = ROPE_BASE ** (jnp.arange(half_width, dtype=jnp.float32) * (-2.0 / HD))
    angles = position.reshape(-1, 1) * frequency[None, :]
    tables = (
        jnp.tile(jnp.cos(angles), (1, 4)),
        jnp.tile(jnp.sin(angles), (1, 4)),
        allowed.astype(jnp.float32),
        jnp.pad(
            jnp.stack([jnp.tile(query_gain, 2), jnp.tile(key_gain, 2)]), ((0, 6), (0, 0))
        ),
    )
    sums, *kept = attend(normed_low, own_qkv, own_out, tables, 3)

    def back(branch_own):
        normed_one_grad, part_attn, gain_grads = attend_back(
            branch_own, own_qkv, own_out, tables, kept, 9
        )
        query_gain_grad = gain_grads[0, :HD] + gain_grads[0, HD:]
        return normed_one_grad, part_attn, query_gain_grad, gain_grads[1, :HD]

    return sums, back


def last_kernel(
    ready,
    hidden_ref,
    valid_ref,
    act_a_ref,
    act_b_ref,
    wd_a_ref,
    wd_b_ref,
    half_ref,
    out_ref,
    wide_ref,
    sum_ref,
    own_sem,
    sems,
    *refs,
):
    others = plane_others(lax.axis_index("fsdp"))
    rows, width = out_ref.shape
    block = block_product((act_a_ref, act_b_ref), (wd_a_ref, wd_b_ref), rows, width, False)
    scatter = Scatter(sum_ref, block, refs)
    greet(others)
    order = (6, 7, 2, 4, 3, 5, 1)
    for number in order:
        for copy in put_half(half_ref, wide_ref, others, number, sems):
            copy.start()
    keep = keep_half(half_ref, wide_ref, own_sem)
    for copy in keep:
        copy.start()
    ready()
    scatter.for_sibling(0)
    scatter.for_sibling(1)
    scatter.for_far()
    scatter.for_sibling(2)
    scatter.for_near(0)
    scatter.for_sibling(3)
    scatter.for_near(1)
    scatter.finish_near(0)
    scatter.finish_near(1)
    scatter.own()
    scatter.finish()
    out_ref[...] = (hidden_ref[...] + valid_ref[...] * sum_ref[...]).astype(out_ref.dtype)
    for number in order:
        for copy in put_half(half_ref, wide_ref, others, number, sems):
            copy.wait()
    for copy in keep:
        copy.wait()


def last(hidden, valid_col, act_a, act_b, down_a, down_b, half, count, number):
    rows, width = hidden.shape
    arrays = (hidden, valid_col, act_a, act_b, down_a, down_b)
    places = (0, 2, 3, 4, 5)
    specs, stage = staged_specs(arrays, places)
    return pl.pallas_call(
        staged(last_kernel, len(arrays) + 1, places),
        out_shape=[
            jax.ShapeDtypeStruct((rows, width), jnp.bfloat16),
            jax.ShapeDtypeStruct((count, half.shape[1] * PLANE), half.dtype),
        ],
        in_specs=specs + [ANY],
        out_specs=[VMEM, ANY],
        scratch_shapes=[pltpu.VMEM((rows, width), jnp.float32)]
        + half_scratch()
        + scatter_scratch(rows, width)
        + stage,
        compiler_params=pltpu.CompilerParams(
            collective_id=number, has_side_effects=True, vmem_limit_bytes=56 * 2**20
        ),
        cost_estimate=SHORT,
        name=f"last_{number}",
    )(*arrays, half)


def adam_kernel(chunks, n_grads, per, norm_ref, *refs):
    grads, refs = refs[:n_grads], refs[n_grads:]
    states = [refs[place * per : (place + 1) * per] for place in range(3)]
    outs = [refs[(3 + place) * per : (4 + place) * per] for place in range(3)]
    refs = refs[6 * per :]
    grad_bufs, refs = refs[:n_grads], refs[n_grads:]
    bufs = [refs[place * per : (place + 1) * per] for place in range(3)]
    grad_sems, in_sems, out_sems = refs[3 * per :]
    factor = norm_ref[1:2, 0:1]
    first_scale = 1.0 / (1.0 - FIRST_DECAY**STEP)
    second_scale = 1.0 / (1.0 - SECOND_DECAY**STEP)

    def fetch(number):
        which, rows, sources, _ = chunks[number]
        copies = [
            pltpu.make_async_copy(
                grads[array].at[spot], grad_bufs[array].at[spot], grad_sems.at[number, place]
            )
            for place, (array, spot) in enumerate(sources)
        ]
        for place in range(3):
            copies.append(
                pltpu.make_async_copy(
                    states[place][which].at[rows],
                    bufs[place][which].at[rows],
                    in_sems.at[number, place],
                )
            )
        return copies

    def put(number):
        which, rows, _, _ = chunks[number]
        return [
            pltpu.make_async_copy(
                bufs[place][which].at[rows], outs[place][which].at[rows], out_sems.at[number, place]
            )
            for place in range(3)
        ]

    def update(which, rows, columns, grad):
        weights, firsts, seconds = (bufs[place][which] for place in range(3))
        clipped = grad.astype(jnp.float32) * factor
        weight = weights[rows, columns]
        first = FIRST_DECAY * firsts[rows, columns] + (1.0 - FIRST_DECAY) * clipped
        second = SECOND_DECAY * seconds[rows, columns] + (1.0 - SECOND_DECAY) * clipped * clipped
        root = jnp.sqrt(second * second_scale) + ADAM_EPSILON
        change = first * first_scale / root + WEIGHT_DECAY * weight
        weights[rows, columns] = weight - LEARN_RATE * change
        firsts[rows, columns] = first
        seconds[rows, columns] = second

    for number in range(len(chunks)):
        for copy in fetch(number):
            copy.start()
    for number in range(len(chunks)):
        which, rows, _, loops = chunks[number]
        for copy in fetch(number):
            copy.wait()
        for steps, parts in loops:

            @pl.loop(0, steps)
            def _(step):
                for array, grad_rows, columns_of, grad_columns_of, width in parts:
                    columns = pl.ds(pl.multiple_of(columns_of(step), 128), width)
                    grad_columns = pl.ds(pl.multiple_of(grad_columns_of(step), 128), width)
                    update(which, rows, columns, grad_bufs[array][grad_rows, grad_columns])

        for copy in put(number):
            copy.start()
    for number in range(len(chunks)):
        for copy in put(number):
            copy.wait()


def adam_matrices(norm, grad_qkv, grad_out, grad_a, grad_b, sums_b, weights, firsts, seconds):
    half = grad_a.shape[1] // 2 // PLANE
    nd = lax.axis_size("dp")
    unit = half // nd
    count = weights[3].shape[0]
    behind = sums_b.shape[0] - 2 * count
    side_width = sums_b.shape[1]
    width = 512
    chunks = []

    def straight(step):
        return step * width

    for row in range(0, weights[2].shape[0], 16):
        rows = pl.ds(row, 16)
        parts = []
        for part in range(2):
            for owner in range(nd):

                def columns_of(step, part=part, owner=owner):
                    return step * 2 * half + (2 * owner + part) * unit

                def grad_columns_of(step, owner=owner):
                    return step * half + owner * unit

                parts.append((2 + part, rows, columns_of, grad_columns_of, unit))
        loops = [(2 * PLANE, parts)]
        chunks.append((2, rows, [(2, rows), (3, rows)], loops))
    for row in range(0, count, 64):
        sources, loops = [], []
        for side in range(2):
            spot = pl.ds(behind + side * count + row, 64)
            sources.append((4, spot))

            def columns_of(step, side=side):
                return side * side_width + step * width

            loops.append((side_width // width, [(4, spot, columns_of, straight, width)]))
        chunks.append((3, pl.ds(row, 64), sources, loops))
    for which in range(2):
        for row in range(0, weights[which].shape[0], 32):
            rows = pl.ds(row, 32)
            steps = weights[which].shape[1] // width
            loops = [(steps, [(which, rows, straight, straight, width)])]
            chunks.append((which, rows, [(which, rows)], loops))
    grads = (grad_qkv, grad_out, grad_a, grad_b, sums_b)
    per = len(weights)
    number = len(chunks)
    outs = pl.pallas_call(
        functools.partial(adam_kernel, chunks, len(grads), per),
        out_shape=[jax.ShapeDtypeStruct(weight.shape, jnp.float32) for weight in weights] * 3,
        in_specs=[VMEM] + [ANY] * (len(grads) + 3 * per),
        out_specs=[ANY] * (3 * per),
        scratch_shapes=[pltpu.VMEM(grad.shape, grad.dtype) for grad in grads]
        + [pltpu.VMEM(weight.shape, jnp.float32) for weight in weights] * 3
        + [
            pltpu.SemaphoreType.DMA((number, 2)),
            pltpu.SemaphoreType.DMA((number, 3)),
            pltpu.SemaphoreType.DMA((number, 3)),
        ],
        compiler_params=pltpu.CompilerParams(vmem_limit_bytes=60 * 2**20),
        name="adam_matrices",
    )(norm, *grads, *weights, *firsts, *seconds)
    return outs[:per], outs[per : 2 * per], outs[2 * per :]


def scatter_rows(values, axis):
    return lax.psum_scatter(values, "dp", scatter_dimension=axis, tiled=True)


def per_device_plane(
    nf,
    nd,
    tokens,
    cotangent,
    order,
    lengths,
    w_qkv,
    w_out,
    w_gate_up,
    w_down,
    gains,
    first_qkv,
    first_out,
    first_gate_up,
    first_down,
    first_gains,
    second_qkv,
    second_out,
    second_gate_up,
    second_down,
    second_gains,
):
    low = jnp.bfloat16
    q_width = HEADS // nf * HD
    kv_all = KVH * HD
    hidden_own = FF // nf
    rows_own = w_qkv.shape[0]

    order_row = order[0]
    places = jnp.arange(TOK_DEV, dtype=jnp.int32)
    inverse = jnp.zeros((TOK_DEV,), jnp.int32).at[order_row].set(places)
    rows_in = tokens[order_row].astype(jnp.float32)
    back_rows = cotangent[order_row].astype(jnp.float32)
    attn_gain = gains[:D]
    ffn_gain = gains[D : 2 * D]
    query_gain = gains[2 * D : 2 * D + HD]
    key_gain = gains[2 * D + HD :]

    _, valid_rows, _ = layout(lengths)
    valid_col = valid_rows.reshape(TOK_DEV, 1)

    qkv_low = w_qkv.astype(low)

    def head_blocks(rows, width):
        return jnp.swapaxes(rows.reshape(rows_own, -1, width), 0, 1)

    qkv_blocks = jnp.concatenate(
        [
            head_blocks(qkv_low[:, :D], q_width),
            head_blocks(qkv_low[:, D : D + kv_all], HD),
            head_blocks(qkv_low[:, D + kv_all :], HD),
        ],
        axis=2,
    )
    wide = q_width + 2 * HD
    down_low = w_down.astype(low)
    units = down_low.shape[0] // 2
    down_a = lax.all_gather(down_low[:units], "dp", axis=0, tiled=True)
    own_qkv, own_out, half_a, half_b, down_back, notes = start(
        qkv_blocks,
        w_out.astype(low),
        w_gate_up,
        (valid_col * back_rows).astype(low),
        jnp.pad(lengths, ((0, 8 - MB), (0, 128 - SEQS))),
        1,
    )
    own_qkv = own_qkv.reshape(D, wide)
    lengths_all = notes[:, :MB, :SEQS].reshape(nf * MB, SEQS)
    half_a, down_a = lax.optimization_barrier((half_a, down_a))
    own_a = lax.all_gather(half_a, "dp", axis=1, tiled=True).reshape(D, hidden_own)
    with_down = jnp.concatenate(
        [half_b.reshape(nf * rows_own, hidden_own), down_low[units:, :hidden_own]]
        + [down_low[units:, hidden_own:]],
        axis=0,
    )
    gathered_b = lax.all_gather(with_down, "dp", axis=0)

    normed_one, norm_one_pull = jax.vjp(rms_norm, rows_in, attn_gain)
    attention_sums, attention_back = attention(
        normed_one.astype(low), own_qkv, own_out, lengths_all, query_gain, key_gain
    )
    hidden = rows_in + valid_col * attention_sums

    normed_two, norm_two_pull = jax.vjp(rms_norm, hidden, ffn_gain)
    norm_two_all, act_a, back_a, grad_down_a, part_a = gather_glu(
        normed_two.astype(low), own_a, down_a, down_back, 5
    )
    sums_a = scatter_rows(part_a.reshape(nf, nd * rows_own, hidden_own), 1)
    act_b, back_b, part_b, own_b, down_b = glu(norm_two_all, down_back, gathered_b, grad_down_a, 6)
    sums_b = scatter_rows(part_b, 0)[0]
    normed_two_grad = product_scatter((back_a, back_b), (own_a, own_b), 8, turned=True)
    hidden_norm_grad, ffn_gain_grad = norm_two_pull(normed_two_grad)
    hidden_grad = back_rows + hidden_norm_grad

    branch_own = (valid_col * hidden_grad).astype(low)
    branch_own, sums_a = lax.optimization_barrier((branch_own, sums_a))
    normed_one_grad, part_attn, query_gain_grad, key_gain_grad = attention_back(branch_own)
    sums_attn = scatter_rows(part_attn.reshape(nf, nd * rows_own, wide + q_width), 1)
    normed_one_grad, act_a = lax.optimization_barrier((normed_one_grad, act_a))
    output, grad_a = last(
        hidden,
        valid_col,
        act_a,
        act_b,
        down_a,
        down_b,
        sums_a.reshape(nf * rows_own, hidden_own),
        rows_own,
        7,
    )
    output, sums_b = lax.optimization_barrier((output, sums_b))
    grad_b, squares_b = exchange_half(sums_b, rows_own, 11)
    rows_grad, attn_gain_grad = norm_one_pull(normed_one_grad)
    input_grad = (hidden_grad + rows_grad)[inverse]
    output_all = output[inverse]

    early_squares = jnp.sum(jnp.square(sums_a.astype(jnp.float32))) + jnp.sum(squares_b)
    input_grad, output_all, early_squares, sums_attn = lax.optimization_barrier(
        (input_grad, output_all, early_squares, sums_attn)
    )
    gain_sum = jnp.concatenate([attn_gain_grad, ffn_gain_grad, query_gain_grad, key_gain_grad])
    gain_total, norm, grad_qkv, grad_out = sum_everywhere(
        gain_sum, early_squares, sums_attn, wide, 13
    )
    global_norm, factor = norm[0, 0], norm[1, 0]
    new_matrices, next_firsts, next_seconds = adam_matrices(
        norm,
        grad_qkv,
        grad_out,
        grad_a,
        grad_b,
        sums_b,
        (w_qkv, w_out, w_gate_up, w_down),
        (first_qkv, first_out, first_gate_up, first_down),
        (second_qkv, second_out, second_gate_up, second_down),
    )
    new_gains, next_first_gains, next_second_gains = adam_step(
        gains, first_gains, second_gains, gain_total, factor, GAIN_RATE, 0.0
    )
    return (
        output_all,
        input_grad,
        global_norm,
        *new_matrices,
        new_gains,
        *next_firsts,
        next_first_gains,
        *next_seconds,
        next_second_gains,
    )


def gather_tokens(rows):
    return lax.all_gather(rows, "fsdp", axis=0, tiled=True)


def scatter_tokens(rows):
    return lax.psum_scatter(
        rows.astype(jnp.bfloat16), "fsdp", scatter_dimension=0, tiled=True
    ).astype(jnp.float32)


def swap(blocks):
    return lax.all_to_all(blocks, "fsdp", split_axis=0, concat_axis=0, tiled=True)


def per_device_plain(
    nf,
    nd,
    tokens,
    cotangent,
    order,
    lengths,
    w_qkv,
    w_out,
    w_gate_up,
    w_down,
    gains,
    first_qkv,
    first_out,
    first_gate_up,
    first_down,
    first_gains,
    second_qkv,
    second_out,
    second_gate_up,
    second_down,
    second_gains,
):
    low = jnp.bfloat16
    kvl = max(KVH // nf, 1)
    rep = max(nf // KVH, 1)
    heads_own = HEADS // nf
    group = heads_own // kvl
    q_width, kv_width = heads_own * HD, kvl * HD
    kv_all = KVH * HD
    hidden_own = FF // nf
    rows_own = w_qkv.shape[0]
    n_mb = nf * MB

    def head_blocks(rows, width):
        return jnp.swapaxes(rows.reshape(rows_own, -1, width), 0, 1)

    qkv_low = w_qkv.astype(low)
    qkv_blocks = jnp.concatenate(
        [
            head_blocks(qkv_low[:, :D], q_width),
            jnp.repeat(head_blocks(qkv_low[:, D : D + kv_all], kv_width), rep, axis=0),
            jnp.repeat(head_blocks(qkv_low[:, D + kv_all :], kv_width), rep, axis=0),
        ],
        axis=2,
    )
    wide = q_width + 2 * kv_width
    own_qkv = lax.all_gather(swap(qkv_blocks), "dp", axis=1, tiled=True).reshape(D, wide)
    own_out = lax.all_gather(w_out.astype(low), "dp", axis=0, tiled=True)
    gate_up_blocks = jnp.transpose(
        w_gate_up.astype(low).reshape(rows_own, 2, nf, hidden_own), (2, 0, 1, 3)
    ).reshape(nf, rows_own, 2 * hidden_own)
    own_gate_up = lax.all_gather(swap(gate_up_blocks), "dp", axis=1, tiled=True).reshape(
        D, 2 * hidden_own
    )
    own_down = lax.all_gather(w_down.astype(low), "dp", axis=0, tiled=True)

    order_row = order[0]
    places = jnp.arange(TOK_DEV, dtype=jnp.int32)
    inverse = jnp.zeros((TOK_DEV,), jnp.int32).at[order_row].set(places)
    rows_in = tokens[order_row].astype(jnp.float32)
    back_rows = cotangent[order_row].astype(jnp.float32)
    attn_gain = gains[:D]
    ffn_gain = gains[D : 2 * D]
    query_gain = gains[2 * D : 2 * D + HD]
    key_gain = gains[2 * D + HD :]
    score_scale = HD ** (-0.5)

    lengths_all = gather_tokens(lengths)
    position, _, allowed = layout(lengths_all)
    _, valid_rows, _ = layout(lengths)
    valid_col = valid_rows.reshape(TOK_DEV, 1)
    allowed = allowed[:, None, None]
    cosine_table, sine_table = rope_tables(position.reshape(-1))

    normed_one, norm_one_pull = jax.vjp(rms_norm, rows_in, attn_gain)
    norm_one_all = gather_tokens(normed_one.astype(low))
    projected = product(norm_one_all, own_qkv)
    n_rows = norm_one_all.shape[0]
    query_raw = projected[:, :q_width].reshape(n_rows, heads_own, HD)
    key_raw = projected[:, q_width : q_width + kv_width].reshape(n_rows, kvl, HD)
    values_low = projected[:, q_width + kv_width :].reshape(n_mb, MB_TOK, kvl, HD).astype(low)

    def turn_heads(query_in, key_in, query_scale, key_scale):
        return (
            rotate(rms_norm(query_in, query_scale), cosine_table, sine_table),
            rotate(rms_norm(key_in, key_scale), cosine_table, sine_table),
        )

    turned, turn_pull = jax.vjp(turn_heads, query_raw, key_raw, query_gain, key_gain)
    queries_low = turned[0].astype(low).reshape(n_mb, MB_TOK, kvl, group, HD)
    keys_low = turned[1].astype(low).reshape(n_mb, MB_TOK, kvl, HD)
    scores = (
        jnp.einsum("mtkgd,mukd->mkgtu", queries_low, keys_low, preferred_element_type=jnp.float32)
        * score_scale
    )
    scores = jnp.where(allowed, scores, MASKED)
    row_peak = jnp.max(scores, axis=-1, keepdims=True)
    powers = jnp.exp(scores - row_peak)
    totals = jnp.sum(powers, axis=-1, keepdims=True)
    probs = powers / totals
    probs_low = probs.astype(low)
    attended = jnp.einsum(
        "mkgtu,mukd->mtkgd", probs_low, values_low, preferred_element_type=jnp.float32
    )
    attended_low = attended.reshape(n_rows, q_width).astype(low)
    hidden = rows_in + valid_col * scatter_tokens(product(attended_low, own_out))

    normed_two, norm_two_pull = jax.vjp(rms_norm, hidden, ffn_gain)
    norm_two_all = gather_tokens(normed_two.astype(low))
    down_back = gather_tokens((valid_col * back_rows).astype(low))
    gate_up = product(norm_two_all, own_gate_up)
    activation, glu_pull = jax.vjp(swiglu, gate_up[:, :hidden_own], gate_up[:, hidden_own:])
    activation_low = activation.astype(low)
    output = hidden + valid_col * scatter_tokens(product(activation_low, own_down))
    gate_back, up_back = glu_pull(contract_last(down_back, own_down))
    gate_up_back = jnp.concatenate([gate_back.astype(low), up_back.astype(low)], axis=1)
    normed_two_grad = scatter_tokens(contract_last(gate_up_back, own_gate_up))
    grad_down = lax.psum_scatter(
        column_product(activation_low, down_back).astype(low),
        "dp",
        scatter_dimension=0,
        tiled=True,
    ).astype(jnp.float32)
    grad_gate_up = lax.psum_scatter(
        column_product(norm_two_all, gate_up_back)
        .astype(low)
        .reshape(nf, nd * rows_own, 2 * hidden_own),
        "dp",
        scatter_dimension=1,
        tiled=True,
    )
    grad_gate_up = jnp.transpose(
        swap(grad_gate_up).reshape(nf, rows_own, 2, hidden_own), (1, 2, 0, 3)
    ).reshape(rows_own, 2 * FF)
    grad_gate_up = grad_gate_up.astype(jnp.float32)
    hidden_norm_grad, ffn_gain_grad = norm_two_pull(normed_two_grad)
    hidden_grad = back_rows + hidden_norm_grad

    branch_back = gather_tokens((valid_col * hidden_grad).astype(low))
    attended_back = contract_last(branch_back, own_out).astype(low)
    grad_out = lax.psum_scatter(
        column_product(attended_low, branch_back).astype(low),
        "dp",
        scatter_dimension=0,
        tiled=True,
    ).astype(jnp.float32)
    attended_five = attended_back.reshape(n_mb, MB_TOK, kvl, group, HD)
    probs_grad = jnp.einsum(
        "mtkgd,mukd->mkgtu", attended_five, values_low, preferred_element_type=jnp.float32
    )
    spread = jnp.sum(probs * probs_grad, axis=-1, keepdims=True)
    score_back = (probs * (probs_grad - spread)).astype(low)
    query_grad = (
        jnp.einsum("mkgtu,mukd->mtkgd", score_back, keys_low, preferred_element_type=jnp.float32)
        * score_scale
    )
    key_grad = (
        jnp.einsum("mkgtu,mtkgd->mukd", score_back, queries_low, preferred_element_type=jnp.float32)
        * score_scale
    )
    value_grad = jnp.einsum(
        "mkgtu,mtkgd->mukd", probs_low, attended_five, preferred_element_type=jnp.float32
    )
    query_in_grad, key_in_grad, query_gain_grad, key_gain_grad = turn_pull(
        (query_grad.reshape(n_rows, heads_own, HD), key_grad.reshape(n_rows, kvl, HD))
    )
    projected_back = jnp.concatenate(
        [
            query_in_grad.reshape(n_rows, q_width),
            key_in_grad.reshape(n_rows, kv_width),
            value_grad.reshape(n_rows, kv_width),
        ],
        axis=1,
    ).astype(low)
    normed_one_grad = scatter_tokens(contract_last(projected_back, own_qkv))
    grad_qkv = lax.psum_scatter(
        column_product(norm_one_all, projected_back)
        .astype(low)
        .reshape(nf, nd * rows_own, wide),
        "dp",
        scatter_dimension=1,
        tiled=True,
    )
    grad_blocks = swap(grad_qkv).astype(jnp.float32)

    def head_rows(blocks, times):
        merged = jnp.sum(blocks.reshape(nf // times, times, rows_own, -1), axis=1)
        return jnp.swapaxes(merged, 0, 1).reshape(rows_own, -1)

    grad_qkv = jnp.concatenate(
        [
            head_rows(grad_blocks[:, :, :q_width], 1),
            head_rows(grad_blocks[:, :, q_width : q_width + kv_width], rep),
            head_rows(grad_blocks[:, :, q_width + kv_width :], rep),
        ],
        axis=1,
    )
    rows_grad, attn_gain_grad = norm_one_pull(normed_one_grad)
    input_grad = (hidden_grad + rows_grad)[inverse]
    output_all = output.astype(low)[inverse]

    owned = (grad_qkv, grad_out, grad_gate_up, grad_down)
    local_squares = (
        jnp.sum(owned[0] * owned[0])
        + jnp.sum(owned[1] * owned[1])
        + jnp.sum(owned[2] * owned[2])
        + jnp.sum(owned[3] * owned[3])
    )
    gain_sum = jnp.concatenate([attn_gain_grad, ffn_gain_grad, query_gain_grad, key_gain_grad])
    gain_total, square_total = lax.psum((gain_sum, local_squares), ("fsdp", "dp"))
    global_norm = jnp.sqrt(square_total + jnp.sum(gain_total * gain_total))
    factor = CLIP_NORM / jnp.maximum(global_norm, CLIP_NORM)
    new_qkv, next_first_qkv, next_second_qkv = adam_step(
        w_qkv, first_qkv, second_qkv, owned[0], factor, LEARN_RATE, WEIGHT_DECAY
    )
    new_out, next_first_out, next_second_out = adam_step(
        w_out, first_out, second_out, owned[1], factor, LEARN_RATE, WEIGHT_DECAY
    )
    new_gate_up, next_first_gate_up, next_second_gate_up = adam_step(
        w_gate_up, first_gate_up, second_gate_up, owned[2], factor, LEARN_RATE, WEIGHT_DECAY
    )
    new_down, next_first_down, next_second_down = adam_step(
        w_down, first_down, second_down, owned[3], factor, LEARN_RATE, WEIGHT_DECAY
    )
    new_gains, next_first_gains, next_second_gains = adam_step(
        gains, first_gains, second_gains, gain_total, factor, GAIN_RATE, 0.0
    )
    return (
        output_all,
        input_grad,
        global_norm,
        new_qkv,
        new_out,
        new_gate_up,
        new_down,
        new_gains,
        next_first_qkv,
        next_first_out,
        next_first_gate_up,
        next_first_down,
        next_first_gains,
        next_second_qkv,
        next_second_out,
        next_second_gate_up,
        next_second_down,
        next_second_gains,
    )


def solution(mesh):
    nf, nd = mesh.shape["fsdp"], mesh.shape["dp"]
    fits = nf == PLANE and KVH == PLANE and nd > 1 and FF // nf % (256 * nd) == 0
    per_device = per_device_plane if fits else per_device_plain
    in_specs = (
        P(("fsdp", "dp"), None),
        P(("fsdp", "dp"), None),
        P(("fsdp", "dp"), None),
        P(("fsdp", "dp"), None),
        P(("fsdp", "dp"), None),
        P(("fsdp", "dp"), None),
        P(("fsdp", "dp"), None),
        P(("fsdp", "dp"), None),
        P(),
        P(("fsdp", "dp"), None),
        P(("fsdp", "dp"), None),
        P(("fsdp", "dp"), None),
        P(("fsdp", "dp"), None),
        P(),
        P(("fsdp", "dp"), None),
        P(("fsdp", "dp"), None),
        P(("fsdp", "dp"), None),
        P(("fsdp", "dp"), None),
        P(),
    )
    out_specs = (
        P(("fsdp", "dp"), None),
        P(("fsdp", "dp"), None),
        P(),
        P(("fsdp", "dp"), None),
        P(("fsdp", "dp"), None),
        P(("fsdp", "dp"), None),
        P(("fsdp", "dp"), None),
        P(),
        P(("fsdp", "dp"), None),
        P(("fsdp", "dp"), None),
        P(("fsdp", "dp"), None),
        P(("fsdp", "dp"), None),
        P(),
        P(("fsdp", "dp"), None),
        P(("fsdp", "dp"), None),
        P(("fsdp", "dp"), None),
        P(("fsdp", "dp"), None),
        P(),
    )
    return jax.shard_map(
        functools.partial(per_device, nf, nd), mesh=mesh, in_specs=in_specs, out_specs=out_specs, check_vma=False
    )
```

```python
import functools

import jax
import jax.numpy as jnp
from jax import lax
from jax.experimental import pallas as pl
from jax.experimental.pallas import tpu as pltpu
from jax.sharding import PartitionSpec as P

D = 2048
HEADS = 32
HD = 64
KVH = 8
FF = 8192
TOK_DEV = 256
MB = 2
SEQS = 3
STEP = 10
MB_TOK = 128


EPSILON = 1e-05
ROPE_BASE = 1000000.0
FIRST_DECAY = 0.9
SECOND_DECAY = 0.95
LEARN_RATE = 0.05
GAIN_RATE = 2.0
WEIGHT_DECAY = 0.1
ADAM_EPSILON = 1e-08
CLIP_NORM = 1.0
GAIN_LINES = (2 * D + 2 * HD) // 128
MASKED = -1e30


def rms_norm(values, gain_vec):
    return (
        values * lax.rsqrt(jnp.mean(values * values, axis=-1, keepdims=True) + EPSILON) * gain_vec
    )


def rope_tables(position):
    half_width = HD // 2
    frequency = ROPE_BASE ** (jnp.arange(half_width, dtype=jnp.float32) * (-2.0 / HD))
    angles = position[:, None] * frequency[None, :]
    return (jnp.cos(angles)[:, None, :], jnp.sin(angles)[:, None, :])


def rotate(values, cosine_table, sine_table):
    half_width = HD // 2
    first_part = values[..., :half_width]
    second_part = values[..., half_width:]
    return jnp.concatenate(
        [
            first_part * cosine_table - second_part * sine_table,
            second_part * cosine_table + first_part * sine_table,
        ],
        axis=-1,
    )


def layout(lengths_rows):
    seq_ends = jnp.cumsum(lengths_rows, axis=-1)
    places = jnp.arange(MB_TOK, dtype=jnp.int32)
    passed = (places[None, :, None] >= seq_ends[:, None, :]).astype(jnp.int32)
    segment = jnp.sum(passed, axis=-1)
    starts = jnp.sum(passed * lengths_rows[:, None, :], axis=-1)
    position = (places[None, :] - starts).astype(jnp.float32)
    valid_rows = (segment < SEQS - 1).astype(jnp.float32)
    allowed = (segment[:, :, None] == segment[:, None, :]) & (
        places[None, None, :] <= places[None, :, None]
    )
    return (position, valid_rows, allowed)


def swiglu(gate, up):
    return jax.nn.silu(gate) * up


def column_product(left_side, right_side):
    return lax.dot_general(
        left_side, right_side, (((0,), (0,)), ((), ())), preferred_element_type=jnp.float32
    )


def contract_last(left_side, right_side):
    return lax.dot_general(
        left_side, right_side, (((1,), (1,)), ((), ())), preferred_element_type=jnp.float32
    )


def product(left_side, right_side):
    return jnp.dot(left_side, right_side, preferred_element_type=jnp.float32)


def adam_step(weight, first_state, second, gradient, factor, step_rate, decay_rate):
    clipped = gradient * factor
    first_new = FIRST_DECAY * first_state + (1.0 - FIRST_DECAY) * clipped
    second_new = SECOND_DECAY * second + (1.0 - SECOND_DECAY) * clipped * clipped
    first_hat = first_new / (1.0 - FIRST_DECAY**STEP)
    second_hat = second_new / (1.0 - SECOND_DECAY**STEP)
    weight_new = weight - step_rate * (
        first_hat / (jnp.sqrt(second_hat) + ADAM_EPSILON) + decay_rate * weight
    )
    return (weight_new, first_new, second_new)


MESH = pl.DeviceIdType.MESH
ANY = pl.BlockSpec(memory_space=pl.ANY)
VMEM = pl.BlockSpec(memory_space=pltpu.VMEM)
PLANE = 8
TILE = 512
GLU_TILE = 256
SHORT = pl.CostEstimate(flops=0, bytes_accessed=1024, transcendentals=0)


def flip(index, bit):
    step = 2**bit
    return index + step * (1 - 2 * lax.rem(lax.div(index, step), 2))


def plane_others(me):
    others = []
    for number in range(1, PLANE):
        other = me
        for bit in range(3):
            if (number >> bit) & 1:
                other = flip(other, bit)
        others.append(other)
    return others


def greet(devices):
    barrier = pltpu.get_barrier_semaphore()
    for device in devices:
        pl.semaphore_signal(barrier, inc=1, device_id={"fsdp": device}, device_id_type=MESH)
    pl.semaphore_wait(barrier, len(devices))


def half_pieces(half_ref, wide_ref, me, other, count):
    half_width = half_ref.shape[1] // 2
    for side in range(2):
        first = pl.multiple_of(side * half_width * PLANE + me * half_width, 128)
        source = half_ref.at[pl.ds(pl.multiple_of(other * count, count), count)]
        yield (
            source.at[:, pl.ds(side * half_width, half_width)],
            wide_ref.at[:, pl.ds(first, half_width)],
        )


def put_half(half_ref, wide_ref, others, number, sems):
    me, other = lax.axis_index("fsdp"), others[number - 1]
    pairs = half_pieces(half_ref, wide_ref, me, other, wide_ref.shape[0])
    return [
        pltpu.make_async_remote_copy(
            src_ref=source,
            dst_ref=target,
            send_sem=sems.at[0, 2 * number + side],
            recv_sem=sems.at[1, 2 * number + side],
            device_id={"fsdp": other},
            device_id_type=MESH,
        )
        for side, (source, target) in enumerate(pairs)
    ]


def keep_half(half_ref, wide_ref, sems):
    me = lax.axis_index("fsdp")
    return [
        pltpu.make_async_copy(source, target, sems.at[side])
        for side, (source, target) in enumerate(
            half_pieces(half_ref, wide_ref, me, me, wide_ref.shape[0])
        )
    ]


def columns_kernel(half_ref, wide_ref, squares_ref, own_sem, sems):
    others = plane_others(lax.axis_index("fsdp"))
    greet(others)
    order = (6, 7, 2, 4, 3, 5, 1)
    for number in order:
        for copy in put_half(half_ref, wide_ref, others, number, sems):
            copy.start()
    keep = keep_half(half_ref, wide_ref, own_sem)
    for copy in keep:
        copy.start()
    squares_ref[...] = jnp.zeros_like(squares_ref)

    @pl.loop(0, half_ref.shape[0] // 128)
    def _(step):
        spot = pl.ds(pl.multiple_of(step * 128, 128), 128)
        values = half_ref[spot, :].astype(jnp.float32)
        squares_ref[...] += jnp.sum(values * values, axis=0, keepdims=True)

    for number in order:
        for copy in put_half(half_ref, wide_ref, others, number, sems):
            copy.wait()
    for copy in keep:
        copy.wait()


def half_scratch():
    return [pltpu.SemaphoreType.DMA((2,)), pltpu.SemaphoreType.DMA((2, 2 * PLANE))]


def exchange_half(half, count, number):
    return pl.pallas_call(
        columns_kernel,
        out_shape=[
            jax.ShapeDtypeStruct((count, half.shape[1] * PLANE), half.dtype),
            jax.ShapeDtypeStruct((1, half.shape[1]), jnp.float32),
        ],
        in_specs=[VMEM],
        out_specs=[ANY, VMEM],
        scratch_shapes=half_scratch(),
        compiler_params=pltpu.CompilerParams(collective_id=number, has_side_effects=True),
        cost_estimate=SHORT,
        name=f"exchange_half_{number}",
    )(half)


def sum_kernel(
    nd,
    x_ref,
    blocks_ref,
    out_ref,
    norm_ref,
    qkv_ref,
    gout_ref,
    swapped_ref,
    plane_in,
    line_in,
    total,
    mine,
    own_sem,
    plane_sems,
    line_sems,
    block_sems,
):
    me, line = lax.axis_index("fsdp"), lax.axis_index("dp")
    wide = swapped_ref.shape[2]
    q_width = wide - 2 * HD
    blocks = blocks_ref[...].astype(jnp.float32)
    squares = jnp.sum(blocks * blocks, axis=(0, 1, 2), keepdims=True).reshape(1, 1)
    lines = lax.broadcasted_iota(jnp.int32, x_ref.shape, 0)
    lane = lax.broadcasted_iota(jnp.int32, x_ref.shape, 1)
    spot = jnp.logical_and(lines == GAIN_LINES, lane == 0)
    mine[...] = x_ref[...] + jnp.where(spot, squares, 0.0)
    others = plane_others(me)
    steps = [lax.rem(line + step, nd) for step in range(1, nd)]
    barrier = pltpu.get_barrier_semaphore()
    for other in others:
        pl.semaphore_signal(barrier, inc=1, device_id={"fsdp": other}, device_id_type=MESH)
    for other in steps:
        pl.semaphore_signal(barrier, inc=1, device_id={"dp": other}, device_id_type=MESH)
    pl.semaphore_wait(barrier, len(others) + len(steps))

    def to_plane(number):
        return pltpu.make_async_remote_copy(
            src_ref=mine,
            dst_ref=plane_in.at[me],
            send_sem=plane_sems.at[0, number],
            recv_sem=plane_sems.at[1, number],
            device_id={"fsdp": others[number]},
            device_id_type=MESH,
        )

    def to_line(number):
        return pltpu.make_async_remote_copy(
            src_ref=total,
            dst_ref=line_in.at[line],
            send_sem=line_sems.at[0, number],
            recv_sem=line_sems.at[1, number],
            device_id={"dp": steps[number]},
            device_id_type=MESH,
        )

    def put_block(number):
        return pltpu.make_async_remote_copy(
            src_ref=blocks_ref.at[others[number], :, pl.ds(0, wide)],
            dst_ref=swapped_ref.at[me],
            send_sem=block_sems.at[0, number],
            recv_sem=block_sems.at[1, number],
            device_id={"fsdp": others[number]},
            device_id_type=MESH,
        )

    keep = [
        pltpu.make_async_copy(
            blocks_ref.at[me, :, pl.ds(0, wide)], swapped_ref.at[me], own_sem.at[PLANE]
        )
    ]
    for place in range(PLANE):
        keep.append(
            pltpu.make_async_copy(
                blocks_ref.at[place, :, pl.ds(wide, q_width)],
                gout_ref.at[:, pl.ds(place * q_width, q_width)],
                own_sem.at[place],
            )
        )
    for number in range(PLANE - 1):
        to_plane(number).start()
    for number in range(PLANE - 1):
        put_block(number).start()
    for copy in keep:
        copy.start()
    plane_in[me] = mine[...]
    for number in range(PLANE - 1):
        to_plane(number).wait()
    part = plane_in[0]
    for place in range(1, PLANE):
        part = part + plane_in[place]
    total[...] = part
    line_in[line] = part
    for number in range(nd - 1):
        to_line(number).start()
    for number in range(PLANE - 1):
        put_block(number).wait()
    for copy in keep:
        copy.wait()
    first_head = lax.broadcasted_iota(jnp.int32, (1, 2 * HD), 1) < HD
    for place in range(0, PLANE, 2):
        pair = []
        for block in (place, place + 1):
            values = swapped_ref[block].astype(jnp.float32)
            qkv_ref[:, block * q_width : (block + 1) * q_width] = swapped_ref[block, :, :q_width]
            pair.append(values[:, q_width:])
        columns = pl.ds(PLANE * q_width + place * HD, 2 * HD)
        both = jnp.where(first_head, pair[0], pltpu.roll(pair[1], HD, 1))
        qkv_ref[:, columns] = both.astype(qkv_ref.dtype)
        columns = pl.ds(PLANE * (q_width + HD) + place * HD, 2 * HD)
        both = jnp.where(first_head, pltpu.roll(pair[0], HD, 1), pair[1])
        qkv_ref[:, columns] = both.astype(qkv_ref.dtype)
    for number in range(nd - 1):
        to_line(number).wait()
    part = line_in[0]
    for place in range(1, nd):
        part = part + line_in[place]
    out_ref[...] = part
    gains = part[:GAIN_LINES]
    lane = lax.broadcasted_iota(jnp.int32, (1, 128), 1)
    squares = jnp.where(lane == 0, part[GAIN_LINES : GAIN_LINES + 1], 0.0)
    squares = squares + jnp.sum(gains * gains, axis=0, keepdims=True)
    norm = jnp.sqrt(jnp.sum(squares, axis=1, keepdims=True))
    factor = CLIP_NORM / jnp.maximum(norm, CLIP_NORM)
    line_number = lax.broadcasted_iota(jnp.int32, norm_ref.shape, 0)
    norm_ref[...] = jnp.where(line_number == 0, norm, factor)


def sum_everywhere(gain_sum, squares, blocks, wide, number):
    values = jnp.concatenate([gain_sum, squares.reshape(1)])
    nd = lax.axis_size("dp")
    count = values.shape[0]
    lines = -(-count // 1024) * 8
    padded = jnp.pad(values, (0, lines * 128 - count)).reshape(lines, 128)
    q_width = wide - 2 * HD
    summed, norm, grad_qkv, grad_out = pl.pallas_call(
        functools.partial(sum_kernel, nd),
        out_shape=[
            jax.ShapeDtypeStruct(padded.shape, jnp.float32),
            jax.ShapeDtypeStruct((8, 128), jnp.float32),
            jax.ShapeDtypeStruct((blocks.shape[1], PLANE * wide), blocks.dtype),
            jax.ShapeDtypeStruct((blocks.shape[1], PLANE * q_width), blocks.dtype),
        ],
        in_specs=[VMEM, VMEM],
        out_specs=[VMEM] * 4,
        scratch_shapes=[
            pltpu.VMEM((PLANE, blocks.shape[1], wide), blocks.dtype),
            pltpu.VMEM((PLANE,) + padded.shape, jnp.float32),
            pltpu.VMEM((nd,) + padded.shape, jnp.float32),
            pltpu.VMEM(padded.shape, jnp.float32),
            pltpu.VMEM(padded.shape, jnp.float32),
            pltpu.SemaphoreType.DMA((PLANE + 1,)),
            pltpu.SemaphoreType.DMA((2, PLANE - 1)),
            pltpu.SemaphoreType.DMA((2, nd - 1)),
            pltpu.SemaphoreType.DMA((2, PLANE - 1)),
        ],
        compiler_params=pltpu.CompilerParams(collective_id=number, has_side_effects=True),
        cost_estimate=SHORT,
        name=f"sum_everywhere_{number}",
    )(padded, blocks)
    return summed.reshape(-1)[: count - 1], norm, grad_qkv, grad_out


def greet_line(nd, others):
    line = lax.axis_index("dp")
    barrier = pltpu.get_barrier_semaphore()
    for other in others:
        pl.semaphore_signal(barrier, inc=1, device_id={"fsdp": other}, device_id_type=MESH)

    @pl.when(line < nd - 1)
    def _():
        pl.semaphore_signal(barrier, inc=1, device_id={"dp": line + 1}, device_id_type=MESH)

    @pl.when(line > 0)
    def _():
        pl.semaphore_signal(barrier, inc=1, device_id={"dp": line - 1}, device_id_type=MESH)

    neighbours = lax.div(line + nd - 1, nd) + lax.div(2 * nd - 2 - line, nd)
    pl.semaphore_wait(barrier, len(others) + neighbours)


class Gather:
    def __init__(self, own_ref, all_ref, send_sem, recv_sem):
        self.own_ref, self.all_ref = own_ref, all_ref
        self.send_sem, self.recv_sem = send_sem, recv_sem
        self.me = lax.axis_index("fsdp")
        self.sibling, self.x_next, self.y_next = flip(self.me, 0), flip(self.me, 1), flip(self.me, 2)
        self.diagonal = flip(self.x_next, 2)
        self.rows = own_ref.shape[0]
        self.sent = []

    def put(self, slot, owner, part, target, own=False):
        half = self.rows // 2
        if part is None:
            spot = self.all_ref.at[pl.ds(pl.multiple_of(owner * self.rows, half), self.rows)]
            source = self.own_ref
        else:
            first = pl.multiple_of(owner * self.rows + part * half, half)
            spot = self.all_ref.at[pl.ds(first, half)]
            source = self.own_ref.at[pl.ds(part * half, half)]
        return pltpu.make_async_remote_copy(
            src_ref=source if own else spot,
            dst_ref=spot,
            send_sem=self.send_sem.at[slot],
            recv_sem=self.recv_sem.at[slot],
            device_id={"fsdp": target},
            device_id_type=MESH,
        )

    def begin(self):
        for slot, part, target in (
            (0, 0, self.x_next),
            (2, 1, self.y_next),
            (4, None, self.sibling),
            (1, 1, self.x_next),
            (3, 0, self.y_next),
        ):
            copy = self.put(slot, self.me, part, target, own=True)
            copy.start()
            self.sent.append(copy)

    def take(self, slot):
        sibling = self.sibling
        owner, part, onward = {
            0: (self.x_next, 0, ((5, self.y_next), (7, sibling))),
            1: (self.x_next, 1, ((8, sibling),)),
            2: (self.y_next, 1, ((6, self.x_next), (9, sibling))),
            3: (self.y_next, 0, ((10, sibling),)),
            4: (sibling, None, ()),
            5: (self.diagonal, 0, ((11, sibling),)),
            6: (self.diagonal, 1, ((12, sibling),)),
            7: (flip(self.x_next, 0), 0, ()),
            8: (flip(self.x_next, 0), 1, ()),
            9: (flip(self.y_next, 0), 1, ()),
            10: (flip(self.y_next, 0), 0, ()),
            11: (flip(self.diagonal, 0), 0, ()),
            12: (flip(self.diagonal, 0), 1, ()),
        }[slot]
        self.put(slot, owner, part, sibling).wait_recv()
        for next_slot, target in onward:
            copy = self.put(next_slot, owner, part, target)
            copy.start()
            self.sent.append(copy)

    def finish(self):
        for copy in self.sent:
            copy.wait_send()


def gather_scratch():
    return [pltpu.SemaphoreType.DMA((13,)), pltpu.SemaphoreType.DMA((13,))]


class Scatter:
    def __init__(self, out_ref, block, refs):
        self.out_ref, self.block = out_ref, block
        (self.sib_out, self.sib_in, self.far_out, self.far_in, self.near_out, self.near_in) = refs[:6]
        self.late = refs[6]
        self.sib_sems, self.far_sems, self.near_sems = refs[7:9], refs[9:11], refs[11:13]
        self.me = lax.axis_index("fsdp")
        self.sibling, self.x_next, self.y_next = flip(self.me, 0), flip(self.me, 1), flip(self.me, 2)
        self.targets = (flip(self.x_next, 2), self.x_next, self.y_next, self.me)
        self.half = out_ref.shape[0] // 2

    def send(self, source, target, sems, slot, device):
        return pltpu.make_async_remote_copy(
            src_ref=source.at[slot],
            dst_ref=target.at[slot],
            send_sem=sems[0].at[slot],
            recv_sem=sems[1].at[slot],
            device_id={"fsdp": device},
            device_id_type=MESH,
        )

    def to_sibling(self, place):
        return self.send(self.sib_out, self.sib_in, self.sib_sems, place, self.sibling)

    def to_far(self, part):
        device = (self.x_next, self.y_next)[part]
        return self.send(self.far_out, self.far_in, self.far_sems, part, device)

    def to_near(self, place, part):
        device = (self.x_next, self.y_next)[place]
        return self.send(self.near_out, self.near_in, self.near_sems, 2 * place + part, device)

    def for_sibling(self, place):
        def write(columns, part):
            self.sib_out[place, :, columns] = part.astype(jnp.bfloat16)

        self.block(flip(self.targets[place], 0), write)
        self.to_sibling(place).start()

    def for_far(self):
        self.to_sibling(0).wait_recv()

        def write(columns, part):
            whole = (part + self.sib_in[0, :, columns].astype(jnp.float32)).astype(jnp.bfloat16)
            self.far_out[0, :, columns] = whole[: self.half]
            self.far_out[1, :, columns] = whole[self.half :]

        self.block(self.targets[0], write)
        self.to_far(0).start()
        self.to_far(1).start()

    def for_near(self, place):
        self.to_sibling(1 + place).wait_recv()
        other = 1 - place

        def write(columns, part):
            whole = part + self.sib_in[1 + place, :, columns].astype(jnp.float32)
            halves = (whole[: self.half], whole[self.half :])
            self.near_out[2 * place + place, :, columns] = halves[place].astype(jnp.bfloat16)
            self.late[place, :, columns] = halves[other]

        self.block(self.targets[1 + place], write)
        self.to_near(place, place).start()

    def finish_near(self, place):
        other = 1 - place
        self.to_far(other).wait_recv()
        whole = self.late[place] + self.far_in[other].astype(jnp.float32)
        self.near_out[2 * place + other] = whole.astype(jnp.bfloat16)
        self.to_near(place, other).start()

    def own(self):
        def write(columns, part):
            self.out_ref[:, columns] = part

        self.block(self.me, write)

    def finish(self):
        self.to_sibling(3).wait_recv()
        self.out_ref[...] = self.out_ref[...] + self.sib_in[3].astype(jnp.float32)
        for part, place in ((0, 0), (1, 1), (1, 0), (0, 1)):
            self.to_near(place, part).wait_recv()
            spot = pl.ds(part * self.half, self.half)
            part_in = self.near_in[2 * place + part].astype(jnp.float32)
            self.out_ref[spot, :] = self.out_ref[spot, :] + part_in
        for place in range(4):
            self.to_sibling(place).wait_send()
            self.to_near(place // 2, place % 2).wait_send()
        for part in range(2):
            self.to_far(part).wait_send()


def staged(kernel, n_in, places):
    def body(*refs):
        stage, sems = refs[-len(places) - 1 : -1], refs[-1]
        inputs, rest = list(refs[:n_in]), refs[n_in : -len(places) - 1]
        copies = [
            pltpu.make_async_copy(inputs[place], buffer, sems.at[index])
            for index, (place, buffer) in enumerate(zip(places, stage))
        ]
        for copy in copies:
            copy.start()
        for place, buffer in zip(places, stage):
            inputs[place] = buffer

        def ready():
            for copy in copies:
                copy.wait()

        kernel(ready, *inputs, *rest)

    return body


def staged_specs(arrays, places):
    specs = [ANY if place in places else VMEM for place in range(len(arrays))]
    scratch = [pltpu.VMEM(arrays[place].shape, arrays[place].dtype) for place in places]
    return specs, scratch + [pltpu.SemaphoreType.DMA((len(places),))]


def scatter_scratch(rows, width):
    low, half = jnp.bfloat16, rows // 2
    return [
        pltpu.VMEM((4, rows, width), low),
        pltpu.VMEM((4, rows, width), low),
        pltpu.VMEM((2, half, width), low),
        pltpu.VMEM((2, half, width), low),
        pltpu.VMEM((4, half, width), low),
        pltpu.VMEM((4, half, width), low),
        pltpu.VMEM((2, half, width), jnp.float32),
        pltpu.SemaphoreType.DMA((4,)),
        pltpu.SemaphoreType.DMA((4,)),
        pltpu.SemaphoreType.DMA((2,)),
        pltpu.SemaphoreType.DMA((2,)),
        pltpu.SemaphoreType.DMA((4,)),
        pltpu.SemaphoreType.DMA((4,)),
    ]


def block_product(left_refs, right_refs, rows, width, turned):
    def block(owner, write):
        @pl.loop(0, width // TILE)
        def _(step):
            columns = pl.ds(pl.multiple_of(step * TILE, TILE), TILE)
            spot = pl.ds(pl.multiple_of(owner * rows, rows), rows)
            total = None
            for left_ref, right_ref in zip(left_refs, right_refs):
                if turned:
                    part = contract_last(left_ref[spot, :], right_ref[columns, :])
                else:
                    part = product(left_ref[spot, :], right_ref[:, columns])
                total = part if total is None else total + part
            write(columns, total)

    return block


def scatter_kernel(turned, count, *refs):
    left_hbm, right_hbm, out_ref = refs[:count], refs[count : 2 * count], refs[2 * count]
    refs = refs[2 * count + 1 :]
    left_refs, right_refs = refs[:count], refs[count : 2 * count]
    left_sems, right_sems, refs = refs[2 * count], refs[2 * count + 1], refs[2 * count + 2 :]
    rows, width = out_ref.shape
    whole = block_product(left_refs, right_refs, rows, width, turned)

    def fetch(place, owner):
        spot = pl.ds(pl.multiple_of(owner * rows, rows), rows)
        return pltpu.make_async_copy(
            left_hbm[place].at[spot], left_refs[place].at[spot], left_sems.at[place, owner]
        )

    def block(owner, write):
        for place in range(count):
            fetch(place, owner).wait()
        whole(owner, write)

    scatter = Scatter(out_ref, block, refs)
    rights = [
        pltpu.make_async_copy(right_hbm[place], right_refs[place], right_sems.at[place])
        for place in range(count)
    ]
    for copy in rights:
        copy.start()
    far, x_next, y_next, me = scatter.targets
    for owner in (
        flip(far, 0),
        flip(x_next, 0),
        far,
        flip(y_next, 0),
        x_next,
        flip(me, 0),
        y_next,
        me,
    ):
        for place in range(count):
            fetch(place, owner).start()
    greet((scatter.sibling, scatter.x_next, scatter.y_next))
    for copy in rights:
        copy.wait()
    scatter.for_sibling(0)
    scatter.for_sibling(1)
    scatter.for_far()
    scatter.for_sibling(2)
    scatter.for_near(0)
    scatter.for_sibling(3)
    scatter.for_near(1)
    scatter.finish_near(0)
    scatter.finish_near(1)
    scatter.own()
    scatter.finish()


def pass_through(ready, gather, scatter, work, between):
    me, sibling, x_next, y_next = gather.me, gather.sibling, gather.x_next, gather.y_next
    diagonal = gather.diagonal
    greet((sibling, x_next, y_next))
    gather.begin()
    gather.all_ref[pl.ds(pl.multiple_of(me * gather.rows, gather.rows), gather.rows), :] = (
        gather.own_ref[...]
    )
    ready()
    work((me,))
    gather.take(0)
    gather.take(2)
    gather.take(4)
    work((sibling,))
    scatter.for_sibling(3)
    gather.take(1)
    gather.take(3)
    work((x_next, y_next))
    gather.take(5)
    gather.take(6)
    for slot in (7, 8, 9, 10):
        gather.take(slot)
    work((flip(x_next, 0), flip(y_next, 0)))
    scatter.for_sibling(1)
    scatter.for_sibling(2)
    scatter.for_near(0)
    scatter.for_near(1)
    gather.take(11)
    gather.take(12)
    work((flip(diagonal, 0),))
    scatter.for_sibling(0)
    work((diagonal,))
    scatter.for_far()
    scatter.own()
    between[0]()
    scatter.finish_near(0)
    scatter.finish_near(1)
    between[1]()
    scatter.finish()
    gather.finish()


def each_owner(owners, rows, one):
    if len(owners) == 1:
        one(owners[0])
        return

    @pl.loop(0, len(owners))
    def _(step):
        one(owners[0] + step * (owners[1] - owners[0]))


def lanes():
    lane = lax.broadcasted_iota(jnp.int32, (1, 2 * HD), 1)
    row_head = lax.broadcasted_iota(jnp.int32, (2 * HD, 2 * HD), 0) // HD
    column_head = lax.broadcasted_iota(jnp.int32, (2 * HD, 2 * HD), 1) // HD
    spread = jnp.where(row_head == column_head, 1.0 / HD, 0.0).astype(jnp.float32)

    def head_mean(values):
        return jnp.dot(
            values, spread, precision=lax.Precision.HIGHEST, preferred_element_type=jnp.float32
        )

    first_half = lax.rem(lane, HD) < HD // 2

    def turn_quarter(values):
        return jnp.where(
            first_half,
            -pltpu.roll(values, 2 * HD - HD // 2, 1),
            pltpu.roll(values, HD // 2, 1),
        )

    def sides(values):
        return [
            jnp.where(chosen, values, 0.0).astype(jnp.bfloat16)
            for chosen in (lane < HD, lane >= HD)
        ]

    return lane, sides, head_mean, turn_quarter


def twice(values):
    return jnp.concatenate([values, values], axis=0)


def stacked(ref, spot):
    width = 2 * HD
    return jnp.concatenate([ref[spot, :width], ref[spot, width : 2 * width]], axis=0)


def attend_kernel(
    ready,
    x_ref,
    wqkv_ref,
    wo_ref,
    cos_ref,
    sin_ref,
    mask_ref,
    gain_ref,
    out_ref,
    all_out_ref,
    proj_ref,
    q_ref,
    kk_ref,
    vv_ref,
    o_ref,
    lse_ref,
    all_ref,
    out_sem,
    gather_send,
    gather_recv,
    *refs,
):
    rows, width = out_ref.shape
    low = jnp.bfloat16
    pair_width = 2 * HD
    lane, sides, head_mean, turn_quarter = lanes()
    first_head = lane < HD
    scale = HD ** (-0.5)

    def normed(values, gain):
        return values * lax.rsqrt(head_mean(values * values) + EPSILON) * gain

    def one(owner):
        base = pl.multiple_of(owner * rows, rows)
        spot = pl.ds(base, rows)
        proj_ref[spot, :] = product(all_ref[spot, :], wqkv_ref[...])

        for part in range(MB):
            micro(pl.multiple_of(base + part * MB_TOK, MB_TOK), owner * MB + part)

    def micro(first, number):
        spot = pl.ds(first, MB_TOK)
        cosine, sine = cos_ref[spot, :], sin_ref[spot, :]
        allowed = twice(mask_ref[number]) > 0.5
        kv = proj_ref[spot, 2 * pair_width : 3 * pair_width]
        swapped = pltpu.roll(kv, HD, 1)
        values = jnp.where(first_head, swapped, kv)
        keys = normed(jnp.where(first_head, kv, swapped), gain_ref[1:2, :])
        keys = (keys * cosine + turn_quarter(keys) * sine).astype(low)
        kk_ref[spot, :] = keys
        vv_ref[spot, :] = values.astype(low)
        query = normed(stacked(proj_ref, spot), gain_ref[0:1, :])
        query = (query * twice(cosine) + turn_quarter(query) * twice(sine)).astype(low)
        q_ref[spot, :pair_width] = query[:MB_TOK]
        q_ref[spot, pair_width : 2 * pair_width] = query[MB_TOK:]
        probs, logs = [], []
        for one_query in sides(query.astype(jnp.float32) * scale):
            scores = jnp.where(allowed, contract_last(one_query, keys), MASKED)
            peak = jnp.max(scores, axis=-1, keepdims=True)
            powers = jnp.exp(scores - peak)
            total = jnp.sum(powers, axis=-1, keepdims=True)
            probs.append((powers * (1.0 / total)).astype(low))
            logs.append(peak + jnp.log(total))
        wide_values = jnp.concatenate(sides(values), axis=0)
        attended = product(jnp.concatenate(probs, axis=1), wide_values).astype(low)
        o_ref[spot, :pair_width] = attended[:MB_TOK]
        o_ref[spot, pair_width : 2 * pair_width] = attended[MB_TOK:]
        log_totals = jnp.where(lane == 0, logs[0][:MB_TOK], logs[1][:MB_TOK])
        log_totals = jnp.where(lane == 2, logs[0][MB_TOK:], log_totals)
        lse_ref[spot, :] = jnp.where(lane == 3, logs[1][MB_TOK:], log_totals)

    gather = Gather(x_ref, all_ref, gather_send, gather_recv)
    scatter = Scatter(out_ref, block_product((o_ref,), (wo_ref,), rows, width, False), refs)
    keep = pltpu.make_async_copy(all_ref, all_out_ref, out_sem)
    pass_through(
        ready,
        gather,
        scatter,
        lambda owners: each_owner(owners, rows, one),
        (keep.start, lambda: None),
    )
    keep.wait()


def attend_back_kernel(
    ready,
    x_ref,
    wqkv_ref,
    wo_ref,
    cos_ref,
    sin_ref,
    mask_ref,
    gain_ref,
    proj_ref,
    q_ref,
    kk_ref,
    vv_ref,
    o_ref,
    lse_ref,
    normed_hbm,
    out_ref,
    grad_ref,
    ggain_ref,
    all_ref,
    normed_ref,
    do_ref,
    dproj_ref,
    in_sem,
    gather_send,
    gather_recv,
    *refs,
):
    rows, width = out_ref.shape
    low = jnp.bfloat16
    pair_width = 2 * HD
    lane, sides, head_mean, turn_quarter = lanes()
    first_head = lane < HD
    scale = HD ** (-0.5)
    fetch = pltpu.make_async_copy(normed_hbm, normed_ref, in_sem)
    fetch.start()
    ggain_ref[...] = jnp.zeros_like(ggain_ref)

    def through_norm(grad, cosine, sine, raw, gain, row):
        grad = grad * cosine - turn_quarter(grad) * sine
        root = lax.rsqrt(head_mean(raw * raw) + EPSILON)
        normed = raw * root
        ggain_ref[row : row + 1, :] += jnp.sum(grad * normed, axis=0, keepdims=True)
        scaled = grad * gain
        return root * (scaled - normed * head_mean(scaled * normed))

    def one(owner):
        base = pl.multiple_of(owner * rows, rows)
        do_ref[...] = contract_last(all_ref[pl.ds(base, rows), :], wo_ref[...]).astype(low)

        for part in range(MB):
            here = pl.ds(part * MB_TOK, MB_TOK)
            micro(pl.multiple_of(base + part * MB_TOK, MB_TOK), here, owner * MB + part)

    def micro(first, here, number):
        spot = pl.ds(first, MB_TOK)
        cosine, sine = cos_ref[spot, :], sin_ref[spot, :]
        allowed = twice(mask_ref[number]) > 0.5
        keys, values = kk_ref[spot, :], vv_ref[spot, :]
        logs = lse_ref[spot, :]
        queries = sides(stacked(q_ref, spot).astype(jnp.float32) * scale)
        branches = sides(stacked(do_ref, here).astype(jnp.float32))
        probs_low, scores_back = [], []
        for side in range(2):
            log_total = jnp.concatenate(
                [logs[:, side : side + 1], logs[:, 2 + side : 3 + side]], axis=0
            )
            scores = jnp.where(allowed, contract_last(queries[side], keys), MASKED)
            probs = jnp.exp(scores - log_total)
            probs_grad = contract_last(branches[side], values)
            spread = jnp.sum(probs * probs_grad, axis=-1, keepdims=True)
            scores_back.append((probs * (probs_grad - spread)).astype(low))
            probs_low.append(probs.astype(low))
        wide_keys = jnp.concatenate(sides(keys.astype(jnp.float32)), axis=0)
        query_grad = product(jnp.concatenate(scores_back, axis=1), wide_keys) * scale
        key_grad = column_product(
            jnp.concatenate(scores_back, axis=0), jnp.concatenate(queries, axis=0)
        )
        value_grad = column_product(
            jnp.concatenate(probs_low, axis=0), jnp.concatenate(branches, axis=0)
        )
        raw = stacked(proj_ref, spot)
        grad = through_norm(query_grad, twice(cosine), twice(sine), raw, gain_ref[0:1, :], 0)
        dproj_ref[spot, :pair_width] = grad[:MB_TOK].astype(low)
        dproj_ref[spot, pair_width : 2 * pair_width] = grad[MB_TOK:].astype(low)
        kv = proj_ref[spot, 2 * pair_width : 3 * pair_width]
        raw = jnp.where(first_head, kv, pltpu.roll(kv, HD, 1))
        key_grad = key_grad + pltpu.roll(key_grad, HD, 1)
        value_grad = value_grad + pltpu.roll(value_grad, HD, 1)
        grad = through_norm(key_grad, cosine, sine, raw, gain_ref[1:2, :], 1)
        both = jnp.where(first_head, grad, value_grad).astype(low)
        dproj_ref[spot, 2 * pair_width : 3 * pair_width] = both

    wide, q_width = dproj_ref.shape[1], o_ref.shape[1]

    def out_grad():
        @pl.loop(0, width // TILE)
        def _(step):
            columns = pl.ds(pl.multiple_of(step * TILE, TILE), TILE)
            part = column_product(o_ref[...], all_ref[:, columns]).astype(low)
            for first in range(0, TILE, q_width):
                spot = pl.ds(pl.multiple_of(step * TILE + first, q_width), q_width)
                grad_ref[spot, wide:] = part[:, first : first + q_width]

    def qkv_grad():
        fetch.wait()

        @pl.loop(0, width // TILE)
        def _(step):
            columns = pl.ds(pl.multiple_of(step * TILE, TILE), TILE)
            part = column_product(dproj_ref[...], normed_ref[:, columns])
            grad_ref[columns, :wide] = jnp.transpose(part).astype(low)

    gather = Gather(x_ref, all_ref, gather_send, gather_recv)
    scatter = Scatter(out_ref, block_product((dproj_ref,), (wqkv_ref,), rows, width, True), refs)
    pass_through(
        ready, gather, scatter, lambda owners: each_owner(owners, rows, one), (out_grad, qkv_grad)
    )


def attend(own_rows, own_qkv, own_out, tables, number):
    rows, width = own_rows.shape
    count, wide, q_width = PLANE * rows, own_qkv.shape[1], own_out.shape[0]
    low = jnp.bfloat16
    arrays = (own_rows, own_qkv, own_out, *tables)
    places = tuple(range(1, len(arrays)))
    specs, stage = staged_specs(arrays, places)
    return pl.pallas_call(
        staged(attend_kernel, len(arrays), places),
        out_shape=[
            jax.ShapeDtypeStruct((rows, width), jnp.float32),
            jax.ShapeDtypeStruct((count, width), low),
            jax.ShapeDtypeStruct((count, wide), jnp.float32),
            jax.ShapeDtypeStruct((count, q_width), low),
            jax.ShapeDtypeStruct((count, 2 * HD), low),
            jax.ShapeDtypeStruct((count, 2 * HD), low),
            jax.ShapeDtypeStruct((count, q_width), low),
            jax.ShapeDtypeStruct((count, 2 * HD), jnp.float32),
        ],
        in_specs=specs,
        out_specs=[VMEM, ANY] + [VMEM] * 6,
        scratch_shapes=[pltpu.VMEM((count, width), low), pltpu.SemaphoreType.DMA]
        + gather_scratch()
        + scatter_scratch(rows, width)
        + stage,
        compiler_params=pltpu.CompilerParams(
            collective_id=number, has_side_effects=True, vmem_limit_bytes=56 * 2**20
        ),
        cost_estimate=SHORT,
        name=f"attend_{number}",
    )(*arrays)


def attend_back(own_rows, own_qkv, own_out, tables, kept, number):
    rows, width = own_rows.shape
    count, wide, q_width = PLANE * rows, own_qkv.shape[1], own_out.shape[0]
    low = jnp.bfloat16
    normed_all, proj, query, keys, values, attended, log_totals = kept
    arrays = (
        own_rows,
        own_qkv,
        own_out,
        *tables,
        proj,
        query,
        keys,
        values,
        attended,
        log_totals,
        normed_all,
    )
    places = tuple(range(1, len(arrays) - 1))
    specs, stage = staged_specs(arrays[:-1], places)
    return pl.pallas_call(
        staged(attend_back_kernel, len(arrays), places),
        out_shape=[
            jax.ShapeDtypeStruct((rows, width), jnp.float32),
            jax.ShapeDtypeStruct((width, wide + q_width), low),
            jax.ShapeDtypeStruct((8, 2 * HD), jnp.float32),
        ],
        in_specs=specs + [ANY],
        out_specs=[VMEM] * 3,
        scratch_shapes=[
            pltpu.VMEM((count, width), low),
            pltpu.VMEM((count, width), low),
            pltpu.VMEM((rows, q_width), low),
            pltpu.VMEM((count, wide), low),
            pltpu.SemaphoreType.DMA,
        ]
        + gather_scratch()
        + scatter_scratch(rows, width)
        + stage,
        compiler_params=pltpu.CompilerParams(
            collective_id=number, has_side_effects=True, vmem_limit_bytes=58 * 2**20
        ),
        cost_estimate=SHORT,
        name=f"attend_back_{number}",
    )(*arrays)


def product_scatter(left_sides, right_sides, number, turned=False):
    width = right_sides[0].shape[0] if turned else right_sides[0].shape[1]
    rows = left_sides[0].shape[0] // PLANE
    return pl.pallas_call(
        functools.partial(scatter_kernel, turned, len(left_sides)),
        out_shape=jax.ShapeDtypeStruct((rows, width), jnp.float32),
        in_specs=[ANY] * (2 * len(left_sides)),
        out_specs=VMEM,
        scratch_shapes=[pltpu.VMEM(side.shape, side.dtype) for side in left_sides + right_sides]
        + [
            pltpu.SemaphoreType.DMA((len(left_sides), PLANE)),
            pltpu.SemaphoreType.DMA((len(left_sides),)),
        ]
        + scatter_scratch(rows, width),
        compiler_params=pltpu.CompilerParams(
            collective_id=number, has_side_effects=True, vmem_limit_bytes=56 * 2**20
        ),
        cost_estimate=SHORT,
        name=f"product_scatter_{number}",
    )(*left_sides, *right_sides)


def gather_kernel(x_ref, all_ref, own_sem, gather_send, gather_recv):
    gather = Gather(x_ref, all_ref, gather_send, gather_recv)
    rows = gather.rows
    spot = pl.ds(pl.multiple_of(gather.me * rows, rows), rows)
    keep = pltpu.make_async_copy(x_ref, all_ref.at[spot], own_sem)
    greet((gather.sibling, gather.x_next, gather.y_next))
    gather.begin()
    keep.start()
    for slot in (0, 2, 1, 3, 5, 6, 4, 7, 9, 8, 10, 11, 12):
        gather.take(slot)
    gather.finish()
    keep.wait()


def plane_gather(rows, number):
    return pl.pallas_call(
        gather_kernel,
        out_shape=jax.ShapeDtypeStruct((PLANE * rows.shape[0], rows.shape[1]), rows.dtype),
        in_specs=[ANY],
        out_specs=ANY,
        scratch_shapes=[pltpu.SemaphoreType.DMA] + gather_scratch(),
        compiler_params=pltpu.CompilerParams(collective_id=number, has_side_effects=True),
        cost_estimate=SHORT,
        name=f"plane_gather_{number}",
    )(rows)


def start_kernel(
    nd,
    qkv_ref,
    out_rows_ref,
    wide_hbm,
    note_ref,
    own_qkv_ref,
    own_out_ref,
    half_a_ref,
    half_b_ref,
    notes_ref,
    own_sem,
    block_send,
    block_recv,
    note_send,
    note_recv,
    piece_send,
    piece_recv,
    line_send,
    line_recv,
    wide_full,
    wide_ref,
    wide_sem,
):
    me, line = lax.axis_index("fsdp"), lax.axis_index("dp")
    others = plane_others(me)
    count = qkv_ref.shape[1]
    half_width = half_a_ref.shape[2] // 2
    hidden = 2 * half_width
    whole = hidden * PLANE
    fetch = pltpu.make_async_copy(wide_hbm, wide_full, wide_sem)
    fetch.start()
    greet_line(nd, others)

    def line_spot(array, owner):
        rows = pl.ds(pl.multiple_of(owner * count, count), count)
        if array == 1:
            return own_out_ref.at[rows]
        return own_qkv_ref.at[pl.ds(array // 2 * (PLANE // 2), PLANE // 2), rows]

    def along(array, owner, side, source=None):
        spot = line_spot(array, owner)
        return pltpu.make_async_remote_copy(
            src_ref=spot if source is None else source,
            dst_ref=spot,
            send_sem=line_send.at[array, side, owner],
            recv_sem=line_recv.at[array, owner],
            device_id={"dp": line + 1 if side == 0 else line - 1},
            device_id_type=MESH,
        )

    def send_own(array, source=None):
        @pl.when(line < nd - 1)
        def _():
            along(array, line, 0, source).start()

        @pl.when(line > 0)
        def _():
            along(array, line, 1, source).start()

    def line_step(array, step):
        @pl.when(line >= step)
        def _():
            along(array, line - step, 0).wait_recv()

            @pl.when(line < nd - 1)
            def _():
                along(array, line - step, 0).start()

        @pl.when(line + step < nd)
        def _():
            along(array, line + step, 1).wait_recv()

            @pl.when(line > 0)
            def _():
                along(array, line + step, 1).start()

    def put_block(number):
        other = others[number - 1]
        return pltpu.make_async_remote_copy(
            src_ref=qkv_ref.at[other],
            dst_ref=own_qkv_ref.at[me, pl.ds(pl.multiple_of(line * count, count), count)],
            send_sem=block_send.at[number],
            recv_sem=block_recv.at[number],
            device_id={"fsdp": other},
            device_id_type=MESH,
        )

    def put_note(number):
        return pltpu.make_async_remote_copy(
            src_ref=note_ref,
            dst_ref=notes_ref.at[me],
            send_sem=note_send.at[number],
            recv_sem=note_recv.at[number],
            device_id={"fsdp": others[number - 1]},
            device_id_type=MESH,
        )

    def pieces(other):
        for half, half_ref in enumerate((half_a_ref, half_b_ref)):
            for side in range(2):
                first = side * whole + other * hidden + half * half_width
                source = wide_ref.at[:, pl.ds(pl.multiple_of(first, 128), half_width)]
                yield source, half_ref.at[me, :, pl.ds(side * half_width, half_width)]

    def put_pieces(number):
        return [
            pltpu.make_async_remote_copy(
                src_ref=source,
                dst_ref=target,
                send_sem=piece_send.at[4 * number + index],
                recv_sem=piece_recv.at[4 * number + index],
                device_id={"fsdp": others[number - 1]},
                device_id_type=MESH,
            )
            for index, (source, target) in enumerate(pieces(others[number - 1]))
        ]

    own_block = own_qkv_ref.at[me, pl.ds(pl.multiple_of(line * count, count), count)]

    def local(index, source, target):
        return pltpu.make_async_copy(source, target, own_sem.at[index])

    keep = [
        local(0, qkv_ref.at[me], own_block),
        local(1, out_rows_ref, line_spot(1, line)),
        local(2, note_ref, notes_ref.at[me]),
    ]
    keep_pieces = [
        local(3 + index, source, target) for index, (source, target) in enumerate(pieces(me))
    ]
    order = (6, 7, 2, 4, 3, 5, 1)
    for number in order:
        put_block(number).start()
        put_note(number).start()
    keep[0].start()
    send_own(1, out_rows_ref)
    for copy in keep[1:]:
        copy.start()
    for number in order:
        put_block(number).wait_recv()
    keep[0].wait()
    send_own(0)
    send_own(2)
    fetch.wait()

    part_width = half_width // nd

    @pl.loop(0, 2 * PLANE)
    def _(step):
        for owner in range(nd):
            for half in range(2):
                first = step * hidden + (2 * owner + half) * part_width
                target = step * hidden + half * half_width + owner * part_width
                columns = pl.ds(pl.multiple_of(first, 128), part_width)
                target = pl.ds(pl.multiple_of(target, 128), part_width)
                wide_ref[:, target] = wide_full[:, columns].astype(wide_ref.dtype)

    for number in order:
        for copy in put_pieces(number):
            copy.start()
    for copy in keep_pieces:
        copy.start()
    for step in range(1, nd):
        for array in (1, 0, 2):
            line_step(array, step)
    for number in order:
        put_block(number).wait_send()
        put_note(number).wait()
        for copy in put_pieces(number):
            copy.wait()
    for copy in keep[1:] + keep_pieces:
        copy.wait()
    for array in (1, 0, 2):
        source = out_rows_ref if array == 1 else None

        @pl.when(line < nd - 1)
        def _():
            along(array, line, 0, source).wait_send()

        @pl.when(line > 0)
        def _():
            along(array, line, 1, source).wait_send()

        for step in range(1, nd):

            @pl.when(jnp.logical_and(line >= step, line < nd - 1))
            def _():
                along(array, line - step, 0).wait_send()

            @pl.when(jnp.logical_and(line + step < nd, line > 0))
            def _():
                along(array, line + step, 1).wait_send()


def start(qkv_blocks, out_rows, wide_rows, note, number):
    nd = lax.axis_size("dp")
    count, whole = wide_rows.shape
    half = whole // 4 // PLANE
    low = jnp.bfloat16
    return pl.pallas_call(
        functools.partial(start_kernel, nd),
        out_shape=[
            jax.ShapeDtypeStruct((PLANE, nd * count, qkv_blocks.shape[2]), low),
            jax.ShapeDtypeStruct((nd * count, out_rows.shape[1]), low),
            jax.ShapeDtypeStruct((PLANE, count, 2 * half), low),
            jax.ShapeDtypeStruct((PLANE, count, 2 * half), low),
            jax.ShapeDtypeStruct((PLANE,) + note.shape, note.dtype),
        ],
        in_specs=[ANY] * 4,
        out_specs=[ANY] * 5,
        scratch_shapes=[pltpu.SemaphoreType.DMA((7,))]
        + [pltpu.SemaphoreType.DMA((PLANE,))] * 4
        + [pltpu.SemaphoreType.DMA((4 * PLANE,))] * 2
        + [pltpu.SemaphoreType.DMA((3, 2, nd)), pltpu.SemaphoreType.DMA((3, nd))]
        + [
            pltpu.VMEM(wide_rows.shape, wide_rows.dtype),
            pltpu.VMEM(wide_rows.shape, low),
            pltpu.SemaphoreType.DMA,
        ],
        compiler_params=pltpu.CompilerParams(
            collective_id=number, has_side_effects=True, vmem_limit_bytes=56 * 2**20
        ),
        cost_estimate=SHORT,
        name=f"start_{number}",
    )(qkv_blocks, out_rows, wide_rows, note)


def glu_block(
    rows_ref, df_ref, wgu, wd, act_ref, dgu_ref, down_sum, wide_sum, results=None
):
    half = wd.shape[0]
    count, width = rows_ref.shape

    @pl.loop(0, count // 256)
    def _(step):
        spot = pl.ds(pl.multiple_of(step * 256, 256), 256)
        for first in range(0, half, GLU_TILE):
            units = slice(first, first + GLU_TILE)
            up_units = slice(half + first, half + first + GLU_TILE)
            gate = product(rows_ref[spot, :], wgu[:, units])
            up = product(rows_ref[spot, :], wgu[:, up_units])
            back = contract_last(df_ref[spot, :], wd[units, :])
            sigmoid = jax.nn.sigmoid(gate)
            silu = gate * sigmoid
            act_ref[spot, units] = (silu * up).astype(jnp.bfloat16)
            gate_back = back * up * sigmoid * (1.0 + gate * (1.0 - sigmoid))
            dgu_ref[spot, units] = gate_back.astype(jnp.bfloat16)
            dgu_ref[spot, up_units] = (back * silu).astype(jnp.bfloat16)

    @pl.loop(0, width // TILE)
    def _(step):
        columns = pl.ds(pl.multiple_of(step * TILE, TILE), TILE)
        down = column_product(act_ref[...], df_ref[:, columns])
        wide = column_product(rows_ref[:, columns], dgu_ref[...])
        if results is None:
            down_sum[:, columns] += down
            wide_sum[columns, :] += wide
        else:
            down_ref, wide_ref = results
            down_ref[:, columns] = (down_sum[:, columns] + down).astype(down_ref.dtype)
            wide_ref[columns, :] = (wide_sum[columns, :] + wide).astype(wide_ref.dtype)


def gather_glu_kernel(
    x_ref,
    wgu_hbm,
    wd_hbm,
    df_hbm,
    all_out_ref,
    act_ref,
    dgu_ref,
    down_ref,
    wide_ref,
    all_ref,
    wgu_ref,
    wd_ref,
    df_ref,
    down_sum,
    wide_sum,
    in_sem,
    out_sem,
    gather_send,
    gather_recv,
):
    rows = x_ref.shape[0]
    half = wd_ref.shape[0]
    fetch = [
        pltpu.make_async_copy(wgu_hbm, wgu_ref, in_sem.at[0]),
        pltpu.make_async_copy(wd_hbm.at[pl.ds(0, half)], wd_ref, in_sem.at[1]),
        pltpu.make_async_copy(df_hbm, df_ref, in_sem.at[2]),
    ]
    for copy in fetch:
        copy.start()
    gather = Gather(x_ref, all_ref, gather_send, gather_recv)
    me, x_next, y_next = gather.me, gather.x_next, gather.y_next
    greet((gather.sibling, x_next, y_next))
    gather.begin()
    all_ref[pl.ds(pl.multiple_of(me * rows, rows), rows), :] = x_ref[...]
    down_sum[...] = jnp.zeros_like(down_sum)
    wide_sum[...] = jnp.zeros_like(wide_sum)
    for copy in fetch:
        copy.wait()

    def work(owner, results=None):
        first = owner - lax.rem(owner, 2)
        spot = pl.ds(pl.multiple_of(first * rows, 2 * rows), 2 * rows)
        glu_block(
            all_ref.at[spot],
            df_ref.at[spot],
            wgu_ref,
            wd_ref,
            act_ref.at[spot],
            dgu_ref.at[spot],
            down_sum,
            wide_sum,
            results,
        )

    gather.take(4)
    work(me)
    for slot in (0, 2, 1, 3, 7, 8):
        gather.take(slot)
    work(x_next)
    for slot in (5, 6, 9, 10):
        gather.take(slot)
    work(y_next)
    gather.take(11)
    gather.take(12)
    keep = pltpu.make_async_copy(all_ref, all_out_ref, out_sem)
    keep.start()
    work(gather.diagonal, (down_ref, wide_ref))
    gather.finish()
    keep.wait()


def gather_glu(own_rows, wgu, own_down, df_all, number):
    rows, width = own_rows.shape
    count, half = PLANE * rows, wgu.shape[1] // 2
    low = jnp.bfloat16
    return pl.pallas_call(
        gather_glu_kernel,
        out_shape=[
            jax.ShapeDtypeStruct((count, width), low),
            jax.ShapeDtypeStruct((count, half), low),
            jax.ShapeDtypeStruct((count, 2 * half), low),
            jax.ShapeDtypeStruct((half, width), low),
            jax.ShapeDtypeStruct((width, 2 * half), low),
        ],
        in_specs=[VMEM, ANY, ANY, ANY],
        out_specs=[ANY] + [VMEM] * 4,
        scratch_shapes=[
            pltpu.VMEM((count, width), low),
            pltpu.VMEM(wgu.shape, low),
            pltpu.VMEM((half, width), low),
            pltpu.VMEM((count, width), low),
            pltpu.VMEM((half, width), jnp.float32),
            pltpu.VMEM((width, 2 * half), jnp.float32),
            pltpu.SemaphoreType.DMA((3,)),
            pltpu.SemaphoreType.DMA,
        ]
        + gather_scratch(),
        compiler_params=pltpu.CompilerParams(
            collective_id=number, has_side_effects=True, vmem_limit_bytes=58 * 2**20
        ),
        cost_estimate=SHORT,
        name=f"gather_glu_{number}",
    )(own_rows, wgu, own_down, df_all)


def glu_kernel(
    x_ref,
    df_ref,
    first_ref,
    both_hbm,
    act_ref,
    dgu_ref,
    grad_ref,
    wgu_ref,
    wd_ref,
    down_sum,
    wide_sum,
    sems,
):
    step = pl.program_id(0)
    half = wd_ref.shape[0]
    nd, _, both = grad_ref.shape
    count, units = wide_sum.shape[0] // PLANE // nd, half // nd

    @pl.when(step == 0)
    def _():
        copies = []
        for owner in range(nd):
            for place in range(PLANE):
                source = both_hbm.at[owner, pl.ds(place * count, count)]
                target = wgu_ref.at[pl.ds((place * nd + owner) * count, count)]
                copies.append(pltpu.make_async_copy(source, target, sems.at[owner, place]))
            for side in range(2):
                source = both_hbm.at[owner, pl.ds(PLANE * count + side * units, units)]
                target = wd_ref.at[pl.ds(owner * units, units), pl.ds(side * both, both)]
                copies.append(
                    pltpu.make_async_copy(source, target, sems.at[owner, PLANE + side])
                )
        for copy in copies:
            copy.start()
        down_sum[...] = jnp.zeros_like(down_sum)
        wide_sum[...] = jnp.zeros_like(wide_sum)
        for copy in copies:
            copy.wait()

    glu_block(x_ref, df_ref, wgu_ref, wd_ref, act_ref, dgu_ref, down_sum, wide_sum)

    @pl.when(step == pl.num_programs(0) - 1)
    def _():
        low = grad_ref.dtype
        for owner in range(nd):
            for place in range(PLANE):
                first = (place * nd + owner) * count
                part = wide_sum[first : first + count, :].astype(low)
                grad_ref[owner, place * count : (place + 1) * count, :] = part
            spot = slice(owner * units, (owner + 1) * units)
            for side in range(2):
                columns = slice(side * both, (side + 1) * both)
                start = PLANE * count + side * 2 * units
                grad_ref[owner, start : start + units, :] = first_ref[spot, columns]
                part = down_sum[spot, columns].astype(low)
                grad_ref[owner, start + units : start + 2 * units, :] = part


def glu(rows_all, df_all, gathered, down_first, number):
    nd = lax.axis_size("dp")
    count, width = rows_all.shape
    half, both = down_first.shape[0], gathered.shape[2]
    low = jnp.bfloat16
    step = 512
    once = pl.Buffered(1)
    return pl.pallas_call(
        glu_kernel,
        grid=(count // step,),
        out_shape=[
            jax.ShapeDtypeStruct((count, half), low),
            jax.ShapeDtypeStruct((count, 2 * half), low),
            jax.ShapeDtypeStruct((nd, 2 * width // nd, 2 * half), low),
            jax.ShapeDtypeStruct((width, both), low),
            jax.ShapeDtypeStruct((half, width), low),
        ],
        in_specs=[
            pl.BlockSpec((step, width), lambda i: (i, 0)),
            pl.BlockSpec((step, width), lambda i: (i, 0)),
            pl.BlockSpec((half, width), lambda i: (0, 0), pipeline_mode=once),
            ANY,
        ],
        out_specs=[
            pl.BlockSpec((step, half), lambda i: (i, 0)),
            pl.BlockSpec((step, 2 * half), lambda i: (i, 0)),
            pl.BlockSpec(
                (nd, 2 * width // nd, 2 * half), lambda i: (0, 0, 0), pipeline_mode=once
            ),
            pl.BlockSpec((width, both), lambda i: (0, 0), pipeline_mode=once),
            pl.BlockSpec((half, width), lambda i: (0, 0), pipeline_mode=once),
        ],
        scratch_shapes=[
            pltpu.VMEM((half, width), jnp.float32),
            pltpu.VMEM((width, 2 * half), jnp.float32),
            pltpu.SemaphoreType.DMA((nd, PLANE + 2)),
        ],
        compiler_params=pltpu.CompilerParams(vmem_limit_bytes=56 * 2**20),
        cost_estimate=SHORT,
        name=f"glu_{number}",
    )(rows_all, df_all, down_first, gathered)


def attention(normed_low, own_qkv, own_out, lengths_all, query_gain, key_gain):
    position, _, allowed = layout(lengths_all)
    half_width = HD // 2
    frequency = ROPE_BASE ** (jnp.arange(half_width, dtype=jnp.float32) * (-2.0 / HD))
    angles = position.reshape(-1, 1) * frequency[None, :]
    tables = (
        jnp.tile(jnp.cos(angles), (1, 4)),
        jnp.tile(jnp.sin(angles), (1, 4)),
        allowed.astype(jnp.float32),
        jnp.pad(
            jnp.stack([jnp.tile(query_gain, 2), jnp.tile(key_gain, 2)]), ((0, 6), (0, 0))
        ),
    )
    sums, *kept = attend(normed_low, own_qkv, own_out, tables, 3)

    def back(branch_own):
        normed_one_grad, part_attn, gain_grads = attend_back(
            branch_own, own_qkv, own_out, tables, kept, 9
        )
        query_gain_grad = gain_grads[0, :HD] + gain_grads[0, HD:]
        return normed_one_grad, part_attn, query_gain_grad, gain_grads[1, :HD]

    return sums, back


def last_kernel(
    ready,
    hidden_ref,
    valid_ref,
    act_a_ref,
    act_b_ref,
    wd_a_ref,
    wd_b_ref,
    half_ref,
    out_ref,
    wide_ref,
    sum_ref,
    own_sem,
    sems,
    *refs,
):
    others = plane_others(lax.axis_index("fsdp"))
    rows, width = out_ref.shape
    block = block_product((act_a_ref, act_b_ref), (wd_a_ref, wd_b_ref), rows, width, False)
    scatter = Scatter(sum_ref, block, refs)
    greet(others)
    order = (6, 7, 2, 4, 3, 5, 1)
    for number in order:
        for copy in put_half(half_ref, wide_ref, others, number, sems):
            copy.start()
    keep = keep_half(half_ref, wide_ref, own_sem)
    for copy in keep:
        copy.start()
    ready()
    scatter.for_sibling(0)
    scatter.for_sibling(1)
    scatter.for_far()
    scatter.for_sibling(2)
    scatter.for_near(0)
    scatter.for_sibling(3)
    scatter.for_near(1)
    scatter.finish_near(0)
    scatter.finish_near(1)
    scatter.own()
    scatter.finish()
    out_ref[...] = (hidden_ref[...] + valid_ref[...] * sum_ref[...]).astype(out_ref.dtype)
    for number in order:
        for copy in put_half(half_ref, wide_ref, others, number, sems):
            copy.wait()
    for copy in keep:
        copy.wait()


def last(hidden, valid_col, act_a, act_b, down_a, down_b, half, count, number):
    rows, width = hidden.shape
    arrays = (hidden, valid_col, act_a, act_b, down_a, down_b)
    places = (0, 2, 3, 4, 5)
    specs, stage = staged_specs(arrays, places)
    return pl.pallas_call(
        staged(last_kernel, len(arrays) + 1, places),
        out_shape=[
            jax.ShapeDtypeStruct((rows, width), jnp.bfloat16),
            jax.ShapeDtypeStruct((count, half.shape[1] * PLANE), half.dtype),
        ],
        in_specs=specs + [ANY],
        out_specs=[VMEM, ANY],
        scratch_shapes=[pltpu.VMEM((rows, width), jnp.float32)]
        + half_scratch()
        + scatter_scratch(rows, width)
        + stage,
        compiler_params=pltpu.CompilerParams(
            collective_id=number, has_side_effects=True, vmem_limit_bytes=56 * 2**20
        ),
        cost_estimate=SHORT,
        name=f"last_{number}",
    )(*arrays, half)


def adam_kernel(chunks, n_grads, per, norm_ref, *refs):
    grads, refs = refs[:n_grads], refs[n_grads:]
    states = [refs[place * per : (place + 1) * per] for place in range(3)]
    outs = [refs[(3 + place) * per : (4 + place) * per] for place in range(3)]
    refs = refs[6 * per :]
    grad_bufs, refs = refs[:n_grads], refs[n_grads:]
    bufs = [refs[place * per : (place + 1) * per] for place in range(3)]
    grad_sems, in_sems, out_sems = refs[3 * per :]
    factor = norm_ref[1:2, 0:1]
    first_scale = 1.0 / (1.0 - FIRST_DECAY**STEP)
    second_scale = 1.0 / (1.0 - SECOND_DECAY**STEP)

    def fetch(number):
        which, rows, sources, _ = chunks[number]
        copies = [
            pltpu.make_async_copy(
                grads[array].at[spot], grad_bufs[array].at[spot], grad_sems.at[number, place]
            )
            for place, (array, spot) in enumerate(sources)
        ]
        for place in range(3):
            copies.append(
                pltpu.make_async_copy(
                    states[place][which].at[rows],
                    bufs[place][which].at[rows],
                    in_sems.at[number, place],
                )
            )
        return copies

    def put(number):
        which, rows, _, _ = chunks[number]
        return [
            pltpu.make_async_copy(
                bufs[place][which].at[rows], outs[place][which].at[rows], out_sems.at[number, place]
            )
            for place in range(3)
        ]

    def update(which, rows, columns, grad):
        weights, firsts, seconds = (bufs[place][which] for place in range(3))
        clipped = grad.astype(jnp.float32) * factor
        weight = weights[rows, columns]
        first = FIRST_DECAY * firsts[rows, columns] + (1.0 - FIRST_DECAY) * clipped
        second = SECOND_DECAY * seconds[rows, columns] + (1.0 - SECOND_DECAY) * clipped * clipped
        root = jnp.sqrt(second * second_scale) + ADAM_EPSILON
        change = first * first_scale / root + WEIGHT_DECAY * weight
        weights[rows, columns] = weight - LEARN_RATE * change
        firsts[rows, columns] = first
        seconds[rows, columns] = second

    for number in range(len(chunks)):
        for copy in fetch(number):
            copy.start()
    for number in range(len(chunks)):
        which, rows, _, loops = chunks[number]
        for copy in fetch(number):
            copy.wait()
        for steps, parts in loops:

            @pl.loop(0, steps)
            def _(step):
                for array, grad_rows, columns_of, grad_columns_of, width in parts:
                    columns = pl.ds(pl.multiple_of(columns_of(step), 128), width)
                    grad_columns = pl.ds(pl.multiple_of(grad_columns_of(step), 128), width)
                    update(which, rows, columns, grad_bufs[array][grad_rows, grad_columns])

        for copy in put(number):
            copy.start()
    for number in range(len(chunks)):
        for copy in put(number):
            copy.wait()


def adam_matrices(norm, grad_qkv, grad_out, grad_a, grad_b, sums_b, weights, firsts, seconds):
    half = grad_a.shape[1] // 2 // PLANE
    nd = lax.axis_size("dp")
    unit = half // nd
    count = weights[3].shape[0]
    behind = sums_b.shape[0] - 2 * count
    side_width = sums_b.shape[1]
    width = 512
    chunks = []

    def straight(step):
        return step * width

    for row in range(0, weights[2].shape[0], 16):
        rows = pl.ds(row, 16)
        parts = []
        for part in range(2):
            for owner in range(nd):

                def columns_of(step, part=part, owner=owner):
                    return step * 2 * half + (2 * owner + part) * unit

                def grad_columns_of(step, owner=owner):
                    return step * half + owner * unit

                parts.append((2 + part, rows, columns_of, grad_columns_of, unit))
        loops = [(2 * PLANE, parts)]
        chunks.append((2, rows, [(2, rows), (3, rows)], loops))
    for row in range(0, count, 64):
        sources, loops = [], []
        for side in range(2):
            spot = pl.ds(behind + side * count + row, 64)
            sources.append((4, spot))

            def columns_of(step, side=side):
                return side * side_width + step * width

            loops.append((side_width // width, [(4, spot, columns_of, straight, width)]))
        chunks.append((3, pl.ds(row, 64), sources, loops))
    for which in range(2):
        for row in range(0, weights[which].shape[0], 32):
            rows = pl.ds(row, 32)
            steps = weights[which].shape[1] // width
            loops = [(steps, [(which, rows, straight, straight, width)])]
            chunks.append((which, rows, [(which, rows)], loops))
    grads = (grad_qkv, grad_out, grad_a, grad_b, sums_b)
    per = len(weights)
    number = len(chunks)
    outs = pl.pallas_call(
        functools.partial(adam_kernel, chunks, len(grads), per),
        out_shape=[jax.ShapeDtypeStruct(weight.shape, jnp.float32) for weight in weights] * 3,
        in_specs=[VMEM] + [ANY] * (len(grads) + 3 * per),
        out_specs=[ANY] * (3 * per),
        scratch_shapes=[pltpu.VMEM(grad.shape, grad.dtype) for grad in grads]
        + [pltpu.VMEM(weight.shape, jnp.float32) for weight in weights] * 3
        + [
            pltpu.SemaphoreType.DMA((number, 2)),
            pltpu.SemaphoreType.DMA((number, 3)),
            pltpu.SemaphoreType.DMA((number, 3)),
        ],
        compiler_params=pltpu.CompilerParams(vmem_limit_bytes=60 * 2**20),
        name="adam_matrices",
    )(norm, *grads, *weights, *firsts, *seconds)
    return outs[:per], outs[per : 2 * per], outs[2 * per :]


def scatter_rows(values, axis):
    return lax.psum_scatter(values, "dp", scatter_dimension=axis, tiled=True)


def per_device_plane(
    nf,
    nd,
    tokens,
    cotangent,
    order,
    lengths,
    w_qkv,
    w_out,
    w_gate_up,
    w_down,
    gains,
    first_qkv,
    first_out,
    first_gate_up,
    first_down,
    first_gains,
    second_qkv,
    second_out,
    second_gate_up,
    second_down,
    second_gains,
):
    low = jnp.bfloat16
    q_width = HEADS // nf * HD
    kv_all = KVH * HD
    hidden_own = FF // nf
    rows_own = w_qkv.shape[0]

    order_row = order[0]
    places = jnp.arange(TOK_DEV, dtype=jnp.int32)
    inverse = jnp.zeros((TOK_DEV,), jnp.int32).at[order_row].set(places)
    rows_in = tokens[order_row].astype(jnp.float32)
    back_rows = cotangent[order_row].astype(jnp.float32)
    attn_gain = gains[:D]
    ffn_gain = gains[D : 2 * D]
    query_gain = gains[2 * D : 2 * D + HD]
    key_gain = gains[2 * D + HD :]

    _, valid_rows, _ = layout(lengths)
    valid_col = valid_rows.reshape(TOK_DEV, 1)

    qkv_low = w_qkv.astype(low)

    def head_blocks(rows, width):
        return jnp.swapaxes(rows.reshape(rows_own, -1, width), 0, 1)

    qkv_blocks = jnp.concatenate(
        [
            head_blocks(qkv_low[:, :D], q_width),
            head_blocks(qkv_low[:, D : D + kv_all], HD),
            head_blocks(qkv_low[:, D + kv_all :], HD),
        ],
        axis=2,
    )
    wide = q_width + 2 * HD
    down_low = w_down.astype(low)
    units = down_low.shape[0] // 2
    down_a = lax.all_gather(down_low[:units], "dp", axis=0, tiled=True)
    own_qkv, own_out, half_a, half_b, notes = start(
        qkv_blocks,
        w_out.astype(low),
        w_gate_up,
        jnp.pad(lengths, ((0, 8 - MB), (0, 128 - SEQS))),
        1,
    )
    own_qkv = own_qkv.reshape(D, wide)
    lengths_all = notes[:, :MB, :SEQS].reshape(nf * MB, SEQS)
    half_a, down_a = lax.optimization_barrier((half_a, down_a))
    own_a = lax.all_gather(half_a, "dp", axis=1, tiled=True).reshape(D, hidden_own)
    with_down = jnp.concatenate(
        [half_b.reshape(nf * rows_own, hidden_own), down_low[units:, :hidden_own]]
        + [down_low[units:, hidden_own:]],
        axis=0,
    )
    gathered_b = lax.all_gather(with_down, "dp", axis=0)

    normed_one, norm_one_pull = jax.vjp(rms_norm, rows_in, attn_gain)
    attention_sums, attention_back = attention(
        normed_one.astype(low), own_qkv, own_out, lengths_all, query_gain, key_gain
    )
    back_low = (valid_col * back_rows).astype(low)
    back_low, attention_sums = lax.optimization_barrier((back_low, attention_sums))
    down_back = plane_gather(back_low, 4)
    hidden = rows_in + valid_col * attention_sums

    normed_two, norm_two_pull = jax.vjp(rms_norm, hidden, ffn_gain)
    norm_two_all, act_a, back_a, grad_down_a, part_a = gather_glu(
        normed_two.astype(low), own_a, down_a, down_back, 5
    )
    sums_a = scatter_rows(part_a.reshape(nf, nd * rows_own, hidden_own), 1)
    act_b, back_b, part_b, own_b, down_b = glu(norm_two_all, down_back, gathered_b, grad_down_a, 6)
    sums_b = scatter_rows(part_b, 0)[0]
    normed_two_grad = product_scatter((back_a, back_b), (own_a, own_b), 8, turned=True)
    hidden_norm_grad, ffn_gain_grad = norm_two_pull(normed_two_grad)
    hidden_grad = back_rows + hidden_norm_grad

    branch_own = (valid_col * hidden_grad).astype(low)
    branch_own, sums_a = lax.optimization_barrier((branch_own, sums_a))
    normed_one_grad, part_attn, query_gain_grad, key_gain_grad = attention_back(branch_own)
    sums_attn = scatter_rows(part_attn.reshape(nf, nd * rows_own, wide + q_width), 1)
    normed_one_grad, act_a = lax.optimization_barrier((normed_one_grad, act_a))
    output, grad_a = last(
        hidden,
        valid_col,
        act_a,
        act_b,
        down_a,
        down_b,
        sums_a.reshape(nf * rows_own, hidden_own),
        rows_own,
        7,
    )
    output, sums_b = lax.optimization_barrier((output, sums_b))
    grad_b, squares_b = exchange_half(sums_b, rows_own, 11)
    rows_grad, attn_gain_grad = norm_one_pull(normed_one_grad)
    input_grad = (hidden_grad + rows_grad)[inverse]
    output_all = output[inverse]

    early_squares = jnp.sum(jnp.square(sums_a.astype(jnp.float32))) + jnp.sum(squares_b)
    input_grad, output_all, early_squares, sums_attn = lax.optimization_barrier(
        (input_grad, output_all, early_squares, sums_attn)
    )
    gain_sum = jnp.concatenate([attn_gain_grad, ffn_gain_grad, query_gain_grad, key_gain_grad])
    gain_total, norm, grad_qkv, grad_out = sum_everywhere(
        gain_sum, early_squares, sums_attn, wide, 13
    )
    global_norm, factor = norm[0, 0], norm[1, 0]
    new_matrices, next_firsts, next_seconds = adam_matrices(
        norm,
        grad_qkv,
        grad_out,
        grad_a,
        grad_b,
        sums_b,
        (w_qkv, w_out, w_gate_up, w_down),
        (first_qkv, first_out, first_gate_up, first_down),
        (second_qkv, second_out, second_gate_up, second_down),
    )
    new_gains, next_first_gains, next_second_gains = adam_step(
        gains, first_gains, second_gains, gain_total, factor, GAIN_RATE, 0.0
    )
    return (
        output_all,
        input_grad,
        global_norm,
        *new_matrices,
        new_gains,
        *next_firsts,
        next_first_gains,
        *next_seconds,
        next_second_gains,
    )


def gather_tokens(rows):
    return lax.all_gather(rows, "fsdp", axis=0, tiled=True)


def scatter_tokens(rows):
    return lax.psum_scatter(
        rows.astype(jnp.bfloat16), "fsdp", scatter_dimension=0, tiled=True
    ).astype(jnp.float32)


def swap(blocks):
    return lax.all_to_all(blocks, "fsdp", split_axis=0, concat_axis=0, tiled=True)


def per_device_plain(
    nf,
    nd,
    tokens,
    cotangent,
    order,
    lengths,
    w_qkv,
    w_out,
    w_gate_up,
    w_down,
    gains,
    first_qkv,
    first_out,
    first_gate_up,
    first_down,
    first_gains,
    second_qkv,
    second_out,
    second_gate_up,
    second_down,
    second_gains,
):
    low = jnp.bfloat16
    kvl = max(KVH // nf, 1)
    rep = max(nf // KVH, 1)
    heads_own = HEADS // nf
    group = heads_own // kvl
    q_width, kv_width = heads_own * HD, kvl * HD
    kv_all = KVH * HD
    hidden_own = FF // nf
    rows_own = w_qkv.shape[0]
    n_mb = nf * MB

    def head_blocks(rows, width):
        return jnp.swapaxes(rows.reshape(rows_own, -1, width), 0, 1)

    qkv_low = w_qkv.astype(low)
    qkv_blocks = jnp.concatenate(
        [
            head_blocks(qkv_low[:, :D], q_width),
            jnp.repeat(head_blocks(qkv_low[:, D : D + kv_all], kv_width), rep, axis=0),
            jnp.repeat(head_blocks(qkv_low[:, D + kv_all :], kv_width), rep, axis=0),
        ],
        axis=2,
    )
    wide = q_width + 2 * kv_width
    own_qkv = lax.all_gather(swap(qkv_blocks), "dp", axis=1, tiled=True).reshape(D, wide)
    own_out = lax.all_gather(w_out.astype(low), "dp", axis=0, tiled=True)
    gate_up_blocks = jnp.transpose(
        w_gate_up.astype(low).reshape(rows_own, 2, nf, hidden_own), (2, 0, 1, 3)
    ).reshape(nf, rows_own, 2 * hidden_own)
    own_gate_up = lax.all_gather(swap(gate_up_blocks), "dp", axis=1, tiled=True).reshape(
        D, 2 * hidden_own
    )
    own_down = lax.all_gather(w_down.astype(low), "dp", axis=0, tiled=True)

    order_row = order[0]
    places = jnp.arange(TOK_DEV, dtype=jnp.int32)
    inverse = jnp.zeros((TOK_DEV,), jnp.int32).at[order_row].set(places)
    rows_in = tokens[order_row].astype(jnp.float32)
    back_rows = cotangent[order_row].astype(jnp.float32)
    attn_gain = gains[:D]
    ffn_gain = gains[D : 2 * D]
    query_gain = gains[2 * D : 2 * D + HD]
    key_gain = gains[2 * D + HD :]
    score_scale = HD ** (-0.5)

    lengths_all = gather_tokens(lengths)
    position, _, allowed = layout(lengths_all)
    _, valid_rows, _ = layout(lengths)
    valid_col = valid_rows.reshape(TOK_DEV, 1)
    allowed = allowed[:, None, None]
    cosine_table, sine_table = rope_tables(position.reshape(-1))

    normed_one, norm_one_pull = jax.vjp(rms_norm, rows_in, attn_gain)
    norm_one_all = gather_tokens(normed_one.astype(low))
    projected = product(norm_one_all, own_qkv)
    n_rows = norm_one_all.shape[0]
    query_raw = projected[:, :q_width].reshape(n_rows, heads_own, HD)
    key_raw = projected[:, q_width : q_width + kv_width].reshape(n_rows, kvl, HD)
    values_low = projected[:, q_width + kv_width :].reshape(n_mb, MB_TOK, kvl, HD).astype(low)

    def turn_heads(query_in, key_in, query_scale, key_scale):
        return (
            rotate(rms_norm(query_in, query_scale), cosine_table, sine_table),
            rotate(rms_norm(key_in, key_scale), cosine_table, sine_table),
        )

    turned, turn_pull = jax.vjp(turn_heads, query_raw, key_raw, query_gain, key_gain)
    queries_low = turned[0].astype(low).reshape(n_mb, MB_TOK, kvl, group, HD)
    keys_low = turned[1].astype(low).reshape(n_mb, MB_TOK, kvl, HD)
    scores = (
        jnp.einsum("mtkgd,mukd->mkgtu", queries_low, keys_low, preferred_element_type=jnp.float32)
        * score_scale
    )
    scores = jnp.where(allowed, scores, MASKED)
    row_peak = jnp.max(scores, axis=-1, keepdims=True)
    powers = jnp.exp(scores - row_peak)
    totals = jnp.sum(powers, axis=-1, keepdims=True)
    probs = powers / totals
    probs_low = probs.astype(low)
    attended = jnp.einsum(
        "mkgtu,mukd->mtkgd", probs_low, values_low, preferred_element_type=jnp.float32
    )
    attended_low = attended.reshape(n_rows, q_width).astype(low)
    hidden = rows_in + valid_col * scatter_tokens(product(attended_low, own_out))

    normed_two, norm_two_pull = jax.vjp(rms_norm, hidden, ffn_gain)
    norm_two_all = gather_tokens(normed_two.astype(low))
    down_back = gather_tokens((valid_col * back_rows).astype(low))
    gate_up = product(norm_two_all, own_gate_up)
    activation, glu_pull = jax.vjp(swiglu, gate_up[:, :hidden_own], gate_up[:, hidden_own:])
    activation_low = activation.astype(low)
    output = hidden + valid_col * scatter_tokens(product(activation_low, own_down))
    gate_back, up_back = glu_pull(contract_last(down_back, own_down))
    gate_up_back = jnp.concatenate([gate_back.astype(low), up_back.astype(low)], axis=1)
    normed_two_grad = scatter_tokens(contract_last(gate_up_back, own_gate_up))
    grad_down = lax.psum_scatter(
        column_product(activation_low, down_back).astype(low),
        "dp",
        scatter_dimension=0,
        tiled=True,
    ).astype(jnp.float32)
    grad_gate_up = lax.psum_scatter(
        column_product(norm_two_all, gate_up_back)
        .astype(low)
        .reshape(nf, nd * rows_own, 2 * hidden_own),
        "dp",
        scatter_dimension=1,
        tiled=True,
    )
    grad_gate_up = jnp.transpose(
        swap(grad_gate_up).reshape(nf, rows_own, 2, hidden_own), (1, 2, 0, 3)
    ).reshape(rows_own, 2 * FF)
    grad_gate_up = grad_gate_up.astype(jnp.float32)
    hidden_norm_grad, ffn_gain_grad = norm_two_pull(normed_two_grad)
    hidden_grad = back_rows + hidden_norm_grad

    branch_back = gather_tokens((valid_col * hidden_grad).astype(low))
    attended_back = contract_last(branch_back, own_out).astype(low)
    grad_out = lax.psum_scatter(
        column_product(attended_low, branch_back).astype(low),
        "dp",
        scatter_dimension=0,
        tiled=True,
    ).astype(jnp.float32)
    attended_five = attended_back.reshape(n_mb, MB_TOK, kvl, group, HD)
    probs_grad = jnp.einsum(
        "mtkgd,mukd->mkgtu", attended_five, values_low, preferred_element_type=jnp.float32
    )
    spread = jnp.sum(probs * probs_grad, axis=-1, keepdims=True)
    score_back = (probs * (probs_grad - spread)).astype(low)
    query_grad = (
        jnp.einsum("mkgtu,mukd->mtkgd", score_back, keys_low, preferred_element_type=jnp.float32)
        * score_scale
    )
    key_grad = (
        jnp.einsum("mkgtu,mtkgd->mukd", score_back, queries_low, preferred_element_type=jnp.float32)
        * score_scale
    )
    value_grad = jnp.einsum(
        "mkgtu,mtkgd->mukd", probs_low, attended_five, preferred_element_type=jnp.float32
    )
    query_in_grad, key_in_grad, query_gain_grad, key_gain_grad = turn_pull(
        (query_grad.reshape(n_rows, heads_own, HD), key_grad.reshape(n_rows, kvl, HD))
    )
    projected_back = jnp.concatenate(
        [
            query_in_grad.reshape(n_rows, q_width),
            key_in_grad.reshape(n_rows, kv_width),
            value_grad.reshape(n_rows, kv_width),
        ],
        axis=1,
    ).astype(low)
    normed_one_grad = scatter_tokens(contract_last(projected_back, own_qkv))
    grad_qkv = lax.psum_scatter(
        column_product(norm_one_all, projected_back)
        .astype(low)
        .reshape(nf, nd * rows_own, wide),
        "dp",
        scatter_dimension=1,
        tiled=True,
    )
    grad_blocks = swap(grad_qkv).astype(jnp.float32)

    def head_rows(blocks, times):
        merged = jnp.sum(blocks.reshape(nf // times, times, rows_own, -1), axis=1)
        return jnp.swapaxes(merged, 0, 1).reshape(rows_own, -1)

    grad_qkv = jnp.concatenate(
        [
            head_rows(grad_blocks[:, :, :q_width], 1),
            head_rows(grad_blocks[:, :, q_width : q_width + kv_width], rep),
            head_rows(grad_blocks[:, :, q_width + kv_width :], rep),
        ],
        axis=1,
    )
    rows_grad, attn_gain_grad = norm_one_pull(normed_one_grad)
    input_grad = (hidden_grad + rows_grad)[inverse]
    output_all = output.astype(low)[inverse]

    owned = (grad_qkv, grad_out, grad_gate_up, grad_down)
    local_squares = (
        jnp.sum(owned[0] * owned[0])
        + jnp.sum(owned[1] * owned[1])
        + jnp.sum(owned[2] * owned[2])
        + jnp.sum(owned[3] * owned[3])
    )
    gain_sum = jnp.concatenate([attn_gain_grad, ffn_gain_grad, query_gain_grad, key_gain_grad])
    gain_total, square_total = lax.psum((gain_sum, local_squares), ("fsdp", "dp"))
    global_norm = jnp.sqrt(square_total + jnp.sum(gain_total * gain_total))
    factor = CLIP_NORM / jnp.maximum(global_norm, CLIP_NORM)
    new_qkv, next_first_qkv, next_second_qkv = adam_step(
        w_qkv, first_qkv, second_qkv, owned[0], factor, LEARN_RATE, WEIGHT_DECAY
    )
    new_out, next_first_out, next_second_out = adam_step(
        w_out, first_out, second_out, owned[1], factor, LEARN_RATE, WEIGHT_DECAY
    )
    new_gate_up, next_first_gate_up, next_second_gate_up = adam_step(
        w_gate_up, first_gate_up, second_gate_up, owned[2], factor, LEARN_RATE, WEIGHT_DECAY
    )
    new_down, next_first_down, next_second_down = adam_step(
        w_down, first_down, second_down, owned[3], factor, LEARN_RATE, WEIGHT_DECAY
    )
    new_gains, next_first_gains, next_second_gains = adam_step(
        gains, first_gains, second_gains, gain_total, factor, GAIN_RATE, 0.0
    )
    return (
        output_all,
        input_grad,
        global_norm,
        new_qkv,
        new_out,
        new_gate_up,
        new_down,
        new_gains,
        next_first_qkv,
        next_first_out,
        next_first_gate_up,
        next_first_down,
        next_first_gains,
        next_second_qkv,
        next_second_out,
        next_second_gate_up,
        next_second_down,
        next_second_gains,
    )


def solution(mesh):
    nf, nd = mesh.shape["fsdp"], mesh.shape["dp"]
    fits = nf == PLANE and KVH == PLANE and nd > 1 and FF // nf % (256 * nd) == 0
    per_device = per_device_plane if fits else per_device_plain
    in_specs = (
        P(("fsdp", "dp"), None),
        P(("fsdp", "dp"), None),
        P(("fsdp", "dp"), None),
        P(("fsdp", "dp"), None),
        P(("fsdp", "dp"), None),
        P(("fsdp", "dp"), None),
        P(("fsdp", "dp"), None),
        P(("fsdp", "dp"), None),
        P(),
        P(("fsdp", "dp"), None),
        P(("fsdp", "dp"), None),
        P(("fsdp", "dp"), None),
        P(("fsdp", "dp"), None),
        P(),
        P(("fsdp", "dp"), None),
        P(("fsdp", "dp"), None),
        P(("fsdp", "dp"), None),
        P(("fsdp", "dp"), None),
        P(),
    )
    out_specs = (
        P(("fsdp", "dp"), None),
        P(("fsdp", "dp"), None),
        P(),
        P(("fsdp", "dp"), None),
        P(("fsdp", "dp"), None),
        P(("fsdp", "dp"), None),
        P(("fsdp", "dp"), None),
        P(),
        P(("fsdp", "dp"), None),
        P(("fsdp", "dp"), None),
        P(("fsdp", "dp"), None),
        P(("fsdp", "dp"), None),
        P(),
        P(("fsdp", "dp"), None),
        P(("fsdp", "dp"), None),
        P(("fsdp", "dp"), None),
        P(("fsdp", "dp"), None),
        P(),
    )
    return jax.shard_map(
        functools.partial(per_device, nf, nd), mesh=mesh, in_specs=in_specs, out_specs=out_specs, check_vma=False
    )
```
